32 devices in a mesh: replica: 8 (over z, core), mp: 4 (over y, x).
Axes of the slice: x: 2, y: 2, z: 4, core: 2. Of those that a mesh axis runs over, the one named last changes fastest.
Arguments:
- gradients: bfloat16 [8, 8, 768, 3072], P('replica', None, 'mp'), may hold values from -6 to 6
- feedback: bfloat16 [8, 8, 768, 3072], P('replica', None, 'mp'), may hold values from -4 to 4
- right_init: bfloat16 [8, 3072, 32], replicated, may hold values from -0.109375 to 0.109375
- gram_root: float32 [8, 32, 32], replicated, as said below
- owners: int32 [8], replicated, may hold values from 0 to 3, as said below
- momentum: float32 [4, 2, 768, 3072], P('mp', None, 'replica'), may hold values from -4 to 4
- master_weights: float32 [4, 2, 768, 3072], P('mp', None, 'replica'), may hold values from -1.5 to 1.5
- vector_grads: float32 [8, 10752], P('replica', 'mp'), may hold values from -6 to 6
- vector_momentum: float32 [10752], P('mp'), may hold values from -6 to 6
- vector_params: float32 [10752], P('mp'), may hold values from -6 to 6
Outputs:
- new_feedback: bfloat16 [8, 8, 768, 3072], P('replica', None, 'mp')
- new_momentum: float32 [4, 2, 768, 3072], P('mp', None, 'replica')
- new_master: float32 [4, 2, 768, 3072], P('mp', None, 'replica')
- new_weights: bfloat16 [8, 768, 3072], P(None, 'replica')
- new_vector_momentum: float32 [10752], P('mp')
- new_vector_params: float32 [10752], P('mp')
The draws below stay inside these ranges and needn't reach their ends.
Inputs may be any that keep to these rules, and one draw needn't show every extreme that they name: `owners`: every matrix has one owner; no owner holds more than 2 of the 8 matrices, and one owner holds exactly 2. `gram_root`: each matrix is the identity plus off-diagonal terms, times a positive scale.
All inputs are finite; a program needn't handle non-finite values.
Results may differ from the reference program's by a relative error of at most 0.007.
Values may be sent and summed in bfloat16 or wider, within the bound.
No kernel may reach another device: no remote copies, remote signals or barrier semaphores. Data moves between devices by JAX's collectives and lax.ppermute only.
A program may use at most 192 MiB of HBM per device.

```python
import jax
import jax.numpy as jnp
from jax import lax

M = 768
N = 3072
RANK = 32
NMAT = 8
CAP = 2
NVEC = 10752
N_REPLICA = 8
N_MP = 4


def draw_owners(key, part):
    slot_key = jax.random.fold_in(key, 11)
    chosen = jax.random.permutation(slot_key, N_MP * CAP)[:NMAT]
    return (chosen // CAP).astype(jnp.int32)


def draw_gram_root(key, part):
    base_key = jax.random.fold_in(key, 23)
    spread = 0.5 * jax.random.normal(base_key, (NMAT, RANK, RANK), jnp.float32)
    eye = jnp.eye(RANK, dtype=jnp.float32)
    matrix = eye[None] + (1.0 - eye[None]) * spread * RANK ** (-0.5)
    return (matrix * (M * N_REPLICA) ** (-0.5)).astype(jnp.float32)


def steps_of(own_key, extent, pieces, smallest, high):
    def one(dim, shards_of):
        draws = jax.random.uniform(jax.random.fold_in(jax.random.fold_in(own_key, 6), dim), (shards_of,), jnp.float32, smallest / len(pieces), high / len(pieces))
        return jnp.repeat(jnp.exp(draws), extent[dim] // shards_of).reshape((-1,) + (1,) * (len(extent) - dim - 1))

    gain = one(*pieces[0])
    for cut in pieces[1:]:
        gain = gain * one(*cut)
    return gain


def centred(key, extent, deviation, most, pieces=(), kind=jnp.bfloat16):
    drawn = deviation * jax.random.normal(key, extent, jnp.float32)
    if pieces:
        drawn = drawn * steps_of(key, extent, pieces, -0.22, 0.18)
    return jnp.clip(drawn, -most, most).astype(kind)


def setup_inputs(seed: int = 0) -> dict:
    arg_keys = jax.random.split(jax.random.key(seed), 11)
    return {
        "gradients": centred(arg_keys[0], (N_REPLICA, NMAT, M, N), 1.0, 6.0, ((0, 8), (2, 4))),
        "feedback": centred(arg_keys[1], (N_REPLICA, NMAT, M, N), 0.3, 4.0, ((0, 8), (2, 4))),
        "right_init": centred(arg_keys[2], (NMAT, N, RANK), N ** -0.5, 0.109375),
        "gram_root": draw_gram_root(jax.random.fold_in(arg_keys[10], 71), 0),
        "owners": draw_owners(jax.random.fold_in(arg_keys[10], 71), 0),
        "momentum": centred(arg_keys[5], (N_MP, CAP, M, N), 0.3, 4.0, ((0, 4), (2, 8)), jnp.float32),
        "master_weights": centred(arg_keys[6], (N_MP, CAP, M, N), 0.1, 1.5, ((0, 4), (2, 8)), jnp.float32),
        "vector_grads": centred(arg_keys[7], (N_REPLICA, NVEC), 1.0, 6.0, ((0, 8), (1, 4)), jnp.float32),
        "vector_momentum": centred(arg_keys[8], (NVEC,), 1.0, 6.0, ((0, 4),), jnp.float32),
        "vector_params": centred(arg_keys[9], (NVEC,), 1.0, 6.0, ((0, 4),), jnp.float32),
    }


def reference(gradients, feedback, right_init, gram_root, owners, momentum, master_weights, vector_grads, vector_momentum, vector_params):
    highest = lax.Precision.HIGHEST
    replicas = gradients.shape[0]

    def compensated_of(index):
        return (gradients[index].astype(jnp.float32) + feedback[index].astype(jnp.float32)).astype(jnp.bfloat16)

    right_wide = right_init.astype(jnp.float32)

    def left_step(total, index):
        wide = compensated_of(index).astype(jnp.float32)
        return total + jnp.einsum("kmn,knr->kmr", wide, right_wide), None

    left_sum, _ = lax.scan(left_step, jnp.zeros((NMAT, M, RANK), jnp.float32), jnp.arange(replicas))
    left_hat = jnp.einsum("kmr,krs->kms", left_sum, gram_root, precision=highest).astype(jnp.bfloat16)
    left_wide = left_hat.astype(jnp.float32)

    def right_step(total, index):
        wide = compensated_of(index).astype(jnp.float32)
        return total + jnp.einsum("kmn,kms->kns", wide, left_wide), None

    right_new, _ = lax.scan(right_step, jnp.zeros((NMAT, N, RANK), jnp.float32), jnp.arange(replicas))
    approx = jnp.einsum("kms,kns->kmn", left_wide, right_new, precision=highest)
    new_feedback = lax.map(lambda index: (compensated_of(index).astype(jnp.float32) - approx).astype(jnp.bfloat16), jnp.arange(replicas))

    same_owner = owners[:, None] == owners[None, :]
    earlier = jnp.arange(NMAT)[:, None] < jnp.arange(NMAT)[None, :]
    ranks = jnp.sum((same_owner & earlier).astype(jnp.int32), axis=0)
    slots = owners * CAP + ranks
    slot_table = (slots[None, :] == jnp.arange(N_MP * CAP)[:, None]).astype(jnp.float32)
    approx_slots = jnp.einsum("sk,kmn->smn", slot_table, approx, precision=highest).reshape(N_MP, CAP, M, N)
    new_momentum = 0.9 * momentum + approx_slots
    new_master = master_weights - 0.1 * new_momentum
    new_weights = jnp.einsum("sk,smn->kmn", slot_table, new_master.reshape(N_MP * CAP, M, N), precision=highest).astype(jnp.bfloat16)
    vector_total = jnp.sum(vector_grads, axis=0)
    new_vector_momentum = 0.9 * vector_momentum + vector_total
    new_vector_params = vector_params - 0.1 * new_vector_momentum
    return new_feedback, new_momentum, new_master, new_weights, new_vector_momentum, new_vector_params
```

```python
import functools

import jax
import jax.numpy as jnp
from jax import lax
from jax.experimental import pallas as pl
from jax.experimental.pallas import tpu as pltpu
from jax.sharding import PartitionSpec as P

CORES = 2
LANES = 128
VMEM_LIMIT = 48 * 1024 * 1024
F32 = jnp.float32
BF16 = jnp.bfloat16


def params():
    return pltpu.CompilerParams(vmem_limit_bytes=VMEM_LIMIT)


def tree_sum(terms):
    while len(terms) > 1:
        terms = [terms[i] + terms[i + 1] for i in range(0, len(terms), 2)]
    return terms[0]


def exchange(x, axis, distance):
    size = lax.axis_size(axis)
    return lax.ppermute(x, axis, [(i, i ^ distance) for i in range(size)])


def left_kernel(g_ref, f_ref, q_ref, vec_ref, comp_ref, left_ref):
    k = pl.program_id(0)
    rows = g_ref.shape[2]
    rank = q_ref.shape[1]
    group = LANES // rank

    @pl.when(k == 0)
    def _():
        left_ref[:rows, :] = jnp.zeros((rows, left_ref.shape[1]), F32)
        left_ref[rows:, :] = vec_ref[...]

    comp = (g_ref[0, 0].astype(F32) + f_ref[0, 0].astype(F32)).astype(BF16)
    comp_ref[0] = comp
    q = q_ref[0]
    wide = jnp.concatenate([q] * group, axis=0)
    member = lax.broadcasted_iota(jnp.int32, wide.shape, 0) // rank
    wide = jnp.where(member == k % group, wide, jnp.zeros_like(wide))
    terms = lax.dot_general(comp, wide, (((1,), (1,)), ((), ())), preferred_element_type=F32)
    cols = pl.ds(pl.multiple_of((k // group) * LANES, LANES), LANES)
    left_ref[:rows, cols] += terms


def left_terms(gradients, feedback, right_t, vec):
    _, nmat, rows, n = gradients.shape
    rank = right_t.shape[1]
    total = rows + vec.shape[0]
    return pl.pallas_call(
        left_kernel,
        grid=(nmat,),
        in_specs=[
            pl.BlockSpec((1, 1, rows, n), lambda k: (0, k, 0, 0)),
            pl.BlockSpec((1, 1, rows, n), lambda k: (0, k, 0, 0)),
            pl.BlockSpec((1, rank, n), lambda k: (k, 0, 0)),
            pl.BlockSpec(vec.shape, lambda k: (0, 0)),
        ],
        out_specs=[
            pl.BlockSpec((1, rows, n), lambda k: (k, 0, 0)),
            pl.BlockSpec((total, nmat * rank), lambda k: (0, 0)),
        ],
        out_shape=[
            jax.ShapeDtypeStruct((nmat, rows, n), BF16),
            jax.ShapeDtypeStruct((total, nmat * rank), F32),
        ],
        compiler_params=params(),
        cost_estimate=pl.CostEstimate(
            flops=2 * nmat * rows * n * LANES, bytes_accessed=6 * nmat * rows * n, transcendentals=0
        ),
        name="left_terms",
    )(gradients, feedback, right_t, vec)


def right_kernel(half, pos, mine_ref, other_ref, gram_ref, comp_ref, send_ref, keep_ref, lt_ref, left):
    t = pl.program_id(0)
    rows = comp_ref.shape[1]
    part = mine_ref.shape[0]
    upm, unit = send_ref.shape[1], send_ref.shape[2]
    rank = upm * unit

    @pl.when(t == 0)
    def _():
        left[pl.ds(pl.multiple_of(pos[2] * part, 8), part), :] = mine_ref[...]
        left[pl.ds(pl.multiple_of((1 - pos[2]) * part, 8), part), :] = other_ref[...]
        hat = jnp.dot(
            left[:rows, :], gram_ref[...], precision=lax.Precision.HIGHEST, preferred_element_type=F32
        )
        lt_ref[...] = hat.T.astype(BF16)

    k = lax.rem(t + half, 2 * half) ^ pos[0]
    lt = lt_ref[pl.ds(pl.multiple_of(k * rank, rank), rank), :]
    terms = jnp.dot(lt, comp_ref[0], preferred_element_type=F32)

    @pl.when(t < half)
    def _():
        for i in range(upm):
            send_ref[0, i ^ pos[1]] = terms[i * unit : (i + 1) * unit].astype(BF16)

    @pl.when(t >= half)
    def _():
        for i in range(upm):
            keep_ref[0, i ^ pos[1]] = terms[i * unit : (i + 1) * unit]


def right_terms(pos, mine, other, gram, comp, upm):
    nmat, rows, n = comp.shape
    rank = gram.shape[0] // nmat
    unit = rank // upm
    half = nmat // 2
    return pl.pallas_call(
        functools.partial(right_kernel, half),
        grid_spec=pltpu.PrefetchScalarGridSpec(
            num_scalar_prefetch=1,
            grid=(nmat,),
            in_specs=[
                pl.BlockSpec(mine.shape, lambda t, pos: (0, 0)),
                pl.BlockSpec(other.shape, lambda t, pos: (0, 0)),
                pl.BlockSpec(gram.shape, lambda t, pos: (0, 0)),
                pl.BlockSpec((1, rows, n), lambda t, pos: (lax.rem(t + half, nmat) ^ pos[0], 0, 0)),
            ],
            out_specs=[
                pl.BlockSpec((1, upm, unit, n), lambda t, pos: (jnp.minimum(t, half - 1), 0, 0, 0)),
                pl.BlockSpec((1, upm, unit, n), lambda t, pos: (jnp.maximum(t - half, 0), 0, 0, 0)),
                pl.BlockSpec((nmat * rank, rows), lambda t, pos: (0, 0)),
            ],
            scratch_shapes=[pltpu.VMEM((2 * mine.shape[0], mine.shape[1]), F32)],
        ),
        out_shape=[
            jax.ShapeDtypeStruct((half, upm, unit, n), BF16),
            jax.ShapeDtypeStruct((half, upm, unit, n), F32),
            jax.ShapeDtypeStruct((nmat * rank, rows), BF16),
        ],
        compiler_params=params(),
        cost_estimate=pl.CostEstimate(
            flops=2 * nmat * rows * n * LANES, bytes_accessed=2 * nmat * rows * n, transcendentals=0
        ),
        name="right_terms",
    )(pos, mine, other, gram, comp)


def matrix_of(right_ref, sub):
    upm = right_ref.shape[1]
    parts = [right_ref[0, i ^ sub] for i in range(upm)]
    return parts[0] if upm == 1 else jnp.concatenate(parts, axis=0)


def product(lt, right):
    return lax.dot_general(lt, right, (((0,), (0,)), ((), ())), preferred_element_type=F32)


def outputs_kernel(pos, comp_ref, right_ref, lt_ref, ltr_ref, base_ref, *refs):
    feedback_ref, weights_ref = refs[-2:]
    right = matrix_of(right_ref, pos[1])
    feedback_ref[0, 0] = (comp_ref[0].astype(F32) - product(lt_ref[...], right)).astype(BF16)
    weights_ref[0] = (base_ref[0].astype(F32) - 0.1 * product(ltr_ref[...], right)).astype(BF16)


def outputs(pos, start, comp, right, lt, ltr, base, earlier):
    nmat, rows, n = comp.shape
    rank = lt.shape[0] // nmat
    half, upm, unit, _ = right.shape
    replica_rows = base.shape[1]

    def matrix(j, pos):
        return (j + start) ^ pos[0]

    any_spec = pl.BlockSpec(memory_space=pl.ANY)
    return pl.pallas_call(
        outputs_kernel,
        grid_spec=pltpu.PrefetchScalarGridSpec(
            num_scalar_prefetch=1,
            grid=(half,),
            in_specs=[
                pl.BlockSpec((1, rows, n), lambda j, pos: (matrix(j, pos), 0, 0)),
                pl.BlockSpec((1, upm, unit, n), lambda j, pos: (j, 0, 0, 0)),
                pl.BlockSpec((rank, rows), lambda j, pos: (matrix(j, pos), 0)),
                pl.BlockSpec((rank, replica_rows), lambda j, pos: (matrix(j, pos), 0)),
                pl.BlockSpec((1, replica_rows, n), lambda j, pos: (pos[3 + matrix(j, pos)], 0, 0)),
            ]
            + [any_spec] * len(earlier),
            out_specs=[
                pl.BlockSpec((1, 1, rows, n), lambda j, pos: (0, matrix(j, pos), 0, 0)),
                pl.BlockSpec((1, replica_rows, n), lambda j, pos: (matrix(j, pos), 0, 0)),
            ],
        ),
        out_shape=[
            jax.ShapeDtypeStruct((1, nmat, rows, n), BF16),
            jax.ShapeDtypeStruct((nmat, replica_rows, n), BF16),
        ],
        input_output_aliases={6 + i: i for i in range(len(earlier))},
        compiler_params=params(),
        cost_estimate=pl.CostEstimate(
            flops=2 * half * (rows + replica_rows) * n * LANES,
            bytes_accessed=4 * half * (rows + replica_rows) * n,
            transcendentals=0,
        ),
        name="outputs",
    )(pos, comp, right, lt, ltr, base, *earlier)


def owned_kernel(half, held, pos, momentum_ref, master_ref, near_ref, far_ref, ltr_ref, new_momentum_ref, new_master_ref):
    c = pl.program_id(0)
    matrix = pos[held + c]
    near = matrix_of(near_ref, pos[1])
    far = matrix_of(far_ref, pos[1])
    slot = jnp.maximum(matrix, 0) ^ pos[0]
    right = jnp.where(slot < half, near, far)
    approx = jnp.where(matrix >= 0, product(ltr_ref[...], right), 0.0)
    momentum = 0.9 * momentum_ref[0, 0] + approx
    new_momentum_ref[0, 0] = momentum
    new_master_ref[0, 0] = master_ref[0, 0] - 0.1 * momentum


def owned(pos, held, momentum, master, near, far, ltr):
    _, capacity, rows, n = momentum.shape
    half, upm, unit, _ = near.shape
    rank = upm * unit

    def matrix(c, pos):
        return jnp.maximum(pos[held + c], 0)

    state = pl.BlockSpec((1, 1, rows, n), lambda c, pos: (0, c, 0, 0))
    right = pl.BlockSpec((1, upm, unit, n), lambda c, pos: (lax.rem(matrix(c, pos) ^ pos[0], half), 0, 0, 0))
    return pl.pallas_call(
        functools.partial(owned_kernel, half, held),
        grid_spec=pltpu.PrefetchScalarGridSpec(
            num_scalar_prefetch=1,
            grid=(capacity,),
            in_specs=[
                state,
                state,
                right,
                right,
                pl.BlockSpec((rank, rows), lambda c, pos: (matrix(c, pos), 0)),
            ],
            out_specs=[state, state],
        ),
        out_shape=[jax.ShapeDtypeStruct(momentum.shape, F32)] * 2,
        compiler_params=params(),
        cost_estimate=pl.CostEstimate(
            flops=2 * capacity * rows * n * LANES, bytes_accessed=16 * capacity * rows * n, transcendentals=0
        ),
        name="owned",
    )(pos, momentum, master, near, far, ltr)


def per_device(
    gradients,
    feedback,
    right_init,
    gram_root,
    owners,
    momentum,
    master_weights,
    vector_grads,
    vector_momentum,
    vector_params,
):
    nmat, rows, n = gradients.shape[1:]
    rank = right_init.shape[2]
    n_mp = lax.axis_size("mp")
    n_z = lax.axis_size("replica") // CORES
    capacity, replica_rows = momentum.shape[1:3]
    p = lax.axis_index("mp")
    r = lax.axis_index("replica")
    core, z = r % CORES, r // CORES
    upm = CORES * n_mp // nmat
    half = nmat // CORES
    code = core * n_mp + p

    base = (master_weights[0] - 0.09 * momentum[0]).astype(BF16)
    base_all = jnp.concatenate([base] + [exchange(base, "mp", d) for d in range(1, n_mp)], axis=0)

    same_owner = owners[:, None] == owners[None, :]
    earlier = jnp.arange(nmat)[:, None] < jnp.arange(nmat)[None, :]
    ranks = jnp.sum((same_owner & earlier).astype(jnp.int32), axis=0)
    relative = (owners ^ p) * capacity + ranks
    mine = relative[None, :] == jnp.arange(capacity)[:, None]
    held = jnp.max(jnp.where(mine, jnp.arange(nmat)[None, :], -1), axis=1)
    pos = jnp.concatenate([jnp.stack([code // upm, code % upm, core]), relative, held]).astype(jnp.int32)

    nvec = vector_grads.shape[1]
    width = nmat * rank
    vec = jnp.pad(vector_grads[0], (0, 16 * width - nvec)).reshape(16, width)
    comp, terms = left_terms(gradients, feedback, jnp.swapaxes(right_init, 1, 2), vec)
    chip = terms + exchange(terms, "replica", 1)
    part = terms.shape[0] // CORES
    piece = lax.dynamic_slice_in_dim(chip, core * part, part, 0)
    piece = tree_sum([piece] + [exchange(piece, "replica", CORES * d) for d in range(1, n_z)])
    other = exchange(piece, "replica", 1)
    vector_half = jnp.where(core == 1, piece, other)
    vector_total = vector_half[part - 16 :].reshape(-1)[:nvec]

    block = jnp.eye(nmat, dtype=bool)[:, None, :, None]
    gram = jnp.where(block, gram_root[:, :, None, :], 0.0).reshape(width, width)
    send, keep, lt = right_terms(pos, piece, other, gram, comp, upm)
    chip = keep + exchange(send, "replica", 1).astype(F32)
    chip = chip.reshape(n_mp, rank // upm, n)
    narrow = chip.astype(BF16)
    plane = tree_sum([chip[0]] + [exchange(narrow[d], "mp", d).astype(F32) for d in range(1, n_mp)])
    cols = n // n_z
    plane_narrow = plane.astype(BF16)
    final = [lax.dynamic_slice_in_dim(plane, z * cols, cols, 1)]
    for d in range(1, n_z):
        sent = lax.dynamic_slice_in_dim(plane_narrow, (z ^ d) * cols, cols, 1)
        final.append(exchange(sent, "replica", CORES * d).astype(F32))
    final = tree_sum(final).astype(BF16)

    whole = jnp.zeros((rank // upm, n), BF16)
    whole = lax.dynamic_update_slice_in_dim(whole, final, z * cols, 1)
    for d in range(1, n_z):
        whole = lax.dynamic_update_slice_in_dim(
            whole, exchange(final, "replica", CORES * d), (z ^ d) * cols, 1
        )
    near = jnp.stack([whole] + [exchange(whole, "mp", d) for d in range(1, n_mp)])
    near = near.reshape(half, upm, rank // upm, n)
    far = exchange(near, "replica", 1)

    first = r * replica_rows
    strip = lax.dynamic_slice_in_dim(lt, first % rows, replica_rows, 1)
    strips = jnp.stack([strip] + [exchange(strip, "mp", d) for d in range(1, n_mp)])
    ltr = lax.dynamic_index_in_dim(strips, (first // rows) ^ p, 0, keepdims=False)

    done = outputs(pos, 0, comp, near, lt, ltr, base_all, ())
    new_feedback, new_weights = outputs(pos, half, comp, far, lt, ltr, base_all, done)
    new_momentum, new_master = owned(pos, 3 + nmat, momentum, master_weights, near, far, ltr)

    new_vector_momentum = 0.9 * vector_momentum + vector_total
    new_vector_params = vector_params - 0.1 * new_vector_momentum
    return new_feedback, new_momentum, new_master, new_weights, new_vector_momentum, new_vector_params


def solution(mesh):
    return jax.shard_map(
        per_device,
        mesh=mesh,
        in_specs=(
            P("replica", None, "mp", None),
            P("replica", None, "mp", None),
            P(),
            P(),
            P(),
            P("mp", None, "replica", None),
            P("mp", None, "replica", None),
            P("replica", "mp"),
            P("mp"),
            P("mp"),
        ),
        out_specs=(
            P("replica", None, "mp", None),
            P("mp", None, "replica", None),
            P("mp", None, "replica", None),
            P(None, "replica", None),
            P("mp"),
            P("mp"),
        ),
        check_vma=False,
    )
```

```python
import functools

import jax
import jax.numpy as jnp
from jax import lax
from jax.experimental import pallas as pl
from jax.experimental.pallas import tpu as pltpu
from jax.sharding import PartitionSpec as P

CORES = 2
LANES = 128
PLACES = 5
VMEM_LIMIT = 24 * 1024 * 1024
F32 = jnp.float32
BF16 = jnp.bfloat16


def params():
    return pltpu.CompilerParams(vmem_limit_bytes=VMEM_LIMIT)


def cost():
    return pl.CostEstimate(flops=1000, bytes_accessed=1000, transcendentals=0)


def tree_sum(terms):
    while len(terms) > 1:
        terms = [terms[i] + terms[i + 1] for i in range(0, len(terms), 2)]
    return terms[0]


def exchange(x, axis, distance):
    size = lax.axis_size(axis)
    return lax.ppermute(x, axis, [(i, i ^ distance) for i in range(size)])


def left_kernel(pos, g_ref, f_ref, q_ref, vec_ref, comp_ref, near_ref, far_ref, total):
    k = pl.program_id(0)
    rows = g_ref.shape[2]
    rank = q_ref.shape[1]
    group = LANES // rank
    near, piece, _ = near_ref.shape

    @pl.when(k == 0)
    def _():
        total[:rows, :] = jnp.zeros((rows, total.shape[1]), F32)
        total[rows:, :] = vec_ref[...]

    comp = (g_ref[0, 0].astype(F32) + f_ref[0, 0].astype(F32)).astype(BF16)
    comp_ref[0] = comp
    q = q_ref[0]
    wide = jnp.concatenate([q] * group, axis=0)
    member = lax.broadcasted_iota(jnp.int32, wide.shape, 0) // rank
    wide = jnp.where(member == k % group, wide, jnp.zeros_like(wide))
    terms = lax.dot_general(comp, wide, (((1,), (1,)), ((), ())), preferred_element_type=F32)
    cols = pl.ds(pl.multiple_of((k // group) * LANES, LANES), LANES)
    total[:rows, cols] += terms

    @pl.when(k == pl.num_programs(0) - 1)
    def _():
        for s in range(near):
            for out, slot in ((near_ref, s), (far_ref, s + near)):
                out[s] = total[pl.ds(pl.multiple_of((slot ^ pos[3]) * piece, piece), piece), :]


def left_terms(pos, gradients, feedback, right_t, vec, n_z):
    _, nmat, rows, n = gradients.shape
    rank = right_t.shape[1]
    width = nmat * rank
    total = rows + vec.shape[0]
    pieces = jax.ShapeDtypeStruct((n_z, total // (CORES * n_z), width), F32)
    return pl.pallas_call(
        left_kernel,
        grid_spec=pltpu.PrefetchScalarGridSpec(
            num_scalar_prefetch=1,
            grid=(nmat,),
            in_specs=[
                pl.BlockSpec((1, 1, rows, n), lambda k, pos: (0, k, 0, 0)),
                pl.BlockSpec((1, 1, rows, n), lambda k, pos: (0, k, 0, 0)),
                pl.BlockSpec((1, rank, n), lambda k, pos: (k, 0, 0)),
                pl.BlockSpec(vec.shape, lambda k, pos: (0, 0)),
            ],
            out_specs=[
                pl.BlockSpec((1, rows, n), lambda k, pos: (k, 0, 0)),
                pl.BlockSpec(pieces.shape, lambda k, pos: (0, 0, 0)),
                pl.BlockSpec(pieces.shape, lambda k, pos: (0, 0, 0)),
            ],
            scratch_shapes=[pltpu.VMEM((total, width), F32)],
        ),
        out_shape=[jax.ShapeDtypeStruct((nmat, rows, n), BF16), pieces, pieces],
        compiler_params=params(),
        cost_estimate=cost(),
        name="left_terms",
    )(pos, gradients, feedback, right_t, vec)


def right_kernel(half, pos, near_ref, far_ref, gram_ref, comp_ref, *refs):
    send_ref, keep_ref, lt_ref, vec_ref, left = refs[-5:]
    t = pl.program_id(0)
    rows = comp_ref.shape[1]
    upm, unit = send_ref.shape[1], send_ref.shape[2]
    rank = upm * unit

    @pl.when(t == 0)
    def _():
        near, piece, _ = near_ref.shape
        for s in range(near):
            for part, slot in ((near_ref, s), (far_ref, s + near)):
                left[pl.ds(pl.multiple_of((slot ^ pos[3]) * piece, piece), piece), :] = part[s]
        vec_ref[...] = left[rows:, :]
        hat = jnp.dot(
            left[:rows, :], gram_ref[...], precision=lax.Precision.HIGHEST, preferred_element_type=F32
        )
        lt_ref[...] = hat.T.astype(BF16)

    k = lax.rem(t + half, 2 * half) ^ pos[0]
    lt = lt_ref[pl.ds(pl.multiple_of(k * rank, rank), rank), :]
    terms = jnp.dot(lt, comp_ref[0], preferred_element_type=F32)

    @pl.when(t < half)
    def _():
        for i in range(upm):
            send_ref[0, i ^ pos[1]] = terms[i * unit : (i + 1) * unit].astype(BF16)

    @pl.when(t >= half)
    def _():
        for i in range(upm):
            keep_ref[0, i ^ pos[1]] = terms[i * unit : (i + 1) * unit]


def right_terms(pos, near, far, gram, comp, upm, after):
    nmat, rows, n = comp.shape
    rank = gram.shape[0] // nmat
    unit = rank // upm
    half = nmat // CORES
    total = CORES * near.shape[0] * near.shape[1]
    return pl.pallas_call(
        functools.partial(right_kernel, half),
        grid_spec=pltpu.PrefetchScalarGridSpec(
            num_scalar_prefetch=1,
            grid=(nmat,),
            in_specs=[
                pl.BlockSpec(near.shape, lambda t, pos: (0, 0, 0)),
                pl.BlockSpec(far.shape, lambda t, pos: (0, 0, 0)),
                pl.BlockSpec(gram.shape, lambda t, pos: (0, 0)),
                pl.BlockSpec((1, rows, n), lambda t, pos: (lax.rem(t + half, nmat) ^ pos[0], 0, 0)),
            ]
            + [pl.BlockSpec(memory_space=pl.ANY)] * len(after),
            out_specs=[
                pl.BlockSpec((1, upm, unit, n), lambda t, pos: (jnp.minimum(t, half - 1), 0, 0, 0)),
                pl.BlockSpec((1, upm, unit, n), lambda t, pos: (jnp.maximum(t - half, 0), 0, 0, 0)),
                pl.BlockSpec((nmat * rank, rows), lambda t, pos: (0, 0)),
                pl.BlockSpec((total - rows, nmat * rank), lambda t, pos: (0, 0)),
            ],
            scratch_shapes=[pltpu.VMEM((total, nmat * rank), F32)],
        ),
        out_shape=[
            jax.ShapeDtypeStruct((half, upm, unit, n), BF16),
            jax.ShapeDtypeStruct((half, upm, unit, n), F32),
            jax.ShapeDtypeStruct((nmat * rank, rows), BF16),
            jax.ShapeDtypeStruct((total - rows, nmat * rank), F32),
        ],
        compiler_params=params(),
        cost_estimate=cost(),
        name="right_terms",
    )(pos, near, far, gram, comp, *after)


def chip_kernel(keep_ref, recv_ref, *refs):
    n_out = keep_ref.shape[0] * keep_ref.shape[1]
    upm = keep_ref.shape[1]
    for d, out in enumerate(refs[-n_out:]):
        j, i = d // upm, d % upm
        out[...] = (keep_ref[j, i] + recv_ref[j, i].astype(F32)).astype(out.dtype)


def chip_sum(keep, recv, after):
    half, upm, unit, n = keep.shape
    vmem = pl.BlockSpec(memory_space=pltpu.VMEM)
    return pl.pallas_call(
        chip_kernel,
        in_specs=[vmem] * 2 + [pl.BlockSpec(memory_space=pl.ANY)] * len(after),
        out_specs=[vmem] * (half * upm),
        out_shape=[jax.ShapeDtypeStruct((unit, n), BF16 if d else F32) for d in range(half * upm)],
        compiler_params=params(),
        cost_estimate=cost(),
        name="chip_sum",
    )(keep, recv, *after)


def column_kernel(n_z, pos, *refs):
    out = refs[-1]
    cols = out.shape[1] // n_z
    for d in range(n_z):
        out[:, pl.ds(pl.multiple_of((pos[4] ^ d) * cols, cols), cols)] = refs[d][...]


def column_gather(pos, parts, after):
    unit, cols = parts[0].shape
    vmem = pl.BlockSpec(memory_space=pltpu.VMEM)
    return pl.pallas_call(
        functools.partial(column_kernel, len(parts)),
        grid_spec=pltpu.PrefetchScalarGridSpec(
            num_scalar_prefetch=1,
            grid=(1,),
            in_specs=[vmem] * len(parts) + [pl.BlockSpec(memory_space=pl.ANY)] * len(after),
            out_specs=vmem,
        ),
        out_shape=jax.ShapeDtypeStruct((unit, cols * len(parts)), BF16),
        compiler_params=params(),
        cost_estimate=cost(),
        name="column_gather",
    )(pos, *parts, *after)


def plane_kernel(count, n_z, pos, *refs):
    terms, outs = refs[:count], refs[-n_z:]
    cols = outs[0].shape[1]
    for d, out in enumerate(outs):
        block = pl.ds(pl.multiple_of((pos[4] ^ d) * cols, cols), cols)
        out[...] = tree_sum([term[:, block].astype(F32) for term in terms]).astype(out.dtype)


def plane_sum(pos, terms, n_z):
    unit, n = terms[0].shape
    cols = n // n_z
    whole = pl.BlockSpec((unit, n), lambda i, pos: (0, 0))
    part = pl.BlockSpec((unit, cols), lambda i, pos: (0, 0))
    return pl.pallas_call(
        functools.partial(plane_kernel, len(terms), n_z),
        grid_spec=pltpu.PrefetchScalarGridSpec(
            num_scalar_prefetch=1,
            grid=(1,),
            in_specs=[whole] * len(terms),
            out_specs=[part] * n_z,
        ),
        out_shape=[jax.ShapeDtypeStruct((unit, cols), BF16 if d else F32) for d in range(n_z)],
        compiler_params=params(),
        cost_estimate=cost(),
        name="plane_sum",
    )(pos, *terms)


def matrix_of(right_ref, sub):
    upm = right_ref.shape[1]
    parts = [right_ref[0, i ^ sub] for i in range(upm)]
    return parts[0] if upm == 1 else jnp.concatenate(parts, axis=0)


def product(lt, right):
    return lax.dot_general(lt, right, (((0,), (0,)), ((), ())), preferred_element_type=F32)


def outputs_kernel(pos, comp_ref, right_ref, lt_ref, ltr_ref, base_ref, *refs):
    feedback_ref, weights_ref = refs[-2:]
    right = matrix_of(right_ref, pos[1])
    feedback_ref[0, 0] = (comp_ref[0].astype(F32) - product(lt_ref[...], right)).astype(BF16)
    weights_ref[0] = (base_ref[0].astype(F32) - 0.1 * product(ltr_ref[...], right)).astype(BF16)


def outputs(pos, start, comp, right, lt, ltr, base, earlier):
    nmat, rows, n = comp.shape
    rank = lt.shape[0] // nmat
    half, upm, unit, _ = right.shape
    replica_rows = base.shape[1]

    def matrix(j, pos):
        return (j + start) ^ pos[0]

    any_spec = pl.BlockSpec(memory_space=pl.ANY)
    return pl.pallas_call(
        outputs_kernel,
        grid_spec=pltpu.PrefetchScalarGridSpec(
            num_scalar_prefetch=1,
            grid=(half,),
            in_specs=[
                pl.BlockSpec((1, rows, n), lambda j, pos: (matrix(j, pos), 0, 0)),
                pl.BlockSpec((1, upm, unit, n), lambda j, pos: (j, 0, 0, 0)),
                pl.BlockSpec((rank, rows), lambda j, pos: (matrix(j, pos), 0)),
                pl.BlockSpec((rank, replica_rows), lambda j, pos: (matrix(j, pos), 0)),
                pl.BlockSpec((1, replica_rows, n), lambda j, pos: (pos[PLACES + matrix(j, pos)], 0, 0)),
            ]
            + [any_spec] * len(earlier),
            out_specs=[
                pl.BlockSpec((1, 1, rows, n), lambda j, pos: (0, matrix(j, pos), 0, 0)),
                pl.BlockSpec((1, replica_rows, n), lambda j, pos: (matrix(j, pos), 0, 0)),
            ],
        ),
        out_shape=[
            jax.ShapeDtypeStruct((1, nmat, rows, n), BF16),
            jax.ShapeDtypeStruct((nmat, replica_rows, n), BF16),
        ],
        input_output_aliases={6 + i: i for i in range(len(earlier))},
        compiler_params=params(),
        cost_estimate=cost(),
        name="outputs",
    )(pos, comp, right, lt, ltr, base, *earlier)


def owned_kernel(half, held, pos, momentum_ref, master_ref, near_ref, far_ref, ltr_ref, new_momentum_ref, new_master_ref):
    c = pl.program_id(0)
    matrix = pos[held + c]
    near = matrix_of(near_ref, pos[1])
    far = matrix_of(far_ref, pos[1])
    slot = jnp.maximum(matrix, 0) ^ pos[0]
    right = jnp.where(slot < half, near, far)
    approx = jnp.where(matrix >= 0, product(ltr_ref[...], right), 0.0)
    momentum = 0.9 * momentum_ref[0, 0] + approx
    new_momentum_ref[0, 0] = momentum
    new_master_ref[0, 0] = master_ref[0, 0] - 0.1 * momentum


def owned(pos, held, momentum, master, near, far, ltr):
    _, capacity, rows, n = momentum.shape
    half, upm, unit, _ = near.shape
    rank = upm * unit

    def matrix(c, pos):
        return jnp.maximum(pos[held + c], 0)

    state = pl.BlockSpec((1, 1, rows, n), lambda c, pos: (0, c, 0, 0))
    right = pl.BlockSpec((1, upm, unit, n), lambda c, pos: (lax.rem(matrix(c, pos) ^ pos[0], half), 0, 0, 0))
    return pl.pallas_call(
        functools.partial(owned_kernel, half, held),
        grid_spec=pltpu.PrefetchScalarGridSpec(
            num_scalar_prefetch=1,
            grid=(capacity,),
            in_specs=[
                state,
                state,
                right,
                right,
                pl.BlockSpec((rank, rows), lambda c, pos: (matrix(c, pos), 0)),
            ],
            out_specs=[state, state],
        ),
        out_shape=[jax.ShapeDtypeStruct(momentum.shape, F32)] * 2,
        compiler_params=params(),
        cost_estimate=cost(),
        name="owned",
    )(pos, momentum, master, near, far, ltr)


def per_device(
    gradients,
    feedback,
    right_init,
    gram_root,
    owners,
    momentum,
    master_weights,
    vector_grads,
    vector_momentum,
    vector_params,
):
    nmat, rows, n = gradients.shape[1:]
    rank = right_init.shape[2]
    n_mp = lax.axis_size("mp")
    n_z = lax.axis_size("replica") // CORES
    capacity, replica_rows = momentum.shape[1:3]
    p = lax.axis_index("mp")
    r = lax.axis_index("replica")
    core, z = r % CORES, r // CORES
    upm = CORES * n_mp // nmat
    half = nmat // CORES
    code = core * n_mp + p

    held_rows = capacity * replica_rows
    old_master = master_weights.reshape(held_rows, n)
    old_momentum = momentum.reshape(held_rows, n)
    cuts = [0, held_rows // 2, 2 * held_rows // 3, held_rows]
    bases = []
    for first, last in zip(cuts, cuts[1:]):
        base = (old_master[first:last] - 0.09 * old_momentum[first:last]).astype(BF16)
        bases.append([base] + [exchange(base, "mp", d) for d in range(1, n_mp)])

    same_owner = owners[:, None] == owners[None, :]
    earlier = jnp.arange(nmat)[:, None] < jnp.arange(nmat)[None, :]
    ranks = jnp.sum((same_owner & earlier).astype(jnp.int32), axis=0)
    relative = (owners ^ p) * capacity + ranks
    mine = relative[None, :] == jnp.arange(capacity)[:, None]
    held = jnp.max(jnp.where(mine, jnp.arange(nmat)[None, :], -1), axis=1)
    pos = jnp.concatenate([jnp.stack([code // upm, code % upm, core, core * n_z + z, z]), relative, held]).astype(jnp.int32)

    nvec = vector_grads.shape[1]
    width = nmat * rank
    pieces = CORES * n_z
    extra = -(-nvec // width)
    extra += -(rows + extra) % (8 * pieces)
    vec = jnp.pad(vector_grads[0], (0, extra * width - nvec)).reshape(extra, width)
    comp, near, far = left_terms(
        pos,
        pltpu.with_memory_space_constraint(gradients, pltpu.HBM),
        pltpu.with_memory_space_constraint(feedback, pltpu.HBM),
        jnp.swapaxes(right_init, 1, 2),
        vec,
        n_z,
    )
    chip = near + exchange(far, "replica", 1)
    piece = tree_sum([chip[0]] + [exchange(chip[d], "replica", CORES * d) for d in range(1, n_z)])
    near = jnp.stack([piece] + [exchange(piece, "replica", CORES * d) for d in range(1, n_z)])
    far = exchange(near, "replica", 1)

    block = jnp.eye(nmat, dtype=bool)[:, None, :, None]
    gram = jnp.where(block, gram_root[:, :, None, :], 0.0).reshape(width, width)
    send, keep, lt, vector_rows = right_terms(pos, near, far, gram, comp, upm, bases[0][1:])
    vector_total = vector_rows.reshape(-1)[:nvec]
    chip = chip_sum(keep, exchange(send, "replica", 1), bases[1][1:])
    plane = [chip[0]] + [exchange(chip[d], "mp", d) for d in range(1, n_mp)]
    final = plane_sum(pos, plane, n_z)
    final = [final[0]] + [exchange(final[d], "replica", CORES * d).astype(F32) for d in range(1, n_z)]
    final = tree_sum(final).astype(BF16)

    final = [final] + [exchange(final, "replica", CORES * d) for d in range(1, n_z)]
    whole = column_gather(pos, final, bases[2][1:])
    near = jnp.stack([whole] + [exchange(whole, "mp", d) for d in range(1, n_mp)])
    near = near.reshape(half, upm, rank // upm, n)
    far = exchange(near, "replica", 1)

    first = r * replica_rows
    strip = lax.dynamic_slice_in_dim(lt, first % rows, replica_rows, 1)
    strips = jnp.stack([strip] + [exchange(strip, "mp", d) for d in range(1, n_mp)])
    ltr = lax.dynamic_index_in_dim(strips, (first // rows) ^ p, 0, keepdims=False)

    base_all = jnp.concatenate([part[d] for d in range(n_mp) for part in bases], axis=0)
    base_all = base_all.reshape(n_mp * capacity, replica_rows, n)
    done = outputs(pos, 0, comp, near, lt, ltr, base_all, ())
    new_feedback, new_weights = outputs(pos, half, comp, far, lt, ltr, base_all, done)
    new_momentum, new_master = owned(pos, PLACES + nmat, momentum, master_weights, near, far, ltr)

    new_vector_momentum = 0.9 * vector_momentum + vector_total
    new_vector_params = vector_params - 0.1 * new_vector_momentum
    return new_feedback, new_momentum, new_master, new_weights, new_vector_momentum, new_vector_params


def solution(mesh):
    return jax.shard_map(
        per_device,
        mesh=mesh,
        in_specs=(
            P("replica", None, "mp", None),
            P("replica", None, "mp", None),
            P(),
            P(),
            P(),
            P("mp", None, "replica", None),
            P("mp", None, "replica", None),
            P("replica", "mp"),
            P("mp"),
            P("mp"),
        ),
        out_specs=(
            P("replica", None, "mp", None),
            P("mp", None, "replica", None),
            P("mp", None, "replica", None),
            P(None, "replica", None),
            P("mp"),
            P("mp"),
        ),
        check_vma=False,
    )
```

```python
import functools

import jax
import jax.numpy as jnp
from jax import lax
from jax.experimental import pallas as pl
from jax.experimental.pallas import tpu as pltpu
from jax.sharding import PartitionSpec as P

CORES = 2
LANES = 128
VMEM_LIMIT = 24 * 1024 * 1024
F32 = jnp.float32
BF16 = jnp.bfloat16


def params():
    return pltpu.CompilerParams(vmem_limit_bytes=VMEM_LIMIT)


def cost(bytes_accessed=1000):
    return pl.CostEstimate(flops=1000, bytes_accessed=bytes_accessed, transcendentals=0)


def tree_sum(terms):
    while len(terms) > 1:
        terms = [terms[i] + terms[i + 1] for i in range(0, len(terms), 2)]
    return terms[0]


def exchange(x, axis, distance):
    size = lax.axis_size(axis)
    return lax.ppermute(x, axis, [(i, i ^ distance) for i in range(size)])


def left_kernel(pos, g_ref, f_ref, q_ref, vec_ref, comp_ref, near_ref, far_ref, total):
    k = pl.program_id(0)
    rows = g_ref.shape[2]
    rank = q_ref.shape[1]
    group = LANES // rank
    near, piece, _ = near_ref.shape

    @pl.when(k == 0)
    def _():
        total[...] = jnp.zeros(total.shape, F32)
        width, nvec = total.shape[1], vec_ref.shape[1]
        for i, first in enumerate(range(0, nvec, width)):
            count = min(width, nvec - first)
            total[rows + i : rows + i + 1, :count] = vec_ref[:, first : first + count]

    comp = g_ref[0, 0] + f_ref[0, 0]
    comp_ref[0] = comp
    q = q_ref[0]
    wide = jnp.concatenate([q] * group, axis=0)
    member = lax.broadcasted_iota(jnp.int32, wide.shape, 0) // rank
    wide = jnp.where(member == k % group, wide, jnp.zeros_like(wide))
    terms = lax.dot_general(comp, wide, (((1,), (1,)), ((), ())), preferred_element_type=F32)
    cols = pl.ds(pl.multiple_of((k // group) * LANES, LANES), LANES)
    total[:rows, cols] += terms

    @pl.when(k == pl.num_programs(0) - 1)
    def _():
        for s in range(near):
            for out, slot in ((near_ref, s), (far_ref, s + near)):
                out[s] = total[pl.ds(pl.multiple_of((slot ^ pos[3]) * piece, piece), piece), :]


def left_terms(pos, gradients, feedback, right_t, vec, n_z):
    _, nmat, rows, n = gradients.shape
    rank = right_t.shape[1]
    width = nmat * rank
    total = rows + -(-vec.shape[1] // width)
    total += -total % (8 * CORES * n_z)
    pieces = jax.ShapeDtypeStruct((n_z, total // (CORES * n_z), width), F32)
    return pl.pallas_call(
        left_kernel,
        grid_spec=pltpu.PrefetchScalarGridSpec(
            num_scalar_prefetch=1,
            grid=(nmat,),
            in_specs=[
                pl.BlockSpec((1, 1, rows, n), lambda k, pos: (0, k, 0, 0)),
                pl.BlockSpec((1, 1, rows, n), lambda k, pos: (0, k, 0, 0)),
                pl.BlockSpec((1, rank, n), lambda k, pos: (k, 0, 0)),
                pl.BlockSpec(vec.shape, lambda k, pos: (0, 0)),
            ],
            out_specs=[
                pl.BlockSpec((1, rows, n), lambda k, pos: (k, 0, 0)),
                pl.BlockSpec(pieces.shape, lambda k, pos: (0, 0, 0)),
                pl.BlockSpec(pieces.shape, lambda k, pos: (0, 0, 0)),
            ],
            scratch_shapes=[pltpu.VMEM((total, width), F32)],
        ),
        out_shape=[jax.ShapeDtypeStruct((nmat, rows, n), BF16), pieces, pieces],
        compiler_params=params(),
        cost_estimate=cost(),
        name="left_terms",
    )(pos, gradients, feedback, right_t, vec)


def send_kernel(half, pos, near_ref, far_ref, gram_ref, comp_ref, *refs):
    send_ref, lt_ref, vec_ref, left, gram = refs[-5:]
    t = pl.program_id(0)
    rows = comp_ref.shape[1]
    rank = gram_ref.shape[1]

    @pl.when(t == 0)
    def _():
        near, piece, _ = near_ref.shape
        for s in range(near):
            for part, slot in ((near_ref, s), (far_ref, s + near)):
                left[pl.ds(pl.multiple_of((slot ^ pos[3]) * piece, piece), piece), :] = part[s]
        vec_ref[...] = left[rows:, :]
        gram[...] = jnp.zeros(gram.shape, F32)
        for i in range(gram_ref.shape[0]):
            gram[i * rank : (i + 1) * rank, i * rank : (i + 1) * rank] = gram_ref[i]
        hat = jnp.dot(
            left[:rows, :], gram[...], precision=lax.Precision.HIGHEST, preferred_element_type=F32
        )
        lt_ref[...] = hat.T.astype(BF16)

    right_rows(half, pos, lt_ref, comp_ref, send_ref)


def right_rows(start, pos, lt_ref, comp_ref, out_ref):
    upm, unit = out_ref.shape[1], out_ref.shape[2]
    k = (pl.program_id(0) + start) ^ pos[0]
    rows = pl.ds(pl.multiple_of(k * upm * unit, upm * unit), upm * unit)
    terms = jnp.dot(lt_ref[rows, :], comp_ref[0], preferred_element_type=F32)
    for i in range(upm):
        out_ref[0, i ^ pos[1]] = terms[i * unit : (i + 1) * unit].astype(out_ref.dtype)


def keep_kernel(pos, lt_ref, comp_ref, keep_ref):
    right_rows(0, pos, lt_ref, comp_ref, keep_ref)


def right_terms(pos, near, far, gram, comp, upm, after):
    nmat, rows, n = comp.shape
    rank = gram.shape[1]
    width = nmat * rank
    half = nmat // CORES
    total = CORES * near.shape[0] * near.shape[1]
    shape = (half, upm, rank // upm, n)
    vmem = pl.BlockSpec(memory_space=pltpu.VMEM)
    out = pl.BlockSpec((1,) + shape[1:], lambda t, pos: (t, 0, 0, 0))
    send, lt, vec = pl.pallas_call(
        functools.partial(send_kernel, half),
        grid_spec=pltpu.PrefetchScalarGridSpec(
            num_scalar_prefetch=1,
            grid=(half,),
            in_specs=[
                vmem,
                vmem,
                vmem,
                pl.BlockSpec((1, rows, n), lambda t, pos: ((t + half) ^ pos[0], 0, 0)),
            ]
            + [pl.BlockSpec(memory_space=pl.ANY)] * len(after),
            out_specs=[out, vmem, vmem],
            scratch_shapes=[pltpu.VMEM((total, width), F32), pltpu.VMEM((width, width), F32)],
        ),
        out_shape=[
            jax.ShapeDtypeStruct(shape, BF16),
            jax.ShapeDtypeStruct((width, rows), BF16),
            jax.ShapeDtypeStruct((total - rows, width), F32),
        ],
        compiler_params=params(),
        cost_estimate=cost(),
        name="right_send",
    )(pos, near, far, gram, comp, *after)
    keep = pl.pallas_call(
        keep_kernel,
        grid_spec=pltpu.PrefetchScalarGridSpec(
            num_scalar_prefetch=1,
            grid=(half,),
            in_specs=[vmem, pl.BlockSpec((1, rows, n), lambda t, pos: (t ^ pos[0], 0, 0))],
            out_specs=out,
        ),
        out_shape=jax.ShapeDtypeStruct(shape, F32),
        compiler_params=params(),
        cost_estimate=cost(4 * nmat * rows * n),
        name="right_keep",
    )(pos, lt, comp)
    return send, keep, lt, vec


def chip_kernel(pos, keep_ref, recv_ref, lt_ref, *refs):
    upm = keep_ref.shape[1]
    for d, out in enumerate(refs[:-1]):
        j, i = d // upm, d % upm
        out[...] = (keep_ref[j, i] + recv_ref[j, i].astype(F32)).astype(out.dtype)
    strip_ref = refs[-1]
    count = strip_ref.shape[1]
    strip = lt_ref[:, :count]
    for i in range(1, lt_ref.shape[1] // count):
        strip = jnp.where(pos[6] == i, lt_ref[:, i * count : (i + 1) * count], strip)
    strip_ref[...] = strip


def chip_sum(pos, keep, recv, lt, replica_rows):
    half, upm, unit, n = keep.shape
    vmem = pl.BlockSpec(memory_space=pltpu.VMEM)
    outs = [jax.ShapeDtypeStruct((unit, n), BF16 if d else F32) for d in range(half * upm)]
    outs.append(jax.ShapeDtypeStruct((lt.shape[0], replica_rows), BF16))
    return pl.pallas_call(
        chip_kernel,
        grid_spec=pltpu.PrefetchScalarGridSpec(
            num_scalar_prefetch=1,
            grid=(1,),
            in_specs=[vmem] * 3,
            out_specs=[vmem] * len(outs),
        ),
        out_shape=outs,
        compiler_params=params(),
        cost_estimate=cost(),
        name="chip_sum",
    )(pos, keep, recv, lt)


def column_kernel(n_z, pos, *refs):
    out = refs[-1]
    cols = out.shape[1] // n_z
    for d in range(n_z):
        out[:, pl.ds(pl.multiple_of((pos[4] ^ d) * cols, cols), cols)] = refs[d][...]


def column_gather(pos, parts, after):
    unit, cols = parts[0].shape
    vmem = pl.BlockSpec(memory_space=pltpu.VMEM)
    return pl.pallas_call(
        functools.partial(column_kernel, len(parts)),
        grid_spec=pltpu.PrefetchScalarGridSpec(
            num_scalar_prefetch=1,
            grid=(1,),
            in_specs=[vmem] * len(parts) + [pl.BlockSpec(memory_space=pl.ANY)] * len(after),
            out_specs=vmem,
        ),
        out_shape=jax.ShapeDtypeStruct((unit, cols * len(parts)), BF16),
        compiler_params=params(),
        cost_estimate=cost(),
        name="column_gather",
    )(pos, *parts, *after)


def plane_kernel(count, cuts, pos, *refs):
    terms, wholes, outs = refs[:count], refs[count : count + len(cuts)], refs[count + len(cuts) + 1 :]
    cols = outs[0].shape[1]
    n_z = len(outs) - len(cuts)
    for d, out in enumerate(outs[:n_z]):
        block = pl.ds(pl.multiple_of((pos[4] ^ d) * cols, cols), cols)
        out[...] = tree_sum([term[:, block].astype(F32) for term in terms]).astype(out.dtype)
    for whole, out, first in zip(wholes, outs[n_z:], cuts):
        out[...] = whole[first : first + out.shape[0]]


def plane_sum(pos, terms, n_z, wholes, cuts, after):
    unit, n = terms[0].shape
    cols = n // n_z
    outs = [jax.ShapeDtypeStruct((unit, cols), BF16 if d else F32) for d in range(n_z)]
    outs += [jax.ShapeDtypeStruct((x.shape[0] // 2,) + x.shape[1:], x.dtype) for x in wholes]
    vmem = pl.BlockSpec(memory_space=pltpu.VMEM)
    return pl.pallas_call(
        functools.partial(plane_kernel, len(terms), cuts),
        grid_spec=pltpu.PrefetchScalarGridSpec(
            num_scalar_prefetch=1,
            grid=(1,),
            in_specs=[vmem] * (len(terms) + len(wholes)) + [pl.BlockSpec(memory_space=pl.ANY)],
            out_specs=[vmem] * len(outs),
        ),
        out_shape=outs,
        compiler_params=params(),
        cost_estimate=cost(),
        name="plane_sum",
    )(pos, *terms, *wholes, after)


def matrix_of(right_ref, slot, sub):
    upm = right_ref.shape[1]
    parts = [right_ref[slot, i ^ sub] for i in range(upm)]
    return parts[0] if upm == 1 else jnp.concatenate(parts, axis=0)


def product(lt, right):
    return lax.dot_general(lt, right, (((0,), (0,)), ((), ())), preferred_element_type=F32)


def rank_of(owners, k, nmat):
    count = jnp.int32(0)
    for j in range(nmat):
        count += jnp.where((owners[j] == owners[k]) & (j < k), 1, 0)
    return count


def outputs_kernel(start, places, pos, owners, comp_ref, right_ref, lt_ref, ltr_ref, *refs):
    n_base = len({a for a, _ in places.values()})
    bases, (feedback_ref, weights_ref, held, sem) = refs[:n_base], refs[-4:]
    j = pl.program_id(0)
    rank = right_ref.shape[1] * right_ref.shape[2]
    capacity = max(c for _, c in places) + 1

    def fetch(step, start_it):
        k = (step + start) ^ pos[0]
        slot = (owners[k] ^ pos[5]) * capacity + rank_of(owners, k, owners.shape[0])
        buffer = lax.rem(step, 2)
        if not start_it:
            pltpu.make_async_copy(bases[0].at[0], held.at[buffer], sem.at[buffer]).wait()
            return
        for (d, c), (a, row) in places.items():

            @pl.when(slot == d * capacity + c)
            def _():
                pltpu.make_async_copy(bases[a].at[row], held.at[buffer], sem.at[buffer]).start()

    @pl.when(j == 0)
    def _():
        fetch(j, True)

    @pl.when(j + 1 < pl.num_programs(0))
    def _():
        fetch(j + 1, True)

    right = matrix_of(right_ref, j, pos[1])
    k = (j + start) ^ pos[0]
    rows = pl.ds(pl.multiple_of(k * rank, rank), rank)
    feedback_ref[0, 0] = (comp_ref[0].astype(F32) - product(lt_ref[rows, :], right)).astype(BF16)
    fetch(j, False)
    base = held[lax.rem(j, 2)].astype(F32)
    weights_ref[0] = (base - 0.1 * product(ltr_ref[rows, :], right)).astype(BF16)


def outputs(pos, owners, start, comp, right, lt, ltr, bases, places, earlier):
    nmat, rows, n = comp.shape
    half = right.shape[0]
    replica_rows = bases[0].shape[1]

    def matrix(j, pos):
        return (j + start) ^ pos[0]

    any_spec = pl.BlockSpec(memory_space=pl.ANY)
    vmem = pl.BlockSpec(memory_space=pltpu.VMEM)
    return pl.pallas_call(
        functools.partial(outputs_kernel, start, places),
        grid_spec=pltpu.PrefetchScalarGridSpec(
            num_scalar_prefetch=2,
            grid=(half,),
            in_specs=[pl.BlockSpec((1, rows, n), lambda j, pos, own: (matrix(j, pos), 0, 0))]
            + [vmem] * 3
            + [any_spec] * (len(bases) + len(earlier)),
            out_specs=[
                pl.BlockSpec((1, 1, rows, n), lambda j, pos, own: (0, matrix(j, pos), 0, 0)),
                pl.BlockSpec((1, replica_rows, n), lambda j, pos, own: (matrix(j, pos), 0, 0)),
            ],
            scratch_shapes=[
                pltpu.VMEM((2, replica_rows, n), BF16),
                pltpu.SemaphoreType.DMA((2,)),
            ],
        ),
        out_shape=[
            jax.ShapeDtypeStruct((1, nmat, rows, n), BF16),
            jax.ShapeDtypeStruct((nmat, replica_rows, n), BF16),
        ],
        input_output_aliases={6 + len(bases) + i: i for i in range(len(earlier))},
        compiler_params=params(),
        cost_estimate=cost(),
        name="outputs",
    )(pos, owners, comp, right, lt, ltr, *bases, *earlier)


def owned_kernel(pos, owners, momentum_ref, master_ref, near_ref, far_ref, ltr_ref, new_momentum_ref, new_master_ref):
    c = pl.program_id(0)
    nmat = owners.shape[0]
    half = near_ref.shape[0]
    rank = near_ref.shape[1] * near_ref.shape[2]
    matrix = jnp.int32(-1)
    for k in range(nmat):
        matrix = jnp.where((owners[k] == pos[5]) & (rank_of(owners, k, nmat) == c), k, matrix)
    safe = jnp.maximum(matrix, 0)
    slot = safe ^ pos[0]
    inner = lax.rem(slot, half)
    right = jnp.where(slot < half, matrix_of(near_ref, inner, pos[1]), matrix_of(far_ref, inner, pos[1]))
    lt = ltr_ref[pl.ds(pl.multiple_of(safe * rank, rank), rank), :]
    approx = jnp.where(matrix >= 0, product(lt, right), 0.0)
    momentum = 0.9 * momentum_ref[0, 0] + approx
    new_momentum_ref[0, 0] = momentum
    new_master_ref[0, 0] = master_ref[0, 0] - 0.1 * momentum


def owned(pos, owners, momentum, master, near, far, ltr):
    _, capacity, rows, n = momentum.shape
    state = pl.BlockSpec((1, 1, rows, n), lambda c, pos, own: (0, c, 0, 0))
    vmem = pl.BlockSpec(memory_space=pltpu.VMEM)
    return pl.pallas_call(
        owned_kernel,
        grid_spec=pltpu.PrefetchScalarGridSpec(
            num_scalar_prefetch=2,
            grid=(capacity,),
            in_specs=[state, state, vmem, vmem, vmem],
            out_specs=[state, state],
        ),
        out_shape=[jax.ShapeDtypeStruct(momentum.shape, F32)] * 2,
        compiler_params=params(),
        cost_estimate=cost(),
        name="owned",
    )(pos, owners, momentum, master, near, far, ltr)


def base_kernel(momentum_ref, master_ref, out_ref):
    out_ref[0] = (master_ref[0, 0] - 0.09 * momentum_ref[0, 0]).astype(BF16)


def base_of(momentum, master):
    _, capacity, rows, n = momentum.shape
    cuts = 2
    state = pl.BlockSpec((1, 1, rows, n // cuts), lambda c, i: (0, c, 0, i))
    return pl.pallas_call(
        base_kernel,
        grid=(capacity, cuts),
        in_specs=[state, state],
        out_specs=pl.BlockSpec((1, rows, n // cuts), lambda c, i: (c, 0, i)),
        out_shape=jax.ShapeDtypeStruct((capacity, rows, n), BF16),
        compiler_params=params(),
        cost_estimate=cost(),
        name="base",
    )(momentum, master)


def stack_kernel(*refs):
    out = refs[-1]
    for i, part in enumerate(refs[:-1]):
        out[i] = part[...]


def stack(parts):
    vmem = pl.BlockSpec(memory_space=pltpu.VMEM)
    return pl.pallas_call(
        stack_kernel,
        in_specs=[vmem] * len(parts),
        out_specs=vmem,
        out_shape=jax.ShapeDtypeStruct((len(parts),) + parts[0].shape, parts[0].dtype),
        compiler_params=params(),
        cost_estimate=cost(),
        name="stack",
    )(*parts)


def per_device(
    gradients,
    feedback,
    right_init,
    gram_root,
    owners,
    momentum,
    master_weights,
    vector_grads,
    vector_momentum,
    vector_params,
):
    nmat, rows, n = gradients.shape[1:]
    rank = right_init.shape[2]
    n_mp = lax.axis_size("mp")
    n_z = lax.axis_size("replica") // CORES
    capacity, replica_rows = momentum.shape[1:3]
    p = lax.axis_index("mp")
    r = lax.axis_index("replica")
    core, z = r % CORES, r // CORES
    upm = CORES * n_mp // nmat
    half = nmat // CORES
    code = core * n_mp + p

    pos = jnp.stack([code // upm, code % upm, core, core * n_z + z, z, p, r * replica_rows % rows // replica_rows]).astype(jnp.int32)
    in_hbm = lambda x: pltpu.with_memory_space_constraint(x, pltpu.HBM)
    momentum, master_weights = in_hbm(momentum), in_hbm(master_weights)

    base = base_of(momentum, master_weights)
    bases = [base] + [exchange(base, "mp", d) for d in range(1, 3 if n_mp == 4 else n_mp)]
    places = {(d, c): (d, c) for d in range(len(bases)) for c in range(capacity)}
    early, cuts = bases[1:], []
    if n_mp == 4:
        cut = capacity // 2
        cuts = [0, cut]
        for c in range(capacity):
            places[3, c] = (3, c) if c < cut else (4, c - cut)

    nvec = vector_grads.shape[1]
    comp, near, far = left_terms(
        pos,
        in_hbm(gradients),
        in_hbm(feedback),
        in_hbm(jnp.swapaxes(right_init, 1, 2)),
        vector_grads,
        n_z,
    )
    chip = near + exchange(far, "replica", 1)
    piece = tree_sum([chip[0]] + [exchange(chip[d], "replica", CORES * d) for d in range(1, n_z)])
    near = stack([piece] + [exchange(piece, "replica", CORES * d) for d in range(1, n_z)])
    far = exchange(near, "replica", 1)

    send, keep, lt, vector_rows = right_terms(pos, near, far, gram_root, comp, upm, early)
    vector_total = vector_rows.reshape(-1)[:nvec]
    *chip, strip = chip_sum(pos, keep, exchange(send, "replica", 1), lt, replica_rows)
    plane = [chip[0]] + [exchange(chip[d], "mp", d) for d in range(1, n_mp)]
    strips = jnp.stack([strip] + [exchange(strip, "mp", d) for d in range(1, n_mp)])
    ltr = lax.dynamic_index_in_dim(strips, (r * replica_rows // rows) ^ p, 0, keepdims=False)
    final = plane_sum(pos, plane, n_z, early[: len(cuts)], cuts, ltr)
    late = [exchange(part, "mp", 2 - i) for i, part in enumerate(final[n_z:])]
    bases += late
    final = [final[0]] + [exchange(final[d], "replica", CORES * d).astype(F32) for d in range(1, n_z)]
    final = tree_sum(final).astype(BF16)

    final = [final] + [exchange(final, "replica", CORES * d) for d in range(1, n_z)]
    whole = column_gather(pos, final, late)
    near = stack([whole] + [exchange(whole, "mp", d) for d in range(1, n_mp)])
    near = near.reshape(half, upm, rank // upm, n)
    far = exchange(near, "replica", 1)

    done = outputs(pos, owners, 0, comp, near, lt, ltr, bases, places, ())
    new_feedback, new_weights = outputs(pos, owners, half, comp, far, lt, ltr, bases, places, done)
    new_momentum, new_master = owned(pos, owners, momentum, master_weights, near, far, ltr)

    new_vector_momentum = 0.9 * vector_momentum + vector_total
    new_vector_params = vector_params - 0.1 * new_vector_momentum
    return new_feedback, new_momentum, new_master, new_weights, new_vector_momentum, new_vector_params


def solution(mesh):
    return jax.shard_map(
        per_device,
        mesh=mesh,
        in_specs=(
            P("replica", None, "mp", None),
            P("replica", None, "mp", None),
            P(),
            P(),
            P(),
            P("mp", None, "replica", None),
            P("mp", None, "replica", None),
            P("replica", "mp"),
            P("mp"),
            P("mp"),
        ),
        out_specs=(
            P("replica", None, "mp", None),
            P("mp", None, "replica", None),
            P("mp", None, "replica", None),
            P(None, "replica", None),
            P("mp"),
            P("mp"),
        ),
        check_vma=False,
    )
```

```python
import functools

import jax
import jax.numpy as jnp
from jax import lax
from jax.experimental import pallas as pl
from jax.experimental.pallas import tpu as pltpu
from jax.sharding import PartitionSpec as P

CORES = 2
BASE_ROWS = 16
COLUMNS = 512
F32 = jnp.float32
BF16 = jnp.bfloat16


def params(mib=12):
    return pltpu.CompilerParams(vmem_limit_bytes=mib * 1024 * 1024)


def cost(bytes_accessed=1000):
    return pl.CostEstimate(flops=1000, bytes_accessed=bytes_accessed, transcendentals=0)


def tree_sum(terms):
    while len(terms) > 1:
        terms = [terms[i] + terms[i + 1] for i in range(0, len(terms), 2)]
    return terms[0]


def exchange(x, axis, distance):
    size = lax.axis_size(axis)
    return lax.ppermute(x, axis, [(i, i ^ distance) for i in range(size)])


def left_kernel(pos, g_ref, f_ref, q_ref, vec_ref, comp_ref, near_ref, far_ref, total):
    k = pl.program_id(0)
    rows = g_ref.shape[2]
    rank = q_ref.shape[1]
    part = near_ref.shape[0]

    @pl.when(k == 0)
    def _():
        total[...] = jnp.zeros(total.shape, F32)
        width, nvec = total.shape[1], vec_ref.shape[1]
        for i, first in enumerate(range(0, nvec, width)):
            count = min(width, nvec - first)
            total[rows + i : rows + i + 1, :count] = vec_ref[:, first : first + count]

    comp = g_ref[0, 0] + f_ref[0, 0]
    comp_ref[k] = comp
    terms = lax.dot_general(comp, q_ref[0], (((1,), (1,)), ((), ())), preferred_element_type=F32)
    for i in range(total.shape[1] // rank):

        @pl.when(k == i)
        def _():
            total[:rows, i * rank : (i + 1) * rank] = terms

    @pl.when(k == pl.num_programs(0) - 1)
    def _():
        for ref, core in ((near_ref, pos[2]), (far_ref, 1 - pos[2])):
            ref[...] = total[pl.ds(pl.multiple_of(core * part, 16), part), :]


def left_terms(pos, gradients, feedback, right_t, vec):
    _, nmat, rows, n = gradients.shape
    rank = right_t.shape[1]
    width = nmat * rank
    total = rows + -(-vec.shape[1] // width)
    total += -total % (16 * CORES)
    part = jax.ShapeDtypeStruct((total // CORES, width), F32)
    vmem = pl.BlockSpec(memory_space=pltpu.VMEM)
    return pl.pallas_call(
        left_kernel,
        grid_spec=pltpu.PrefetchScalarGridSpec(
            num_scalar_prefetch=1,
            grid=(nmat,),
            in_specs=[
                pl.BlockSpec((1, 1, rows, n), lambda k, pos: (0, k, 0, 0)),
                pl.BlockSpec((1, 1, rows, n), lambda k, pos: (0, k, 0, 0)),
                pl.BlockSpec((1, rank, n), lambda k, pos: (k, 0, 0)),
                vmem,
            ],
            out_specs=[vmem] * 3,
            scratch_shapes=[pltpu.VMEM((total, width), F32)],
        ),
        out_shape=[jax.ShapeDtypeStruct((nmat, rows, n), BF16), part, part],
        compiler_params=params(16),
        cost_estimate=cost(),
        name="left_terms",
    )(pos, gradients, feedback, right_t, vec)


def add_kernel(*refs):
    out = refs[-1]
    out[...] = tree_sum([ref[...].astype(F32) for ref in refs[:-1]]).astype(out.dtype)


def add(parts, dtype):
    vmem = pl.BlockSpec(memory_space=pltpu.VMEM)
    return pl.pallas_call(
        add_kernel,
        in_specs=[vmem] * len(parts),
        out_specs=vmem,
        out_shape=jax.ShapeDtypeStruct(parts[0].shape, dtype),
        compiler_params=params(),
        cost_estimate=cost(),
        name="add",
    )(*parts)


def send_kernel(half, pos, near_ref, far_ref, gram_ref, comp_ref, *refs):
    send_ref, lt_ref, vec_ref, left, gram = refs[-5:]
    t = pl.program_id(0)
    rows = comp_ref.shape[1]
    rank = gram_ref.shape[1]

    @pl.when(t == 0)
    def _():
        part = near_ref.shape[0]
        for ref, core in ((near_ref, pos[2]), (far_ref, 1 - pos[2])):
            left[pl.ds(pl.multiple_of(core * part, 16), part), :] = ref[...]
        vec_ref[...] = left[rows:, :]
        gram[...] = jnp.zeros(gram.shape, F32)
        for i in range(gram_ref.shape[0]):
            gram[i * rank : (i + 1) * rank, i * rank : (i + 1) * rank] = gram_ref[i]
        hat = jnp.dot(
            left[:rows, :], gram[...], precision=lax.Precision.HIGHEST, preferred_element_type=F32
        )
        lt_ref[...] = hat.T.astype(BF16)

    right_rows(half, pos, lt_ref, comp_ref, send_ref)


def right_rows(start, pos, lt_ref, comp_ref, out_ref):
    upm, unit = out_ref.shape[1], out_ref.shape[2]
    k = (pl.program_id(0) + start) ^ pos[0]
    rows = pl.ds(pl.multiple_of(k * upm * unit, upm * unit), upm * unit)
    terms = jnp.dot(lt_ref[rows, :], comp_ref[k], preferred_element_type=F32)
    for i in range(upm):
        out_ref[0, i ^ pos[1]] = terms[i * unit : (i + 1) * unit].astype(out_ref.dtype)


def keep_kernel(pos, lt_ref, comp_ref, keep_ref):
    right_rows(0, pos, lt_ref, comp_ref, keep_ref)


def right_terms(pos, near, far, gram, comp, upm, after):
    nmat, rows, n = comp.shape
    rank = gram.shape[1]
    width = nmat * rank
    half = nmat // CORES
    total = CORES * near.shape[0]
    shape = (half, upm, rank // upm, n)
    vmem = pl.BlockSpec(memory_space=pltpu.VMEM)
    out = pl.BlockSpec((1,) + shape[1:], lambda t, pos: (t, 0, 0, 0))
    send, lt, vec = pl.pallas_call(
        functools.partial(send_kernel, half),
        grid_spec=pltpu.PrefetchScalarGridSpec(
            num_scalar_prefetch=1,
            grid=(half,),
            in_specs=[
                vmem,
                vmem,
                vmem,
                vmem,
            ]
            + [pl.BlockSpec(memory_space=pl.ANY)] * len(after),
            out_specs=[out, vmem, vmem],
            scratch_shapes=[pltpu.VMEM((total, width), F32), pltpu.VMEM((width, width), F32)],
        ),
        out_shape=[
            jax.ShapeDtypeStruct(shape, BF16),
            jax.ShapeDtypeStruct((width, rows), BF16),
            jax.ShapeDtypeStruct((total - rows, width), F32),
        ],
        compiler_params=params(),
        cost_estimate=cost(),
        name="right_send",
    )(pos, near, far, gram, comp, *after)
    keep = pl.pallas_call(
        keep_kernel,
        grid_spec=pltpu.PrefetchScalarGridSpec(
            num_scalar_prefetch=1,
            grid=(half,),
            in_specs=[vmem, vmem],
            out_specs=out,
        ),
        out_shape=jax.ShapeDtypeStruct(shape, F32),
        compiler_params=params(),
        cost_estimate=cost(4 * nmat * rows * n),
        name="right_keep",
    )(pos, lt, comp)
    return send, keep, lt, vec


def chip_kernel(replica_rows, pos, keep_ref, recv_ref, lt_ref, own_ref, strip_ref, *sends):
    upm = keep_ref.shape[1]
    n = own_ref.shape[1]
    left = lt_ref[...].astype(F32).T
    strip = left[:replica_rows]
    for i in range(1, left.shape[0] // replica_rows):
        strip = jnp.where(pos[6] == i, left[i * replica_rows : (i + 1) * replica_rows], strip)
    height = strip_ref.shape[0]
    strip = jnp.concatenate(
        [strip[i * height : (i + 1) * height] for i in range(replica_rows // height)], axis=1
    )
    strip_ref[...] = strip
    own_ref[...] = keep_ref[0, 0] + recv_ref[0, 0].astype(F32)
    for d, out in enumerate(sends, 1):
        j, i = d // upm, d % upm
        terms = keep_ref[j, i] + recv_ref[j, i].astype(F32)
        out[...] = jnp.concatenate([terms, strip], axis=0).astype(BF16)


def chip_sum(pos, keep, recv, lt, replica_rows):
    half, upm, unit, n = keep.shape
    height = lt.shape[0] * replica_rows // n
    vmem = pl.BlockSpec(memory_space=pltpu.VMEM)
    outs = [jax.ShapeDtypeStruct((unit, n), F32), jax.ShapeDtypeStruct((height, n), F32)]
    outs += [jax.ShapeDtypeStruct((unit + height, n), BF16)] * (half * upm - 1)
    return pl.pallas_call(
        functools.partial(chip_kernel, replica_rows),
        grid_spec=pltpu.PrefetchScalarGridSpec(
            num_scalar_prefetch=1,
            grid=(1,),
            in_specs=[vmem] * 3,
            out_specs=[vmem] * len(outs),
        ),
        out_shape=outs,
        compiler_params=params(),
        cost_estimate=cost(),
        name="chip_sum",
    )(pos, keep, recv, lt)


def column_kernel(n_z, pos, *refs):
    out = refs[-1]
    cols = out.shape[1] // n_z
    for d in range(n_z):
        out[:, pl.ds(pl.multiple_of((pos[4] ^ d) * cols, cols), cols)] = refs[d][...]


def column_gather(pos, parts, after):
    unit, cols = parts[0].shape
    vmem = pl.BlockSpec(memory_space=pltpu.VMEM)
    return pl.pallas_call(
        functools.partial(column_kernel, len(parts)),
        grid_spec=pltpu.PrefetchScalarGridSpec(
            num_scalar_prefetch=1,
            grid=(1,),
            in_specs=[vmem] * len(parts) + [pl.BlockSpec(memory_space=pl.ANY)] * len(after),
            out_specs=vmem,
        ),
        out_shape=jax.ShapeDtypeStruct((unit, cols * len(parts)), BF16),
        compiler_params=params(),
        cost_estimate=cost(),
        name="column_gather",
    )(pos, *parts, *after)


def plane_kernel(count, cuts, n_z, pos, own_ref, strip_ref, *refs):
    terms, wholes, refs = refs[:count], refs[count : count + len(cuts)], refs[count + len(cuts) :]
    outs, forwards, ltr_ref = refs[:n_z], refs[n_z:-1], refs[-1]
    unit, n = own_ref.shape
    cols = n // n_z
    for d, out in enumerate(outs):
        block = pl.ds(pl.multiple_of((pos[4] ^ d) * cols, cols), cols)
        parts = [own_ref[:, block]] + [term[:, block].astype(F32)[:unit] for term in terms]
        out[...] = tree_sum(parts).astype(out.dtype)
    strip = strip_ref[...]
    for d, term in enumerate(terms, 1):
        strip = jnp.where(pos[7] == d, term[...].astype(F32)[unit:], strip)
    width = ltr_ref.shape[0]
    rows = [strip[:, i * width : (i + 1) * width] for i in range(n // width)]
    ltr_ref[...] = jnp.concatenate(rows, axis=0).T.astype(BF16)
    for whole, out, first in zip(wholes, forwards, cuts):
        out[...] = whole[first : first + out.shape[0]]


def plane_sum(pos, own, strip, terms, n_z, width, wholes, cuts):
    unit, n = own.shape
    cols = n // n_z
    outs = [jax.ShapeDtypeStruct((unit, cols), BF16 if d else F32) for d in range(n_z)]
    outs += [jax.ShapeDtypeStruct((x.shape[0] // 2,) + x.shape[1:], x.dtype) for x in wholes]
    outs.append(jax.ShapeDtypeStruct((width, strip.size // width), BF16))
    vmem = pl.BlockSpec(memory_space=pltpu.VMEM)
    return pl.pallas_call(
        functools.partial(plane_kernel, len(terms), cuts, n_z),
        grid_spec=pltpu.PrefetchScalarGridSpec(
            num_scalar_prefetch=1,
            grid=(1,),
            in_specs=[vmem] * (2 + len(terms) + len(wholes)),
            out_specs=[vmem] * len(outs),
        ),
        out_shape=outs,
        compiler_params=params(),
        cost_estimate=cost(),
        name="plane_sum",
    )(pos, own, strip, *terms, *wholes)


def matrix_of(right_ref, slot, sub):
    upm = right_ref.shape[1]
    parts = [right_ref[slot, i ^ sub] for i in range(upm)]
    return parts[0] if upm == 1 else jnp.concatenate(parts, axis=0)


def product(lt, right):
    return lax.dot_general(lt, right, (((0,), (0,)), ((), ())), preferred_element_type=F32)


def rank_of(owners, k, nmat):
    count = jnp.int32(0)
    for j in range(nmat):
        count += jnp.where((owners[j] == owners[k]) & (j < k), 1, 0)
    return count


def outputs_kernel(start, places, pos, owners, comp_ref, right_ref, lt_ref, ltr_ref, *refs):
    n_base = len({a for a, _ in places.values()})
    bases, (feedback_ref, weights_ref, held, sem) = refs[:n_base], refs[-4:]
    j = pl.program_id(0)
    rank = right_ref.shape[1] * right_ref.shape[2]
    capacity = max(c for _, c in places) + 1

    def fetch(step, start_it):
        k = (step + start) ^ pos[0]
        slot = (owners[k] ^ pos[5]) * capacity + rank_of(owners, k, owners.shape[0])
        buffer = lax.rem(step, 2)
        if not start_it:
            pltpu.make_async_copy(bases[0].at[0], held.at[buffer], sem.at[buffer]).wait()
            return
        for (d, c), (a, row) in places.items():

            @pl.when(slot == d * capacity + c)
            def _():
                pltpu.make_async_copy(bases[a].at[row], held.at[buffer], sem.at[buffer]).start()

    @pl.when(j == 0)
    def _():
        fetch(j, True)

    @pl.when(j + 1 < pl.num_programs(0))
    def _():
        fetch(j + 1, True)

    right = matrix_of(right_ref, j, pos[1])
    k = (j + start) ^ pos[0]
    rows = pl.ds(pl.multiple_of(k * rank, rank), rank)
    lt, ltr = lt_ref[rows, :], ltr_ref[rows, :]
    fetch(j, False)
    buffer = lax.rem(j, 2)
    n = right.shape[1]
    for first in range(0, n, COLUMNS):
        block = slice(first, first + COLUMNS)
        approx = product(lt, right[:, block])
        feedback_ref[0, 0, :, block] = (comp_ref[k, :, block].astype(F32) - approx).astype(BF16)
        approx = product(ltr, right[:, block])
        weights_ref[0, :, block] = (held[buffer, :, block].astype(F32) - 0.1 * approx).astype(BF16)


def outputs(pos, owners, start, comp, right, lt, ltr, bases, places, earlier):
    nmat, rows, n = comp.shape
    half = right.shape[0]
    replica_rows = bases[0].shape[1]

    def matrix(j, pos):
        return (j + start) ^ pos[0]

    any_spec = pl.BlockSpec(memory_space=pl.ANY)
    vmem = pl.BlockSpec(memory_space=pltpu.VMEM)
    return pl.pallas_call(
        functools.partial(outputs_kernel, start, places),
        grid_spec=pltpu.PrefetchScalarGridSpec(
            num_scalar_prefetch=2,
            grid=(half,),
            in_specs=[vmem] * 4
            + [any_spec] * (len(bases) + len(earlier)),
            out_specs=[
                pl.BlockSpec((1, 1, rows, n), lambda j, pos, own: (0, matrix(j, pos), 0, 0)),
                pl.BlockSpec((1, replica_rows, n), lambda j, pos, own: (matrix(j, pos), 0, 0)),
            ],
            scratch_shapes=[
                pltpu.VMEM((2, replica_rows, n), BF16),
                pltpu.SemaphoreType.DMA((2,)),
            ],
        ),
        out_shape=[
            jax.ShapeDtypeStruct((1, nmat, rows, n), BF16),
            jax.ShapeDtypeStruct((nmat, replica_rows, n), BF16),
        ],
        input_output_aliases={6 + len(bases) + i: i for i in range(len(earlier))},
        compiler_params=params(16),
        cost_estimate=cost(),
        name="outputs",
    )(pos, owners, comp, right, lt, ltr, *bases, *earlier)


def owned_kernel(pos, owners, momentum_ref, master_ref, near_ref, far_ref, ltr_ref, new_momentum_ref, new_master_ref):
    c = pl.program_id(0)
    nmat = owners.shape[0]
    half = near_ref.shape[0]
    rank = near_ref.shape[1] * near_ref.shape[2]
    matrix = jnp.int32(-1)
    for k in range(nmat):
        matrix = jnp.where((owners[k] == pos[5]) & (rank_of(owners, k, nmat) == c), k, matrix)
    safe = jnp.maximum(matrix, 0)
    slot = safe ^ pos[0]
    inner = lax.rem(slot, half)
    right = jnp.where(slot < half, matrix_of(near_ref, inner, pos[1]), matrix_of(far_ref, inner, pos[1]))
    lt = ltr_ref[pl.ds(pl.multiple_of(safe * rank, rank), rank), :]
    approx = jnp.where(matrix >= 0, product(lt, right), 0.0)
    momentum = 0.9 * momentum_ref[0, 0] + approx
    new_momentum_ref[0, 0] = momentum
    new_master_ref[0, 0] = master_ref[0, 0] - 0.1 * momentum


def owned(pos, owners, momentum, master, near, far, ltr):
    _, capacity, rows, n = momentum.shape
    state = pl.BlockSpec((1, 1, rows, n), lambda c, pos, own: (0, c, 0, 0))
    vmem = pl.BlockSpec(memory_space=pltpu.VMEM)
    return pl.pallas_call(
        owned_kernel,
        grid_spec=pltpu.PrefetchScalarGridSpec(
            num_scalar_prefetch=2,
            grid=(capacity,),
            in_specs=[state, state, vmem, vmem, vmem],
            out_specs=[state, state],
        ),
        out_shape=[jax.ShapeDtypeStruct(momentum.shape, F32)] * 2,
        compiler_params=params(20),
        cost_estimate=cost(),
        name="owned",
    )(pos, owners, momentum, master, near, far, ltr)


def base_kernel(momentum_ref, master_ref, out_ref, momentum, master, sems):
    capacity, rows, _ = out_ref.shape
    blocks = [(c, first) for c in range(capacity) for first in range(0, rows, BASE_ROWS)]

    def copies(i):
        c, first = blocks[i]
        part = pl.ds(first, BASE_ROWS)
        return [
            pltpu.make_async_copy(source.at[0, c, part], target.at[c, part], sems.at[j, i])
            for j, (source, target) in enumerate(((momentum_ref, momentum), (master_ref, master)))
        ]

    for i in range(len(blocks)):
        for copy in copies(i):
            copy.start()
    for i, (c, first) in enumerate(blocks):
        for copy in copies(i):
            copy.wait()
        part = slice(first, first + BASE_ROWS)
        out_ref[c, part] = (master[c, part] - 0.09 * momentum[c, part]).astype(BF16)


def base_of(momentum, master):
    _, capacity, rows, n = momentum.shape
    state = pltpu.VMEM((capacity, rows, n), F32)
    return pl.pallas_call(
        base_kernel,
        in_specs=[pl.BlockSpec(memory_space=pl.ANY)] * 2,
        out_specs=pl.BlockSpec(memory_space=pltpu.VMEM),
        out_shape=jax.ShapeDtypeStruct((capacity, rows, n), BF16),
        scratch_shapes=[state, state, pltpu.SemaphoreType.DMA((2, capacity * rows // BASE_ROWS))],
        compiler_params=params(),
        cost_estimate=cost(),
        name="base",
    )(momentum, master)


def stack_kernel(*refs):
    out = refs[-1]
    for i, part in enumerate(refs[:-1]):
        out[i] = part[...]


def stack(parts):
    vmem = pl.BlockSpec(memory_space=pltpu.VMEM)
    return pl.pallas_call(
        stack_kernel,
        in_specs=[vmem] * len(parts),
        out_specs=vmem,
        out_shape=jax.ShapeDtypeStruct((len(parts),) + parts[0].shape, parts[0].dtype),
        compiler_params=params(),
        cost_estimate=cost(),
        name="stack",
    )(*parts)


def per_device(
    gradients,
    feedback,
    right_init,
    gram_root,
    owners,
    momentum,
    master_weights,
    vector_grads,
    vector_momentum,
    vector_params,
):
    nmat, rows, n = gradients.shape[1:]
    rank = right_init.shape[2]
    n_mp = lax.axis_size("mp")
    n_z = lax.axis_size("replica") // CORES
    capacity, replica_rows = momentum.shape[1:3]
    p = lax.axis_index("mp")
    r = lax.axis_index("replica")
    core, z = r % CORES, r // CORES
    upm = CORES * n_mp // nmat
    half = nmat // CORES
    code = core * n_mp + p
    first = r * replica_rows

    pos = jnp.stack([code // upm, code % upm, core, core * n_z + z, z, p, first % rows // replica_rows, first // rows ^ p]).astype(jnp.int32)
    in_hbm = lambda x: pltpu.with_memory_space_constraint(x, pltpu.HBM)

    base = base_of(in_hbm(momentum), in_hbm(master_weights))
    bases = [base] + [exchange(base, "mp", d) for d in range(1, 3 if n_mp == 4 else n_mp)]
    places = {(d, c): (d, c) for d in range(len(bases)) for c in range(capacity)}
    early, cuts = bases[1:], []
    if n_mp == 4:
        cut = capacity // 2
        cuts = [0, cut]
        for c in range(capacity):
            places[3, c] = (3, c) if c < cut else (4, c - cut)

    nvec = vector_grads.shape[1]
    comp, near, far = left_terms(
        pos,
        in_hbm(gradients),
        in_hbm(feedback),
        in_hbm(jnp.swapaxes(right_init, 1, 2)),
        vector_grads,
    )
    chip = add([near, exchange(far, "replica", 1)], BF16)
    near = add([chip] + [exchange(chip, "replica", CORES * d) for d in range(1, n_z)], F32)
    far = exchange(near, "replica", 1)

    send, keep, lt, vector_rows = right_terms(pos, near, far, gram_root, comp, upm, early)
    vector_total = vector_rows.reshape(-1)[:nvec]
    own, strip, *chip = chip_sum(pos, keep, exchange(send, "replica", 1), lt, replica_rows)
    plane = [exchange(part, "mp", d) for d, part in enumerate(chip, 1)]
    final = plane_sum(pos, own, strip, plane, n_z, nmat * rank, early[: len(cuts)], cuts)
    final, forwards, ltr = final[:n_z], final[n_z:-1], final[-1]
    late = [exchange(part, "mp", 2 - i) for i, part in enumerate(forwards)]
    bases += late
    final = [final[0]] + [exchange(final[d], "replica", CORES * d).astype(F32) for d in range(1, n_z)]
    final = tree_sum(final).astype(BF16)

    final = [final] + [exchange(final, "replica", CORES * d) for d in range(1, n_z)]
    whole = column_gather(pos, final, late)
    near = stack([whole] + [exchange(whole, "mp", d) for d in range(1, n_mp)])
    near = near.reshape(half, upm, rank // upm, n)
    far = exchange(near, "replica", 1)

    done = outputs(pos, owners, 0, comp, near, lt, ltr, bases, places, ())
    new_feedback, new_weights = outputs(pos, owners, half, comp, far, lt, ltr, bases, places, done)
    new_momentum, new_master = owned(pos, owners, momentum, master_weights, near, far, ltr)

    new_vector_momentum = 0.9 * vector_momentum + vector_total
    new_vector_params = vector_params - 0.1 * new_vector_momentum
    return new_feedback, new_momentum, new_master, new_weights, new_vector_momentum, new_vector_params


def solution(mesh):
    return jax.shard_map(
        per_device,
        mesh=mesh,
        in_specs=(
            P("replica", None, "mp", None),
            P("replica", None, "mp", None),
            P(),
            P(),
            P(),
            P("mp", None, "replica", None),
            P("mp", None, "replica", None),
            P("replica", "mp"),
            P("mp"),
            P("mp"),
        ),
        out_specs=(
            P("replica", None, "mp", None),
            P("mp", None, "replica", None),
            P("mp", None, "replica", None),
            P(None, "replica", None),
            P("mp"),
            P("mp"),
        ),
        check_vma=False,
    )
```

```python
import functools

import jax
import jax.numpy as jnp
from jax import lax
from jax.experimental import pallas as pl
from jax.experimental.pallas import tpu as pltpu
from jax.sharding import PartitionSpec as P

CORES = 2
AHEAD = 3
BASE_ROWS = 16
COLUMNS = 512
F32 = jnp.float32
BF16 = jnp.bfloat16


def params(mib=12):
    return pltpu.CompilerParams(vmem_limit_bytes=mib * 1024 * 1024)


def cost(bytes_accessed=1000):
    return pl.CostEstimate(flops=1000, bytes_accessed=bytes_accessed, transcendentals=0)


def tree_sum(terms):
    while len(terms) > 1:
        terms = [terms[i] + terms[i + 1] for i in range(0, len(terms), 2)]
    return terms[0]


def exchange(x, axis, distance):
    size = lax.axis_size(axis)
    return lax.ppermute(x, axis, [(i, i ^ distance) for i in range(size)])


def left_kernel(pos, g_ref, f_ref, q_ref, vec_ref, comp_ref, near_ref, far_ref, total, feedback, right, sems):
    nmat, rows, _ = comp_ref.shape
    rank = q_ref.shape[1]
    part = near_ref.shape[0]
    cut = rows // 2 if rows % 32 == 0 else rows

    def copies(k):
        out = [pltpu.make_async_copy(q_ref.at[k], right.at[k], sems.at[k, 4])]
        for i, first in enumerate(range(0, rows, cut)):
            block = pl.ds(first, cut)
            for j, (source, target) in enumerate(((g_ref, comp_ref), (f_ref, feedback))):
                source, target = source.at[0, k, block], target.at[k, block]
                out.append(pltpu.make_async_copy(source, target, sems.at[k, 2 * i + j]))
        return out

    for k in range(min(AHEAD, nmat)):
        for copy in copies(k):
            copy.start()
    total[...] = jnp.zeros(total.shape, F32)
    width, nvec = total.shape[1], vec_ref.shape[1]
    for i, first in enumerate(range(0, nvec, width)):
        count = min(width, nvec - first)
        total[rows + i : rows + i + 1, :count] = vec_ref[:, first : first + count]

    for k in range(nmat):
        for copy in copies(k):
            copy.wait()
        if k + AHEAD < nmat:
            for copy in copies(k + AHEAD):
                copy.start()
        comp = comp_ref[k] + feedback[k]
        comp_ref[k] = comp
        total[:rows, k * rank : (k + 1) * rank] = lax.dot_general(
            comp, right[k], (((1,), (1,)), ((), ())), preferred_element_type=F32
        )

    for ref, core in ((near_ref, pos[2]), (far_ref, 1 - pos[2])):
        ref[...] = total[pl.ds(pl.multiple_of(core * part, 16), part), :]


def left_terms(pos, gradients, feedback, right_t, vec):
    _, nmat, rows, n = gradients.shape
    rank = right_t.shape[1]
    width = nmat * rank
    total = rows + -(-vec.shape[1] // width)
    total += -total % (16 * CORES)
    part = jax.ShapeDtypeStruct((total // CORES, width), F32)
    vmem = pl.BlockSpec(memory_space=pltpu.VMEM)
    any_spec = pl.BlockSpec(memory_space=pl.ANY)
    return pl.pallas_call(
        left_kernel,
        grid_spec=pltpu.PrefetchScalarGridSpec(
            num_scalar_prefetch=1,
            grid=(1,),
            in_specs=[any_spec] * 3 + [vmem],
            out_specs=[vmem] * 3,
            scratch_shapes=[
                pltpu.VMEM((total, width), F32),
                pltpu.VMEM((nmat, rows, n), BF16),
                pltpu.VMEM((nmat, rank, n), BF16),
                pltpu.SemaphoreType.DMA((nmat, 5)),
            ],
        ),
        out_shape=[jax.ShapeDtypeStruct((nmat, rows, n), BF16), part, part],
        compiler_params=params(20),
        cost_estimate=cost(),
        name="left_terms",
    )(pos, gradients, feedback, right_t, vec)


def add_kernel(copies, *refs):
    out = refs[-1]
    parts = [ref[...].astype(F32) for ref in refs[:-1]]
    if len(parts) == 1:
        parts = [refs[0][i].astype(F32) for i in range(refs[0].shape[0])]
    total = tree_sum(parts).astype(out.dtype)
    if copies:
        for i in range(copies):
            out[i] = total
    else:
        out[...] = total


def add(parts, dtype, copies=0):
    vmem = pl.BlockSpec(memory_space=pltpu.VMEM)
    shape = parts[0].shape if len(parts) > 1 else parts[0].shape[1:]
    shape = (copies,) + shape if copies else shape
    return pl.pallas_call(
        functools.partial(add_kernel, copies),
        in_specs=[vmem] * len(parts),
        out_specs=vmem,
        out_shape=jax.ShapeDtypeStruct(shape, dtype),
        compiler_params=params(),
        cost_estimate=cost(),
        name="add",
    )(*parts)


def send_kernel(half, pos, near_ref, far_ref, gram_ref, comp_ref, *refs):
    send_ref, lt_ref, vec_ref, left, gram = refs[-5:]
    t = pl.program_id(0)
    rows = comp_ref.shape[1]
    rank = gram_ref.shape[1]

    @pl.when(t == 0)
    def _():
        part = near_ref.shape[0]
        for ref, core in ((near_ref, pos[2]), (far_ref, 1 - pos[2])):
            left[pl.ds(pl.multiple_of(core * part, 16), part), :] = ref[...]
        vec_ref[...] = left[rows:, :]
        gram[...] = jnp.zeros(gram.shape, F32)
        for i in range(gram_ref.shape[0]):
            gram[i * rank : (i + 1) * rank, i * rank : (i + 1) * rank] = gram_ref[i]
        hat = jnp.dot(
            left[:rows, :], gram[...], precision=lax.Precision.HIGHEST, preferred_element_type=F32
        )
        lt_ref[...] = hat.T.astype(BF16)

    right_rows((1 - pos[2]) * half, lt_ref, comp_ref, send_ref)


def right_rows(start, lt_ref, comp_ref, out_ref):
    upm, unit = out_ref.shape[1], out_ref.shape[2]
    k = pl.program_id(0) + start
    rows = pl.ds(pl.multiple_of(k * upm * unit, upm * unit), upm * unit)
    terms = jnp.dot(lt_ref[rows, :], comp_ref[k], preferred_element_type=F32)
    for i in range(upm):
        out_ref[0, i] = terms[i * unit : (i + 1) * unit].astype(out_ref.dtype)


def keep_kernel(half, pos, lt_ref, comp_ref, keep_ref):
    right_rows(pos[2] * half, lt_ref, comp_ref, keep_ref)


def right_terms(pos, near, far, gram, comp, upm):
    nmat, rows, n = comp.shape
    rank = gram.shape[1]
    width = nmat * rank
    half = nmat // CORES
    total = CORES * near.shape[0]
    shape = (half, upm, rank // upm, n)
    vmem = pl.BlockSpec(memory_space=pltpu.VMEM)
    out = pl.BlockSpec((1,) + shape[1:], lambda t, pos: (t, 0, 0, 0))
    send, lt, vec = pl.pallas_call(
        functools.partial(send_kernel, half),
        grid_spec=pltpu.PrefetchScalarGridSpec(
            num_scalar_prefetch=1,
            grid=(half,),
            in_specs=[
                vmem,
                vmem,
                vmem,
                vmem,
            ],
            out_specs=[out, vmem, vmem],
            scratch_shapes=[pltpu.VMEM((total, width), F32), pltpu.VMEM((width, width), F32)],
        ),
        out_shape=[
            jax.ShapeDtypeStruct(shape, BF16),
            jax.ShapeDtypeStruct((width, rows), BF16),
            jax.ShapeDtypeStruct((total - rows, width), F32),
        ],
        compiler_params=params(),
        cost_estimate=cost(),
        name="right_send",
    )(pos, near, far, gram, comp)
    keep = pl.pallas_call(
        functools.partial(keep_kernel, half),
        grid_spec=pltpu.PrefetchScalarGridSpec(
            num_scalar_prefetch=1,
            grid=(half,),
            in_specs=[vmem, vmem],
            out_specs=out,
        ),
        out_shape=jax.ShapeDtypeStruct(shape, F32),
        compiler_params=params(),
        cost_estimate=cost(4 * nmat * rows * n),
        name="right_keep",
    )(pos, lt, comp)
    return send, keep, lt, vec


def chip_kernel(replica_rows, pos, keep_ref, recv_ref, lt_ref, *refs):
    out_ref = refs[-1]
    upm = keep_ref.shape[1]
    count, height, n = out_ref.shape
    height -= keep_ref.shape[2]
    left = lt_ref[...].astype(F32).T
    strip = left[:replica_rows]
    for i in range(1, left.shape[0] // replica_rows):
        strip = jnp.where(pos[3] == i, left[i * replica_rows : (i + 1) * replica_rows], strip)
    strip = jnp.concatenate(
        [strip[i * height : (i + 1) * height] for i in range(replica_rows // height)], axis=1
    )
    for i in range(count):
        terms = keep_ref[i // upm, i % upm] + recv_ref[i // upm, i % upm].astype(F32)
        out_ref[i] = jnp.concatenate([terms, strip], axis=0).astype(BF16)


def chip_sum(pos, keep, recv, lt, replica_rows, after):
    half, upm, unit, n = keep.shape
    height = lt.shape[0] * replica_rows // n
    vmem = pl.BlockSpec(memory_space=pltpu.VMEM)
    return pl.pallas_call(
        functools.partial(chip_kernel, replica_rows),
        grid_spec=pltpu.PrefetchScalarGridSpec(
            num_scalar_prefetch=1,
            grid=(1,),
            in_specs=[vmem] * 3 + [pl.BlockSpec(memory_space=pl.ANY)] * len(after),
            out_specs=vmem,
        ),
        out_shape=jax.ShapeDtypeStruct((half * upm, unit + height, n), BF16),
        compiler_params=params(),
        cost_estimate=cost(),
        name="chip_sum",
    )(pos, keep, recv, lt, *after)


def plane_kernel(cuts, pos, terms_ref, *refs):
    wholes, (out_ref, ltr_ref, *forwards) = refs[: len(cuts)], refs[len(cuts) :]
    n_z, unit, cols = out_ref.shape
    for z in range(n_z):
        block = slice(z * cols, (z + 1) * cols)
        parts = [terms_ref[i, :, block].astype(F32)[:unit] for i in range(terms_ref.shape[0])]
        out_ref[z] = tree_sum(parts).astype(BF16)
    strip = terms_ref[pos[4]].astype(F32)[unit:]
    width = ltr_ref.shape[0]
    rows = [strip[:, i * width : (i + 1) * width] for i in range(strip.shape[1] // width)]
    ltr_ref[...] = jnp.concatenate(rows, axis=0).T.astype(BF16)
    for whole, out, first in zip(wholes, forwards, cuts):
        out[...] = whole[first : first + out.shape[0]]


def plane_sum(pos, terms, unit, n_z, width, wholes, cuts):
    _, height, n = terms.shape
    outs = [
        jax.ShapeDtypeStruct((n_z, unit, n // n_z), BF16),
        jax.ShapeDtypeStruct((width, (height - unit) * n // width), BF16),
    ]
    outs += [jax.ShapeDtypeStruct((x.shape[0] // 2,) + x.shape[1:], x.dtype) for x in wholes]
    vmem = pl.BlockSpec(memory_space=pltpu.VMEM)
    return pl.pallas_call(
        functools.partial(plane_kernel, cuts),
        grid_spec=pltpu.PrefetchScalarGridSpec(
            num_scalar_prefetch=1,
            grid=(1,),
            in_specs=[vmem] * (1 + len(wholes)),
            out_specs=[vmem] * len(outs),
        ),
        out_shape=outs,
        compiler_params=params(),
        cost_estimate=cost(),
        name="plane_sum",
    )(pos, terms, *wholes)


def column_kernel(parts_ref, *refs):
    out_ref = refs[-1]
    cols = parts_ref.shape[2]
    for z in range(parts_ref.shape[0]):
        part = parts_ref[z]
        for i in range(out_ref.shape[0]):
            out_ref[i, :, z * cols : (z + 1) * cols] = part


def column_gather(parts, copies, after):
    n_z, unit, cols = parts.shape
    vmem = pl.BlockSpec(memory_space=pltpu.VMEM)
    return pl.pallas_call(
        column_kernel,
        in_specs=[vmem] + [pl.BlockSpec(memory_space=pl.ANY)] * len(after),
        out_specs=vmem,
        out_shape=jax.ShapeDtypeStruct((copies, unit, cols * n_z), BF16),
        compiler_params=params(),
        cost_estimate=cost(),
        name="column_gather",
    )(parts, *after)


def matrix_of(right_ref, slot):
    parts = [right_ref[slot, i] for i in range(right_ref.shape[1])]
    return parts[0] if len(parts) == 1 else jnp.concatenate(parts, axis=0)


def product(lt, right):
    return lax.dot_general(lt, right, (((0,), (0,)), ((), ())), preferred_element_type=F32)


def rank_of(owners, k):
    count = jnp.int32(0)
    for j in range(owners.shape[0]):
        count += jnp.where((owners[j] == owners[k]) & (j < k), 1, 0)
    return count


def outputs_kernel(second, places, pos, owners, comp_ref, near_ref, lt_ref, ltr_ref, *refs):
    n_base = len({a for a, _ in places.values()})
    n_state = 2 if second else 0
    bases, refs = refs[:n_base], refs[n_base:]
    if second:
        far_ref, refs = refs[0], refs[1:]
        states, refs = refs[:n_state], refs[n_state + 2 :]
    outs, refs = refs[: 2 + n_state], refs[2 + n_state :]
    held, feedback, weights, fetch_sem, out_sem = refs[:5]
    half, rank = near_ref.shape[0], near_ref.shape[1] * near_ref.shape[2]
    rows, n = feedback.shape[1:]
    capacity = max(c for _, c in places) + 1
    core = 1 - pos[2] if second else pos[2]
    right_ref = far_ref if second else near_ref

    for j in range(half):
        k = core * half + j
        slot = (owners[k] ^ pos[5]) * capacity + rank_of(owners, k)
        for (d, c), (a, row) in places.items():

            @pl.when(slot == d * capacity + c)
            def _():
                pltpu.make_async_copy(bases[a].at[row], held.at[j], fetch_sem.at[j]).start()

    if second:
        scratch, state_in, state_out = refs[5:7], refs[7], refs[8]
        loads = [
            pltpu.make_async_copy(states[i].at[0, c], scratch[i].at[c], state_in.at[i, c])
            for c in range(capacity)
            for i in range(n_state)
        ]
        for load in loads:
            load.start()

    stores = []
    for j in range(half):
        k = core * half + j
        part = pl.ds(pl.multiple_of(k * rank, rank), rank)
        lt, ltr = lt_ref[part, :], ltr_ref[part, :]
        right = matrix_of(right_ref, j)
        pltpu.make_async_copy(bases[0].at[0], held.at[j], fetch_sem.at[j]).wait()
        for first in range(0, n, COLUMNS):
            block = slice(first, first + COLUMNS)
            approx = product(ltr, right[:, block])
            weights[j, :, block] = (held[j, :, block].astype(F32) - 0.1 * approx).astype(BF16)
        copies = [pltpu.make_async_copy(weights.at[j], outs[1].at[k], out_sem.at[j, 2])]
        copies[0].start()
        cut = rows // 2 if rows % 32 == 0 else rows
        for i, top in enumerate(range(0, rows, cut)):
            for first in range(0, n, COLUMNS):
                block = slice(first, first + COLUMNS)
                approx = product(lt[:, top : top + cut], right[:, block])
                wide = comp_ref[k, top : top + cut, block].astype(F32)
                feedback[j, top : top + cut, block] = (wide - approx).astype(BF16)
            source, target = feedback.at[j, pl.ds(top, cut)], outs[0].at[0, k, pl.ds(top, cut)]
            copies.append(pltpu.make_async_copy(source, target, out_sem.at[j, i]))
            copies[-1].start()
        stores += copies

    for c in range(capacity if second else 0):
        matrix = jnp.int32(-1)
        for k in range(owners.shape[0]):
            matrix = jnp.where((owners[k] == pos[5]) & (rank_of(owners, k) == c), k, matrix)
        safe = jnp.maximum(matrix, 0)
        inner = lax.rem(safe, half)
        is_far = safe // half == core
        right = jnp.where(is_far, matrix_of(far_ref, inner), matrix_of(near_ref, inner))
        ltr = ltr_ref[pl.ds(pl.multiple_of(safe * rank, rank), rank), :]
        for load in loads[c * n_state : (c + 1) * n_state]:
            load.wait()
        for first in range(0, n, COLUMNS):
            block = slice(first, first + COLUMNS)
            approx = jnp.where(matrix >= 0, product(ltr, right[:, block]), 0.0)
            momentum = 0.9 * scratch[0][c, :, block] + approx
            scratch[0][c, :, block] = momentum
            scratch[1][c, :, block] -= 0.1 * momentum
        for i in range(n_state):
            copy = pltpu.make_async_copy(scratch[i].at[c], outs[2 + i].at[0, c], state_out.at[i, c])
            copy.start()
            stores.append(copy)

    for copy in stores:
        copy.wait()


def outputs(pos, owners, comp, near, lt, ltr, bases, places, far=None, states=(), earlier=()):
    nmat, rows, n = comp.shape
    half = near.shape[0]
    capacity, replica_rows = bases[0].shape[:2]
    second = far is not None
    any_spec = pl.BlockSpec(memory_space=pl.ANY)
    vmem = pl.BlockSpec(memory_space=pltpu.VMEM)
    scratch = [
        pltpu.VMEM((half, replica_rows, n), BF16),
        pltpu.VMEM((half, rows, n), BF16),
        pltpu.VMEM((half, replica_rows, n), BF16),
        pltpu.SemaphoreType.DMA((half,)),
        pltpu.SemaphoreType.DMA((half, 3)),
    ]
    if second:
        scratch += [pltpu.VMEM((capacity, replica_rows, n), F32)] * 2
        scratch += [pltpu.SemaphoreType.DMA((2, capacity))] * 2
    outs = [
        jax.ShapeDtypeStruct((1, nmat, rows, n), BF16),
        jax.ShapeDtypeStruct((nmat, replica_rows, n), BF16),
    ] + [jax.ShapeDtypeStruct(x.shape, F32) for x in states]
    fars = [far] if second else []
    return pl.pallas_call(
        functools.partial(outputs_kernel, second, places),
        grid_spec=pltpu.PrefetchScalarGridSpec(
            num_scalar_prefetch=2,
            grid=(1,),
            in_specs=[vmem] * 4
            + [any_spec] * len(bases)
            + [vmem] * len(fars)
            + [any_spec] * (len(states) + len(earlier)),
            out_specs=[any_spec] * len(outs),
            scratch_shapes=scratch,
        ),
        out_shape=outs,
        input_output_aliases={
            6 + len(bases) + len(fars) + len(states) + i: i for i in range(len(earlier))
        },
        compiler_params=params(24),
        cost_estimate=cost(),
        name="outputs",
    )(pos, owners, comp, near, lt, ltr, *bases, *fars, *states, *earlier)


def base_kernel(momentum_ref, master_ref, out_ref, momentum, master, sems):
    capacity, rows, _ = out_ref.shape
    blocks = [(c, first) for c in range(capacity) for first in range(0, rows, BASE_ROWS)]

    def copies(i):
        c, first = blocks[i]
        part = pl.ds(first, BASE_ROWS)
        return [
            pltpu.make_async_copy(source.at[0, c, part], target.at[c, part], sems.at[j, i])
            for j, (source, target) in enumerate(((momentum_ref, momentum), (master_ref, master)))
        ]

    for i in range(len(blocks)):
        for copy in copies(i):
            copy.start()
    for i, (c, first) in enumerate(blocks):
        for copy in copies(i):
            copy.wait()
        part = slice(first, first + BASE_ROWS)
        out_ref[c, part] = (master[c, part] - 0.09 * momentum[c, part]).astype(BF16)


def base_of(momentum, master):
    _, capacity, rows, n = momentum.shape
    state = pltpu.VMEM((capacity, rows, n), F32)
    return pl.pallas_call(
        base_kernel,
        in_specs=[pl.BlockSpec(memory_space=pl.ANY)] * 2,
        out_specs=pl.BlockSpec(memory_space=pltpu.VMEM),
        out_shape=jax.ShapeDtypeStruct((capacity, rows, n), BF16),
        scratch_shapes=[state, state, pltpu.SemaphoreType.DMA((2, capacity * rows // BASE_ROWS))],
        compiler_params=params(),
        cost_estimate=cost(),
        name="base",
    )(momentum, master)


def per_device(
    gradients,
    feedback,
    right_init,
    gram_root,
    owners,
    momentum,
    master_weights,
    vector_grads,
    vector_momentum,
    vector_params,
):
    nmat, rows, n = gradients.shape[1:]
    rank = right_init.shape[2]
    n_mp = lax.axis_size("mp")
    n_z = lax.axis_size("replica") // CORES
    capacity, replica_rows = momentum.shape[1:3]
    p = lax.axis_index("mp")
    r = lax.axis_index("replica")
    core, z = r % CORES, r // CORES
    upm = CORES * n_mp // nmat
    half = nmat // CORES
    code = core * n_mp + p
    first = r * replica_rows

    pos = jnp.stack([p, z, core, first % rows // replica_rows, first // rows, p]).astype(jnp.int32)
    in_hbm = lambda x: pltpu.with_memory_space_constraint(x, pltpu.HBM)

    base = base_of(in_hbm(momentum), in_hbm(master_weights))
    bases = [base] + [exchange(base, "mp", d) for d in range(1, 3 if n_mp == 4 else n_mp)]
    places = {(d, c): (d, c) for d in range(len(bases)) for c in range(capacity)}
    early, cuts = bases[1:], []
    if n_mp == 4:
        cut = capacity // 2
        cuts = [0, cut]
        for c in range(capacity):
            places[3, c] = (3, c) if c < cut else (4, c - cut)

    nvec = vector_grads.shape[1]
    comp, near, far = left_terms(
        pos,
        in_hbm(gradients),
        in_hbm(feedback),
        in_hbm(jnp.swapaxes(right_init, 1, 2)),
        vector_grads,
    )
    columns = [[d * CORES + c for d in range(n_z)] for c in range(CORES)]
    along_z = lambda x: lax.all_to_all(x, "replica", 0, 0, axis_index_groups=columns, tiled=True)
    in_plane = lambda x: lax.all_to_all(x, "mp", 0, 0, tiled=True)
    chip = add([near, exchange(far, "replica", 1)], BF16, n_z)
    near = add([along_z(chip)], F32)
    far = exchange(near, "replica", 1)

    unit = rank // upm
    send, keep, lt, vector_rows = right_terms(pos, near, far, gram_root, comp, upm)
    vector_total = vector_rows.reshape(-1)[:nvec]
    chip = chip_sum(pos, keep, exchange(send, "replica", 1), lt, replica_rows, early)
    final, ltr, *forwards = plane_sum(
        pos, in_plane(chip), unit, n_z, nmat * rank, early[: len(cuts)], cuts
    )
    late = [exchange(part, "mp", 2 - i) for i, part in enumerate(forwards)]
    bases += late
    final = add([along_z(final)], BF16, n_z)

    whole = column_gather(along_z(final), n_mp, late)
    near = in_plane(whole).reshape(half, upm, unit, n)
    far = exchange(near, "replica", 1)

    done = outputs(pos, owners, comp, near, lt, ltr, bases, places)
    new_feedback, new_weights, new_momentum, new_master = outputs(
        pos, owners, comp, near, lt, ltr, bases, places, far, (momentum, master_weights), done
    )

    new_vector_momentum = 0.9 * vector_momentum + vector_total
    new_vector_params = vector_params - 0.1 * new_vector_momentum
    return new_feedback, new_momentum, new_master, new_weights, new_vector_momentum, new_vector_params


def solution(mesh):
    return jax.shard_map(
        per_device,
        mesh=mesh,
        in_specs=(
            P("replica", None, "mp", None),
            P("replica", None, "mp", None),
            P(),
            P(),
            P(),
            P("mp", None, "replica", None),
            P("mp", None, "replica", None),
            P("replica", "mp"),
            P("mp"),
            P("mp"),
        ),
        out_specs=(
            P("replica", None, "mp", None),
            P("mp", None, "replica", None),
            P("mp", None, "replica", None),
            P(None, "replica", None),
            P("mp"),
            P("mp"),
        ),
        check_vma=False,
    )
```

```python
import functools

import jax
import jax.numpy as jnp
from jax import lax
from jax.experimental import pallas as pl
from jax.experimental.pallas import tpu as pltpu
from jax.sharding import PartitionSpec as P

CORES = 2
AHEAD = 4
BASE_ROWS = 16
COLUMNS = 256
F32 = jnp.float32
BF16 = jnp.bfloat16


def params(mib=12):
    return pltpu.CompilerParams(vmem_limit_bytes=mib * 1024 * 1024)


def cost(flops=1000, bytes_accessed=1000):
    return pl.CostEstimate(flops=flops, bytes_accessed=bytes_accessed, transcendentals=0)


def tree_sum(terms):
    while len(terms) > 1:
        terms = [terms[i] + terms[i + 1] for i in range(0, len(terms), 2)]
    return terms[0]


def exchange(x, axis, distance):
    size = lax.axis_size(axis)
    return lax.ppermute(x, axis, [(i, i ^ distance) for i in range(size)])


def left_kernel(pos, g_ref, f_ref, q_ref, vec_ref, comp_ref, near_ref, far_ref, total, feedback, right, sems):
    nmat, rows, _ = comp_ref.shape
    rank = q_ref.shape[1]
    part = near_ref.shape[0]
    cut = rows // 2 if rows % 32 == 0 else rows

    def copies(k):
        out = [pltpu.make_async_copy(q_ref.at[k], right.at[k], sems.at[k, 4])]
        for i, first in enumerate(range(0, rows, cut)):
            block = pl.ds(first, cut)
            for j, (source, target) in enumerate(((g_ref, comp_ref), (f_ref, feedback))):
                source, target = source.at[0, k, block], target.at[k, block]
                out.append(pltpu.make_async_copy(source, target, sems.at[k, 2 * i + j]))
        return out

    for k in range(min(AHEAD, nmat)):
        for copy in copies(k):
            copy.start()
    total[...] = jnp.zeros(total.shape, F32)
    width, nvec = total.shape[1], vec_ref.shape[1]
    for i, first in enumerate(range(0, nvec, width)):
        count = min(width, nvec - first)
        total[rows + i : rows + i + 1, :count] = vec_ref[:, first : first + count]

    for k in range(nmat):
        for copy in copies(k):
            copy.wait()
        if k + AHEAD < nmat:
            for copy in copies(k + AHEAD):
                copy.start()
        comp = comp_ref[k] + feedback[k]
        comp_ref[k] = comp
        total[:rows, k * rank : (k + 1) * rank] = lax.dot_general(
            comp, right[k], (((1,), (1,)), ((), ())), preferred_element_type=F32
        )

    for ref, core in ((near_ref, pos[2]), (far_ref, 1 - pos[2])):
        ref[...] = total[pl.ds(pl.multiple_of(core * part, 16), part), :]


def left_terms(pos, gradients, feedback, right_t, vec):
    _, nmat, rows, n = gradients.shape
    rank = right_t.shape[1]
    width = nmat * rank
    total = rows + -(-vec.shape[1] // width)
    total += -total % (16 * CORES)
    part = jax.ShapeDtypeStruct((total // CORES, width), F32)
    vmem = pl.BlockSpec(memory_space=pltpu.VMEM)
    any_spec = pl.BlockSpec(memory_space=pl.ANY)
    return pl.pallas_call(
        left_kernel,
        grid_spec=pltpu.PrefetchScalarGridSpec(
            num_scalar_prefetch=1,
            grid=(1,),
            in_specs=[any_spec] * 3 + [vmem],
            out_specs=[vmem] * 3,
            scratch_shapes=[
                pltpu.VMEM((total, width), F32),
                pltpu.VMEM((nmat, rows, n), BF16),
                pltpu.VMEM((nmat, rank, n), BF16),
                pltpu.SemaphoreType.DMA((nmat, 5)),
            ],
        ),
        out_shape=[jax.ShapeDtypeStruct((nmat, rows, n), BF16), part, part],
        compiler_params=params(20),
        cost_estimate=cost(),
        name="left_terms",
    )(pos, gradients, feedback, right_t, vec)


def add_kernel(*refs):
    out = refs[-1]
    out[...] = tree_sum([ref[...].astype(F32) for ref in refs[:-1]]).astype(out.dtype)


def add(parts, dtype):
    vmem = pl.BlockSpec(memory_space=pltpu.VMEM)
    return pl.pallas_call(
        add_kernel,
        in_specs=[vmem] * len(parts),
        out_specs=vmem,
        out_shape=jax.ShapeDtypeStruct(parts[0].shape, dtype),
        compiler_params=params(),
        cost_estimate=cost(),
        name="add",
    )(*parts)


def send_kernel(half, pos, near_ref, far_ref, gram_ref, comp_ref, *refs):
    send_ref, lt_ref, left_ref, vec_ref, left, gram = refs
    t = pl.program_id(0)
    rows = comp_ref.shape[1]
    rank = gram_ref.shape[1]

    @pl.when(t == 0)
    def _():
        part = near_ref.shape[0]
        for ref, core in ((near_ref, pos[2]), (far_ref, 1 - pos[2])):
            left[pl.ds(pl.multiple_of(core * part, 16), part), :] = ref[...]
        vec_ref[...] = left[rows:, :]
        gram[...] = jnp.zeros(gram.shape, F32)
        for i in range(gram_ref.shape[0]):
            gram[i * rank : (i + 1) * rank, i * rank : (i + 1) * rank] = gram_ref[i]
        hat = jnp.dot(
            left[:rows, :], gram[...], precision=lax.Precision.HIGHEST, preferred_element_type=F32
        )
        lt_ref[...] = hat.T.astype(BF16)
        for i in range(gram_ref.shape[0]):
            left_ref[i] = hat[:, i * rank : (i + 1) * rank].astype(BF16)

    right_rows(half, pos, lt_ref, comp_ref, send_ref)


def right_rows(start, pos, lt_ref, comp_ref, out_ref):
    upm, unit = out_ref.shape[1], out_ref.shape[2]
    k = (pl.program_id(0) + start) ^ pos[0]
    rows = pl.ds(pl.multiple_of(k * upm * unit, upm * unit), upm * unit)
    terms = jnp.dot(lt_ref[rows, :], comp_ref[k], preferred_element_type=F32)
    for i in range(upm):
        out_ref[0, i ^ pos[1]] = terms[i * unit : (i + 1) * unit].astype(out_ref.dtype)


def keep_kernel(pos, lt_ref, comp_ref, *refs):
    right_rows(0, pos, lt_ref, comp_ref, refs[-1])


def right_terms(pos, near, far, gram, comp, upm, after):
    nmat, rows, n = comp.shape
    rank = gram.shape[1]
    width = nmat * rank
    half = nmat // CORES
    total = CORES * near.shape[0]
    shape = (half, upm, rank // upm, n)
    vmem = pl.BlockSpec(memory_space=pltpu.VMEM)
    out = pl.BlockSpec((1,) + shape[1:], lambda t, pos: (t, 0, 0, 0))
    send, lt, left, vec = pl.pallas_call(
        functools.partial(send_kernel, half),
        grid_spec=pltpu.PrefetchScalarGridSpec(
            num_scalar_prefetch=1,
            grid=(half,),
            in_specs=[
                vmem,
                vmem,
                vmem,
                vmem,
            ],
            out_specs=[out, vmem, vmem, vmem],
            scratch_shapes=[pltpu.VMEM((total, width), F32), pltpu.VMEM((width, width), F32)],
        ),
        out_shape=[
            jax.ShapeDtypeStruct(shape, BF16),
            jax.ShapeDtypeStruct((width, rows), BF16),
            jax.ShapeDtypeStruct((nmat, rows, rank), BF16),
            jax.ShapeDtypeStruct((total - rows, width), F32),
        ],
        compiler_params=params(),
        cost_estimate=cost(),
        name="right_send",
    )(pos, near, far, gram, comp)
    keep = pl.pallas_call(
        keep_kernel,
        grid_spec=pltpu.PrefetchScalarGridSpec(
            num_scalar_prefetch=1,
            grid=(half,),
            in_specs=[vmem, vmem] + [pl.BlockSpec(memory_space=pl.ANY)] * len(after),
            out_specs=out,
        ),
        out_shape=jax.ShapeDtypeStruct(shape, F32),
        compiler_params=params(),
        cost_estimate=cost(2000 * nmat * rows * n),
        name="right_keep",
    )(pos, lt, comp, *after)
    return send, keep, lt, left, vec


def chip_kernel(replica_rows, pos, keep_ref, recv_ref, lt_ref, own_ref, strip_ref, *sends):
    upm = keep_ref.shape[1]
    n = own_ref.shape[1]
    left = lt_ref[...].astype(F32).T
    strip = left[:replica_rows]
    for i in range(1, left.shape[0] // replica_rows):
        strip = jnp.where(pos[6] == i, left[i * replica_rows : (i + 1) * replica_rows], strip)
    height = strip_ref.shape[0]
    strip = jnp.concatenate(
        [strip[i * height : (i + 1) * height] for i in range(replica_rows // height)], axis=1
    )
    strip_ref[...] = strip
    own_ref[...] = keep_ref[0, 0] + recv_ref[0, 0].astype(F32)
    for d, out in enumerate(sends, 1):
        j, i = d // upm, d % upm
        terms = keep_ref[j, i] + recv_ref[j, i].astype(F32)
        out[...] = jnp.concatenate([terms, strip], axis=0).astype(BF16)


def chip_sum(pos, keep, recv, lt, replica_rows):
    half, upm, unit, n = keep.shape
    height = lt.shape[0] * replica_rows // n
    vmem = pl.BlockSpec(memory_space=pltpu.VMEM)
    outs = [jax.ShapeDtypeStruct((unit, n), F32), jax.ShapeDtypeStruct((height, n), F32)]
    outs += [jax.ShapeDtypeStruct((unit + height, n), BF16)] * (half * upm - 1)
    return pl.pallas_call(
        functools.partial(chip_kernel, replica_rows),
        grid_spec=pltpu.PrefetchScalarGridSpec(
            num_scalar_prefetch=1,
            grid=(1,),
            in_specs=[vmem] * 3,
            out_specs=[vmem] * len(outs),
        ),
        out_shape=outs,
        compiler_params=params(),
        cost_estimate=cost(),
        name="chip_sum",
    )(pos, keep, recv, lt)


def column_kernel(n_z, pos, *refs):
    out = refs[-1]
    cols = out.shape[1] // n_z
    for d in range(n_z):
        out[:, pl.ds(pl.multiple_of((pos[4] ^ d) * cols, cols), cols)] = refs[d][...]


def column_gather(pos, parts, after):
    unit, cols = parts[0].shape
    vmem = pl.BlockSpec(memory_space=pltpu.VMEM)
    return pl.pallas_call(
        functools.partial(column_kernel, len(parts)),
        grid_spec=pltpu.PrefetchScalarGridSpec(
            num_scalar_prefetch=1,
            grid=(1,),
            in_specs=[vmem] * len(parts) + [pl.BlockSpec(memory_space=pl.ANY)] * len(after),
            out_specs=vmem,
        ),
        out_shape=jax.ShapeDtypeStruct((unit, cols * len(parts)), BF16),
        compiler_params=params(),
        cost_estimate=cost(),
        name="column_gather",
    )(pos, *parts, *after)


def plane_kernel(pos, own_ref, strip_ref, *refs):
    n_z = own_ref.shape[1] // refs[-2].shape[1]
    terms, outs, ltr_ref = refs[: -n_z - 1], refs[-n_z - 1 : -1], refs[-1]
    unit, n = own_ref.shape
    cols = n // n_z
    for d, out in enumerate(outs):
        block = pl.ds(pl.multiple_of((pos[4] ^ d) * cols, cols), cols)
        parts = [own_ref[:, block]] + [term[:, block].astype(F32)[:unit] for term in terms]
        out[...] = tree_sum(parts).astype(out.dtype)
    strip = strip_ref[...]
    for d, term in enumerate(terms, 1):
        strip = jnp.where(pos[7] == d, term[...].astype(F32)[unit:], strip)
    nmat, _, rank = ltr_ref.shape
    width = nmat * rank
    rows = [strip[:, i * width : (i + 1) * width] for i in range(n // width)]
    rows = jnp.concatenate(rows, axis=0)
    for i in range(nmat):
        ltr_ref[i] = rows[:, i * rank : (i + 1) * rank].astype(BF16)


def plane_sum(pos, own, strip, terms, n_z, nmat, rank):
    unit, n = own.shape
    outs = [jax.ShapeDtypeStruct((unit, n // n_z), BF16 if d else F32) for d in range(n_z)]
    outs.append(jax.ShapeDtypeStruct((nmat, strip.size // (nmat * rank), rank), BF16))
    vmem = pl.BlockSpec(memory_space=pltpu.VMEM)
    return pl.pallas_call(
        plane_kernel,
        grid_spec=pltpu.PrefetchScalarGridSpec(
            num_scalar_prefetch=1,
            grid=(1,),
            in_specs=[vmem] * (2 + len(terms)),
            out_specs=[vmem] * len(outs),
        ),
        out_shape=outs,
        compiler_params=params(),
        cost_estimate=cost(),
        name="plane_sum",
    )(pos, own, strip, *terms)


def forward_kernel(cuts, *refs):
    for whole, out, first in zip(refs, refs[-len(cuts) :], cuts):
        out[...] = whole[first : first + out.shape[0]]


def forward(wholes, cuts, count, after):
    vmem = pl.BlockSpec(memory_space=pltpu.VMEM)
    shapes = [(count,) + x.shape[1:] for x in wholes]
    return pl.pallas_call(
        functools.partial(forward_kernel, cuts),
        in_specs=[vmem] * len(wholes) + [pl.BlockSpec(memory_space=pl.ANY)],
        out_specs=[vmem] * len(wholes),
        out_shape=[jax.ShapeDtypeStruct(shape, BF16) for shape in shapes],
        compiler_params=params(),
        cost_estimate=cost(20000 * wholes[0].size),
        name="forward",
    )(*wholes, after)


def rank_of(owners, k):
    count = jnp.int32(0)
    for j in range(owners.shape[0]):
        count += jnp.where((owners[j] == owners[k]) & (j < k), 1, 0)
    return count


def outputs_kernel(jobs, upm, places, n_state, pos, owners, comp_ref, left_ref, ltr_ref, *refs):
    n_base = len({a for a, _ in places.values()})
    half = comp_ref.shape[0] // CORES
    n_right = CORES * half * upm if n_state else len(jobs) * upm
    bases, rights, states = refs[:n_base], refs[n_base:][:n_right], refs[n_base + n_right :][:n_state]
    refs = refs[len(refs) - (3 + n_state) - 6 - (4 if n_state else 0) :]
    outs, token, refs = refs[: 2 + n_state], refs[2 + n_state], refs[3 + n_state :]
    token[...] = jnp.zeros(token.shape, F32)
    held, feedback, weights, gathered, fetch_sem, out_sem = refs[:6]
    rows, n = feedback.shape[1:]
    capacity = max(c for _, c in places) + 1

    def matrix(other, j):
        core = 1 - pos[2] if other else pos[2]
        return core * half + (lax.rem(pos[0], half) ^ j)

    def right_of(i):
        if upm == 1:
            return rights[i][...]
        for u in range(upm):
            gathered[u ^ pos[1]] = rights[i * upm + u][...]
        return jnp.concatenate([gathered[u] for u in range(upm)], axis=0)

    for i, job in enumerate(jobs):
        k = matrix(*job)
        slot = (owners[k] ^ pos[5]) * capacity + rank_of(owners, k)
        for (d, c), (a, row) in places.items():

            @pl.when(slot == d * capacity + c)
            def _():
                pltpu.make_async_copy(bases[a].at[row], held.at[i], fetch_sem.at[i]).start()

    if n_state:
        scratch, state_in, state_out = refs[6:8], refs[8], refs[9]
        loads = [
            pltpu.make_async_copy(states[i].at[0, c], scratch[i].at[c], state_in.at[i, c])
            for c in range(capacity)
            for i in range(n_state)
        ]
        for load in loads:
            load.start()

    stores = []
    for i, (other, j) in enumerate(jobs):
        k = matrix(other, j)
        right = right_of(other * half + j if n_state else i)
        left, ltr = left_ref[k], ltr_ref[k]
        pltpu.make_async_copy(bases[0].at[0], held.at[i], fetch_sem.at[i]).wait()
        for first in range(0, n, COLUMNS):
            block = slice(first, first + COLUMNS)
            approx = jnp.dot(ltr, right[:, block], preferred_element_type=F32)
            weights[i, :, block] = (held[i, :, block].astype(F32) - 0.1 * approx).astype(BF16)
        stores.append(pltpu.make_async_copy(weights.at[i], outs[1].at[k], out_sem.at[i, 1]))
        stores[-1].start()
        for first in range(0, n, COLUMNS):
            block = slice(first, first + COLUMNS)
            approx = jnp.dot(left, right[:, block], preferred_element_type=F32)
            feedback[i, :, block] = (comp_ref[k, :, block].astype(F32) - approx).astype(BF16)
        stores.append(pltpu.make_async_copy(feedback.at[i], outs[0].at[0, k], out_sem.at[i, 0]))
        stores[-1].start()

    for c in range(capacity if n_state else 0):
        mine = jnp.int32(-1)
        for k in range(owners.shape[0]):
            mine = jnp.where((owners[k] == pos[5]) & (rank_of(owners, k) == c), k, mine)
        for other in range(CORES):
            for j in range(half):

                @pl.when(jnp.maximum(mine, 0) == matrix(other, j))
                def _():
                    for u in range(upm):
                        unit = rights[(other * half + j) * upm + u][...]
                        gathered[u ^ pos[1] if upm > 1 else 0] = unit

        right = jnp.concatenate([gathered[u] for u in range(upm)], axis=0)
        ltr = ltr_ref[jnp.maximum(mine, 0)]
        for load in loads[c * n_state : (c + 1) * n_state]:
            load.wait()
        for first in range(0, n, COLUMNS):
            block = slice(first, first + COLUMNS)
            approx = jnp.dot(ltr, right[:, block], preferred_element_type=F32)
            momentum = 0.9 * scratch[0][c, :, block] + jnp.where(mine >= 0, approx, 0.0)
            scratch[0][c, :, block] = momentum
            scratch[1][c, :, block] -= 0.1 * momentum
        for i in range(n_state):
            copy = pltpu.make_async_copy(scratch[i].at[c], outs[2 + i].at[0, c], state_out.at[i, c])
            copy.start()
            stores.append(copy)

    for copy in stores:
        copy.wait()


def outputs(pos, owners, comp, left, ltr, bases, places, jobs, rights, upm, states=(), earlier=()):
    nmat, rows, n = comp.shape
    capacity, replica_rows = bases[0].shape[:2]
    any_spec = pl.BlockSpec(memory_space=pl.ANY)
    vmem = pl.BlockSpec(memory_space=pltpu.VMEM)
    count = len(jobs)
    scratch = [
        pltpu.VMEM((count, replica_rows, n), BF16),
        pltpu.VMEM((count, rows, n), BF16),
        pltpu.VMEM((count, replica_rows, n), BF16),
        pltpu.VMEM((upm,) + rights[0].shape, BF16),
        pltpu.SemaphoreType.DMA((count,)),
        pltpu.SemaphoreType.DMA((count, 2)),
    ]
    if states:
        scratch += [pltpu.VMEM((capacity, replica_rows, n), F32)] * 2
        scratch += [pltpu.SemaphoreType.DMA((2, capacity))] * 2
    outs = [
        jax.ShapeDtypeStruct((1, nmat, rows, n), BF16),
        jax.ShapeDtypeStruct((nmat, replica_rows, n), BF16),
    ] + [jax.ShapeDtypeStruct(x.shape, F32) for x in states]
    token = jax.ShapeDtypeStruct((8, 128), F32)
    first = 5 + len(bases) + len(rights) + len(states)
    return pl.pallas_call(
        functools.partial(outputs_kernel, jobs, upm, places, len(states)),
        grid_spec=pltpu.PrefetchScalarGridSpec(
            num_scalar_prefetch=2,
            grid=(1,),
            in_specs=[vmem] * 3
            + [any_spec] * len(bases)
            + [vmem] * len(rights)
            + [any_spec] * (len(states) + len(earlier)),
            out_specs=[any_spec] * len(outs) + [vmem],
            scratch_shapes=scratch,
        ),
        out_shape=outs + [token],
        input_output_aliases={first + i: i for i in range(len(earlier))},
        compiler_params=params(20),
        cost_estimate=cost(20000 * len(jobs) * rows * n),
        name="outputs",
    )(pos, owners, comp, left, ltr, *bases, *rights, *states, *earlier)


def base_kernel(momentum_ref, master_ref, out_ref, momentum, master, sems):
    capacity, rows, _ = out_ref.shape
    blocks = [(c, first) for c in range(capacity) for first in range(0, rows, BASE_ROWS)]

    def copies(i):
        c, first = blocks[i]
        part = pl.ds(first, BASE_ROWS)
        return [
            pltpu.make_async_copy(source.at[0, c, part], target.at[c, part], sems.at[j, i])
            for j, (source, target) in enumerate(((momentum_ref, momentum), (master_ref, master)))
        ]

    for i in range(len(blocks)):
        for copy in copies(i):
            copy.start()
    for i, (c, first) in enumerate(blocks):
        for copy in copies(i):
            copy.wait()
        part = slice(first, first + BASE_ROWS)
        out_ref[c, part] = (master[c, part] - 0.09 * momentum[c, part]).astype(BF16)


def base_of(momentum, master):
    _, capacity, rows, n = momentum.shape
    state = pltpu.VMEM((capacity, rows, n), F32)
    return pl.pallas_call(
        base_kernel,
        in_specs=[pl.BlockSpec(memory_space=pl.ANY)] * 2,
        out_specs=pl.BlockSpec(memory_space=pltpu.VMEM),
        out_shape=jax.ShapeDtypeStruct((capacity, rows, n), BF16),
        scratch_shapes=[state, state, pltpu.SemaphoreType.DMA((2, capacity * rows // BASE_ROWS))],
        compiler_params=params(),
        cost_estimate=cost(),
        name="base",
    )(momentum, master)


def per_device(
    gradients,
    feedback,
    right_init,
    gram_root,
    owners,
    momentum,
    master_weights,
    vector_grads,
    vector_momentum,
    vector_params,
):
    nmat, rows, n = gradients.shape[1:]
    rank = right_init.shape[2]
    unit = rank * nmat // (CORES * lax.axis_size("mp"))
    n_mp = lax.axis_size("mp")
    n_z = lax.axis_size("replica") // CORES
    capacity, replica_rows = momentum.shape[1:3]
    p = lax.axis_index("mp")
    r = lax.axis_index("replica")
    core, z = r % CORES, r // CORES
    upm = CORES * n_mp // nmat
    half = nmat // CORES
    code = core * n_mp + p
    first = r * replica_rows

    places_of = [code // upm, code % upm, core, r, z, p, first % rows // replica_rows, first // rows ^ p]
    pos = jnp.stack(places_of).astype(jnp.int32)
    in_hbm = lambda x: pltpu.with_memory_space_constraint(x, pltpu.HBM)

    base = base_of(in_hbm(momentum), in_hbm(master_weights))
    bases = [base] + [exchange(base, "mp", d) for d in range(1, 3 if n_mp == 4 else n_mp)]
    places = {(d, c): (d, c) for d in range(len(bases)) for c in range(capacity)}
    early, cuts = bases[1:], []
    if n_mp == 4:
        cut = capacity // 2
        cuts = [0, cut]
        for c in range(capacity):
            places[3, c] = (3, c) if c < cut else (4, c - cut)

    nvec = vector_grads.shape[1]
    comp, near, far = left_terms(
        pos,
        in_hbm(gradients),
        in_hbm(feedback),
        in_hbm(jnp.swapaxes(right_init, 1, 2)),
        vector_grads,
    )
    chip = add([near, exchange(far, "replica", 1)], BF16)
    near = add([chip] + [exchange(chip, "replica", CORES * d) for d in range(1, n_z)], F32)
    far = exchange(near, "replica", 1)

    send, keep, lt, left, vector_rows = right_terms(pos, near, far, gram_root, comp, upm, early)
    vector_total = vector_rows.reshape(-1)[:nvec]
    own, strip, *chip = chip_sum(pos, keep, exchange(send, "replica", 1), lt, replica_rows)
    plane = [exchange(part, "mp", d) for d, part in enumerate(chip, 1)]
    *final, ltr = plane_sum(pos, own, strip, plane, n_z, nmat, rank)
    arrived = [exchange(final[d], "replica", CORES * d) for d in range(1, n_z)]
    if cuts:
        forwards = forward(early, cuts, capacity // 2, ltr)
        bases += [exchange(part, "mp", 2 - i) for i, part in enumerate(forwards)]
    final = tree_sum([final[0]] + [part.astype(F32) for part in arrived]).astype(BF16)

    final = [final] + [exchange(final, "replica", CORES * d) for d in range(1, n_z)]
    whole = column_gather(pos, final, ())
    near = [whole] + [exchange(whole, "mp", d) for d in range(1, n_mp)]
    far, groups, done = [], [], ()
    for j in range(half):
        group = near[j * upm : (j + 1) * upm]
        sent = forward(group, [0] * upm, unit, token) if j else group
        groups.append([group, [exchange(part, "replica", 1) for part in sent]])
        far += groups[-1][1]
        jobs = [(0, j)] + ([(1, j - 1)] if j else [])
        rights = sum((groups[i][other] for other, i in jobs), [])
        *done, token = outputs(
            pos, owners, comp, left, ltr, bases, places, jobs, rights, upm, earlier=done
        )
    new_feedback, new_weights, new_momentum, new_master, _ = outputs(
        pos,
        owners,
        comp,
        left,
        ltr,
        bases,
        places,
        [(1, half - 1)],
        near + far,
        upm,
        (momentum, master_weights),
        done,
    )

    new_vector_momentum = 0.9 * vector_momentum + vector_total
    new_vector_params = vector_params - 0.1 * new_vector_momentum
    return new_feedback, new_momentum, new_master, new_weights, new_vector_momentum, new_vector_params


def solution(mesh):
    return jax.shard_map(
        per_device,
        mesh=mesh,
        in_specs=(
            P("replica", None, "mp", None),
            P("replica", None, "mp", None),
            P(),
            P(),
            P(),
            P("mp", None, "replica", None),
            P("mp", None, "replica", None),
            P("replica", "mp"),
            P("mp"),
            P("mp"),
        ),
        out_specs=(
            P("replica", None, "mp", None),
            P("mp", None, "replica", None),
            P("mp", None, "replica", None),
            P(None, "replica", None),
            P("mp"),
            P("mp"),
        ),
        check_vma=False,
    )
```

```python
import functools

import jax
import jax.numpy as jnp
from jax import lax
from jax.experimental import pallas as pl
from jax.experimental.pallas import tpu as pltpu
from jax.sharding import PartitionSpec as P

CORES = 2
AHEAD = 4
BASE_ROWS = 16
COLUMNS = 256
F32 = jnp.float32
BF16 = jnp.bfloat16


def params(mib=12):
    return pltpu.CompilerParams(vmem_limit_bytes=mib * 1024 * 1024)


def cost(flops=1000, bytes_accessed=1000):
    return pl.CostEstimate(flops=flops, bytes_accessed=bytes_accessed, transcendentals=0)


def tree_sum(terms):
    while len(terms) > 1:
        terms = [terms[i] + terms[i + 1] for i in range(0, len(terms), 2)]
    return terms[0]


def exchange(x, axis, distance):
    size = lax.axis_size(axis)
    return lax.ppermute(x, axis, [(i, i ^ distance) for i in range(size)])


def left_kernel(pos, g_ref, f_ref, q_ref, vec_ref, comp_ref, near_ref, far_ref, total, feedback, right, sems):
    nmat, rows, _ = comp_ref.shape
    rank = q_ref.shape[1]
    part = near_ref.shape[0]
    cut = rows // 2 if rows % 32 == 0 else rows

    def copies(k):
        out = [pltpu.make_async_copy(q_ref.at[k], right.at[k], sems.at[k, 4])]
        for i, first in enumerate(range(0, rows, cut)):
            block = pl.ds(first, cut)
            for j, (source, target) in enumerate(((g_ref, comp_ref), (f_ref, feedback))):
                source, target = source.at[0, k, block], target.at[k, block]
                out.append(pltpu.make_async_copy(source, target, sems.at[k, 2 * i + j]))
        return out

    for k in range(min(AHEAD, nmat)):
        for copy in copies(k):
            copy.start()
    total[...] = jnp.zeros(total.shape, F32)
    width, nvec = total.shape[1], vec_ref.shape[1]
    for i, first in enumerate(range(0, nvec, width)):
        count = min(width, nvec - first)
        total[rows + i : rows + i + 1, :count] = vec_ref[:, first : first + count]

    for k in range(nmat):
        for copy in copies(k):
            copy.wait()
        if k + AHEAD < nmat:
            for copy in copies(k + AHEAD):
                copy.start()
        comp = comp_ref[k] + feedback[k]
        comp_ref[k] = comp
        total[:rows, k * rank : (k + 1) * rank] = lax.dot_general(
            comp, right[k], (((1,), (1,)), ((), ())), preferred_element_type=F32
        )

    for ref, core in ((near_ref, pos[2]), (far_ref, 1 - pos[2])):
        ref[...] = total[pl.ds(pl.multiple_of(core * part, 16), part), :]


def left_terms(pos, gradients, feedback, right_t, vec):
    _, nmat, rows, n = gradients.shape
    rank = right_t.shape[1]
    width = nmat * rank
    total = rows + -(-vec.shape[1] // width)
    total += -total % (16 * CORES)
    part = jax.ShapeDtypeStruct((total // CORES, width), F32)
    vmem = pl.BlockSpec(memory_space=pltpu.VMEM)
    any_spec = pl.BlockSpec(memory_space=pl.ANY)
    return pl.pallas_call(
        left_kernel,
        grid_spec=pltpu.PrefetchScalarGridSpec(
            num_scalar_prefetch=1,
            grid=(1,),
            in_specs=[any_spec] * 3 + [vmem],
            out_specs=[vmem] * 3,
            scratch_shapes=[
                pltpu.VMEM((total, width), F32),
                pltpu.VMEM((nmat, rows, n), BF16),
                pltpu.VMEM((nmat, rank, n), BF16),
                pltpu.SemaphoreType.DMA((nmat, 5)),
            ],
        ),
        out_shape=[jax.ShapeDtypeStruct((nmat, rows, n), BF16), part, part],
        compiler_params=params(20),
        cost_estimate=cost(),
        name="left_terms",
    )(pos, gradients, feedback, right_t, vec)


def add_kernel(one_ref, other_ref, *refs):
    out = refs[-1]
    out[...] = (one_ref[...].astype(F32) + other_ref[...].astype(F32)).astype(out.dtype)


def add(parts, dtype, after=()):
    vmem = pl.BlockSpec(memory_space=pltpu.VMEM)
    return pl.pallas_call(
        add_kernel,
        in_specs=[vmem] * 2 + [pl.BlockSpec(memory_space=pl.ANY)] * len(after),
        out_specs=vmem,
        out_shape=jax.ShapeDtypeStruct(parts[0].shape, dtype),
        compiler_params=params(),
        cost_estimate=cost(),
        name="add",
    )(*parts, *after)


def send_kernel(half, pos, near_ref, far_ref, gram_ref, comp_ref, send_ref, lt_ref, mix_ref, vec_ref, left, gram):
    nmat, rows, _ = comp_ref.shape
    rank = gram_ref.shape[1]
    part = near_ref.shape[0]
    for ref, core in ((near_ref, pos[2]), (far_ref, 1 - pos[2])):
        left[pl.ds(pl.multiple_of(core * part, 16), part), :] = ref[...]
    vec_ref[...] = left[rows:, :]
    gram[...] = jnp.zeros(gram.shape, F32)
    for i in range(nmat):
        gram[i * rank : (i + 1) * rank, i * rank : (i + 1) * rank] = gram_ref[i]
    hat = jnp.dot(
        left[:rows, :], gram[...], precision=lax.Precision.HIGHEST, preferred_element_type=F32
    )
    lt_ref[...] = hat.T.astype(BF16)
    mix_ref[:, :, :rows] = jnp.broadcast_to(unit_matrix(rows), (nmat, rows, rows))
    for i in range(nmat):
        mix_ref[i, :, rows:] = -hat[:, i * rank : (i + 1) * rank].astype(BF16)
    right_rows(half, pos, lt_ref, comp_ref, send_ref)


def unit_matrix(size):
    row = lax.broadcasted_iota(jnp.int32, (size, size), 0)
    col = lax.broadcasted_iota(jnp.int32, (size, size), 1)
    return jnp.where(row == col, 1.0, 0.0).astype(BF16)


def right_rows(start, pos, lt_ref, comp_ref, out_ref):
    half, upm, unit, _ = out_ref.shape
    for t in range(half):
        k = (t + start) ^ pos[0]
        rows = pl.ds(pl.multiple_of(k * upm * unit, upm * unit), upm * unit)
        terms = jnp.dot(lt_ref[rows, :], comp_ref[k], preferred_element_type=F32)
        for i in range(upm):
            out_ref[t, i ^ pos[1]] = terms[i * unit : (i + 1) * unit].astype(out_ref.dtype)


def keep_kernel(pos, lt_ref, comp_ref, *refs):
    right_rows(0, pos, lt_ref, comp_ref, refs[-1])


def right_terms(pos, near, far, gram, comp, upm, after):
    nmat, rows, n = comp.shape
    rank = gram.shape[1]
    width = nmat * rank
    half = nmat // CORES
    total = CORES * near.shape[0]
    shape = (half, upm, rank // upm, n)
    vmem = pl.BlockSpec(memory_space=pltpu.VMEM)
    send, lt, mix, vec = pl.pallas_call(
        functools.partial(send_kernel, half),
        grid_spec=pltpu.PrefetchScalarGridSpec(
            num_scalar_prefetch=1,
            grid=(1,),
            in_specs=[vmem] * 4,
            out_specs=[vmem] * 4,
            scratch_shapes=[pltpu.VMEM((total, width), F32), pltpu.VMEM((width, width), F32)],
        ),
        out_shape=[
            jax.ShapeDtypeStruct(shape, BF16),
            jax.ShapeDtypeStruct((width, rows), BF16),
            jax.ShapeDtypeStruct((nmat, rows, rows + rank), BF16),
            jax.ShapeDtypeStruct((total - rows, width), F32),
        ],
        compiler_params=params(),
        cost_estimate=cost(),
        name="right_send",
    )(pos, near, far, gram, comp)
    keep = pl.pallas_call(
        keep_kernel,
        grid_spec=pltpu.PrefetchScalarGridSpec(
            num_scalar_prefetch=1,
            grid=(1,),
            in_specs=[vmem, vmem] + [pl.BlockSpec(memory_space=pl.ANY)] * len(after),
            out_specs=vmem,
        ),
        out_shape=jax.ShapeDtypeStruct(shape, F32),
        compiler_params=params(),
        cost_estimate=cost(2000 * nmat * rows * n),
        name="right_keep",
    )(pos, lt, comp, *after)
    return send, keep, lt, mix, vec


def chip_kernel(replica_rows, pos, keep_ref, recv_ref, lt_ref, *refs):
    upm = keep_ref.shape[1]
    own_ref, strip_ref, *sends = refs[-(keep_ref.shape[0] * upm + 1) :]
    left = lt_ref[...].astype(F32).T
    strip = left[:replica_rows]
    for i in range(1, left.shape[0] // replica_rows):
        strip = jnp.where(pos[6] == i, left[i * replica_rows : (i + 1) * replica_rows], strip)
    height = strip_ref.shape[0]
    strip = jnp.concatenate(
        [strip[i * height : (i + 1) * height] for i in range(replica_rows // height)], axis=1
    )
    strip_ref[...] = strip
    own_ref[...] = keep_ref[0, 0] + recv_ref[0, 0].astype(F32)
    for d, out in enumerate(sends, 1):
        j, i = d // upm, d % upm
        terms = keep_ref[j, i] + recv_ref[j, i].astype(F32)
        out[...] = jnp.concatenate([terms, strip], axis=0).astype(BF16)


def chip_sum(pos, keep, recv, lt, replica_rows, after):
    half, upm, unit, n = keep.shape
    height = lt.shape[0] * replica_rows // n
    vmem = pl.BlockSpec(memory_space=pltpu.VMEM)
    outs = [jax.ShapeDtypeStruct((unit, n), F32), jax.ShapeDtypeStruct((height, n), F32)]
    outs += [jax.ShapeDtypeStruct((unit + height, n), BF16)] * (half * upm - 1)
    return pl.pallas_call(
        functools.partial(chip_kernel, replica_rows),
        grid_spec=pltpu.PrefetchScalarGridSpec(
            num_scalar_prefetch=1,
            grid=(1,),
            in_specs=[vmem] * 3 + [pl.BlockSpec(memory_space=pl.ANY)] * len(after),
            out_specs=[vmem] * len(outs),
        ),
        out_shape=outs,
        compiler_params=params(),
        cost_estimate=cost(),
        name="chip_sum",
    )(pos, keep, recv, lt, *after)


def column_kernel(places, pos, *refs):
    out = refs[-1]
    for ref, relative in zip(refs, places):
        for i, d in enumerate(relative):
            cols = ref.shape[2]
            out[:, pl.ds(pl.multiple_of((pos[4] ^ d) * cols, cols), cols)] = ref[i]


def column_gather(pos, parts, places, after):
    unit, cols = parts[0].shape[1:]
    vmem = pl.BlockSpec(memory_space=pltpu.VMEM)
    count = sum(part.shape[0] for part in parts)
    return pl.pallas_call(
        functools.partial(column_kernel, places),
        grid_spec=pltpu.PrefetchScalarGridSpec(
            num_scalar_prefetch=1,
            grid=(1,),
            in_specs=[vmem] * len(parts) + [pl.BlockSpec(memory_space=pl.ANY)] * len(after),
            out_specs=vmem,
        ),
        out_shape=jax.ShapeDtypeStruct((unit, cols * count), BF16),
        compiler_params=params(),
        cost_estimate=cost(),
        name="column_gather",
    )(pos, *parts, *after)


def halve_kernel(keep_ref, recv_ref, *outs):
    for i in range(keep_ref.shape[0]):
        out = outs[i % len(outs)]
        out[i // len(outs)] = (keep_ref[i] + recv_ref[i].astype(F32)).astype(out.dtype)


def halve(keep, recv):
    count, unit, cols = keep.shape
    vmem = pl.BlockSpec(memory_space=pltpu.VMEM)
    shape = (max(count // 2, 1), unit, cols)
    kinds = [F32, BF16] if count > 1 else [BF16]
    return pl.pallas_call(
        halve_kernel,
        in_specs=[vmem] * 2,
        out_specs=[vmem] * len(kinds),
        out_shape=[jax.ShapeDtypeStruct(shape, kind) for kind in kinds],
        compiler_params=params(),
        cost_estimate=cost(),
        name="halve",
    )(keep, recv)


def plane_kernel(pos, own_ref, strip_ref, *refs):
    terms, (keep_ref, send_ref, mix_ref) = refs[:-3], refs[-3:]
    unit, n = own_ref.shape
    cols = keep_ref.shape[2]
    for d in range(n // cols):
        block = pl.ds(pl.multiple_of((pos[4] ^ d) * cols, cols), cols)
        parts = [own_ref[:, block]] + [term[:, block].astype(F32)[:unit] for term in terms]
        out = send_ref if d % 2 else keep_ref
        out[d // 2] = tree_sum(parts).astype(out.dtype)
    strip = strip_ref[...]
    for d, term in enumerate(terms, 1):
        strip = jnp.where(pos[7] == d, term[...].astype(F32)[unit:], strip)
    nmat, count, depth = mix_ref.shape
    rank = (depth - count) // 2
    width = nmat * rank
    rows = [strip[:, i * width : (i + 1) * width] for i in range(n // width)]
    rows = -0.1 * jnp.concatenate(rows, axis=0)
    high = rows.astype(BF16)
    low = (rows - high.astype(F32)).astype(BF16)
    mix_ref[:, :, :count] = jnp.broadcast_to(unit_matrix(count), (nmat, count, count))
    for i in range(nmat):
        mix_ref[i, :, count : count + rank] = high[:, i * rank : (i + 1) * rank]
        mix_ref[i, :, count + rank :] = low[:, i * rank : (i + 1) * rank]


def plane_sum(pos, own, strip, terms, n_z, nmat, rank):
    unit, n = own.shape
    count = strip.size // (nmat * rank)
    shape = (n_z // 2, unit, n // n_z)
    outs = [
        jax.ShapeDtypeStruct(shape, F32),
        jax.ShapeDtypeStruct(shape, BF16),
        jax.ShapeDtypeStruct((nmat, count, count + 2 * rank), BF16),
    ]
    vmem = pl.BlockSpec(memory_space=pltpu.VMEM)
    return pl.pallas_call(
        plane_kernel,
        grid_spec=pltpu.PrefetchScalarGridSpec(
            num_scalar_prefetch=1,
            grid=(1,),
            in_specs=[vmem] * (2 + len(terms)),
            out_specs=[vmem] * len(outs),
        ),
        out_shape=outs,
        compiler_params=params(),
        cost_estimate=cost(),
        name="plane_sum",
    )(pos, own, strip, *terms)


def stack_kernel(*refs):
    out, first = refs[-1], 0
    for part in refs[:-1]:
        out[first : first + part.shape[0]] = part[...]
        first += part.shape[0]


def stack(parts):
    vmem = pl.BlockSpec(memory_space=pltpu.VMEM)
    count = sum(part.shape[0] for part in parts)
    return pl.pallas_call(
        stack_kernel,
        in_specs=[vmem] * len(parts),
        out_specs=vmem,
        out_shape=jax.ShapeDtypeStruct((count,) + parts[0].shape[1:], parts[0].dtype),
        compiler_params=params(),
        cost_estimate=cost(),
        name="stack",
    )(*parts)


def forward_kernel(*refs):
    count = len(refs) // 2
    for source, out in zip(refs, refs[-count:]):
        out[...] = source[...]


def forward(parts, after):
    vmem = pl.BlockSpec(memory_space=pltpu.VMEM)
    return pl.pallas_call(
        forward_kernel,
        in_specs=[vmem] * len(parts) + [pl.BlockSpec(memory_space=pl.ANY)],
        out_specs=[vmem] * len(parts),
        out_shape=[jax.ShapeDtypeStruct(part.shape, part.dtype) for part in parts],
        compiler_params=params(),
        cost_estimate=cost(),
        name="forward",
    )(*parts, after)


def rank_of(owners, k):
    count = jnp.int32(0)
    for j in range(owners.shape[0]):
        count += jnp.where((owners[j] == owners[k]) & (j < k), 1, 0)
    return count


def outputs_kernel(second, places, pos, owners, comp_ref, mix_ref, mixr_ref, near_ref, *refs):
    n_base = len(places)
    n_state = 2 if second else 0
    bases, refs = refs[:n_base], refs[n_base:]
    if second:
        far_ref, states, refs = refs[0], refs[1 : 1 + n_state], refs[1 + n_state + 2 :]
    outs, refs = refs[: 2 + n_state], refs[2 + n_state :]
    held, feedback, weights, fetch_sem, out_sem = refs[:5]
    half, upm, unit, n = near_ref.shape
    rows, count = feedback.shape[1], held.shape[1]
    capacity = max(c for _, c in places) + 1

    def right_of(ref, j):
        parts = [ref[j, i ^ pos[1]] for i in range(upm)]
        return parts[0] if upm == 1 else jnp.concatenate(parts, axis=0)

    matrices = [(j + (half if second else 0)) ^ pos[0] for j in range(half)]
    for j, k in enumerate(matrices):
        slot = (owners[k] ^ pos[5]) * capacity + rank_of(owners, k)
        for a, (d, c) in enumerate(places):

            @pl.when(slot == d * capacity + c)
            def _():
                pltpu.make_async_copy(bases[a].at[0], held.at[j], fetch_sem.at[j]).start()

    if second:
        scratch, state_in, state_out = refs[5:7], refs[7], refs[8]
        loads = [
            pltpu.make_async_copy(states[i].at[0, c], scratch[i].at[c], state_in.at[i, c])
            for c in range(capacity)
            for i in range(n_state)
        ]
        for load in loads:
            load.start()

    stores = []
    for j, k in enumerate(matrices):
        right = right_of(far_ref if second else near_ref, j)
        mix, mixr = mix_ref[k], mixr_ref[k]
        pltpu.make_async_copy(bases[0].at[0], held.at[j], fetch_sem.at[j]).wait()
        for first in range(0, n, COLUMNS):
            block = slice(first, first + COLUMNS)
            part = right[:, block]
            both = jnp.concatenate([comp_ref[k, :, block], part], axis=0)
            feedback[j, :, block] = jnp.dot(mix, both, preferred_element_type=F32).astype(BF16)
            both = jnp.concatenate([held[j, :, block], part, part], axis=0)
            weights[j, :, block] = jnp.dot(mixr, both, preferred_element_type=F32).astype(BF16)
        for source, target, i in ((feedback, outs[0].at[0, k], 0), (weights, outs[1].at[k], 1)):
            stores.append(pltpu.make_async_copy(source.at[j], target, out_sem.at[j, i]))
            stores[-1].start()

    for c in range(capacity if second else 0):
        matrix = jnp.int32(-1)
        for k in range(owners.shape[0]):
            matrix = jnp.where((owners[k] == pos[5]) & (rank_of(owners, k) == c), k, matrix)
        safe = jnp.maximum(matrix, 0)
        slot = safe ^ pos[0]
        inner = lax.rem(slot, half)
        right = jnp.where(slot < half, right_of(near_ref, inner), right_of(far_ref, inner))
        both = jnp.concatenate([right, right], axis=0)
        mixr = mixr_ref[safe][:, count:]
        for load in loads[c * n_state : (c + 1) * n_state]:
            load.wait()
        for first in range(0, n, COLUMNS):
            block = slice(first, first + COLUMNS)
            change = jnp.dot(mixr, both[:, block], preferred_element_type=F32)
            momentum = 0.9 * scratch[0][c, :, block] - jnp.where(matrix >= 0, 10.0 * change, 0.0)
            scratch[0][c, :, block] = momentum
            scratch[1][c, :, block] -= 0.1 * momentum
        for i in range(n_state):
            copy = pltpu.make_async_copy(scratch[i].at[c], outs[2 + i].at[0, c], state_out.at[i, c])
            copy.start()
            stores.append(copy)

    for copy in stores:
        copy.wait()


def outputs(pos, owners, comp, mix, mixr, near, bases, places, far=None, states=(), earlier=()):
    nmat, rows, n = comp.shape
    half = near.shape[0]
    capacity = max(c for _, c in places) + 1
    replica_rows = bases[0].shape[1]
    second = far is not None
    any_spec = pl.BlockSpec(memory_space=pl.ANY)
    vmem = pl.BlockSpec(memory_space=pltpu.VMEM)
    scratch = [
        pltpu.VMEM((half, replica_rows, n), BF16),
        pltpu.VMEM((half, rows, n), BF16),
        pltpu.VMEM((half, replica_rows, n), BF16),
        pltpu.SemaphoreType.DMA((half,)),
        pltpu.SemaphoreType.DMA((half, 2)),
    ]
    if second:
        scratch += [pltpu.VMEM((capacity, replica_rows, n), F32)] * 2
        scratch += [pltpu.SemaphoreType.DMA((2, capacity))] * 2
    outs = [
        jax.ShapeDtypeStruct((1, nmat, rows, n), BF16),
        jax.ShapeDtypeStruct((nmat, replica_rows, n), BF16),
    ] + [jax.ShapeDtypeStruct(x.shape, F32) for x in states]
    fars = [far] if second else []
    first = 6 + len(bases) + len(fars) + len(states)
    return pl.pallas_call(
        functools.partial(outputs_kernel, second, places),
        grid_spec=pltpu.PrefetchScalarGridSpec(
            num_scalar_prefetch=2,
            grid=(1,),
            in_specs=[vmem] * 4
            + [any_spec] * len(bases)
            + [vmem] * len(fars)
            + [any_spec] * (len(states) + len(earlier)),
            out_specs=[any_spec] * len(outs),
            scratch_shapes=scratch,
        ),
        out_shape=outs,
        input_output_aliases={first + i: i for i in range(len(earlier))},
        compiler_params=params(24),
        cost_estimate=cost(),
        name="outputs",
    )(pos, owners, comp, mix, mixr, near, *bases, *fars, *states, *earlier)


def base_kernel(momentum_ref, master_ref, *refs):
    outs, (momentum, master, sems) = refs[:-3], refs[-3:]
    rows = outs[0].shape[1]
    blocks = [(c, first) for c in range(len(outs)) for first in range(0, rows, BASE_ROWS)]

    def copies(i):
        c, first = blocks[i]
        part = pl.ds(first, BASE_ROWS)
        return [
            pltpu.make_async_copy(source.at[0, c, part], target.at[c, part], sems.at[j, i])
            for j, (source, target) in enumerate(((momentum_ref, momentum), (master_ref, master)))
        ]

    for i in range(len(blocks)):
        for copy in copies(i):
            copy.start()
    for i, (c, first) in enumerate(blocks):
        for copy in copies(i):
            copy.wait()
        part = slice(first, first + BASE_ROWS)
        outs[c][0, part] = (master[c, part] - 0.09 * momentum[c, part]).astype(BF16)


def base_of(momentum, master):
    _, capacity, rows, n = momentum.shape
    return pl.pallas_call(
        base_kernel,
        in_specs=[pl.BlockSpec(memory_space=pl.ANY)] * 2,
        out_specs=[pl.BlockSpec(memory_space=pltpu.VMEM)] * capacity,
        out_shape=[jax.ShapeDtypeStruct((1, rows, n), BF16)] * capacity,
        scratch_shapes=[pltpu.VMEM((capacity, rows, n), F32)] * 2
        + [pltpu.SemaphoreType.DMA((2, capacity * rows // BASE_ROWS))],
        compiler_params=params(),
        cost_estimate=cost(),
        name="base",
    )(momentum, master)


def per_device(
    gradients,
    feedback,
    right_init,
    gram_root,
    owners,
    momentum,
    master_weights,
    vector_grads,
    vector_momentum,
    vector_params,
):
    nmat, rows, n = gradients.shape[1:]
    rank = right_init.shape[2]
    unit = rank * nmat // (CORES * lax.axis_size("mp"))
    n_mp = lax.axis_size("mp")
    n_z = lax.axis_size("replica") // CORES
    capacity, replica_rows = momentum.shape[1:3]
    p = lax.axis_index("mp")
    r = lax.axis_index("replica")
    core, z = r % CORES, r // CORES
    upm = CORES * n_mp // nmat
    half = nmat // CORES
    code = core * n_mp + p
    first = r * replica_rows

    places_of = [code // upm, code % upm, core, r, z, p, first % rows // replica_rows, first // rows ^ p]
    pos = jnp.stack(places_of).astype(jnp.int32)
    in_hbm = lambda x: pltpu.with_memory_space_constraint(x, pltpu.HBM)

    square = n_mp == 4 and capacity == 2
    near_owners = range(1, 3 if square else n_mp)
    states = in_hbm(momentum), in_hbm(master_weights)
    held = {(0, c): part for c, part in enumerate(base_of(*states))}
    for c in range(capacity):
        for d in near_owners:
            held[d, c] = exchange(held[0, c], "mp", d)

    nvec = vector_grads.shape[1]
    comp, near, far = left_terms(
        pos,
        in_hbm(gradients),
        in_hbm(feedback),
        in_hbm(jnp.swapaxes(right_init, 1, 2)),
        vector_grads,
    )
    piece = add([near, exchange(far, "replica", 1)], BF16)
    early = [held[d, 0] for d in near_owners]
    middle = [held[d, c] for c in range(1, capacity) for d in near_owners]
    steps = [1 << i for i in range(n_z.bit_length() - 1)]
    for d in steps:
        last = d == steps[-1]
        recv = exchange(piece, "replica", CORES * d)
        piece = add([piece, recv], F32 if last else BF16, ())
    near, far = piece, exchange(piece, "replica", 1)

    send, keep, lt, mix, vector_rows = right_terms(pos, near, far, gram_root, comp, upm, early + middle)
    vector_total = vector_rows.reshape(-1)[:nvec]
    recv = exchange(send, "replica", 1)
    own, strip, *chip = chip_sum(pos, keep, recv, lt, replica_rows, [])
    plane = [exchange(part, "mp", d) for d, part in enumerate(chip, 1)]
    kept, *sent, mixr = plane_sum(pos, own, strip, plane, n_z, nmat, rank)
    late = []
    if square:
        late = forward([held[1, 0], held[2, 1]], mixr)
        late = [exchange(late[0], "mp", 2), exchange(late[1], "mp", 1)]
        held[3, 0], held[3, 1] = late
    for d in steps:
        kept, *sent = halve(kept, exchange(sent[0], "replica", CORES * d))

    parts, relative = [kept], [[0]]
    for d in reversed(steps):
        have = stack(parts) if len(parts) > 1 else parts[0]
        order = sum(relative, [])
        parts = [have, exchange(have, "replica", CORES * d)]
        relative = [order, [i ^ d for i in order]]
    whole = column_gather(pos, parts, relative, late)[None]
    near = stack([whole] + [exchange(whole, "mp", d) for d in range(1, n_mp)])
    near = near.reshape(half, upm, unit, n)
    far = exchange(near, "replica", 1)

    places, bases = list(held), list(held.values())
    done = outputs(pos, owners, comp, mix, mixr, near, bases, places)
    new_feedback, new_weights, new_momentum, new_master = outputs(
        pos, owners, comp, mix, mixr, near, bases, places, far, (momentum, master_weights), done
    )

    new_vector_momentum = 0.9 * vector_momentum + vector_total
    new_vector_params = vector_params - 0.1 * new_vector_momentum
    return new_feedback, new_momentum, new_master, new_weights, new_vector_momentum, new_vector_params


def solution(mesh):
    return jax.shard_map(
        per_device,
        mesh=mesh,
        in_specs=(
            P("replica", None, "mp", None),
            P("replica", None, "mp", None),
            P(),
            P(),
            P(),
            P("mp", None, "replica", None),
            P("mp", None, "replica", None),
            P("replica", "mp"),
            P("mp"),
            P("mp"),
        ),
        out_specs=(
            P("replica", None, "mp", None),
            P("mp", None, "replica", None),
            P("mp", None, "replica", None),
            P(None, "replica", None),
            P("mp"),
            P("mp"),
        ),
        check_vma=False,
    )
```

```python
import functools

import jax
import jax.numpy as jnp
from jax import lax
from jax.experimental import pallas as pl
from jax.experimental.pallas import tpu as pltpu
from jax.sharding import PartitionSpec as P

CORES = 2
AHEAD = 4
BASE_ROWS = 16
COLUMNS = 384
F32 = jnp.float32
BF16 = jnp.bfloat16


def params(mib=12):
    return pltpu.CompilerParams(vmem_limit_bytes=mib * 1024 * 1024)


def cost(flops=1000, bytes_accessed=1000):
    return pl.CostEstimate(flops=flops, bytes_accessed=bytes_accessed, transcendentals=0)


def tree_sum(terms):
    while len(terms) > 1:
        terms = [terms[i] + terms[i + 1] for i in range(0, len(terms), 2)]
    return terms[0]


def exchange(x, axis, distance):
    size = lax.axis_size(axis)
    return lax.ppermute(x, axis, [(i, i ^ distance) for i in range(size)])


def left_kernel(pos, g_ref, f_ref, q_ref, vec_ref, comp_ref, near_ref, far_ref, total, feedback, right, sems):
    nmat, rows, _ = comp_ref.shape
    rank = q_ref.shape[1]
    part = near_ref.shape[0]
    cut = rows // 2 if rows % 32 == 0 else rows

    def copies(k):
        out = [pltpu.make_async_copy(q_ref.at[k], right.at[k], sems.at[k, 4])]
        for i, first in enumerate(range(0, rows, cut)):
            block = pl.ds(first, cut)
            for j, (source, target) in enumerate(((g_ref, comp_ref), (f_ref, feedback))):
                source, target = source.at[0, k, block], target.at[k, block]
                out.append(pltpu.make_async_copy(source, target, sems.at[k, 2 * i + j]))
        return out

    for k in range(min(AHEAD, nmat)):
        for copy in copies(k):
            copy.start()
    total[...] = jnp.zeros(total.shape, F32)
    width, nvec = total.shape[1], vec_ref.shape[1]
    for i, first in enumerate(range(0, nvec, width)):
        count = min(width, nvec - first)
        total[rows + i : rows + i + 1, :count] = vec_ref[:, first : first + count]

    for k in range(nmat):
        for copy in copies(k):
            copy.wait()
        if k + AHEAD < nmat:
            for copy in copies(k + AHEAD):
                copy.start()
        comp = comp_ref[k] + feedback[k]
        comp_ref[k] = comp
        total[:rows, k * rank : (k + 1) * rank] = lax.dot_general(
            comp, right[k], (((1,), (1,)), ((), ())), preferred_element_type=F32
        )

    for ref, core in ((near_ref, pos[2]), (far_ref, 1 - pos[2])):
        ref[...] = total[pl.ds(pl.multiple_of(core * part, 16), part), :]


def left_terms(pos, gradients, feedback, right_t, vec):
    _, nmat, rows, n = gradients.shape
    rank = right_t.shape[1]
    width = nmat * rank
    total = rows + -(-vec.shape[1] // width)
    total += -total % (16 * CORES)
    part = jax.ShapeDtypeStruct((total // CORES, width), F32)
    vmem = pl.BlockSpec(memory_space=pltpu.VMEM)
    any_spec = pl.BlockSpec(memory_space=pl.ANY)
    return pl.pallas_call(
        left_kernel,
        grid_spec=pltpu.PrefetchScalarGridSpec(
            num_scalar_prefetch=1,
            grid=(1,),
            in_specs=[any_spec] * 3 + [vmem],
            out_specs=[vmem] * 3,
            scratch_shapes=[
                pltpu.VMEM((total, width), F32),
                pltpu.VMEM((nmat, rows, n), BF16),
                pltpu.VMEM((nmat, rank, n), BF16),
                pltpu.SemaphoreType.DMA((nmat, 5)),
            ],
        ),
        out_shape=[jax.ShapeDtypeStruct((nmat, rows, n), BF16), part, part],
        compiler_params=params(20),
        cost_estimate=cost(),
        name="left_terms",
    )(pos, gradients, feedback, right_t, vec)


def add_kernel(*refs):
    out = refs[-1]
    out[...] = tree_sum([ref[...].astype(F32) for ref in refs[:-1]]).astype(out.dtype)


def add(parts, dtype):
    vmem = pl.BlockSpec(memory_space=pltpu.VMEM)
    return pl.pallas_call(
        add_kernel,
        in_specs=[vmem] * len(parts),
        out_specs=vmem,
        out_shape=jax.ShapeDtypeStruct(parts[0].shape, dtype),
        compiler_params=params(),
        cost_estimate=cost(),
        name="add",
    )(*parts)


def send_kernel(half, pos, near_ref, far_ref, gram_ref, comp_ref, send_ref, lt_ref, mix_ref, vec_ref, left, gram):
    nmat, rows, _ = comp_ref.shape
    rank = gram_ref.shape[1]
    part = near_ref.shape[0]
    for ref, core in ((near_ref, pos[2]), (far_ref, 1 - pos[2])):
        left[pl.ds(pl.multiple_of(core * part, 16), part), :] = ref[...]
    vec_ref[...] = left[rows:, :]
    gram[...] = jnp.zeros(gram.shape, F32)
    for i in range(nmat):
        gram[i * rank : (i + 1) * rank, i * rank : (i + 1) * rank] = gram_ref[i]
    hat = jnp.dot(
        left[:rows, :], gram[...], precision=lax.Precision.HIGHEST, preferred_element_type=F32
    )
    lt_ref[...] = hat.T.astype(BF16)
    mix_ref[:, :, :rows] = jnp.broadcast_to(unit_matrix(rows), (nmat, rows, rows))
    for i in range(nmat):
        mix_ref[i, :, rows:] = -hat[:, i * rank : (i + 1) * rank].astype(BF16)
    right_rows(half, pos, lt_ref, comp_ref, send_ref)


def unit_matrix(size):
    row = lax.broadcasted_iota(jnp.int32, (size, size), 0)
    col = lax.broadcasted_iota(jnp.int32, (size, size), 1)
    return jnp.where(row == col, 1.0, 0.0).astype(BF16)


def right_rows(start, pos, lt_ref, comp_ref, out_ref):
    half, upm, unit, _ = out_ref.shape
    for t in range(half):
        k = (t + start) ^ pos[0]
        rows = pl.ds(pl.multiple_of(k * upm * unit, upm * unit), upm * unit)
        terms = jnp.dot(lt_ref[rows, :], comp_ref[k], preferred_element_type=F32)
        for i in range(upm):
            out_ref[t, i ^ pos[1]] = terms[i * unit : (i + 1) * unit].astype(out_ref.dtype)


def keep_kernel(pos, lt_ref, comp_ref, *refs):
    right_rows(0, pos, lt_ref, comp_ref, refs[-1])


def right_terms(pos, near, far, gram, comp, upm, after):
    nmat, rows, n = comp.shape
    rank = gram.shape[1]
    width = nmat * rank
    half = nmat // CORES
    total = CORES * near.shape[0]
    shape = (half, upm, rank // upm, n)
    vmem = pl.BlockSpec(memory_space=pltpu.VMEM)
    send, lt, mix, vec = pl.pallas_call(
        functools.partial(send_kernel, half),
        grid_spec=pltpu.PrefetchScalarGridSpec(
            num_scalar_prefetch=1,
            grid=(1,),
            in_specs=[vmem] * 4,
            out_specs=[vmem] * 4,
            scratch_shapes=[pltpu.VMEM((total, width), F32), pltpu.VMEM((width, width), F32)],
        ),
        out_shape=[
            jax.ShapeDtypeStruct(shape, BF16),
            jax.ShapeDtypeStruct((width, rows), BF16),
            jax.ShapeDtypeStruct((nmat, rows, rows + rank), BF16),
            jax.ShapeDtypeStruct((total - rows, width), F32),
        ],
        compiler_params=params(),
        cost_estimate=cost(),
        name="right_send",
    )(pos, near, far, gram, comp)
    keep = pl.pallas_call(
        keep_kernel,
        grid_spec=pltpu.PrefetchScalarGridSpec(
            num_scalar_prefetch=1,
            grid=(1,),
            in_specs=[vmem, vmem] + [pl.BlockSpec(memory_space=pl.ANY)] * len(after),
            out_specs=vmem,
        ),
        out_shape=jax.ShapeDtypeStruct(shape, F32),
        compiler_params=params(),
        cost_estimate=cost(2000 * nmat * rows * n),
        name="right_keep",
    )(pos, lt, comp, *after)
    return send, keep, lt, mix, vec


def chip_kernel(replica_rows, pos, keep_ref, recv_ref, lt_ref, *refs):
    upm = keep_ref.shape[1]
    own_ref, strip_ref, *sends = refs[-(keep_ref.shape[0] * upm + 1) :]
    left = lt_ref[...].astype(F32).T
    strip = left[:replica_rows]
    for i in range(1, left.shape[0] // replica_rows):
        strip = jnp.where(pos[6] == i, left[i * replica_rows : (i + 1) * replica_rows], strip)
    height = strip_ref.shape[0]
    strip = jnp.concatenate(
        [strip[i * height : (i + 1) * height] for i in range(replica_rows // height)], axis=1
    )
    strip_ref[...] = strip
    own_ref[...] = keep_ref[0, 0] + recv_ref[0, 0].astype(F32)
    for d, out in enumerate(sends, 1):
        j, i = d // upm, d % upm
        terms = keep_ref[j, i] + recv_ref[j, i].astype(F32)
        out[...] = jnp.concatenate([terms, strip], axis=0).astype(BF16)


def chip_sum(pos, keep, recv, lt, replica_rows, after):
    half, upm, unit, n = keep.shape
    height = lt.shape[0] * replica_rows // n
    vmem = pl.BlockSpec(memory_space=pltpu.VMEM)
    outs = [jax.ShapeDtypeStruct((unit, n), F32), jax.ShapeDtypeStruct((height, n), F32)]
    outs += [jax.ShapeDtypeStruct((unit + height, n), BF16)] * (half * upm - 1)
    return pl.pallas_call(
        functools.partial(chip_kernel, replica_rows),
        grid_spec=pltpu.PrefetchScalarGridSpec(
            num_scalar_prefetch=1,
            grid=(1,),
            in_specs=[vmem] * 3 + [pl.BlockSpec(memory_space=pl.ANY)] * len(after),
            out_specs=[vmem] * len(outs),
        ),
        out_shape=outs,
        compiler_params=params(),
        cost_estimate=cost(),
        name="chip_sum",
    )(pos, keep, recv, lt, *after)


def plane_kernel(pos, own_ref, strip_ref, *refs):
    n_z = own_ref.shape[1] // refs[-2].shape[1]
    terms, outs, mix_ref = refs[: -n_z - 1], refs[-n_z - 1 : -1], refs[-1]
    unit, n = own_ref.shape
    cols = n // n_z
    for d, out in enumerate(outs):
        block = pl.ds(pl.multiple_of((pos[4] ^ d) * cols, cols), cols)
        parts = [own_ref[:, block]] + [term[:, block].astype(F32)[:unit] for term in terms]
        out[...] = tree_sum(parts).astype(out.dtype)
    strip = strip_ref[...]
    for d, term in enumerate(terms, 1):
        strip = jnp.where(pos[7] == d, term[...].astype(F32)[unit:], strip)
    nmat, count, depth = mix_ref.shape
    rank = (depth - count) // 2
    width = nmat * rank
    rows = [strip[:, i * width : (i + 1) * width] for i in range(n // width)]
    rows = -0.1 * jnp.concatenate(rows, axis=0)
    high = rows.astype(BF16)
    low = (rows - high.astype(F32)).astype(BF16)
    mix_ref[:, :, :count] = jnp.broadcast_to(unit_matrix(count), (nmat, count, count))
    for i in range(nmat):
        mix_ref[i, :, count : count + rank] = high[:, i * rank : (i + 1) * rank]
        mix_ref[i, :, count + rank :] = low[:, i * rank : (i + 1) * rank]


def plane_sum(pos, own, strip, terms, n_z, nmat, rank):
    unit, n = own.shape
    count = strip.size // (nmat * rank)
    outs = [jax.ShapeDtypeStruct((unit, n // n_z), BF16 if d else F32) for d in range(n_z)]
    outs.append(jax.ShapeDtypeStruct((nmat, count, count + 2 * rank), BF16))
    vmem = pl.BlockSpec(memory_space=pltpu.VMEM)
    return pl.pallas_call(
        plane_kernel,
        grid_spec=pltpu.PrefetchScalarGridSpec(
            num_scalar_prefetch=1,
            grid=(1,),
            in_specs=[vmem] * (2 + len(terms)),
            out_specs=[vmem] * len(outs),
        ),
        out_shape=outs,
        compiler_params=params(),
        cost_estimate=cost(),
        name="plane_sum",
    )(pos, own, strip, *terms)


def stack_kernel(count, *refs):
    for i in range(count):
        refs[-1][i] = refs[i][...]


def stack(parts, after=()):
    vmem = pl.BlockSpec(memory_space=pltpu.VMEM)
    return pl.pallas_call(
        functools.partial(stack_kernel, len(parts)),
        in_specs=[vmem] * len(parts) + [pl.BlockSpec(memory_space=pl.ANY)] * len(after),
        out_specs=vmem,
        out_shape=jax.ShapeDtypeStruct((len(parts),) + parts[0].shape, parts[0].dtype),
        compiler_params=params(),
        cost_estimate=cost(),
        name="stack",
    )(*parts, *after)


def forward_kernel(cuts, *refs):
    for source, out, first in zip(refs, refs[-len(cuts) :], cuts):
        out[...] = source[first : first + out.shape[0]]


def forward(parts, cuts, count, after):
    vmem = pl.BlockSpec(memory_space=pltpu.VMEM)
    return pl.pallas_call(
        functools.partial(forward_kernel, cuts),
        in_specs=[vmem] * len(parts) + [pl.BlockSpec(memory_space=pl.ANY)],
        out_specs=[vmem] * len(parts),
        out_shape=[jax.ShapeDtypeStruct((count,) + part.shape[1:], part.dtype) for part in parts],
        compiler_params=params(),
        cost_estimate=cost(),
        name="forward",
    )(*parts, after)


def rank_of(owners, k):
    count = jnp.int32(0)
    for j in range(owners.shape[0]):
        count += jnp.where((owners[j] == owners[k]) & (j < k), 1, 0)
    return count


def outputs_kernel(second, places, pos, owners, comp_ref, mix_ref, mixr_ref, near_ref, *refs):
    n_base = len({a for a, _ in places.values()})
    bases, refs = refs[:n_base], refs[n_base:]
    if second:
        far_ref, momentum_ref, master_ref, refs = refs[0], refs[1], refs[2], refs[5:]
    n_out = 4 if second else 2
    outs, refs = refs[:n_out], refs[n_out:]
    held, feedback, weights, fetch_sem, out_sem = refs[:5]
    half, upm, n_z, unit, cols = near_ref.shape
    count = held.shape[1]
    capacity = max(c for _, c in places) + 1

    def right_of(ref, j, d, block):
        parts = [ref[j, i ^ pos[1], d, :, block] for i in range(upm)]
        return parts[0] if upm == 1 else jnp.concatenate(parts, axis=0)

    def columns(d, first=0, size=cols):
        return pl.ds(pl.multiple_of((pos[4] ^ d) * cols + first, 128), size)

    pieces = [slice(first, first + COLUMNS) for first in range(0, cols, COLUMNS)]
    matrices = [(j + (half if second else 0)) ^ pos[0] for j in range(half)]
    for j, k in enumerate(matrices):
        slot = (owners[k] ^ pos[5]) * capacity + rank_of(owners, k)
        for (d, c), (a, row) in places.items():

            @pl.when(slot == d * capacity + c)
            def _():
                pltpu.make_async_copy(bases[a].at[row], held.at[j], fetch_sem.at[j]).start()

    stores = []

    def store(source, target, sem):
        stores.append(pltpu.make_async_copy(source, target, sem))
        stores[-1].start()

    if second:
        new_momentum, new_master, state_sem = refs[5:8]
        for c in range(capacity):
            matrix = jnp.int32(-1)
            for k in range(owners.shape[0]):
                matrix = jnp.where((owners[k] == pos[5]) & (rank_of(owners, k) == c), k, matrix)
            safe = jnp.maximum(matrix, 0)
            slot = safe ^ pos[0]
            inner = lax.rem(slot, half)
            mixr = mixr_ref[safe][:, count:]
            for d in range(n_z):
                for block in pieces:
                    right = jnp.where(
                        slot < half,
                        right_of(near_ref, inner, d, block),
                        right_of(far_ref, inner, d, block),
                    )
                    both = jnp.concatenate([right, right], axis=0)
                    change = jnp.dot(mixr, both, preferred_element_type=F32)
                    change = jnp.where(matrix >= 0, 10.0 * change, 0.0)
                    place = columns(d, block.start, COLUMNS)
                    momentum = 0.9 * momentum_ref[c, :, place] - change
                    new_momentum[c, :, place] = momentum
                    new_master[c, :, place] = master_ref[c, :, place] - 0.1 * momentum
                place = columns(d)
                for i, new in enumerate((new_momentum, new_master)):
                    store(
                        new.at[c, :, place], outs[2 + i].at[0, c, :, place], state_sem.at[i, c, d]
                    )

    for j, k in enumerate(matrices):
        ref = far_ref if second else near_ref
        mix, mixr = mix_ref[k], mixr_ref[k]
        for d in range(n_z):
            for block in pieces:
                right = right_of(ref, j, d, block)
                place = columns(d, block.start, COLUMNS)
                both = jnp.concatenate([comp_ref[k, :, place], right], axis=0)
                feedback[j, :, place] = jnp.dot(mix, both, preferred_element_type=F32).astype(BF16)
            place = columns(d)
            store(feedback.at[j, :, place], outs[0].at[0, k, :, place], out_sem.at[j, d, 0])
        pltpu.make_async_copy(bases[0].at[0], held.at[j], fetch_sem.at[j]).wait()
        for d in range(n_z):
            for block in pieces:
                right = right_of(ref, j, d, block)
                place = columns(d, block.start, COLUMNS)
                both = jnp.concatenate([held[j, :, place], right, right], axis=0)
                weights[j, :, place] = jnp.dot(mixr, both, preferred_element_type=F32).astype(BF16)
            place = columns(d)
            store(weights.at[j, :, place], outs[1].at[k, :, place], out_sem.at[j, d, 1])

    for copy in stores:
        copy.wait()


def outputs(pos, owners, comp, mix, mixr, near, bases, places, far=None, states=(), earlier=()):
    nmat, rows, n = comp.shape
    half, _, n_z = near.shape[:3]
    capacity = max(c for _, c in places) + 1
    replica_rows = bases[0].shape[1]
    second = far is not None
    any_spec = pl.BlockSpec(memory_space=pl.ANY)
    vmem = pl.BlockSpec(memory_space=pltpu.VMEM)
    scratch = [
        pltpu.VMEM((half, replica_rows, n), BF16),
        pltpu.VMEM((half, rows, n), BF16),
        pltpu.VMEM((half, replica_rows, n), BF16),
        pltpu.SemaphoreType.DMA((half,)),
        pltpu.SemaphoreType.DMA((half, n_z, 2)),
    ]
    if second:
        scratch += [pltpu.VMEM((capacity, replica_rows, n), F32)] * 2
        scratch += [pltpu.SemaphoreType.DMA((2, capacity, n_z))]
    outs = [
        jax.ShapeDtypeStruct((1, nmat, rows, n), BF16),
        jax.ShapeDtypeStruct((nmat, replica_rows, n), BF16),
    ] + [jax.ShapeDtypeStruct((1,) + x.shape, F32) for x in states]
    fars = [far] if second else []
    first = 6 + len(bases) + len(fars) + len(states)
    return pl.pallas_call(
        functools.partial(outputs_kernel, second, places),
        grid_spec=pltpu.PrefetchScalarGridSpec(
            num_scalar_prefetch=2,
            grid=(1,),
            in_specs=[vmem] * 4
            + [any_spec] * len(bases)
            + [vmem] * (len(fars) + len(states))
            + [any_spec] * len(earlier),
            out_specs=[any_spec] * len(outs),
            scratch_shapes=scratch,
        ),
        out_shape=outs,
        input_output_aliases={first + i: i for i in range(len(earlier))},
        compiler_params=params(24),
        cost_estimate=cost(),
        name="outputs",
    )(pos, owners, comp, mix, mixr, near, *bases, *fars, *states, *earlier)


def base_kernel(momentum_ref, master_ref, *refs):
    out_ref, momentum, master, sems = refs
    capacity, rows, _ = out_ref.shape
    blocks = [(c, first) for c in range(capacity) for first in range(0, rows, BASE_ROWS)]

    def copies(i):
        c, first = blocks[i]
        part = pl.ds(first, BASE_ROWS)
        return [
            pltpu.make_async_copy(source.at[0, c, part], target.at[c, part], sems.at[j, i])
            for j, (source, target) in enumerate(((momentum_ref, momentum), (master_ref, master)))
        ]

    for i in range(len(blocks)):
        for copy in copies(i):
            copy.start()
    for i, (c, first) in enumerate(blocks):
        for copy in copies(i):
            copy.wait()
        part = slice(first, first + BASE_ROWS)
        out_ref[c, part] = (master[c, part] - 0.09 * momentum[c, part]).astype(BF16)


def base_of(momentum, master):
    _, capacity, rows, n = momentum.shape
    state = jax.ShapeDtypeStruct((capacity, rows, n), F32)
    base, momentum, master = pl.pallas_call(
        base_kernel,
        in_specs=[pl.BlockSpec(memory_space=pl.ANY)] * 2,
        out_specs=[pl.BlockSpec(memory_space=pltpu.VMEM)] * 3,
        out_shape=[jax.ShapeDtypeStruct((capacity, rows, n), BF16), state, state],
        scratch_shapes=[pltpu.SemaphoreType.DMA((2, capacity * rows // BASE_ROWS))],
        compiler_params=params(),
        cost_estimate=cost(),
        name="base",
    )(momentum, master)
    return base, (momentum, master)


def per_device(
    gradients,
    feedback,
    right_init,
    gram_root,
    owners,
    momentum,
    master_weights,
    vector_grads,
    vector_momentum,
    vector_params,
):
    nmat, rows, n = gradients.shape[1:]
    rank = right_init.shape[2]
    unit = rank * nmat // (CORES * lax.axis_size("mp"))
    n_mp = lax.axis_size("mp")
    n_z = lax.axis_size("replica") // CORES
    capacity, replica_rows = momentum.shape[1:3]
    p = lax.axis_index("mp")
    r = lax.axis_index("replica")
    core, z = r % CORES, r // CORES
    upm = CORES * n_mp // nmat
    half = nmat // CORES
    code = core * n_mp + p
    first = r * replica_rows

    places_of = [code // upm, code % upm, core, r, z, p, first % rows // replica_rows, first // rows ^ p]
    pos = jnp.stack(places_of).astype(jnp.int32)
    in_hbm = lambda x: pltpu.with_memory_space_constraint(x, pltpu.HBM)

    square = n_mp == 4 and capacity == 2
    base, states = base_of(in_hbm(momentum), in_hbm(master_weights))
    early = [exchange(base, "mp", d) for d in range(1, 3 if square else n_mp)]
    bases = [base] + early
    places = {(d, c): (d, c) for d in range(len(bases)) for c in range(capacity)}

    nvec = vector_grads.shape[1]
    comp, near, far = left_terms(
        pos,
        in_hbm(gradients),
        in_hbm(feedback),
        in_hbm(jnp.swapaxes(right_init, 1, 2)),
        vector_grads,
    )
    piece = add([near, exchange(far, "replica", 1)], BF16)
    piece = add([near, exchange(far, "replica", 1)], BF16)
    along_z = lambda x: [exchange(x, "replica", CORES * d) for d in range(1, n_z)]
    piece = add([piece] + along_z(piece), F32)
    near, far = piece, exchange(piece, "replica", 1)

    send, keep, lt, mix, vector_rows = right_terms(pos, near, far, gram_root, comp, upm, early)
    vector_total = vector_rows.reshape(-1)[:nvec]
    recv = exchange(send, "replica", 1)
    own, strip, *chip = chip_sum(pos, keep, recv, lt, replica_rows, [])
    plane = [exchange(part, "mp", d) for d, part in enumerate(chip, 1)]
    *final, mixr = plane_sum(pos, own, strip, plane, n_z, nmat, rank)
    late = []
    if square:
        parts = forward(early, [0, 1], 1, mixr)
        late = [exchange(part, "mp", 2 - i) for i, part in enumerate(parts)]
        bases = bases + late
        places[3, 0], places[3, 1] = (3, 0), (4, 0)
    final = [final[0]] + [exchange(final[d], "replica", CORES * d) for d in range(1, n_z)]
    final = add(final, BF16)
    new_vector_momentum = 0.9 * vector_momentum + vector_total
    new_vector_params = vector_params - 0.1 * new_vector_momentum

    whole = stack([final] + along_z(final), late + [new_vector_params])
    near = stack([whole] + [exchange(whole, "mp", d) for d in range(1, n_mp)])
    near = near.reshape((half, upm) + whole.shape)
    far = exchange(near, "replica", 1)

    done = outputs(pos, owners, comp, mix, mixr, near, bases, places)
    new_feedback, new_weights, new_momentum, new_master = outputs(
        pos, owners, comp, mix, mixr, near, bases, places, far, states, done
    )

    return new_feedback, new_momentum, new_master, new_weights, new_vector_momentum, new_vector_params


def solution(mesh):
    return jax.shard_map(
        per_device,
        mesh=mesh,
        in_specs=(
            P("replica", None, "mp", None),
            P("replica", None, "mp", None),
            P(),
            P(),
            P(),
            P("mp", None, "replica", None),
            P("mp", None, "replica", None),
            P("replica", "mp"),
            P("mp"),
            P("mp"),
        ),
        out_specs=(
            P("replica", None, "mp", None),
            P("mp", None, "replica", None),
            P("mp", None, "replica", None),
            P(None, "replica", None),
            P("mp"),
            P("mp"),
        ),
        check_vma=False,
    )
```

```python
import functools

import jax
import jax.numpy as jnp
from jax import lax
from jax.experimental import pallas as pl
from jax.experimental.pallas import tpu as pltpu
from jax.sharding import PartitionSpec as P

CORES = 2
AHEAD = 4
BASE_ROWS = 16
COLUMNS = 384
F32 = jnp.float32
BF16 = jnp.bfloat16


def params(mib=12):
    return pltpu.CompilerParams(vmem_limit_bytes=mib * 1024 * 1024)


def cost(flops=1000, bytes_accessed=1000):
    return pl.CostEstimate(flops=flops, bytes_accessed=bytes_accessed, transcendentals=0)


def tree_sum(terms):
    while len(terms) > 1:
        terms = [terms[i] + terms[i + 1] for i in range(0, len(terms), 2)]
    return terms[0]


def exchange(x, axis, distance):
    size = lax.axis_size(axis)
    return lax.ppermute(x, axis, [(i, i ^ distance) for i in range(size)])


def left_kernel(pos, g_ref, f_ref, q_ref, vec_ref, comp_ref, near_ref, far_ref, total, feedback, right, sems):
    nmat, rows, _ = comp_ref.shape
    rank = q_ref.shape[1]
    part = near_ref.shape[0]
    cut = rows // 2 if rows % 32 == 0 else rows

    def copies(k):
        out = [pltpu.make_async_copy(q_ref.at[k], right.at[k], sems.at[k, 4])]
        for i, first in enumerate(range(0, rows, cut)):
            block = pl.ds(first, cut)
            for j, (source, target) in enumerate(((g_ref, comp_ref), (f_ref, feedback))):
                source, target = source.at[0, k, block], target.at[k, block]
                out.append(pltpu.make_async_copy(source, target, sems.at[k, 2 * i + j]))
        return out

    for k in range(min(AHEAD, nmat)):
        for copy in copies(k):
            copy.start()
    total[...] = jnp.zeros(total.shape, F32)
    width, nvec = total.shape[1], vec_ref.shape[1]
    for i, first in enumerate(range(0, nvec, width)):
        count = min(width, nvec - first)
        total[rows + i : rows + i + 1, :count] = vec_ref[:, first : first + count]

    for k in range(nmat):
        for copy in copies(k):
            copy.wait()
        if k + AHEAD < nmat:
            for copy in copies(k + AHEAD):
                copy.start()
        comp = comp_ref[k] + feedback[k]
        comp_ref[k] = comp
        total[:rows, k * rank : (k + 1) * rank] = lax.dot_general(
            comp, right[k], (((1,), (1,)), ((), ())), preferred_element_type=F32
        )

    for ref, core in ((near_ref, pos[2]), (far_ref, 1 - pos[2])):
        ref[...] = total[pl.ds(pl.multiple_of(core * part, 16), part), :]


def left_terms(pos, gradients, feedback, right_t, vec):
    _, nmat, rows, n = gradients.shape
    rank = right_t.shape[1]
    width = nmat * rank
    total = rows + -(-vec.shape[1] // width)
    total += -total % (16 * CORES)
    part = jax.ShapeDtypeStruct((total // CORES, width), F32)
    vmem = pl.BlockSpec(memory_space=pltpu.VMEM)
    any_spec = pl.BlockSpec(memory_space=pl.ANY)
    return pl.pallas_call(
        left_kernel,
        grid_spec=pltpu.PrefetchScalarGridSpec(
            num_scalar_prefetch=1,
            grid=(1,),
            in_specs=[any_spec] * 3 + [vmem],
            out_specs=[vmem] * 3,
            scratch_shapes=[
                pltpu.VMEM((total, width), F32),
                pltpu.VMEM((nmat, rows, n), BF16),
                pltpu.VMEM((nmat, rank, n), BF16),
                pltpu.SemaphoreType.DMA((nmat, 5)),
            ],
        ),
        out_shape=[jax.ShapeDtypeStruct((nmat, rows, n), BF16), part, part],
        compiler_params=params(20),
        cost_estimate=cost(),
        name="left_terms",
    )(pos, gradients, feedback, right_t, vec)


def add_kernel(*refs):
    out = refs[-1]
    out[...] = tree_sum([ref[...].astype(F32) for ref in refs[:-1]]).astype(out.dtype)


def add(parts, dtype):
    vmem = pl.BlockSpec(memory_space=pltpu.VMEM)
    return pl.pallas_call(
        add_kernel,
        in_specs=[vmem] * len(parts),
        out_specs=vmem,
        out_shape=jax.ShapeDtypeStruct(parts[0].shape, dtype),
        compiler_params=params(),
        cost_estimate=cost(),
        name="add",
    )(*parts)


def send_kernel(half, pos, near_ref, far_ref, gram_ref, comp_ref, send_ref, lt_ref, mix_ref, vec_ref, left, gram):
    nmat, rows, _ = comp_ref.shape
    rank = gram_ref.shape[1]
    part = near_ref.shape[0]
    for ref, core in ((near_ref, pos[2]), (far_ref, 1 - pos[2])):
        left[pl.ds(pl.multiple_of(core * part, 16), part), :] = ref[...]
    vec_ref[...] = left[rows:, :]
    gram[...] = jnp.zeros(gram.shape, F32)
    for i in range(nmat):
        gram[i * rank : (i + 1) * rank, i * rank : (i + 1) * rank] = gram_ref[i]
    hat = jnp.dot(
        left[:rows, :], gram[...], precision=lax.Precision.HIGHEST, preferred_element_type=F32
    )
    lt_ref[...] = hat.T.astype(BF16)
    mix_ref[:, :, :rows] = jnp.broadcast_to(unit_matrix(rows), (nmat, rows, rows))
    for i in range(nmat):
        mix_ref[i, :, rows:] = -hat[:, i * rank : (i + 1) * rank].astype(BF16)
    right_rows(half, pos, lt_ref, comp_ref, send_ref)


def unit_matrix(size):
    row = lax.broadcasted_iota(jnp.int32, (size, size), 0)
    col = lax.broadcasted_iota(jnp.int32, (size, size), 1)
    return jnp.where(row == col, 1.0, 0.0).astype(BF16)


def right_rows(start, pos, lt_ref, comp_ref, out_ref):
    half, upm, unit, _ = out_ref.shape
    for t in range(half):
        k = (t + start) ^ pos[0]
        rows = pl.ds(pl.multiple_of(k * upm * unit, upm * unit), upm * unit)
        terms = jnp.dot(lt_ref[rows, :], comp_ref[k], preferred_element_type=F32)
        for i in range(upm):
            out_ref[t, i ^ pos[1]] = terms[i * unit : (i + 1) * unit].astype(out_ref.dtype)


def keep_kernel(pos, lt_ref, comp_ref, *refs):
    right_rows(0, pos, lt_ref, comp_ref, refs[-1])


def right_terms(pos, near, far, gram, comp, upm, after):
    nmat, rows, n = comp.shape
    rank = gram.shape[1]
    width = nmat * rank
    half = nmat // CORES
    total = CORES * near.shape[0]
    shape = (half, upm, rank // upm, n)
    vmem = pl.BlockSpec(memory_space=pltpu.VMEM)
    send, lt, mix, vec = pl.pallas_call(
        functools.partial(send_kernel, half),
        grid_spec=pltpu.PrefetchScalarGridSpec(
            num_scalar_prefetch=1,
            grid=(1,),
            in_specs=[vmem] * 4,
            out_specs=[vmem] * 4,
            scratch_shapes=[pltpu.VMEM((total, width), F32), pltpu.VMEM((width, width), F32)],
        ),
        out_shape=[
            jax.ShapeDtypeStruct(shape, BF16),
            jax.ShapeDtypeStruct((width, rows), BF16),
            jax.ShapeDtypeStruct((nmat, rows, rows + rank), BF16),
            jax.ShapeDtypeStruct((total - rows, width), F32),
        ],
        compiler_params=params(),
        cost_estimate=cost(),
        name="right_send",
    )(pos, near, far, gram, comp)
    keep = pl.pallas_call(
        keep_kernel,
        grid_spec=pltpu.PrefetchScalarGridSpec(
            num_scalar_prefetch=1,
            grid=(1,),
            in_specs=[vmem, vmem] + [pl.BlockSpec(memory_space=pl.ANY)] * len(after),
            out_specs=vmem,
        ),
        out_shape=jax.ShapeDtypeStruct(shape, F32),
        compiler_params=params(),
        cost_estimate=cost(),
        name="right_keep",
    )(pos, lt, comp, *after)
    return send, keep, lt, mix, vec


def chip_kernel(replica_rows, pos, keep_ref, recv_ref, lt_ref, *refs):
    upm = keep_ref.shape[1]
    own_ref, strip_ref, *sends = refs[-(keep_ref.shape[0] * upm + 1) :]
    left = lt_ref[...].astype(F32).T
    strip = left[:replica_rows]
    for i in range(1, left.shape[0] // replica_rows):
        strip = jnp.where(pos[6] == i, left[i * replica_rows : (i + 1) * replica_rows], strip)
    height = strip_ref.shape[0]
    strip = jnp.concatenate(
        [strip[i * height : (i + 1) * height] for i in range(replica_rows // height)], axis=1
    )
    strip_ref[...] = strip
    own_ref[...] = keep_ref[0, 0] + recv_ref[0, 0].astype(F32)
    for d, out in enumerate(sends, 1):
        j, i = d // upm, d % upm
        terms = keep_ref[j, i] + recv_ref[j, i].astype(F32)
        out[...] = jnp.concatenate([terms, strip], axis=0).astype(BF16)


def chip_sum(pos, keep, recv, lt, replica_rows, after):
    half, upm, unit, n = keep.shape
    height = lt.shape[0] * replica_rows // n
    vmem = pl.BlockSpec(memory_space=pltpu.VMEM)
    outs = [jax.ShapeDtypeStruct((unit, n), F32), jax.ShapeDtypeStruct((height, n), F32)]
    outs += [jax.ShapeDtypeStruct((unit + height, n), BF16)] * (half * upm - 1)
    return pl.pallas_call(
        functools.partial(chip_kernel, replica_rows),
        grid_spec=pltpu.PrefetchScalarGridSpec(
            num_scalar_prefetch=1,
            grid=(1,),
            in_specs=[vmem] * 3 + [pl.BlockSpec(memory_space=pl.ANY)] * len(after),
            out_specs=[vmem] * len(outs),
        ),
        out_shape=outs,
        compiler_params=params(),
        cost_estimate=cost(),
        name="chip_sum",
    )(pos, keep, recv, lt, *after)


def plane_kernel(pos, own_ref, strip_ref, *refs):
    n_z = own_ref.shape[1] // refs[-2].shape[1]
    terms, outs, mix_ref = refs[: -n_z - 1], refs[-n_z - 1 : -1], refs[-1]
    unit, n = own_ref.shape
    cols = n // n_z
    for d, out in enumerate(outs):
        block = pl.ds(pl.multiple_of((pos[4] ^ d) * cols, cols), cols)
        parts = [own_ref[:, block]] + [term[:, block].astype(F32)[:unit] for term in terms]
        out[...] = tree_sum(parts).astype(out.dtype)
    strip = strip_ref[...]
    for d, term in enumerate(terms, 1):
        strip = jnp.where(pos[7] == d, term[...].astype(F32)[unit:], strip)
    nmat, count, depth = mix_ref.shape
    rank = (depth - count) // 2
    width = nmat * rank
    rows = [strip[:, i * width : (i + 1) * width] for i in range(n // width)]
    rows = -0.1 * jnp.concatenate(rows, axis=0)
    high = rows.astype(BF16)
    low = (rows - high.astype(F32)).astype(BF16)
    mix_ref[:, :, :count] = jnp.broadcast_to(unit_matrix(count), (nmat, count, count))
    for i in range(nmat):
        mix_ref[i, :, count : count + rank] = high[:, i * rank : (i + 1) * rank]
        mix_ref[i, :, count + rank :] = low[:, i * rank : (i + 1) * rank]


def plane_sum(pos, own, strip, terms, n_z, nmat, rank):
    unit, n = own.shape
    count = strip.size // (nmat * rank)
    outs = [jax.ShapeDtypeStruct((unit, n // n_z), BF16 if d else F32) for d in range(n_z)]
    outs.append(jax.ShapeDtypeStruct((nmat, count, count + 2 * rank), BF16))
    vmem = pl.BlockSpec(memory_space=pltpu.VMEM)
    return pl.pallas_call(
        plane_kernel,
        grid_spec=pltpu.PrefetchScalarGridSpec(
            num_scalar_prefetch=1,
            grid=(1,),
            in_specs=[vmem] * (2 + len(terms)),
            out_specs=[vmem] * len(outs),
        ),
        out_shape=outs,
        compiler_params=params(),
        cost_estimate=cost(),
        name="plane_sum",
    )(pos, own, strip, *terms)


def stack_kernel(count, *refs):
    for i in range(count):
        refs[-1][i] = refs[i][...]


def stack(parts, after=()):
    vmem = pl.BlockSpec(memory_space=pltpu.VMEM)
    return pl.pallas_call(
        functools.partial(stack_kernel, len(parts)),
        in_specs=[vmem] * len(parts) + [pl.BlockSpec(memory_space=pl.ANY)] * len(after),
        out_specs=vmem,
        out_shape=jax.ShapeDtypeStruct((len(parts),) + parts[0].shape, parts[0].dtype),
        compiler_params=params(),
        cost_estimate=cost(),
        name="stack",
    )(*parts, *after)


def token_kernel(*refs):
    refs[-1][...] = jnp.zeros(refs[-1].shape, F32)


def token(after):
    return pl.pallas_call(
        token_kernel,
        in_specs=[pl.BlockSpec(memory_space=pl.ANY)] * len(after),
        out_specs=pl.BlockSpec(memory_space=pltpu.VMEM),
        out_shape=jax.ShapeDtypeStruct((8, 128), F32),
        compiler_params=params(),
        cost_estimate=cost(),
        name="token",
    )(*after)


def forward_kernel(cuts, *refs):
    for source, out, first in zip(refs, refs[-len(cuts) :], cuts):
        out[...] = source[first : first + out.shape[0]]


def forward(parts, cuts, count, after):
    vmem = pl.BlockSpec(memory_space=pltpu.VMEM)
    return pl.pallas_call(
        functools.partial(forward_kernel, cuts),
        in_specs=[vmem] * len(parts) + [pl.BlockSpec(memory_space=pl.ANY)],
        out_specs=[vmem] * len(parts),
        out_shape=[jax.ShapeDtypeStruct((count,) + part.shape[1:], part.dtype) for part in parts],
        compiler_params=params(),
        cost_estimate=cost(),
        name="forward",
    )(*parts, after)


def rank_of(owners, k):
    count = jnp.int32(0)
    for j in range(owners.shape[0]):
        count += jnp.where((owners[j] == owners[k]) & (j < k), 1, 0)
    return count


def outputs_kernel(second, places, pos, owners, comp_ref, mix_ref, mixr_ref, near_ref, *refs):
    n_base = len({a for a, _ in places.values()})
    bases, refs = refs[:n_base], refs[n_base:]
    if second:
        far_ref, momentum_ref, master_ref, refs = refs[0], refs[1], refs[2], refs[5:]
    n_out = 4 if second else 2
    outs, refs = refs[:n_out], refs[n_out:]
    held, feedback, weights, fetch_sem, out_sem = refs[:5]
    half, upm, n_z, unit, cols = near_ref.shape
    count = held.shape[1]
    capacity = max(c for _, c in places) + 1

    def right_of(ref, j, d, block):
        parts = [ref[j, i ^ pos[1], d, :, block] for i in range(upm)]
        return parts[0] if upm == 1 else jnp.concatenate(parts, axis=0)

    def columns(d, first=0, size=cols):
        return pl.ds(pl.multiple_of((pos[4] ^ d) * cols + first, 128), size)

    pieces = [slice(first, first + COLUMNS) for first in range(0, cols, COLUMNS)]
    matrices = [(j + (half if second else 0)) ^ pos[0] for j in range(half)]
    for j, k in enumerate(matrices):
        slot = (owners[k] ^ pos[5]) * capacity + rank_of(owners, k)
        for (d, c), (a, row) in places.items():

            @pl.when(slot == d * capacity + c)
            def _():
                pltpu.make_async_copy(bases[a].at[row], held.at[j], fetch_sem.at[j]).start()

    stores = []

    def store(source, target, sem):
        stores.append(pltpu.make_async_copy(source, target, sem))
        stores[-1].start()

    if second:
        new_momentum, new_master, state_sem = refs[5:8]
        for c in range(capacity):
            matrix = jnp.int32(-1)
            for k in range(owners.shape[0]):
                matrix = jnp.where((owners[k] == pos[5]) & (rank_of(owners, k) == c), k, matrix)
            safe = jnp.maximum(matrix, 0)
            slot = safe ^ pos[0]
            inner = lax.rem(slot, half)
            mixr = mixr_ref[safe][:, count:]
            for d in range(n_z):
                for block in pieces:
                    right = jnp.where(
                        slot < half,
                        right_of(near_ref, inner, d, block),
                        right_of(far_ref, inner, d, block),
                    )
                    both = jnp.concatenate([right, right], axis=0)
                    change = jnp.dot(mixr, both, preferred_element_type=F32)
                    change = jnp.where(matrix >= 0, 10.0 * change, 0.0)
                    place = columns(d, block.start, COLUMNS)
                    momentum = 0.9 * momentum_ref[c, :, place] - change
                    new_momentum[c, :, place] = momentum
                    new_master[c, :, place] = master_ref[c, :, place] - 0.1 * momentum
                place = columns(d)
                for i, new in enumerate((new_momentum, new_master)):
                    store(
                        new.at[c, :, place], outs[2 + i].at[0, c, :, place], state_sem.at[i, c, d]
                    )

    for j, k in enumerate(matrices):
        ref = far_ref if second else near_ref
        mix, mixr = mix_ref[k], mixr_ref[k]
        for d in range(n_z):
            for block in pieces:
                right = right_of(ref, j, d, block)
                place = columns(d, block.start, COLUMNS)
                both = jnp.concatenate([comp_ref[k, :, place], right], axis=0)
                feedback[j, :, place] = jnp.dot(mix, both, preferred_element_type=F32).astype(BF16)
            place = columns(d)
            store(feedback.at[j, :, place], outs[0].at[0, k, :, place], out_sem.at[j, d, 0])
        pltpu.make_async_copy(bases[0].at[0], held.at[j], fetch_sem.at[j]).wait()
        for d in range(n_z):
            for block in pieces:
                right = right_of(ref, j, d, block)
                place = columns(d, block.start, COLUMNS)
                both = jnp.concatenate([held[j, :, place], right, right], axis=0)
                weights[j, :, place] = jnp.dot(mixr, both, preferred_element_type=F32).astype(BF16)
            place = columns(d)
            store(weights.at[j, :, place], outs[1].at[k, :, place], out_sem.at[j, d, 1])

    for copy in stores:
        copy.wait()


def outputs(pos, owners, comp, mix, mixr, near, bases, places, far=None, states=(), earlier=()):
    nmat, rows, n = comp.shape
    half, _, n_z = near.shape[:3]
    capacity = max(c for _, c in places) + 1
    replica_rows = bases[0].shape[1]
    second = far is not None
    any_spec = pl.BlockSpec(memory_space=pl.ANY)
    vmem = pl.BlockSpec(memory_space=pltpu.VMEM)
    scratch = [
        pltpu.VMEM((half, replica_rows, n), BF16),
        pltpu.VMEM((half, rows, n), BF16),
        pltpu.VMEM((half, replica_rows, n), BF16),
        pltpu.SemaphoreType.DMA((half,)),
        pltpu.SemaphoreType.DMA((half, n_z, 2)),
    ]
    if second:
        scratch += [pltpu.VMEM((capacity, replica_rows, n), F32)] * 2
        scratch += [pltpu.SemaphoreType.DMA((2, capacity, n_z))]
    outs = [
        jax.ShapeDtypeStruct((1, nmat, rows, n), BF16),
        jax.ShapeDtypeStruct((nmat, replica_rows, n), BF16),
    ] + [jax.ShapeDtypeStruct((1,) + x.shape, F32) for x in states]
    fars = [far] if second else []
    first = 6 + len(bases) + len(fars) + len(states)
    return pl.pallas_call(
        functools.partial(outputs_kernel, second, places),
        grid_spec=pltpu.PrefetchScalarGridSpec(
            num_scalar_prefetch=2,
            grid=(1,),
            in_specs=[vmem] * 4
            + [any_spec] * len(bases)
            + [vmem] * (len(fars) + len(states))
            + [any_spec] * len(earlier),
            out_specs=[any_spec] * len(outs),
            scratch_shapes=scratch,
        ),
        out_shape=outs,
        input_output_aliases={first + i: i for i in range(len(earlier))},
        compiler_params=params(24),
        cost_estimate=cost(),
        name="outputs",
    )(pos, owners, comp, mix, mixr, near, *bases, *fars, *states, *earlier)


def base_kernel(pos, momentum_ref, master_ref, *refs):
    out_ref, momentum, master, sems = refs
    capacity, rows, _ = out_ref.shape
    blocks = [(c, first) for c in range(capacity) for first in range(0, rows, BASE_ROWS)]

    def copies(i):
        c, first = blocks[i]
        part = pl.ds(first, BASE_ROWS)
        return [
            pltpu.make_async_copy(source.at[0, c, part], target.at[c, part], sems.at[j, i])
            for j, (source, target) in enumerate(((momentum_ref, momentum), (master_ref, master)))
        ]

    for i in range(len(blocks)):
        for copy in copies(i):
            copy.start()
    for i, (c, first) in enumerate(blocks):
        for copy in copies(i):
            copy.wait()
        part = slice(first, first + BASE_ROWS)
        out_ref[c, part] = (master[c, part] - 0.09 * momentum[c, part]).astype(BF16)


def base_of(pos, momentum, master):
    _, capacity, rows, n = momentum.shape
    state = jax.ShapeDtypeStruct((capacity, rows, n), F32)
    base, momentum, master = pl.pallas_call(
        base_kernel,
        grid_spec=pltpu.PrefetchScalarGridSpec(
            num_scalar_prefetch=1,
            grid=(1,),
            in_specs=[pl.BlockSpec(memory_space=pl.ANY)] * 2,
            out_specs=[pl.BlockSpec(memory_space=pltpu.VMEM)] * 3,
            scratch_shapes=[pltpu.SemaphoreType.DMA((2, capacity * rows // BASE_ROWS))],
        ),
        out_shape=[jax.ShapeDtypeStruct((capacity, rows, n), BF16), state, state],
        compiler_params=params(),
        cost_estimate=cost(),
        name="base",
    )(pos, momentum, master)
    return base, (momentum, master)


def per_device(
    gradients,
    feedback,
    right_init,
    gram_root,
    owners,
    momentum,
    master_weights,
    vector_grads,
    vector_momentum,
    vector_params,
):
    nmat, rows, n = gradients.shape[1:]
    rank = right_init.shape[2]
    unit = rank * nmat // (CORES * lax.axis_size("mp"))
    n_mp = lax.axis_size("mp")
    n_z = lax.axis_size("replica") // CORES
    capacity, replica_rows = momentum.shape[1:3]
    p = lax.axis_index("mp")
    r = lax.axis_index("replica")
    core, z = r % CORES, r // CORES
    upm = CORES * n_mp // nmat
    half = nmat // CORES
    code = core * n_mp + p
    first = r * replica_rows

    places_of = [code // upm, code % upm, core, r, z, p, first % rows // replica_rows, first // rows ^ p]
    pos = jnp.stack(places_of).astype(jnp.int32)
    in_hbm = lambda x: pltpu.with_memory_space_constraint(x, pltpu.HBM)

    square = n_mp == 4 and capacity == 2
    base, states = base_of(pos, in_hbm(momentum), in_hbm(master_weights))
    early = [exchange(base, "mp", d) for d in range(1, 3 if square else n_mp)]
    bases = [base] + early
    places = {(d, c): (d, c) for d in range(len(bases)) for c in range(capacity)}

    nvec = vector_grads.shape[1]
    comp, near, far = left_terms(
        pos,
        in_hbm(gradients),
        in_hbm(feedback),
        in_hbm(jnp.swapaxes(right_init, 1, 2)),
        vector_grads,
    )
    piece = add([near, exchange(far, "replica", 1)], BF16)
    along_z = lambda x: [exchange(x, "replica", CORES * d) for d in range(1, n_z)]
    piece = add([piece] + along_z(piece), F32)
    near, far = piece, exchange(piece, "replica", 1)

    send, keep, lt, mix, vector_rows = right_terms(pos, near, far, gram_root, comp, upm, [])
    vector_total = vector_rows.reshape(-1)[:nvec]
    recv = exchange(send, "replica", 1)
    own, strip, *chip = chip_sum(pos, keep, recv, lt, replica_rows, [token([keep] + early)])
    plane = [exchange(part, "mp", d) for d, part in enumerate(chip, 1)]
    *final, mixr = plane_sum(pos, own, strip, plane, n_z, nmat, rank)
    late = []
    if square:
        parts = forward(early, [0, 1], 1, mixr)
        late = [exchange(part, "mp", 2 - i) for i, part in enumerate(parts)]
        bases = bases + late
        places[3, 0], places[3, 1] = (3, 0), (4, 0)
    final = [final[0]] + [exchange(final[d], "replica", CORES * d) for d in range(1, n_z)]
    final = add(final, BF16)
    new_vector_momentum = 0.9 * vector_momentum + vector_total
    new_vector_params = vector_params - 0.1 * new_vector_momentum

    whole = stack([final] + along_z(final), late + [new_vector_params])
    near = stack([whole] + [exchange(whole, "mp", d) for d in range(1, n_mp)])
    near = near.reshape((half, upm) + whole.shape)
    far = exchange(near, "replica", 1)

    done = outputs(pos, owners, comp, mix, mixr, near, bases, places)
    new_feedback, new_weights, new_momentum, new_master = outputs(
        pos, owners, comp, mix, mixr, near, bases, places, far, states, done
    )

    return new_feedback, new_momentum, new_master, new_weights, new_vector_momentum, new_vector_params


def solution(mesh):
    return jax.shard_map(
        per_device,
        mesh=mesh,
        in_specs=(
            P("replica", None, "mp", None),
            P("replica", None, "mp", None),
            P(),
            P(),
            P(),
            P("mp", None, "replica", None),
            P("mp", None, "replica", None),
            P("replica", "mp"),
            P("mp"),
            P("mp"),
        ),
        out_specs=(
            P("replica", None, "mp", None),
            P("mp", None, "replica", None),
            P("mp", None, "replica", None),
            P(None, "replica", None),
            P("mp"),
            P("mp"),
        ),
        check_vma=False,
    )
```

```python
import functools

import jax
import jax.numpy as jnp
from jax import lax
from jax.experimental import pallas as pl
from jax.experimental.pallas import tpu as pltpu
from jax.sharding import PartitionSpec as P

CORES = 2
AHEAD = 8
BASE_ROWS = 48
COLUMNS = 384
F32 = jnp.float32
BF16 = jnp.bfloat16


def params(mib=12):
    return pltpu.CompilerParams(vmem_limit_bytes=mib * 1024 * 1024)


def cost(flops=1000, bytes_accessed=1000):
    return pl.CostEstimate(flops=flops, bytes_accessed=bytes_accessed, transcendentals=0)


def tree_sum(terms):
    while len(terms) > 1:
        terms = [terms[i] + terms[i + 1] for i in range(0, len(terms), 2)]
    return terms[0]


def exchange(x, axis, distance):
    size = lax.axis_size(axis)
    return lax.ppermute(x, axis, [(i, i ^ distance) for i in range(size)])


def left_kernel(pos, g_ref, f_ref, q_ref, vec_ref, comp_ref, near_ref, far_ref, total, feedback, right, sems):
    nmat, rows, _ = comp_ref.shape
    rank = q_ref.shape[1]
    part = near_ref.shape[0]

    def copies(k):
        return [
            pltpu.make_async_copy(g_ref.at[0, k], comp_ref.at[k], sems.at[k, 0]),
            pltpu.make_async_copy(f_ref.at[0, k], feedback.at[k], sems.at[k, 1]),
            pltpu.make_async_copy(q_ref.at[k], right.at[k], sems.at[k, 2]),
        ]

    for k in range(min(AHEAD, nmat)):
        for copy in copies(k):
            copy.start()
    total[...] = jnp.zeros(total.shape, F32)
    width, nvec = total.shape[1], vec_ref.shape[1]
    for i, first in enumerate(range(0, nvec, width)):
        count = min(width, nvec - first)
        total[rows + i : rows + i + 1, :count] = vec_ref[:, first : first + count]

    for k in range(nmat):
        for copy in copies(k):
            copy.wait()
        if k + AHEAD < nmat:
            for copy in copies(k + AHEAD):
                copy.start()
        comp = comp_ref[k] + feedback[k]
        comp_ref[k] = comp
        total[:rows, k * rank : (k + 1) * rank] = lax.dot_general(
            comp, right[k], (((1,), (1,)), ((), ())), preferred_element_type=F32
        )

    for ref, core in ((near_ref, pos[2]), (far_ref, 1 - pos[2])):
        ref[...] = total[pl.ds(pl.multiple_of(core * part, 16), part), :]


def left_terms(pos, gradients, feedback, right_t, vec):
    _, nmat, rows, n = gradients.shape
    rank = right_t.shape[1]
    width = nmat * rank
    total = rows + -(-vec.shape[1] // width)
    total += -total % (16 * CORES)
    part = jax.ShapeDtypeStruct((total // CORES, width), F32)
    vmem = pl.BlockSpec(memory_space=pltpu.VMEM)
    any_spec = pl.BlockSpec(memory_space=pl.ANY)
    return pl.pallas_call(
        left_kernel,
        grid_spec=pltpu.PrefetchScalarGridSpec(
            num_scalar_prefetch=1,
            grid=(1,),
            in_specs=[any_spec] * 3 + [vmem],
            out_specs=[vmem] * 3,
            scratch_shapes=[
                pltpu.VMEM((total, width), F32),
                pltpu.VMEM((nmat, rows, n), BF16),
                pltpu.VMEM((nmat, rank, n), BF16),
                pltpu.SemaphoreType.DMA((nmat, 3)),
            ],
        ),
        out_shape=[jax.ShapeDtypeStruct((nmat, rows, n), BF16), part, part],
        compiler_params=params(20),
        cost_estimate=cost(),
        name="left_terms",
    )(pos, gradients, feedback, right_t, vec)


def add_kernel(*refs):
    out = refs[-1]
    out[...] = tree_sum([ref[...].astype(F32) for ref in refs[:-1]]).astype(out.dtype)


def add(parts, dtype):
    vmem = pl.BlockSpec(memory_space=pltpu.VMEM)
    return pl.pallas_call(
        add_kernel,
        in_specs=[vmem] * len(parts),
        out_specs=vmem,
        out_shape=jax.ShapeDtypeStruct(parts[0].shape, dtype),
        compiler_params=params(),
        cost_estimate=cost(),
        name="add",
    )(*parts)


def send_kernel(half, pos, near_ref, far_ref, gram_ref, comp_ref, send_ref, lt_ref, mix_ref, vec_ref, left, gram):
    nmat, rows, _ = comp_ref.shape
    rank = gram_ref.shape[1]
    part = near_ref.shape[0]
    for ref, core in ((near_ref, pos[2]), (far_ref, 1 - pos[2])):
        left[pl.ds(pl.multiple_of(core * part, 16), part), :] = ref[...]
    vec_ref[...] = left[rows:, :]
    gram[...] = jnp.zeros(gram.shape, F32)
    for i in range(nmat):
        gram[i * rank : (i + 1) * rank, i * rank : (i + 1) * rank] = gram_ref[i]
    hat = jnp.dot(
        left[:rows, :], gram[...], precision=lax.Precision.HIGHEST, preferred_element_type=F32
    )
    lt_ref[...] = hat.T.astype(BF16)
    mix_ref[:, :, :rows] = jnp.broadcast_to(unit_matrix(rows), (nmat, rows, rows))
    for i in range(nmat):
        mix_ref[i, :, rows:] = -hat[:, i * rank : (i + 1) * rank].astype(BF16)
    right_rows(half, pos, lt_ref, comp_ref, send_ref)


def unit_matrix(size):
    row = lax.broadcasted_iota(jnp.int32, (size, size), 0)
    col = lax.broadcasted_iota(jnp.int32, (size, size), 1)
    return jnp.where(row == col, 1.0, 0.0).astype(BF16)


def right_rows(start, pos, lt_ref, comp_ref, out_ref):
    half, upm, unit, _ = out_ref.shape
    for t in range(half):
        k = (t + start) ^ pos[0]
        rows = pl.ds(pl.multiple_of(k * upm * unit, upm * unit), upm * unit)
        terms = jnp.dot(lt_ref[rows, :], comp_ref[k], preferred_element_type=F32)
        for i in range(upm):
            out_ref[t, i ^ pos[1]] = terms[i * unit : (i + 1) * unit].astype(out_ref.dtype)


def keep_kernel(pos, lt_ref, comp_ref, *refs):
    right_rows(0, pos, lt_ref, comp_ref, refs[-1])


def right_terms(pos, near, far, gram, comp, upm, after):
    nmat, rows, n = comp.shape
    rank = gram.shape[1]
    width = nmat * rank
    half = nmat // CORES
    total = CORES * near.shape[0]
    shape = (half, upm, rank // upm, n)
    vmem = pl.BlockSpec(memory_space=pltpu.VMEM)
    send, lt, mix, vec = pl.pallas_call(
        functools.partial(send_kernel, half),
        grid_spec=pltpu.PrefetchScalarGridSpec(
            num_scalar_prefetch=1,
            grid=(1,),
            in_specs=[vmem] * 4,
            out_specs=[vmem] * 4,
            scratch_shapes=[pltpu.VMEM((total, width), F32), pltpu.VMEM((width, width), F32)],
        ),
        out_shape=[
            jax.ShapeDtypeStruct(shape, BF16),
            jax.ShapeDtypeStruct((width, rows), BF16),
            jax.ShapeDtypeStruct((nmat, rows, rows + rank), BF16),
            jax.ShapeDtypeStruct((total - rows, width), F32),
        ],
        compiler_params=params(),
        cost_estimate=cost(),
        name="right_send",
    )(pos, near, far, gram, comp)
    keep = pl.pallas_call(
        keep_kernel,
        grid_spec=pltpu.PrefetchScalarGridSpec(
            num_scalar_prefetch=1,
            grid=(1,),
            in_specs=[vmem, vmem] + [pl.BlockSpec(memory_space=pl.ANY)] * len(after),
            out_specs=vmem,
        ),
        out_shape=jax.ShapeDtypeStruct(shape, F32),
        compiler_params=params(),
        cost_estimate=cost(),
        name="right_keep",
    )(pos, lt, comp, *after)
    return send, keep, lt, mix, vec


def chip_kernel(replica_rows, pos, keep_ref, recv_ref, lt_ref, *refs):
    upm = keep_ref.shape[1]
    own_ref, strip_ref, *sends = refs[-(keep_ref.shape[0] * upm + 1) :]
    left = lt_ref[...].astype(F32).T
    strip = left[:replica_rows]
    for i in range(1, left.shape[0] // replica_rows):
        strip = jnp.where(pos[6] == i, left[i * replica_rows : (i + 1) * replica_rows], strip)
    height = strip_ref.shape[0]
    strip = jnp.concatenate(
        [strip[i * height : (i + 1) * height] for i in range(replica_rows // height)], axis=1
    )
    strip_ref[...] = strip
    own_ref[...] = keep_ref[0, 0] + recv_ref[0, 0].astype(F32)
    for d, out in enumerate(sends, 1):
        j, i = d // upm, d % upm
        terms = keep_ref[j, i] + recv_ref[j, i].astype(F32)
        out[...] = jnp.concatenate([terms, strip], axis=0).astype(BF16)


def chip_sum(pos, keep, recv, lt, replica_rows, after):
    half, upm, unit, n = keep.shape
    height = lt.shape[0] * replica_rows // n
    vmem = pl.BlockSpec(memory_space=pltpu.VMEM)
    outs = [jax.ShapeDtypeStruct((unit, n), F32), jax.ShapeDtypeStruct((height, n), F32)]
    outs += [jax.ShapeDtypeStruct((unit + height, n), BF16)] * (half * upm - 1)
    return pl.pallas_call(
        functools.partial(chip_kernel, replica_rows),
        grid_spec=pltpu.PrefetchScalarGridSpec(
            num_scalar_prefetch=1,
            grid=(1,),
            in_specs=[vmem] * 3 + [pl.BlockSpec(memory_space=pl.ANY)] * len(after),
            out_specs=[vmem] * len(outs),
        ),
        out_shape=outs,
        compiler_params=params(),
        cost_estimate=cost(),
        name="chip_sum",
    )(pos, keep, recv, lt, *after)


def plane_kernel(pos, own_ref, strip_ref, *refs):
    n_z = own_ref.shape[1] // refs[-2].shape[1]
    terms, outs, mix_ref = refs[: -n_z - 1], refs[-n_z - 1 : -1], refs[-1]
    unit, n = own_ref.shape
    cols = n // n_z
    for d, out in enumerate(outs):
        block = pl.ds(pl.multiple_of((pos[4] ^ d) * cols, cols), cols)
        parts = [own_ref[:, block]] + [term[:, block].astype(F32)[:unit] for term in terms]
        out[...] = tree_sum(parts).astype(out.dtype)
    strip = strip_ref[...]
    for d, term in enumerate(terms, 1):
        strip = jnp.where(pos[7] == d, term[...].astype(F32)[unit:], strip)
    nmat, count, depth = mix_ref.shape
    rank = (depth - count) // 2
    width = nmat * rank
    rows = [strip[:, i * width : (i + 1) * width] for i in range(n // width)]
    rows = -0.1 * jnp.concatenate(rows, axis=0)
    high = rows.astype(BF16)
    low = (rows - high.astype(F32)).astype(BF16)
    mix_ref[:, :, :count] = jnp.broadcast_to(unit_matrix(count), (nmat, count, count))
    for i in range(nmat):
        mix_ref[i, :, count : count + rank] = high[:, i * rank : (i + 1) * rank]
        mix_ref[i, :, count + rank :] = low[:, i * rank : (i + 1) * rank]


def plane_sum(pos, own, strip, terms, n_z, nmat, rank):
    unit, n = own.shape
    count = strip.size // (nmat * rank)
    outs = [jax.ShapeDtypeStruct((unit, n // n_z), BF16 if d else F32) for d in range(n_z)]
    outs.append(jax.ShapeDtypeStruct((nmat, count, count + 2 * rank), BF16))
    vmem = pl.BlockSpec(memory_space=pltpu.VMEM)
    return pl.pallas_call(
        plane_kernel,
        grid_spec=pltpu.PrefetchScalarGridSpec(
            num_scalar_prefetch=1,
            grid=(1,),
            in_specs=[vmem] * (2 + len(terms)),
            out_specs=[vmem] * len(outs),
        ),
        out_shape=outs,
        compiler_params=params(),
        cost_estimate=cost(),
        name="plane_sum",
    )(pos, own, strip, *terms)


def stack_kernel(count, *refs):
    for i in range(count):
        refs[-1][i] = refs[i][...]


def stack(parts, after=()):
    vmem = pl.BlockSpec(memory_space=pltpu.VMEM)
    return pl.pallas_call(
        functools.partial(stack_kernel, len(parts)),
        in_specs=[vmem] * len(parts) + [pl.BlockSpec(memory_space=pl.ANY)] * len(after),
        out_specs=vmem,
        out_shape=jax.ShapeDtypeStruct((len(parts),) + parts[0].shape, parts[0].dtype),
        compiler_params=params(),
        cost_estimate=cost(),
        name="stack",
    )(*parts, *after)


def token_kernel(*refs):
    refs[-1][...] = jnp.zeros(refs[-1].shape, F32)


def token(after):
    return pl.pallas_call(
        token_kernel,
        in_specs=[pl.BlockSpec(memory_space=pl.ANY)] * len(after),
        out_specs=pl.BlockSpec(memory_space=pltpu.VMEM),
        out_shape=jax.ShapeDtypeStruct((8, 128), F32),
        compiler_params=params(),
        cost_estimate=cost(),
        name="token",
    )(*after)


def forward_kernel(cuts, *refs):
    for source, out, first in zip(refs, refs[-len(cuts) :], cuts):
        out[...] = source[first : first + out.shape[0]]


def forward(parts, cuts, count, after):
    vmem = pl.BlockSpec(memory_space=pltpu.VMEM)
    return pl.pallas_call(
        functools.partial(forward_kernel, cuts),
        in_specs=[vmem] * len(parts) + [pl.BlockSpec(memory_space=pl.ANY)],
        out_specs=[vmem] * len(parts),
        out_shape=[jax.ShapeDtypeStruct((count,) + part.shape[1:], part.dtype) for part in parts],
        compiler_params=params(),
        cost_estimate=cost(),
        name="forward",
    )(*parts, after)


def rank_of(owners, k):
    count = jnp.int32(0)
    for j in range(owners.shape[0]):
        count += jnp.where((owners[j] == owners[k]) & (j < k), 1, 0)
    return count


def collect_kernel(places, *refs):
    for i, (a, row) in enumerate(places):
        refs[-1][i] = refs[a][row]


def collect(bases, places):
    vmem = pl.BlockSpec(memory_space=pltpu.VMEM)
    return pl.pallas_call(
        functools.partial(collect_kernel, places),
        in_specs=[vmem] * len(bases),
        out_specs=vmem,
        out_shape=jax.ShapeDtypeStruct((len(places),) + bases[0].shape[1:], BF16),
        compiler_params=params(),
        cost_estimate=cost(),
        name="collect",
    )(*bases)


def outputs_kernel(jobs, where, capacity, pos, owners, comp_ref, mix_ref, mixr_ref, base_ref, *refs):
    n_right = 1 + max(a for a, _ in (where or jobs).values())
    rights, refs = refs[:n_right], refs[n_right:]
    n_scratch = 6 if where else 3
    scratch = refs[-n_scratch:]
    feedback, weights, out_sem = scratch[:3]
    refs = refs[:-n_scratch]
    token_ref, outs = refs[-1], refs[-5:-1] if where else refs[-3:-1]
    token_ref[...] = jnp.zeros(token_ref.shape, F32)
    _, upm, n_z, _, cols = rights[0].shape
    half = comp_ref.shape[0] // CORES
    count = weights.shape[1]

    def right_of(place, d, block):
        a, entry = place
        parts = [rights[a][entry, i ^ pos[1], d, :, block] for i in range(upm)]
        return parts[0] if upm == 1 else jnp.concatenate(parts, axis=0)

    def columns(d, first=0, size=cols):
        return pl.ds(pl.multiple_of((pos[4] ^ d) * cols + first, 128), size)

    def matrix(other, j):
        return (j + half * other) ^ pos[0]

    pieces = [slice(first, first + COLUMNS) for first in range(0, cols, COLUMNS)]
    stores = []

    def store(source, target, sem):
        stores.append(pltpu.make_async_copy(source, target, sem))
        stores[-1].start()

    if where:
        momentum_ref, master_ref = refs[:2]
        new_momentum, new_master, state_sem = scratch[3:]
        for c in range(capacity):
            mine = jnp.int32(-1)
            for k in range(owners.shape[0]):
                mine = jnp.where((owners[k] == pos[5]) & (rank_of(owners, k) == c), k, mine)
            safe = jnp.maximum(mine, 0)
            mixr = mixr_ref[safe][:, count:]
            for d in range(n_z):
                for block in pieces:
                    right = jnp.zeros((mixr.shape[1] // 2, COLUMNS), BF16)
                    for job, place in where.items():
                        right = jnp.where(safe == matrix(*job), right_of(place, d, block), right)
                    both = jnp.concatenate([right, right], axis=0)
                    change = jnp.dot(mixr, both, preferred_element_type=F32)
                    change = jnp.where(mine >= 0, 10.0 * change, 0.0)
                    place = columns(d, block.start, COLUMNS)
                    momentum = 0.9 * momentum_ref[c, :, place] - change
                    new_momentum[c, :, place] = momentum
                    new_master[c, :, place] = master_ref[c, :, place] - 0.1 * momentum
                place = columns(d)
                for i, new in enumerate((new_momentum, new_master)):
                    store(
                        new.at[c, :, place], outs[2 + i].at[0, c, :, place], state_sem.at[i, c, d]
                    )

    for i, (job, where_right) in enumerate(jobs.items()):
        k = matrix(*job)
        slot = (owners[k] ^ pos[5]) * capacity + rank_of(owners, k)
        mix, mixr = mix_ref[k], mixr_ref[k]
        for d in range(n_z):
            for block in pieces:
                right = right_of(where_right, d, block)
                place = columns(d, block.start, COLUMNS)
                both = jnp.concatenate([comp_ref[k, :, place], right], axis=0)
                feedback[i, :, place] = jnp.dot(mix, both, preferred_element_type=F32).astype(BF16)
                both = jnp.concatenate([base_ref[slot, :, place], right, right], axis=0)
                weights[i, :, place] = jnp.dot(mixr, both, preferred_element_type=F32).astype(BF16)
            place = columns(d)
            store(feedback.at[i, :, place], outs[0].at[0, k, :, place], out_sem.at[i, d, 0])
            store(weights.at[i, :, place], outs[1].at[k, :, place], out_sem.at[i, d, 1])

    for copy in stores:
        copy.wait()


def outputs(pos, owners, comp, mix, mixr, base, capacity, rights, jobs, where=None, states=(), earlier=()):
    nmat, rows, n = comp.shape
    n_z = rights[0].shape[2]
    replica_rows = base.shape[1]
    any_spec = pl.BlockSpec(memory_space=pl.ANY)
    vmem = pl.BlockSpec(memory_space=pltpu.VMEM)
    scratch = [
        pltpu.VMEM((len(jobs), rows, n), BF16),
        pltpu.VMEM((len(jobs), replica_rows, n), BF16),
        pltpu.SemaphoreType.DMA((len(jobs), n_z, 2)),
    ]
    if states:
        scratch += [pltpu.VMEM((capacity, replica_rows, n), F32)] * 2
        scratch += [pltpu.SemaphoreType.DMA((2, capacity, n_z))]
    outs = [
        jax.ShapeDtypeStruct((1, nmat, rows, n), BF16),
        jax.ShapeDtypeStruct((nmat, replica_rows, n), BF16),
    ] + [jax.ShapeDtypeStruct((1,) + x.shape, F32) for x in states]
    first = 6 + len(rights) + len(states)
    return pl.pallas_call(
        functools.partial(outputs_kernel, jobs, where, capacity),
        grid_spec=pltpu.PrefetchScalarGridSpec(
            num_scalar_prefetch=2,
            grid=(1,),
            in_specs=[vmem] * (4 + len(rights) + len(states)) + [any_spec] * len(earlier),
            out_specs=[any_spec] * len(outs) + [vmem],
            scratch_shapes=scratch,
        ),
        out_shape=outs + [jax.ShapeDtypeStruct((8, 128), F32)],
        input_output_aliases={first + i: i for i in range(len(earlier))},
        compiler_params=params(24),
        cost_estimate=cost(),
        name="outputs",
    )(pos, owners, comp, mix, mixr, base, *rights, *states, *earlier)


def base_kernel(pos, momentum_ref, master_ref, *refs):
    out_ref, momentum, master, sems = refs
    capacity, rows, _ = out_ref.shape
    blocks = [(c, first) for c in range(capacity) for first in range(0, rows, BASE_ROWS)]

    def copies(i):
        c, first = blocks[i]
        part = pl.ds(first, BASE_ROWS)
        return [
            pltpu.make_async_copy(source.at[0, c, part], target.at[c, part], sems.at[j, i])
            for j, (source, target) in enumerate(((momentum_ref, momentum), (master_ref, master)))
        ]

    for i in range(len(blocks)):
        for copy in copies(i):
            copy.start()
    for i, (c, first) in enumerate(blocks):
        for copy in copies(i):
            copy.wait()
        part = slice(first, first + BASE_ROWS)
        out_ref[c, part] = (master[c, part] - 0.09 * momentum[c, part]).astype(BF16)


def base_of(pos, momentum, master):
    _, capacity, rows, n = momentum.shape
    state = jax.ShapeDtypeStruct((capacity, rows, n), F32)
    base, momentum, master = pl.pallas_call(
        base_kernel,
        grid_spec=pltpu.PrefetchScalarGridSpec(
            num_scalar_prefetch=1,
            grid=(1,),
            in_specs=[pl.BlockSpec(memory_space=pl.ANY)] * 2,
            out_specs=[pl.BlockSpec(memory_space=pltpu.VMEM)] * 3,
            scratch_shapes=[pltpu.SemaphoreType.DMA((2, capacity * rows // BASE_ROWS))],
        ),
        out_shape=[jax.ShapeDtypeStruct((capacity, rows, n), BF16), state, state],
        compiler_params=params(),
        cost_estimate=cost(),
        name="base",
    )(pos, momentum, master)
    return base, (momentum, master)


def per_device(
    gradients,
    feedback,
    right_init,
    gram_root,
    owners,
    momentum,
    master_weights,
    vector_grads,
    vector_momentum,
    vector_params,
):
    nmat, rows, n = gradients.shape[1:]
    rank = right_init.shape[2]
    unit = rank * nmat // (CORES * lax.axis_size("mp"))
    n_mp = lax.axis_size("mp")
    n_z = lax.axis_size("replica") // CORES
    capacity, replica_rows = momentum.shape[1:3]
    p = lax.axis_index("mp")
    r = lax.axis_index("replica")
    core, z = r % CORES, r // CORES
    upm = CORES * n_mp // nmat
    half = nmat // CORES
    code = core * n_mp + p
    first = r * replica_rows

    places_of = [code // upm, code % upm, core, r, z, p, first % rows // replica_rows, first // rows ^ p]
    pos = jnp.stack(places_of).astype(jnp.int32)
    in_hbm = lambda x: pltpu.with_memory_space_constraint(x, pltpu.HBM)

    square = n_mp == 4 and capacity == 2
    base, states = base_of(pos, in_hbm(momentum), in_hbm(master_weights))
    early = [exchange(base, "mp", d) for d in range(1, 3 if square else n_mp)]
    bases = [base] + early
    places = {(d, c): (d, c) for d in range(len(bases)) for c in range(capacity)}

    nvec = vector_grads.shape[1]
    comp, near, far = left_terms(
        pos,
        in_hbm(gradients),
        in_hbm(feedback),
        in_hbm(jnp.swapaxes(right_init, 1, 2)),
        vector_grads,
    )
    piece = add([near, exchange(far, "replica", 1)], BF16)
    along_z = lambda x: [exchange(x, "replica", CORES * d) for d in range(1, n_z)]
    piece = add([piece] + along_z(piece), F32)
    near, far = piece, exchange(piece, "replica", 1)

    send, keep, lt, mix, vector_rows = right_terms(pos, near, far, gram_root, comp, upm, [])
    vector_total = vector_rows.reshape(-1)[:nvec]
    recv = exchange(send, "replica", 1)
    own, strip, *chip = chip_sum(pos, keep, recv, lt, replica_rows, [token([keep] + early)])
    plane = [exchange(part, "mp", d) for d, part in enumerate(chip, 1)]
    *final, mixr = plane_sum(pos, own, strip, plane, n_z, nmat, rank)
    late = []
    if square:
        parts = forward(early, [0, 1], 1, mixr)
        late = [exchange(part, "mp", 2 - i) for i, part in enumerate(parts)]
        bases = bases + late
        places[3, 0], places[3, 1] = (3, 0), (4, 0)
    final = [final[0]] + [exchange(final[d], "replica", CORES * d) for d in range(1, n_z)]
    final = add(final, BF16)
    new_vector_momentum = 0.9 * vector_momentum + vector_total
    new_vector_params = vector_params - 0.1 * new_vector_momentum

    whole = stack([final] + along_z(final), late + [new_vector_params])
    others = [exchange(whole, "mp", d) for d in range(1, n_mp)]
    slots = collect(bases, [places[d, c] for d in range(n_mp) for c in range(capacity)])
    common = (pos, owners, comp, mix, mixr, slots, capacity)
    shape = (half, upm) + whole.shape
    done, near_jobs, after = (), {(0, j): (0, j) for j in range(half)}, [slots]
    if upm == 1:
        *done, after = outputs(*common, [whole[None, None]], {(0, 0): (0, 0)})
        after = [after]
        del near_jobs[0, 0]
    near = stack([whole] + others, after).reshape(shape)
    far = exchange(near, "replica", 1)
    far_jobs = {(1, j): (1, j) for j in range(half)}
    where = {(0, j): (0, j) for j in range(half)} | far_jobs
    *done, _ = outputs(*common, [near], near_jobs, earlier=done)
    new_feedback, new_weights, new_momentum, new_master, _ = outputs(
        *common, [near, far], far_jobs, where, states, done
    )
    return new_feedback, new_momentum, new_master, new_weights, new_vector_momentum, new_vector_params


def solution(mesh):
    return jax.shard_map(
        per_device,
        mesh=mesh,
        in_specs=(
            P("replica", None, "mp", None),
            P("replica", None, "mp", None),
            P(),
            P(),
            P(),
            P("mp", None, "replica", None),
            P("mp", None, "replica", None),
            P("replica", "mp"),
            P("mp"),
            P("mp"),
        ),
        out_specs=(
            P("replica", None, "mp", None),
            P("mp", None, "replica", None),
            P("mp", None, "replica", None),
            P(None, "replica", None),
            P("mp"),
            P("mp"),
        ),
        check_vma=False,
    )
```

```python
import functools

import jax
import jax.numpy as jnp
from jax import lax
from jax.experimental import pallas as pl
from jax.experimental.pallas import tpu as pltpu
from jax.sharding import PartitionSpec as P

CORES = 2
AHEAD = 8
BASE_ROWS = 48
F32 = jnp.float32
BF16 = jnp.bfloat16


def params(mib=12):
    return pltpu.CompilerParams(vmem_limit_bytes=mib * 1024 * 1024)


def cost(flops=1000, bytes_accessed=1000):
    return pl.CostEstimate(flops=flops, bytes_accessed=bytes_accessed, transcendentals=0)


def tree_sum(terms):
    while len(terms) > 1:
        terms = [terms[i] + terms[i + 1] for i in range(0, len(terms), 2)]
    return terms[0]


def exchange(x, axis, distance):
    size = lax.axis_size(axis)
    return lax.ppermute(x, axis, [(i, i ^ distance) for i in range(size)])


def left_kernel(pos, g_ref, f_ref, q_ref, vec_ref, comp_ref, near_ref, far_ref, total, feedback, right, sems):
    nmat, rows, _ = comp_ref.shape
    rank = q_ref.shape[1]
    part = near_ref.shape[0]

    def copies(k):
        return [
            pltpu.make_async_copy(g_ref.at[0, k], comp_ref.at[k], sems.at[k, 0]),
            pltpu.make_async_copy(f_ref.at[0, k], feedback.at[k], sems.at[k, 1]),
            pltpu.make_async_copy(q_ref.at[k], right.at[k], sems.at[k, 2]),
        ]

    for k in range(min(AHEAD, nmat)):
        for copy in copies(k):
            copy.start()
    total[...] = jnp.zeros(total.shape, F32)
    width, nvec = total.shape[1], vec_ref.shape[1]
    for i, first in enumerate(range(0, nvec, width)):
        count = min(width, nvec - first)
        total[rows + i : rows + i + 1, :count] = vec_ref[:, first : first + count]

    for k in range(nmat):
        for copy in copies(k):
            copy.wait()
        if k + AHEAD < nmat:
            for copy in copies(k + AHEAD):
                copy.start()
        comp = comp_ref[k] + feedback[k]
        comp_ref[k] = comp
        total[:rows, k * rank : (k + 1) * rank] = lax.dot_general(
            comp, right[k], (((1,), (1,)), ((), ())), preferred_element_type=F32
        )

    for ref, core in ((near_ref, pos[2]), (far_ref, 1 - pos[2])):
        ref[...] = total[pl.ds(pl.multiple_of(core * part, 16), part), :]


def left_terms(pos, gradients, feedback, right_t, vec):
    _, nmat, rows, n = gradients.shape
    rank = right_t.shape[1]
    width = nmat * rank
    total = rows + -(-vec.shape[1] // width)
    total += -total % (16 * CORES)
    part = jax.ShapeDtypeStruct((total // CORES, width), F32)
    vmem = pl.BlockSpec(memory_space=pltpu.VMEM)
    any_spec = pl.BlockSpec(memory_space=pl.ANY)
    return pl.pallas_call(
        left_kernel,
        grid_spec=pltpu.PrefetchScalarGridSpec(
            num_scalar_prefetch=1,
            grid=(1,),
            in_specs=[any_spec] * 3 + [vmem],
            out_specs=[vmem] * 3,
            scratch_shapes=[
                pltpu.VMEM((total, width), F32),
                pltpu.VMEM((nmat, rows, n), BF16),
                pltpu.VMEM((nmat, rank, n), BF16),
                pltpu.SemaphoreType.DMA((nmat, 3)),
            ],
        ),
        out_shape=[jax.ShapeDtypeStruct((nmat, rows, n), BF16), part, part],
        compiler_params=params(20),
        cost_estimate=cost(),
        name="left_terms",
    )(pos, gradients, feedback, right_t, vec)


def add_kernel(*refs):
    out = refs[-1]
    out[...] = tree_sum([ref[...].astype(F32) for ref in refs[:-1]]).astype(out.dtype)


def add(parts, dtype):
    vmem = pl.BlockSpec(memory_space=pltpu.VMEM)
    return pl.pallas_call(
        add_kernel,
        in_specs=[vmem] * len(parts),
        out_specs=vmem,
        out_shape=jax.ShapeDtypeStruct(parts[0].shape, dtype),
        compiler_params=params(),
        cost_estimate=cost(),
        name="add",
    )(*parts)


def send_kernel(half, pos, near_ref, far_ref, gram_ref, comp_ref, send_ref, lt_ref, left_ref, vec_ref, left, gram):
    nmat, rows, _ = comp_ref.shape
    rank = gram_ref.shape[1]
    part = near_ref.shape[0]
    for ref, core in ((near_ref, pos[2]), (far_ref, 1 - pos[2])):
        left[pl.ds(pl.multiple_of(core * part, 16), part), :] = ref[...]
    vec_ref[...] = left[rows:, :]
    gram[...] = jnp.zeros(gram.shape, F32)
    for i in range(nmat):
        gram[i * rank : (i + 1) * rank, i * rank : (i + 1) * rank] = gram_ref[i]
    hat = jnp.dot(
        left[:rows, :], gram[...], precision=lax.Precision.HIGHEST, preferred_element_type=F32
    )
    lt_ref[...] = hat.T.astype(BF16)
    for i in range(nmat):
        left_ref[i] = hat[:, i * rank : (i + 1) * rank].astype(BF16)
    right_rows(half, pos, lt_ref, comp_ref, send_ref)


def right_rows(start, pos, lt_ref, comp_ref, out_ref):
    half, upm, unit, _ = out_ref.shape
    for t in range(half):
        k = (t + start) ^ pos[0]
        rows = pl.ds(pl.multiple_of(k * upm * unit, upm * unit), upm * unit)
        terms = jnp.dot(lt_ref[rows, :], comp_ref[k], preferred_element_type=F32)
        for i in range(upm):
            out_ref[t, i ^ pos[1]] = terms[i * unit : (i + 1) * unit].astype(out_ref.dtype)


def keep_kernel(pos, lt_ref, comp_ref, *refs):
    right_rows(0, pos, lt_ref, comp_ref, refs[-1])


def right_terms(pos, near, far, gram, comp, upm, after):
    nmat, rows, n = comp.shape
    rank = gram.shape[1]
    width = nmat * rank
    half = nmat // CORES
    total = CORES * near.shape[0]
    shape = (half, upm, rank // upm, n)
    vmem = pl.BlockSpec(memory_space=pltpu.VMEM)
    send, lt, left, vec = pl.pallas_call(
        functools.partial(send_kernel, half),
        grid_spec=pltpu.PrefetchScalarGridSpec(
            num_scalar_prefetch=1,
            grid=(1,),
            in_specs=[vmem] * 4,
            out_specs=[vmem] * 4,
            scratch_shapes=[pltpu.VMEM((total, width), F32), pltpu.VMEM((width, width), F32)],
        ),
        out_shape=[
            jax.ShapeDtypeStruct(shape, BF16),
            jax.ShapeDtypeStruct((width, rows), BF16),
            jax.ShapeDtypeStruct((nmat, rows, rank), BF16),
            jax.ShapeDtypeStruct((total - rows, width), F32),
        ],
        compiler_params=params(),
        cost_estimate=cost(),
        name="right_send",
    )(pos, near, far, gram, comp)
    keep = pl.pallas_call(
        keep_kernel,
        grid_spec=pltpu.PrefetchScalarGridSpec(
            num_scalar_prefetch=1,
            grid=(1,),
            in_specs=[vmem, vmem] + [pl.BlockSpec(memory_space=pl.ANY)] * len(after),
            out_specs=vmem,
        ),
        out_shape=jax.ShapeDtypeStruct(shape, F32),
        compiler_params=params(),
        cost_estimate=cost(),
        name="right_keep",
    )(pos, lt, comp, *after)
    return send, keep, lt, left, vec


def chip_kernel(replica_rows, pos, keep_ref, recv_ref, lt_ref, *refs):
    upm = keep_ref.shape[1]
    own_ref, strip_ref, *sends = refs[-(keep_ref.shape[0] * upm + 1) :]
    left = lt_ref[...].astype(F32).T
    strip = left[:replica_rows]
    for i in range(1, left.shape[0] // replica_rows):
        strip = jnp.where(pos[6] == i, left[i * replica_rows : (i + 1) * replica_rows], strip)
    height = strip_ref.shape[0]
    strip = jnp.concatenate(
        [strip[i * height : (i + 1) * height] for i in range(replica_rows // height)], axis=1
    )
    strip_ref[...] = strip
    own_ref[...] = keep_ref[0, 0] + recv_ref[0, 0].astype(F32)
    for d, out in enumerate(sends, 1):
        j, i = d // upm, d % upm
        terms = keep_ref[j, i] + recv_ref[j, i].astype(F32)
        out[...] = jnp.concatenate([terms, strip], axis=0).astype(BF16)


def chip_sum(pos, keep, recv, lt, replica_rows, after):
    half, upm, unit, n = keep.shape
    height = lt.shape[0] * replica_rows // n
    vmem = pl.BlockSpec(memory_space=pltpu.VMEM)
    outs = [jax.ShapeDtypeStruct((unit, n), F32), jax.ShapeDtypeStruct((height, n), F32)]
    outs += [jax.ShapeDtypeStruct((unit + height, n), BF16)] * (half * upm - 1)
    return pl.pallas_call(
        functools.partial(chip_kernel, replica_rows),
        grid_spec=pltpu.PrefetchScalarGridSpec(
            num_scalar_prefetch=1,
            grid=(1,),
            in_specs=[vmem] * 3 + [pl.BlockSpec(memory_space=pl.ANY)] * len(after),
            out_specs=[vmem] * len(outs),
        ),
        out_shape=outs,
        compiler_params=params(),
        cost_estimate=cost(),
        name="chip_sum",
    )(pos, keep, recv, lt, *after)


def plane_kernel(pos, own_ref, strip_ref, *refs):
    n_z = own_ref.shape[1] // refs[-2].shape[1]
    terms, outs, left_ref = refs[: -n_z - 1], refs[-n_z - 1 : -1], refs[-1]
    unit, n = own_ref.shape
    cols = n // n_z
    for d, out in enumerate(outs):
        block = pl.ds(pl.multiple_of((pos[4] ^ d) * cols, cols), cols)
        parts = [own_ref[:, block]] + [term[:, block].astype(F32)[:unit] for term in terms]
        out[...] = tree_sum(parts).astype(out.dtype)
    strip = strip_ref[...]
    for d, term in enumerate(terms, 1):
        strip = jnp.where(pos[7] == d, term[...].astype(F32)[unit:], strip)
    nmat, _, rank = left_ref.shape
    width = nmat * rank
    rows = [strip[:, i * width : (i + 1) * width] for i in range(n // width)]
    rows = jnp.concatenate(rows, axis=0).astype(BF16)
    for i in range(nmat):
        left_ref[i] = rows[:, i * rank : (i + 1) * rank]


def plane_sum(pos, own, strip, terms, n_z, nmat, rank):
    unit, n = own.shape
    count = strip.size // (nmat * rank)
    outs = [jax.ShapeDtypeStruct((unit, n // n_z), BF16 if d else F32) for d in range(n_z)]
    outs.append(jax.ShapeDtypeStruct((nmat, count, rank), BF16))
    vmem = pl.BlockSpec(memory_space=pltpu.VMEM)
    return pl.pallas_call(
        plane_kernel,
        grid_spec=pltpu.PrefetchScalarGridSpec(
            num_scalar_prefetch=1,
            grid=(1,),
            in_specs=[vmem] * (2 + len(terms)),
            out_specs=[vmem] * len(outs),
        ),
        out_shape=outs,
        compiler_params=params(),
        cost_estimate=cost(),
        name="plane_sum",
    )(pos, own, strip, *terms)


def stack_kernel(count, *refs):
    for i in range(count):
        refs[-1][i] = refs[i][...]


def stack(parts, after=()):
    vmem = pl.BlockSpec(memory_space=pltpu.VMEM)
    return pl.pallas_call(
        functools.partial(stack_kernel, len(parts)),
        in_specs=[vmem] * len(parts) + [pl.BlockSpec(memory_space=pl.ANY)] * len(after),
        out_specs=vmem,
        out_shape=jax.ShapeDtypeStruct((len(parts),) + parts[0].shape, parts[0].dtype),
        compiler_params=params(),
        cost_estimate=cost(),
        name="stack",
    )(*parts, *after)


def token_kernel(*refs):
    refs[-1][...] = jnp.zeros(refs[-1].shape, F32)


def token(after):
    return pl.pallas_call(
        token_kernel,
        in_specs=[pl.BlockSpec(memory_space=pl.ANY)] * len(after),
        out_specs=pl.BlockSpec(memory_space=pltpu.VMEM),
        out_shape=jax.ShapeDtypeStruct((8, 128), F32),
        compiler_params=params(),
        cost_estimate=cost(),
        name="token",
    )(*after)


def forward_kernel(cuts, *refs):
    for source, out, first in zip(refs, refs[-len(cuts) :], cuts):
        out[...] = source[first : first + out.shape[0]]


def forward(parts, cuts, count, after):
    vmem = pl.BlockSpec(memory_space=pltpu.VMEM)
    return pl.pallas_call(
        functools.partial(forward_kernel, cuts),
        in_specs=[vmem] * len(parts) + [pl.BlockSpec(memory_space=pl.ANY)],
        out_specs=[vmem] * len(parts),
        out_shape=[jax.ShapeDtypeStruct((count,) + part.shape[1:], part.dtype) for part in parts],
        compiler_params=params(),
        cost_estimate=cost(),
        name="forward",
    )(*parts, after)


def rank_of(owners, k):
    count = jnp.int32(0)
    for j in range(owners.shape[0]):
        count += jnp.where((owners[j] == owners[k]) & (j < k), 1, 0)
    return count


def collect_kernel(places, *refs):
    for i, (a, row) in enumerate(places):
        refs[-1][i] = refs[a][row]


def collect(bases, places):
    vmem = pl.BlockSpec(memory_space=pltpu.VMEM)
    return pl.pallas_call(
        functools.partial(collect_kernel, places),
        in_specs=[vmem] * len(bases),
        out_specs=vmem,
        out_shape=jax.ShapeDtypeStruct((len(places),) + bases[0].shape[1:], BF16),
        compiler_params=params(),
        cost_estimate=cost(),
        name="collect",
    )(*bases)


def outputs_kernel(jobs, where, capacity, pos, owners, comp_ref, left_ref, strip_ref, base_ref, *refs):
    n_right = 1 + max(a for a, _ in (where or jobs).values())
    rights, refs = refs[:n_right], refs[n_right:]
    n_scratch = 6 if where else 3
    scratch = refs[-n_scratch:]
    feedback, weights, out_sem = scratch[:3]
    refs = refs[:-n_scratch]
    token_ref, outs = refs[-1], refs[-5:-1] if where else refs[-3:-1]
    token_ref[...] = jnp.zeros(token_ref.shape, F32)
    _, upm, n_z, _, cols = rights[0].shape
    half = comp_ref.shape[0] // CORES

    def right_of(place, d, block):
        a, entry = place
        parts = [rights[a][entry, i ^ pos[1], d, :, block] for i in range(upm)]
        return parts[0] if upm == 1 else jnp.concatenate(parts, axis=0)

    def columns(d, first=0, size=cols):
        return pl.ds(pl.multiple_of((pos[4] ^ d) * cols + first, 128), size)

    def matrix(other, j):
        return (j + half * other) ^ pos[0]

    step = 256 if cols % 256 == 0 else 128
    pieces = [slice(first, first + step) for first in range(0, cols, step)]
    stores = []

    def store(source, target, sem):
        stores.append(pltpu.make_async_copy(source, target, sem))
        stores[-1].start()

    if where:
        momentum_ref, master_ref = refs[:2]
        new_momentum, new_master, state_sem = scratch[3:]
        for c in range(capacity):
            mine = jnp.int32(-1)
            for k in range(owners.shape[0]):
                mine = jnp.where((owners[k] == pos[5]) & (rank_of(owners, k) == c), k, mine)
            safe = jnp.maximum(mine, 0)
            strip = strip_ref[safe]
            for d in range(n_z):
                for block in pieces:
                    right = jnp.zeros((strip.shape[1], step), BF16)
                    for job, place in where.items():
                        right = jnp.where(safe == matrix(*job), right_of(place, d, block), right)
                    approx = jnp.dot(strip, right, preferred_element_type=F32)
                    approx = jnp.where(mine >= 0, approx, 0.0)
                    place = columns(d, block.start, step)
                    momentum = 0.9 * momentum_ref[c, :, place] + approx
                    new_momentum[c, :, place] = momentum
                    new_master[c, :, place] = master_ref[c, :, place] - 0.1 * momentum
                place = columns(d)
                for i, new in enumerate((new_momentum, new_master)):
                    store(
                        new.at[c, :, place], outs[2 + i].at[0, c, :, place], state_sem.at[i, c, d]
                    )

    for i, (job, where_right) in enumerate(jobs.items()):
        k = matrix(*job)
        slot = (owners[k] ^ pos[5]) * capacity + rank_of(owners, k)
        left, strip = left_ref[k], strip_ref[k]
        for d in range(n_z):
            for block in pieces:
                right = right_of(where_right, d, block)
                place = columns(d, block.start, step)
                approx = jnp.dot(left, right, preferred_element_type=F32)
                feedback[i, :, place] = (comp_ref[k, :, place].astype(F32) - approx).astype(BF16)
                approx = jnp.dot(strip, right, preferred_element_type=F32)
                base = base_ref[slot, :, place].astype(F32)
                weights[i, :, place] = (base - 0.1 * approx).astype(BF16)
            place = columns(d)
            store(feedback.at[i, :, place], outs[0].at[0, k, :, place], out_sem.at[i, d, 0])
            store(weights.at[i, :, place], outs[1].at[k, :, place], out_sem.at[i, d, 1])

    for copy in stores:
        copy.wait()


def outputs(pos, owners, comp, left, strip, base, capacity, rights, jobs, where=None, states=(), earlier=()):
    nmat, rows, n = comp.shape
    n_z = rights[0].shape[2]
    replica_rows = base.shape[1]
    any_spec = pl.BlockSpec(memory_space=pl.ANY)
    vmem = pl.BlockSpec(memory_space=pltpu.VMEM)
    scratch = [
        pltpu.VMEM((len(jobs), rows, n), BF16),
        pltpu.VMEM((len(jobs), replica_rows, n), BF16),
        pltpu.SemaphoreType.DMA((len(jobs), n_z, 2)),
    ]
    if states:
        scratch += [pltpu.VMEM((capacity, replica_rows, n), F32)] * 2
        scratch += [pltpu.SemaphoreType.DMA((2, capacity, n_z))]
    outs = [
        jax.ShapeDtypeStruct((1, nmat, rows, n), BF16),
        jax.ShapeDtypeStruct((nmat, replica_rows, n), BF16),
    ] + [jax.ShapeDtypeStruct((1,) + x.shape, F32) for x in states]
    first = 6 + len(rights) + len(states)
    return pl.pallas_call(
        functools.partial(outputs_kernel, jobs, where, capacity),
        grid_spec=pltpu.PrefetchScalarGridSpec(
            num_scalar_prefetch=2,
            grid=(1,),
            in_specs=[vmem] * (4 + len(rights) + len(states)) + [any_spec] * len(earlier),
            out_specs=[any_spec] * len(outs) + [vmem],
            scratch_shapes=scratch,
        ),
        out_shape=outs + [jax.ShapeDtypeStruct((8, 128), F32)],
        input_output_aliases={first + i: i for i in range(len(earlier))},
        compiler_params=params(24),
        cost_estimate=cost(),
        name="outputs",
    )(pos, owners, comp, left, strip, base, *rights, *states, *earlier)


def base_kernel(pos, momentum_ref, master_ref, *refs):
    out_ref, momentum, master, sems = refs
    capacity, rows, _ = out_ref.shape
    blocks = [(c, first) for c in range(capacity) for first in range(0, rows, BASE_ROWS)]

    def copies(i):
        c, first = blocks[i]
        part = pl.ds(first, BASE_ROWS)
        return [
            pltpu.make_async_copy(source.at[0, c, part], target.at[c, part], sems.at[j, i])
            for j, (source, target) in enumerate(((momentum_ref, momentum), (master_ref, master)))
        ]

    for i in range(len(blocks)):
        for copy in copies(i):
            copy.start()
    for i, (c, first) in enumerate(blocks):
        for copy in copies(i):
            copy.wait()
        part = slice(first, first + BASE_ROWS)
        out_ref[c, part] = (master[c, part] - 0.09 * momentum[c, part]).astype(BF16)


def base_of(pos, momentum, master):
    _, capacity, rows, n = momentum.shape
    state = jax.ShapeDtypeStruct((capacity, rows, n), F32)
    base, momentum, master = pl.pallas_call(
        base_kernel,
        grid_spec=pltpu.PrefetchScalarGridSpec(
            num_scalar_prefetch=1,
            grid=(1,),
            in_specs=[pl.BlockSpec(memory_space=pl.ANY)] * 2,
            out_specs=[pl.BlockSpec(memory_space=pltpu.VMEM)] * 3,
            scratch_shapes=[pltpu.SemaphoreType.DMA((2, capacity * rows // BASE_ROWS))],
        ),
        out_shape=[jax.ShapeDtypeStruct((capacity, rows, n), BF16), state, state],
        compiler_params=params(),
        cost_estimate=cost(),
        name="base",
    )(pos, momentum, master)
    return base, (momentum, master)


def per_device(
    gradients,
    feedback,
    right_init,
    gram_root,
    owners,
    momentum,
    master_weights,
    vector_grads,
    vector_momentum,
    vector_params,
):
    nmat, rows, n = gradients.shape[1:]
    rank = right_init.shape[2]
    unit = rank * nmat // (CORES * lax.axis_size("mp"))
    n_mp = lax.axis_size("mp")
    n_z = lax.axis_size("replica") // CORES
    capacity, replica_rows = momentum.shape[1:3]
    p = lax.axis_index("mp")
    r = lax.axis_index("replica")
    core, z = r % CORES, r // CORES
    upm = CORES * n_mp // nmat
    half = nmat // CORES
    code = core * n_mp + p
    first = r * replica_rows

    places_of = [code // upm, code % upm, core, r, z, p, first % rows // replica_rows, first // rows ^ p]
    pos = jnp.stack(places_of).astype(jnp.int32)
    in_hbm = lambda x: pltpu.with_memory_space_constraint(x, pltpu.HBM)

    square = n_mp == 4 and capacity == 2
    base, states = base_of(pos, in_hbm(momentum), in_hbm(master_weights))
    early = [exchange(base, "mp", d) for d in range(1, 3 if square else n_mp)]
    bases = [base] + early
    places = {(d, c): (d, c) for d in range(len(bases)) for c in range(capacity)}

    nvec = vector_grads.shape[1]
    comp, near, far = left_terms(
        pos,
        in_hbm(gradients),
        in_hbm(feedback),
        in_hbm(jnp.swapaxes(right_init, 1, 2)),
        vector_grads,
    )
    piece = add([near, exchange(far, "replica", 1)], BF16)
    along_z = lambda x: [exchange(x, "replica", CORES * d) for d in range(1, n_z)]
    piece = add([piece] + along_z(piece), F32)
    near, far = piece, exchange(piece, "replica", 1)

    send, keep, lt, left, vector_rows = right_terms(pos, near, far, gram_root, comp, upm, [])
    vector_total = vector_rows.reshape(-1)[:nvec]
    recv = exchange(send, "replica", 1)
    own, strip, *chip = chip_sum(pos, keep, recv, lt, replica_rows, [token([keep] + early)])
    plane = [exchange(part, "mp", d) for d, part in enumerate(chip, 1)]
    *final, mine = plane_sum(pos, own, strip, plane, n_z, nmat, rank)
    late = []
    if square:
        parts = forward(early, [0, 1], 1, mine)
        late = [exchange(part, "mp", 2 - i) for i, part in enumerate(parts)]
        bases = bases + late
        places[3, 0], places[3, 1] = (3, 0), (4, 0)
    final = [final[0]] + [exchange(final[d], "replica", CORES * d) for d in range(1, n_z)]
    final = add(final, BF16)
    new_vector_momentum = 0.9 * vector_momentum + vector_total
    new_vector_params = vector_params - 0.1 * new_vector_momentum

    whole = stack([final] + along_z(final), late + [new_vector_params])
    others = [exchange(whole, "mp", d) for d in range(1, n_mp)]
    slots = collect(bases, [places[d, c] for d in range(n_mp) for c in range(capacity)])
    common = (pos, owners, comp, left, mine, slots, capacity)
    shape = (half, upm) + whole.shape
    done, near_jobs, after = (), {(0, j): (0, j) for j in range(half)}, [slots]
    if upm == 1:
        *done, after = outputs(*common, [whole[None, None]], {(0, 0): (0, 0)})
        after = [after]
        del near_jobs[0, 0]
    near = stack([whole] + others, after).reshape(shape)
    far = exchange(near, "replica", 1)
    far_jobs = {(1, j): (1, j) for j in range(half)}
    where = {(0, j): (0, j) for j in range(half)} | far_jobs
    *done, _ = outputs(*common, [near], near_jobs, earlier=done)
    new_feedback, new_weights, new_momentum, new_master, _ = outputs(
        *common, [near, far], far_jobs, where, states, done
    )
    return new_feedback, new_momentum, new_master, new_weights, new_vector_momentum, new_vector_params


def solution(mesh):
    return jax.shard_map(
        per_device,
        mesh=mesh,
        in_specs=(
            P("replica", None, "mp", None),
            P("replica", None, "mp", None),
            P(),
            P(),
            P(),
            P("mp", None, "replica", None),
            P("mp", None, "replica", None),
            P("replica", "mp"),
            P("mp"),
            P("mp"),
        ),
        out_specs=(
            P("replica", None, "mp", None),
            P("mp", None, "replica", None),
            P("mp", None, "replica", None),
            P(None, "replica", None),
            P("mp"),
            P("mp"),
        ),
        check_vma=False,
    )
```

```python
import functools

import jax
import jax.numpy as jnp
from jax import lax
from jax.experimental import pallas as pl
from jax.experimental.pallas import tpu as pltpu
from jax.sharding import PartitionSpec as P

CORES = 2
AHEAD = 8
BASE_ROWS = 48
F32 = jnp.float32
BF16 = jnp.bfloat16


def params(mib=12):
    return pltpu.CompilerParams(vmem_limit_bytes=mib * 1024 * 1024)


def cost(flops=1000, bytes_accessed=1000):
    return pl.CostEstimate(flops=flops, bytes_accessed=bytes_accessed, transcendentals=0)


def tree_sum(terms):
    while len(terms) > 1:
        terms = [terms[i] + terms[i + 1] for i in range(0, len(terms), 2)]
    return terms[0]


def exchange(x, axis, distance):
    size = lax.axis_size(axis)
    return lax.ppermute(x, axis, [(i, i ^ distance) for i in range(size)])


def left_kernel(pos, g_ref, f_ref, q_ref, vec_ref, comp_ref, near_ref, far_ref, total, feedback, right, sems):
    nmat, rows, _ = comp_ref.shape
    rank = q_ref.shape[1]
    part = near_ref.shape[1]

    def copies(k):
        return [
            pltpu.make_async_copy(g_ref.at[0, k], comp_ref.at[k], sems.at[k, 0]),
            pltpu.make_async_copy(f_ref.at[0, k], feedback.at[k], sems.at[k, 1]),
            pltpu.make_async_copy(q_ref.at[k], right.at[k], sems.at[k, 2]),
        ]

    for k in range(min(AHEAD, nmat)):
        for copy in copies(k):
            copy.start()
    total[...] = jnp.zeros(total.shape, F32)
    width, nvec = total.shape[1], vec_ref.shape[1]
    for i, first in enumerate(range(0, nvec, width)):
        count = min(width, nvec - first)
        total[rows + i : rows + i + 1, :count] = vec_ref[:, first : first + count]

    for k in range(nmat):
        for copy in copies(k):
            copy.wait()
        if k + AHEAD < nmat:
            for copy in copies(k + AHEAD):
                copy.start()
        comp = comp_ref[k] + feedback[k]
        comp_ref[k] = comp
        total[:rows, k * rank : (k + 1) * rank] = lax.dot_general(
            comp, right[k], (((1,), (1,)), ((), ())), preferred_element_type=F32
        )

    for ref, core in ((near_ref, 1 - pos[2]), (far_ref, pos[2])):
        ref[...] = total[:, pl.ds(pl.multiple_of(core * part, 128), part)]


def left_terms(pos, gradients, feedback, right_t, vec):
    _, nmat, rows, n = gradients.shape
    rank = right_t.shape[1]
    width = nmat * rank
    total = rows + -(-vec.shape[1] // width)
    total += -total % 16
    part = jax.ShapeDtypeStruct((total, width // CORES), F32)
    vmem = pl.BlockSpec(memory_space=pltpu.VMEM)
    any_spec = pl.BlockSpec(memory_space=pl.ANY)
    return pl.pallas_call(
        left_kernel,
        grid_spec=pltpu.PrefetchScalarGridSpec(
            num_scalar_prefetch=1,
            grid=(1,),
            in_specs=[any_spec] * 3 + [vmem],
            out_specs=[vmem] * 3,
            scratch_shapes=[
                pltpu.VMEM((total, width), F32),
                pltpu.VMEM((nmat, rows, n), BF16),
                pltpu.VMEM((nmat, rank, n), BF16),
                pltpu.SemaphoreType.DMA((nmat, 3)),
            ],
        ),
        out_shape=[jax.ShapeDtypeStruct((nmat, rows, n), BF16), part, part],
        compiler_params=params(20),
        cost_estimate=cost(),
        name="left_terms",
    )(pos, gradients, feedback, right_t, vec)


def add_kernel(*refs):
    out = refs[-1]
    out[...] = tree_sum([ref[...].astype(F32) for ref in refs[:-1]]).astype(out.dtype)


def add(parts, dtype):
    vmem = pl.BlockSpec(memory_space=pltpu.VMEM)
    return pl.pallas_call(
        add_kernel,
        in_specs=[vmem] * len(parts),
        out_specs=vmem,
        out_shape=jax.ShapeDtypeStruct(parts[0].shape, dtype),
        compiler_params=params(),
        cost_estimate=cost(),
        name="add",
    )(*parts)


def right_kernel(other, pos, sums_ref, gram_ref, comp_ref, *refs):
    out_ref, hat_ref, left_ref, lt, gram = refs[-5:]
    rows = comp_ref.shape[1]
    half, upm, unit, _ = out_ref.shape
    rank = upm * unit
    core = 1 - pos[2] if other else pos[2]
    gram[...] = jnp.zeros(gram.shape, F32)
    for i in range(half):
        part = slice(i * rank, (i + 1) * rank)
        gram[part, part] = gram_ref[core * half + i]
    hat = jnp.dot(
        sums_ref[:rows, :], gram[...], precision=lax.Precision.HIGHEST, preferred_element_type=F32
    )
    lt[...] = hat.T.astype(BF16)
    hat = hat.astype(BF16)
    hat_ref[...] = hat
    for i in range(half):
        left_ref[i] = hat[:, i * rank : (i + 1) * rank]
    if not other:
        others_ref, vec_ref = refs[0], refs[-6]
        width = sums_ref.shape[1]
        for ref, place in ((sums_ref, core), (others_ref, 1 - core)):
            vec_ref[:, pl.ds(pl.multiple_of(place * width, 128), width)] = ref[rows:, :]
    right_rows(other, range(half // 2 if other else half), pos, lt, comp_ref, out_ref)


def right_rows(other, entries, pos, lt, comp_ref, out_ref):
    half, upm, unit, _ = out_ref.shape
    rank = upm * unit
    for t in entries:
        k = (t + half * other) ^ pos[0]
        part = pl.ds(pl.multiple_of(lax.rem(k, half) * rank, rank), rank)
        terms = jnp.dot(lt[part, :], comp_ref[k], preferred_element_type=F32)
        for i in range(upm):
            out_ref[t, i ^ pos[1]] = terms[i * unit : (i + 1) * unit].astype(out_ref.dtype)


def more_kernel(pos, lt_ref, comp_ref, *refs):
    out_ref = refs[-1]
    half = out_ref.shape[0]
    right_rows(1, range(half // 2, half), pos, lt_ref, comp_ref, out_ref)


def right_more(pos, lt, comp, send, after):
    vmem = pl.BlockSpec(memory_space=pltpu.VMEM)
    return pl.pallas_call(
        more_kernel,
        grid_spec=pltpu.PrefetchScalarGridSpec(
            num_scalar_prefetch=1,
            grid=(1,),
            in_specs=[vmem] * 3 + [pl.BlockSpec(memory_space=pl.ANY)] * len(after),
            out_specs=vmem,
        ),
        out_shape=jax.ShapeDtypeStruct(send.shape, send.dtype),
        input_output_aliases={3: 0},
        compiler_params=params(),
        cost_estimate=cost(),
        name="right_more",
    )(pos, lt, comp, send, *after)


def right_terms(pos, sums, gram, comp, upm, others=None, after=()):
    nmat, rows, n = comp.shape
    rank = gram.shape[1]
    total, width = sums.shape
    half = nmat // CORES
    vmem = pl.BlockSpec(memory_space=pltpu.VMEM)
    own = others is not None
    outs = [
        jax.ShapeDtypeStruct((half, upm, rank // upm, n), F32 if own else BF16),
        jax.ShapeDtypeStruct((rows, width), BF16),
        jax.ShapeDtypeStruct((half, rows, rank), BF16),
        jax.ShapeDtypeStruct((width, rows), BF16),
    ]
    if own:
        outs = [jax.ShapeDtypeStruct((total - rows, CORES * width), F32)] + outs
    return pl.pallas_call(
        functools.partial(right_kernel, 0 if own else 1),
        grid_spec=pltpu.PrefetchScalarGridSpec(
            num_scalar_prefetch=1,
            grid=(1,),
            in_specs=[vmem] * (4 if own else 3) + [pl.BlockSpec(memory_space=pl.ANY)] * len(after),
            out_specs=[vmem] * len(outs),
            scratch_shapes=[pltpu.VMEM((width, width), F32)],
        ),
        out_shape=outs,
        compiler_params=params(),
        cost_estimate=cost(),
        name="right_keep" if own else "right_send",
    )(pos, sums, gram, comp, *([others] if own else []), *after)


def chip_kernel(replica_rows, pos, keep_ref, recv_ref, far_ref, near_ref, *refs):
    upm = keep_ref.shape[1]
    own_ref, strip_ref, *sends = refs[-(keep_ref.shape[0] * upm + 1) :]
    height = strip_ref.shape[0]
    part = pl.ds(pl.multiple_of(pos[6] * replica_rows, 16), replica_rows)
    strip = jnp.concatenate([ref[part, :].astype(F32) for ref in (far_ref, near_ref)], axis=1)
    strip = jnp.concatenate(
        [strip[i * height : (i + 1) * height] for i in range(replica_rows // height)], axis=1
    )
    strip_ref[...] = strip
    own_ref[...] = keep_ref[0, 0] + recv_ref[0, 0].astype(F32)
    for d, out in enumerate(sends, 1):
        j, i = d // upm, d % upm
        terms = keep_ref[j, i] + recv_ref[j, i].astype(F32)
        out[...] = jnp.concatenate([terms, strip], axis=0).astype(BF16)


def chip_sum(pos, keep, recv, hats, replica_rows):
    half, upm, unit, n = keep.shape
    height = CORES * hats[0].shape[1] * replica_rows // n
    vmem = pl.BlockSpec(memory_space=pltpu.VMEM)
    outs = [jax.ShapeDtypeStruct((unit, n), F32), jax.ShapeDtypeStruct((height, n), F32)]
    outs += [jax.ShapeDtypeStruct((unit + height, n), BF16)] * (half * upm - 1)
    return pl.pallas_call(
        functools.partial(chip_kernel, replica_rows),
        grid_spec=pltpu.PrefetchScalarGridSpec(
            num_scalar_prefetch=1,
            grid=(1,),
            in_specs=[vmem] * 4,
            out_specs=[vmem] * len(outs),
        ),
        out_shape=outs,
        compiler_params=params(),
        cost_estimate=cost(),
        name="chip_sum",
    )(pos, keep, recv, *hats)


def plane_kernel(pos, own_ref, strip_ref, *refs):
    n_z = own_ref.shape[1] // refs[-2].shape[1]
    terms, outs, left_ref = refs[: -n_z - 1], refs[-n_z - 1 : -1], refs[-1]
    unit, n = own_ref.shape
    cols = n // n_z
    for d, out in enumerate(outs):
        block = pl.ds(pl.multiple_of((pos[4] ^ d) * cols, cols), cols)
        parts = [own_ref[:, block]] + [term[:, block].astype(F32)[:unit] for term in terms]
        out[...] = tree_sum(parts).astype(out.dtype)
    strip = strip_ref[...]
    for d, term in enumerate(terms, 1):
        strip = jnp.where(pos[7] == d, term[...].astype(F32)[unit:], strip)
    nmat, _, rank = left_ref.shape
    width = nmat * rank
    rows = [strip[:, i * width : (i + 1) * width] for i in range(n // width)]
    rows = jnp.concatenate(rows, axis=0).astype(BF16)
    for i in range(nmat):
        left_ref[i] = rows[:, i * rank : (i + 1) * rank]


def plane_sum(pos, own, strip, terms, n_z, nmat, rank):
    unit, n = own.shape
    count = strip.size // (nmat * rank)
    outs = [jax.ShapeDtypeStruct((unit, n // n_z), BF16 if d else F32) for d in range(n_z)]
    outs.append(jax.ShapeDtypeStruct((nmat, count, rank), BF16))
    vmem = pl.BlockSpec(memory_space=pltpu.VMEM)
    return pl.pallas_call(
        plane_kernel,
        grid_spec=pltpu.PrefetchScalarGridSpec(
            num_scalar_prefetch=1,
            grid=(1,),
            in_specs=[vmem] * (2 + len(terms)),
            out_specs=[vmem] * len(outs),
        ),
        out_shape=outs,
        compiler_params=params(),
        cost_estimate=cost(),
        name="plane_sum",
    )(pos, own, strip, *terms)


def stack_kernel(count, *refs):
    for i in range(count):
        refs[-1][i] = refs[i][...]


def stack(parts, after=()):
    vmem = pl.BlockSpec(memory_space=pltpu.VMEM)
    return pl.pallas_call(
        functools.partial(stack_kernel, len(parts)),
        in_specs=[vmem] * len(parts) + [pl.BlockSpec(memory_space=pl.ANY)] * len(after),
        out_specs=vmem,
        out_shape=jax.ShapeDtypeStruct((len(parts),) + parts[0].shape, parts[0].dtype),
        compiler_params=params(),
        cost_estimate=cost(),
        name="stack",
    )(*parts, *after)


def forward_kernel(later, x_ref, y_ref, base_ref, after_ref, *outs):
    rows = base_ref.shape[1]
    for source, slot, out in ((y_ref, 1, outs[0]), (x_ref, 0, outs[1])):
        out[:rows] = source[:rows]
        out[rows:] = base_ref[slot, rows - later :]


def forward(x, y, base, after):
    _, rows, n = base.shape
    later = 2 * rows - x.shape[0]
    vmem = pl.BlockSpec(memory_space=pltpu.VMEM)
    return pl.pallas_call(
        functools.partial(forward_kernel, later),
        in_specs=[vmem] * 3 + [pl.BlockSpec(memory_space=pl.ANY)],
        out_specs=[vmem] * 2,
        out_shape=[jax.ShapeDtypeStruct((rows + later, n), BF16)] * 2,
        compiler_params=params(),
        cost_estimate=cost(),
        name="forward",
    )(x, y, base, after)


def rank_of(owners, k):
    count = jnp.int32(0)
    for j in range(owners.shape[0]):
        count += jnp.where((owners[j] == owners[k]) & (j < k), 1, 0)
    return count


def collect_kernel(square, base_ref, *refs):
    out = refs[-1]
    capacity, rows, _ = base_ref.shape
    out[:capacity] = base_ref[...]
    if not square:
        for d, ref in enumerate(refs[:-1], 1):
            out[d * capacity : (d + 1) * capacity] = ref[...]
        return
    x, y, more_x, more_y = refs[:-1]
    early = x.shape[0] - rows
    for d, slot, first, second in ((1, 0, x, more_x), (2, 1, y, more_y)):
        out[d * capacity + slot] = first[:rows]
        out[d * capacity + 1 - slot, :early] = first[rows:]
        out[d * capacity + 1 - slot, early:] = second[rows:]
    out[3 * capacity] = more_y[:rows]
    out[3 * capacity + 1] = more_x[:rows]


def collect(square, n_mp, base, parts):
    capacity, rows, n = base.shape
    vmem = pl.BlockSpec(memory_space=pltpu.VMEM)
    return pl.pallas_call(
        functools.partial(collect_kernel, square),
        in_specs=[vmem] * (1 + len(parts)),
        out_specs=vmem,
        out_shape=jax.ShapeDtypeStruct((n_mp * capacity, rows, n), BF16),
        compiler_params=params(),
        cost_estimate=cost(),
        name="collect",
    )(base, *parts)


def outputs_kernel(jobs, where, capacity, pos, owners, comp_ref, near_ref, far_ref, strip_ref, base_ref, *refs):
    n_right = 1 + max(a for a, _ in (where or jobs).values())
    rights, refs = refs[:n_right], refs[n_right:]
    n_scratch = 6 if where else 3
    scratch = refs[-n_scratch:]
    feedback, weights, out_sem = scratch[:3]
    refs = refs[:-n_scratch]
    token_ref, outs = refs[-1], refs[-5:-1] if where else refs[-3:-1]
    token_ref[...] = jnp.zeros(token_ref.shape, F32)
    _, upm, n_z, _, cols = rights[0].shape
    half = near_ref.shape[0]
    turn = (1 - pos[2]) * half

    def right_of(place, d, block):
        a, entry = place
        parts = [rights[a][entry, i ^ pos[1], d, :, block] for i in range(upm)]
        return parts[0] if upm == 1 else jnp.concatenate(parts, axis=0)

    def columns(d, first=0, size=cols):
        return pl.ds(pl.multiple_of((pos[4] ^ d) * cols + first, 128), size)

    def matrix(other, j):
        return (j + half * other) ^ pos[0]

    step = 256 if cols % 256 == 0 else 128
    pieces = [slice(first, first + step) for first in range(0, cols, step)]
    stores = []

    def store(source, target, sem):
        stores.append(pltpu.make_async_copy(source, target, sem))
        stores[-1].start()

    if where:
        momentum_ref, master_ref = refs[:2]
        new_momentum, new_master, state_sem = scratch[3:]
        for c in range(capacity):
            mine = jnp.int32(-1)
            for k in range(owners.shape[0]):
                mine = jnp.where((owners[k] == pos[5]) & (rank_of(owners, k) == c), k, mine)
            safe = jnp.maximum(mine, 0)
            strip = strip_ref[safe ^ turn]
            for d in range(n_z):
                for block in pieces:
                    right = jnp.zeros((strip.shape[1], step), BF16)
                    for job, place in where.items():
                        right = jnp.where(safe == matrix(*job), right_of(place, d, block), right)
                    approx = jnp.dot(strip, right, preferred_element_type=F32)
                    approx = jnp.where(mine >= 0, approx, 0.0)
                    place = columns(d, block.start, step)
                    momentum = 0.9 * momentum_ref[c, :, place] + approx
                    new_momentum[c, :, place] = momentum
                    new_master[c, :, place] = master_ref[c, :, place] - 0.1 * momentum
                place = columns(d)
                for i, new in enumerate((new_momentum, new_master)):
                    store(
                        new.at[c, :, place], outs[2 + i].at[0, c, :, place], state_sem.at[i, c, d]
                    )

    for i, (job, where_right) in enumerate(jobs.items()):
        k = matrix(*job)
        slot = (owners[k] ^ pos[5]) * capacity + rank_of(owners, k)
        left = (far_ref if job[0] else near_ref)[lax.rem(k, half)]
        strip = strip_ref[k ^ turn]
        for d in range(n_z):
            for block in pieces:
                right = right_of(where_right, d, block)
                place = columns(d, block.start, step)
                approx = jnp.dot(left, right, preferred_element_type=F32)
                feedback[i, :, place] = (comp_ref[k, :, place].astype(F32) - approx).astype(BF16)
                approx = jnp.dot(strip, right, preferred_element_type=F32)
                base = base_ref[slot, :, place].astype(F32)
                weights[i, :, place] = (base - 0.1 * approx).astype(BF16)
            place = columns(d)
            store(feedback.at[i, :, place], outs[0].at[0, k, :, place], out_sem.at[i, d, 0])
            store(weights.at[i, :, place], outs[1].at[k, :, place], out_sem.at[i, d, 1])

    for copy in stores:
        copy.wait()


def outputs(pos, owners, comp, near, far, strip, base, capacity, rights, jobs, where=None, states=(), earlier=()):
    nmat, rows, n = comp.shape
    n_z = rights[0].shape[2]
    replica_rows = base.shape[1]
    any_spec = pl.BlockSpec(memory_space=pl.ANY)
    vmem = pl.BlockSpec(memory_space=pltpu.VMEM)
    scratch = [
        pltpu.VMEM((len(jobs), rows, n), BF16),
        pltpu.VMEM((len(jobs), replica_rows, n), BF16),
        pltpu.SemaphoreType.DMA((len(jobs), n_z, 2)),
    ]
    if states:
        scratch += [pltpu.VMEM((capacity, replica_rows, n), F32)] * 2
        scratch += [pltpu.SemaphoreType.DMA((2, capacity, n_z))]
    outs = [
        jax.ShapeDtypeStruct((1, nmat, rows, n), BF16),
        jax.ShapeDtypeStruct((nmat, replica_rows, n), BF16),
    ] + [jax.ShapeDtypeStruct((1,) + x.shape, F32) for x in states]
    first = 7 + len(rights) + len(states)
    return pl.pallas_call(
        functools.partial(outputs_kernel, jobs, where, capacity),
        grid_spec=pltpu.PrefetchScalarGridSpec(
            num_scalar_prefetch=2,
            grid=(1,),
            in_specs=[vmem] * (5 + len(rights) + len(states)) + [any_spec] * len(earlier),
            out_specs=[any_spec] * len(outs) + [vmem],
            scratch_shapes=scratch,
        ),
        out_shape=outs + [jax.ShapeDtypeStruct((8, 128), F32)],
        input_output_aliases={first + i: i for i in range(len(earlier))},
        compiler_params=params(24),
        cost_estimate=cost(),
        name="outputs",
    )(pos, owners, comp, near, far, strip, base, *rights, *states, *earlier)


def base_kernel(pos, momentum_ref, master_ref, out_ref, momentum, master, *refs):
    firsts, sems = refs[:-1], refs[-1]
    capacity, rows, _ = out_ref.shape
    blocks = [(c, first) for c in range(capacity) for first in range(0, rows, BASE_ROWS)]

    def copies(i):
        c, first = blocks[i]
        part = pl.ds(first, BASE_ROWS)
        return [
            pltpu.make_async_copy(source.at[0, c, part], target.at[c, part], sems.at[j, i])
            for j, (source, target) in enumerate(((momentum_ref, momentum), (master_ref, master)))
        ]

    for i in range(len(blocks)):
        for copy in copies(i):
            copy.start()
    for i, (c, first) in enumerate(blocks):
        for copy in copies(i):
            copy.wait()
        part = slice(first, first + BASE_ROWS)
        out_ref[c, part] = (master[c, part] - 0.09 * momentum[c, part]).astype(BF16)
    for slot, ref in enumerate(firsts):
        ref[:rows] = out_ref[slot]
        ref[rows:] = out_ref[1 - slot, : ref.shape[0] - rows]


def base_of(pos, momentum, master, square):
    _, capacity, rows, n = momentum.shape
    state = jax.ShapeDtypeStruct((capacity, rows, n), F32)
    base = jax.ShapeDtypeStruct((capacity, rows, n), BF16)
    firsts = [jax.ShapeDtypeStruct((rows + 2 * rows // 3, n), BF16)] * (2 if square else 0)
    base, momentum, master, *firsts = pl.pallas_call(
        base_kernel,
        grid_spec=pltpu.PrefetchScalarGridSpec(
            num_scalar_prefetch=1,
            grid=(1,),
            in_specs=[pl.BlockSpec(memory_space=pl.ANY)] * 2,
            out_specs=[pl.BlockSpec(memory_space=pltpu.VMEM)] * (3 + len(firsts)),
            scratch_shapes=[pltpu.SemaphoreType.DMA((2, capacity * rows // BASE_ROWS))],
        ),
        out_shape=[base, state, state] + firsts,
        compiler_params=params(),
        cost_estimate=cost(),
        name="base",
    )(pos, momentum, master)
    return base, (momentum, master), firsts


def per_device(
    gradients,
    feedback,
    right_init,
    gram_root,
    owners,
    momentum,
    master_weights,
    vector_grads,
    vector_momentum,
    vector_params,
):
    nmat, rows, n = gradients.shape[1:]
    rank = right_init.shape[2]
    unit = rank * nmat // (CORES * lax.axis_size("mp"))
    n_mp = lax.axis_size("mp")
    n_z = lax.axis_size("replica") // CORES
    capacity, replica_rows = momentum.shape[1:3]
    p = lax.axis_index("mp")
    r = lax.axis_index("replica")
    core, z = r % CORES, r // CORES
    upm = CORES * n_mp // nmat
    half = nmat // CORES
    code = core * n_mp + p
    first = r * replica_rows

    places_of = [code // upm, code % upm, core, r, z, p, first % rows // replica_rows, first // rows ^ p]
    pos = jnp.stack(places_of).astype(jnp.int32)
    in_hbm = lambda x: pltpu.with_memory_space_constraint(x, pltpu.HBM)

    square = n_mp == 4 and capacity == 2 and replica_rows % 48 == 0
    base, states, firsts = base_of(pos, in_hbm(momentum), in_hbm(master_weights), square)
    firsts = firsts or [base] * (n_mp - 1)
    early = [exchange(part, "mp", d) for d, part in enumerate(firsts, 1)]

    nvec = vector_grads.shape[1]
    comp, near, far = left_terms(
        pos,
        in_hbm(gradients),
        in_hbm(feedback),
        in_hbm(jnp.swapaxes(right_init, 1, 2)),
        vector_grads,
    )
    piece = add([near, exchange(far, "replica", 1)], BF16)
    along_z = lambda x: [exchange(x, "replica", CORES * d) for d in range(1, n_z)]
    piece = add([piece] + along_z(piece), F32)

    mine = exchange(piece, "replica", 1)
    send, far_hat, far_left, lt = right_terms(pos, piece, gram_root, comp, upm)
    recv = exchange(right_more(pos, lt, comp, send, [mine] + early), "replica", 1)
    vector_rows, keep, near_hat, near_left, _ = right_terms(
        pos, mine, gram_root, comp, upm, piece
    )
    vector_total = vector_rows.reshape(-1)[:nvec]
    own, strip, *chip = chip_sum(pos, keep, recv, [far_hat, near_hat], replica_rows)
    plane = [exchange(part, "mp", d) for d, part in enumerate(chip, 1)]
    *final, strips = plane_sum(pos, own, strip, plane, n_z, nmat, rank)
    late = []
    if square:
        late = [exchange(part, "mp", d) for d, part in enumerate(forward(*early, base, strips), 1)]
    final = [final[0]] + [exchange(final[d], "replica", CORES * d) for d in range(1, n_z)]
    final = add(final, BF16)
    new_vector_momentum = 0.9 * vector_momentum + vector_total
    new_vector_params = vector_params - 0.1 * new_vector_momentum

    whole = stack([final] + along_z(final), [new_vector_params])
    others = [exchange(whole, "mp", d) for d in range(1, n_mp)]
    slots = collect(square, n_mp, base, early + late)
    common = (pos, owners, comp, near_left, far_left, strips, slots, capacity)
    shape = (half, upm) + whole.shape
    done, near_jobs, after = (), {(0, j): (0, j) for j in range(half)}, [slots]
    if upm == 1:
        *done, after = outputs(*common, [whole[None, None]], {(0, 0): (0, 0)})
        after = [after]
        del near_jobs[0, 0]
    near = stack([whole] + others, after).reshape(shape)
    far = exchange(near, "replica", 1)
    far_jobs = {(1, j): (1, j) for j in range(half)}
    where = {(0, j): (0, j) for j in range(half)} | far_jobs
    *done, _ = outputs(*common, [near], near_jobs, earlier=done)
    new_feedback, new_weights, new_momentum, new_master, _ = outputs(
        *common, [near, far], far_jobs, where, states, done
    )
    return new_feedback, new_momentum, new_master, new_weights, new_vector_momentum, new_vector_params


def solution(mesh):
    return jax.shard_map(
        per_device,
        mesh=mesh,
        in_specs=(
            P("replica", None, "mp", None),
            P("replica", None, "mp", None),
            P(),
            P(),
            P(),
            P("mp", None, "replica", None),
            P("mp", None, "replica", None),
            P("replica", "mp"),
            P("mp"),
            P("mp"),
        ),
        out_specs=(
            P("replica", None, "mp", None),
            P("mp", None, "replica", None),
            P("mp", None, "replica", None),
            P(None, "replica", None),
            P("mp"),
            P("mp"),
        ),
        check_vma=False,
    )
```

```python
import functools

import jax
import jax.numpy as jnp
from jax import lax
from jax.experimental import pallas as pl
from jax.experimental.pallas import tpu as pltpu
from jax.sharding import PartitionSpec as P

CORES = 2
AHEAD = 8
BASE_ROWS = 48
F32 = jnp.float32
BF16 = jnp.bfloat16


def params(mib=12):
    return pltpu.CompilerParams(vmem_limit_bytes=mib * 1024 * 1024)


def cost(flops=1000, bytes_accessed=1000):
    return pl.CostEstimate(flops=flops, bytes_accessed=bytes_accessed, transcendentals=0)


def tree_sum(terms):
    while len(terms) > 1:
        terms = [terms[i] + terms[i + 1] for i in range(0, len(terms), 2)]
    return terms[0]


def exchange(x, axis, distance):
    size = lax.axis_size(axis)
    return lax.ppermute(x, axis, [(i, i ^ distance) for i in range(size)])


def left_kernel(pos, g_ref, f_ref, q_ref, vec_ref, comp_ref, near_ref, far_ref, total, feedback, right, sems):
    nmat, rows, _ = comp_ref.shape
    rank = q_ref.shape[1]
    part = near_ref.shape[0]

    def copies(k):
        return [
            pltpu.make_async_copy(g_ref.at[0, k], comp_ref.at[k], sems.at[k, 0]),
            pltpu.make_async_copy(f_ref.at[0, k], feedback.at[k], sems.at[k, 1]),
            pltpu.make_async_copy(q_ref.at[k], right.at[k], sems.at[k, 2]),
        ]

    for k in range(min(AHEAD, nmat)):
        for copy in copies(k):
            copy.start()
    total[...] = jnp.zeros(total.shape, F32)
    width, nvec = total.shape[1], vec_ref.shape[1]
    for i, first in enumerate(range(0, nvec, width)):
        count = min(width, nvec - first)
        total[rows + i : rows + i + 1, :count] = vec_ref[:, first : first + count]

    for k in range(nmat):
        for copy in copies(k):
            copy.wait()
        if k + AHEAD < nmat:
            for copy in copies(k + AHEAD):
                copy.start()
        comp = comp_ref[k] + feedback[k]
        comp_ref[k] = comp
        total[:rows, k * rank : (k + 1) * rank] = lax.dot_general(
            comp, right[k], (((1,), (1,)), ((), ())), preferred_element_type=F32
        )

    for ref, core in ((near_ref, pos[2]), (far_ref, 1 - pos[2])):
        ref[...] = total[pl.ds(pl.multiple_of(core * part, 16), part), :]


def left_terms(pos, gradients, feedback, right_t, vec):
    _, nmat, rows, n = gradients.shape
    rank = right_t.shape[1]
    width = nmat * rank
    total = rows + -(-vec.shape[1] // width)
    total += -total % (16 * CORES)
    part = jax.ShapeDtypeStruct((total // CORES, width), F32)
    vmem = pl.BlockSpec(memory_space=pltpu.VMEM)
    any_spec = pl.BlockSpec(memory_space=pl.ANY)
    return pl.pallas_call(
        left_kernel,
        grid_spec=pltpu.PrefetchScalarGridSpec(
            num_scalar_prefetch=1,
            grid=(1,),
            in_specs=[any_spec] * 3 + [vmem],
            out_specs=[vmem] * 3,
            scratch_shapes=[
                pltpu.VMEM((total, width), F32),
                pltpu.VMEM((nmat, rows, n), BF16),
                pltpu.VMEM((nmat, rank, n), BF16),
                pltpu.SemaphoreType.DMA((nmat, 3)),
            ],
        ),
        out_shape=[jax.ShapeDtypeStruct((nmat, rows, n), BF16), part, part],
        compiler_params=params(20),
        cost_estimate=cost(),
        name="left_terms",
    )(pos, gradients, feedback, right_t, vec)


def add_kernel(*refs):
    out = refs[-1]
    out[...] = tree_sum([ref[...].astype(F32) for ref in refs[:-1]]).astype(out.dtype)


def add(parts, dtype):
    vmem = pl.BlockSpec(memory_space=pltpu.VMEM)
    return pl.pallas_call(
        add_kernel,
        in_specs=[vmem] * len(parts),
        out_specs=vmem,
        out_shape=jax.ShapeDtypeStruct(parts[0].shape, dtype),
        compiler_params=params(),
        cost_estimate=cost(),
        name="add",
    )(*parts)


def send_kernel(half, pos, near_ref, far_ref, gram_ref, comp_ref, send_ref, lt_ref, left_ref, vec_ref, left, gram):
    nmat, rows, _ = comp_ref.shape
    rank = gram_ref.shape[1]
    part = near_ref.shape[0]
    for ref, core in ((near_ref, pos[2]), (far_ref, 1 - pos[2])):
        left[pl.ds(pl.multiple_of(core * part, 16), part), :] = ref[...]
    vec_ref[...] = left[rows:, :]
    gram[...] = jnp.zeros(gram.shape, F32)
    for i in range(nmat):
        gram[i * rank : (i + 1) * rank, i * rank : (i + 1) * rank] = gram_ref[i]
    hat = jnp.dot(
        left[:rows, :], gram[...], precision=lax.Precision.HIGHEST, preferred_element_type=F32
    )
    lt_ref[...] = hat.T.astype(BF16)
    for i in range(nmat):
        left_ref[i] = hat[:, i * rank : (i + 1) * rank].astype(BF16)
    right_rows(half, pos, lt_ref, comp_ref, send_ref)


def right_rows(start, pos, lt_ref, comp_ref, out_ref):
    half, upm, unit, _ = out_ref.shape
    for t in range(half):
        k = (t + start) ^ pos[0]
        rows = pl.ds(pl.multiple_of(k * upm * unit, upm * unit), upm * unit)
        terms = jnp.dot(lt_ref[rows, :], comp_ref[k], preferred_element_type=F32)
        for i in range(upm):
            out_ref[t, i ^ pos[1]] = terms[i * unit : (i + 1) * unit].astype(out_ref.dtype)


def keep_kernel(pos, lt_ref, comp_ref, *refs):
    right_rows(0, pos, lt_ref, comp_ref, refs[-1])


def right_terms(pos, near, far, gram, comp, upm, after):
    nmat, rows, n = comp.shape
    rank = gram.shape[1]
    width = nmat * rank
    half = nmat // CORES
    total = CORES * near.shape[0]
    shape = (half, upm, rank // upm, n)
    vmem = pl.BlockSpec(memory_space=pltpu.VMEM)
    send, lt, left, vec = pl.pallas_call(
        functools.partial(send_kernel, half),
        grid_spec=pltpu.PrefetchScalarGridSpec(
            num_scalar_prefetch=1,
            grid=(1,),
            in_specs=[vmem] * 4,
            out_specs=[vmem] * 4,
            scratch_shapes=[pltpu.VMEM((total, width), F32), pltpu.VMEM((width, width), F32)],
        ),
        out_shape=[
            jax.ShapeDtypeStruct(shape, BF16),
            jax.ShapeDtypeStruct((width, rows), BF16),
            jax.ShapeDtypeStruct((nmat, rows, rank), BF16),
            jax.ShapeDtypeStruct((total - rows, width), F32),
        ],
        compiler_params=params(),
        cost_estimate=cost(),
        name="right_send",
    )(pos, near, far, gram, comp)
    keep = pl.pallas_call(
        keep_kernel,
        grid_spec=pltpu.PrefetchScalarGridSpec(
            num_scalar_prefetch=1,
            grid=(1,),
            in_specs=[vmem, vmem] + [pl.BlockSpec(memory_space=pl.ANY)] * len(after),
            out_specs=vmem,
        ),
        out_shape=jax.ShapeDtypeStruct(shape, F32),
        compiler_params=params(),
        cost_estimate=cost(),
        name="right_keep",
    )(pos, lt, comp, *after)
    return send, keep, lt, left, vec


def chip_kernel(replica_rows, pos, keep_ref, recv_ref, lt_ref, *refs):
    upm = keep_ref.shape[1]
    own_ref, strip_ref, *sends = refs[-(keep_ref.shape[0] * upm + 1) :]
    left = lt_ref[...].astype(F32).T
    strip = left[:replica_rows]
    for i in range(1, left.shape[0] // replica_rows):
        strip = jnp.where(pos[6] == i, left[i * replica_rows : (i + 1) * replica_rows], strip)
    height = strip_ref.shape[0]
    strip = jnp.concatenate(
        [strip[i * height : (i + 1) * height] for i in range(replica_rows // height)], axis=1
    )
    strip_ref[...] = strip
    own_ref[...] = keep_ref[0, 0] + recv_ref[0, 0].astype(F32)
    for d, out in enumerate(sends, 1):
        j, i = d // upm, d % upm
        terms = keep_ref[j, i] + recv_ref[j, i].astype(F32)
        out[...] = jnp.concatenate([terms, strip], axis=0).astype(BF16)


def chip_sum(pos, keep, recv, lt, replica_rows, after):
    half, upm, unit, n = keep.shape
    height = lt.shape[0] * replica_rows // n
    vmem = pl.BlockSpec(memory_space=pltpu.VMEM)
    outs = [jax.ShapeDtypeStruct((unit, n), F32), jax.ShapeDtypeStruct((height, n), F32)]
    outs += [jax.ShapeDtypeStruct((unit + height, n), BF16)] * (half * upm - 1)
    return pl.pallas_call(
        functools.partial(chip_kernel, replica_rows),
        grid_spec=pltpu.PrefetchScalarGridSpec(
            num_scalar_prefetch=1,
            grid=(1,),
            in_specs=[vmem] * 3 + [pl.BlockSpec(memory_space=pl.ANY)] * len(after),
            out_specs=[vmem] * len(outs),
        ),
        out_shape=outs,
        compiler_params=params(),
        cost_estimate=cost(),
        name="chip_sum",
    )(pos, keep, recv, lt, *after)


def plane_kernel(pos, own_ref, strip_ref, *refs):
    n_z = own_ref.shape[1] // refs[-2].shape[1]
    terms, outs, left_ref = refs[: -n_z - 1], refs[-n_z - 1 : -1], refs[-1]
    unit, n = own_ref.shape
    cols = n // n_z
    for d, out in enumerate(outs):
        block = pl.ds(pl.multiple_of((pos[4] ^ d) * cols, cols), cols)
        parts = [own_ref[:, block]] + [term[:, block].astype(F32)[:unit] for term in terms]
        out[...] = tree_sum(parts).astype(out.dtype)
    strip = strip_ref[...]
    for d, term in enumerate(terms, 1):
        strip = jnp.where(pos[7] == d, term[...].astype(F32)[unit:], strip)
    nmat, _, rank = left_ref.shape
    width = nmat * rank
    rows = [strip[:, i * width : (i + 1) * width] for i in range(n // width)]
    rows = jnp.concatenate(rows, axis=0).astype(BF16)
    for i in range(nmat):
        left_ref[i] = rows[:, i * rank : (i + 1) * rank]


def plane_sum(pos, own, strip, terms, n_z, nmat, rank):
    unit, n = own.shape
    count = strip.size // (nmat * rank)
    outs = [jax.ShapeDtypeStruct((unit, n // n_z), BF16 if d else F32) for d in range(n_z)]
    outs.append(jax.ShapeDtypeStruct((nmat, count, rank), BF16))
    vmem = pl.BlockSpec(memory_space=pltpu.VMEM)
    return pl.pallas_call(
        plane_kernel,
        grid_spec=pltpu.PrefetchScalarGridSpec(
            num_scalar_prefetch=1,
            grid=(1,),
            in_specs=[vmem] * (2 + len(terms)),
            out_specs=[vmem] * len(outs),
        ),
        out_shape=outs,
        compiler_params=params(),
        cost_estimate=cost(),
        name="plane_sum",
    )(pos, own, strip, *terms)


def stack_kernel(count, *refs):
    for i in range(count):
        refs[-1][i] = refs[i][...]


def stack(parts, after=()):
    vmem = pl.BlockSpec(memory_space=pltpu.VMEM)
    return pl.pallas_call(
        functools.partial(stack_kernel, len(parts)),
        in_specs=[vmem] * len(parts) + [pl.BlockSpec(memory_space=pl.ANY)] * len(after),
        out_specs=vmem,
        out_shape=jax.ShapeDtypeStruct((len(parts),) + parts[0].shape, parts[0].dtype),
        compiler_params=params(),
        cost_estimate=cost(),
        name="stack",
    )(*parts, *after)


def token_kernel(*refs):
    refs[-1][...] = jnp.zeros(refs[-1].shape, F32)


def token(after):
    return pl.pallas_call(
        token_kernel,
        in_specs=[pl.BlockSpec(memory_space=pl.ANY)] * len(after),
        out_specs=pl.BlockSpec(memory_space=pltpu.VMEM),
        out_shape=jax.ShapeDtypeStruct((8, 128), F32),
        compiler_params=params(),
        cost_estimate=cost(),
        name="token",
    )(*after)


def forward_kernel(later, x_ref, y_ref, base_ref, after_ref, *outs):
    rows = base_ref.shape[1]
    for source, slot, out in ((y_ref, 1, outs[0]), (x_ref, 0, outs[1])):
        out[:rows] = source[:rows]
        out[rows:] = base_ref[slot, rows - later :]


def forward(x, y, base, after):
    _, rows, n = base.shape
    later = 2 * rows - x.shape[0]
    vmem = pl.BlockSpec(memory_space=pltpu.VMEM)
    return pl.pallas_call(
        functools.partial(forward_kernel, later),
        in_specs=[vmem] * 3 + [pl.BlockSpec(memory_space=pl.ANY)],
        out_specs=[vmem] * 2,
        out_shape=[jax.ShapeDtypeStruct((rows + later, n), BF16)] * 2,
        compiler_params=params(),
        cost_estimate=cost(),
        name="forward",
    )(x, y, base, after)


def rank_of(owners, k):
    count = jnp.int32(0)
    for j in range(owners.shape[0]):
        count += jnp.where((owners[j] == owners[k]) & (j < k), 1, 0)
    return count


def collect_kernel(square, base_ref, *refs):
    out = refs[-1]
    capacity, rows, _ = base_ref.shape
    out[:capacity] = base_ref[...]
    if not square:
        for d, ref in enumerate(refs[:-1], 1):
            out[d * capacity : (d + 1) * capacity] = ref[...]
        return
    x, y, more_x, more_y = refs[:-1]
    early = x.shape[0] - rows
    for d, slot, first, second in ((1, 0, x, more_x), (2, 1, y, more_y)):
        out[d * capacity + slot] = first[:rows]
        out[d * capacity + 1 - slot, :early] = first[rows:]
        out[d * capacity + 1 - slot, early:] = second[rows:]
    out[3 * capacity] = more_y[:rows]
    out[3 * capacity + 1] = more_x[:rows]


def collect(square, n_mp, base, parts):
    capacity, rows, n = base.shape
    vmem = pl.BlockSpec(memory_space=pltpu.VMEM)
    return pl.pallas_call(
        functools.partial(collect_kernel, square),
        in_specs=[vmem] * (1 + len(parts)),
        out_specs=vmem,
        out_shape=jax.ShapeDtypeStruct((n_mp * capacity, rows, n), BF16),
        compiler_params=params(),
        cost_estimate=cost(),
        name="collect",
    )(base, *parts)


def outputs_kernel(jobs, where, capacity, pos, owners, comp_ref, left_ref, strip_ref, base_ref, *refs):
    n_right = 1 + max(a for a, _ in (where or jobs).values())
    rights, refs = refs[:n_right], refs[n_right:]
    n_scratch = 6 if where else 3
    scratch = refs[-n_scratch:]
    feedback, weights, out_sem = scratch[:3]
    refs = refs[:-n_scratch]
    token_ref, outs = refs[-1], refs[-5:-1] if where else refs[-3:-1]
    token_ref[...] = jnp.zeros(token_ref.shape, F32)
    _, upm, n_z, _, cols = rights[0].shape
    half = comp_ref.shape[0] // CORES

    def right_of(place, d, block):
        a, entry = place
        parts = [rights[a][entry, i ^ pos[1], d, :, block] for i in range(upm)]
        return parts[0] if upm == 1 else jnp.concatenate(parts, axis=0)

    def columns(d, first=0, size=cols):
        return pl.ds(pl.multiple_of((pos[4] ^ d) * cols + first, 128), size)

    def matrix(other, j):
        return (j + half * other) ^ pos[0]

    step = 256 if cols % 256 == 0 else 128
    pieces = [slice(first, first + step) for first in range(0, cols, step)]
    stores = []

    def store(source, target, sem):
        stores.append(pltpu.make_async_copy(source, target, sem))
        stores[-1].start()

    if where:
        momentum_ref, master_ref = refs[:2]
        new_momentum, new_master, state_sem = scratch[3:]
        for c in range(capacity):
            mine = jnp.int32(-1)
            for k in range(owners.shape[0]):
                mine = jnp.where((owners[k] == pos[5]) & (rank_of(owners, k) == c), k, mine)
            safe = jnp.maximum(mine, 0)
            strip = strip_ref[safe]
            for d in range(n_z):
                for block in pieces:
                    right = jnp.zeros((strip.shape[1], step), BF16)
                    for job, place in where.items():
                        right = jnp.where(safe == matrix(*job), right_of(place, d, block), right)
                    approx = jnp.dot(strip, right, preferred_element_type=F32)
                    approx = jnp.where(mine >= 0, approx, 0.0)
                    place = columns(d, block.start, step)
                    momentum = 0.9 * momentum_ref[c, :, place] + approx
                    new_momentum[c, :, place] = momentum
                    new_master[c, :, place] = master_ref[c, :, place] - 0.1 * momentum
                place = columns(d)
                for i, new in enumerate((new_momentum, new_master)):
                    store(
                        new.at[c, :, place], outs[2 + i].at[0, c, :, place], state_sem.at[i, c, d]
                    )

    for i, (job, where_right) in enumerate(jobs.items()):
        k = matrix(*job)
        slot = (owners[k] ^ pos[5]) * capacity + rank_of(owners, k)
        left, strip = left_ref[k], strip_ref[k]
        for d in range(n_z):
            for block in pieces:
                right = right_of(where_right, d, block)
                place = columns(d, block.start, step)
                approx = jnp.dot(left, right, preferred_element_type=F32)
                feedback[i, :, place] = (comp_ref[k, :, place].astype(F32) - approx).astype(BF16)
                approx = jnp.dot(strip, right, preferred_element_type=F32)
                base = base_ref[slot, :, place].astype(F32)
                weights[i, :, place] = (base - 0.1 * approx).astype(BF16)
            place = columns(d)
            store(feedback.at[i, :, place], outs[0].at[0, k, :, place], out_sem.at[i, d, 0])
            store(weights.at[i, :, place], outs[1].at[k, :, place], out_sem.at[i, d, 1])

    for copy in stores:
        copy.wait()


def outputs(pos, owners, comp, left, strip, base, capacity, rights, jobs, where=None, states=(), earlier=()):
    nmat, rows, n = comp.shape
    n_z = rights[0].shape[2]
    replica_rows = base.shape[1]
    any_spec = pl.BlockSpec(memory_space=pl.ANY)
    vmem = pl.BlockSpec(memory_space=pltpu.VMEM)
    scratch = [
        pltpu.VMEM((len(jobs), rows, n), BF16),
        pltpu.VMEM((len(jobs), replica_rows, n), BF16),
        pltpu.SemaphoreType.DMA((len(jobs), n_z, 2)),
    ]
    if states:
        scratch += [pltpu.VMEM((capacity, replica_rows, n), F32)] * 2
        scratch += [pltpu.SemaphoreType.DMA((2, capacity, n_z))]
    outs = [
        jax.ShapeDtypeStruct((1, nmat, rows, n), BF16),
        jax.ShapeDtypeStruct((nmat, replica_rows, n), BF16),
    ] + [jax.ShapeDtypeStruct((1,) + x.shape, F32) for x in states]
    first = 6 + len(rights) + len(states)
    return pl.pallas_call(
        functools.partial(outputs_kernel, jobs, where, capacity),
        grid_spec=pltpu.PrefetchScalarGridSpec(
            num_scalar_prefetch=2,
            grid=(1,),
            in_specs=[vmem] * (4 + len(rights) + len(states)) + [any_spec] * len(earlier),
            out_specs=[any_spec] * len(outs) + [vmem],
            scratch_shapes=scratch,
        ),
        out_shape=outs + [jax.ShapeDtypeStruct((8, 128), F32)],
        input_output_aliases={first + i: i for i in range(len(earlier))},
        compiler_params=params(24),
        cost_estimate=cost(),
        name="outputs",
    )(pos, owners, comp, left, strip, base, *rights, *states, *earlier)


def base_kernel(pos, momentum_ref, master_ref, out_ref, momentum, master, *refs):
    firsts, sems = refs[:-1], refs[-1]
    capacity, rows, _ = out_ref.shape
    blocks = [(c, first) for c in range(capacity) for first in range(0, rows, BASE_ROWS)]

    def copies(i):
        c, first = blocks[i]
        part = pl.ds(first, BASE_ROWS)
        return [
            pltpu.make_async_copy(source.at[0, c, part], target.at[c, part], sems.at[j, i])
            for j, (source, target) in enumerate(((momentum_ref, momentum), (master_ref, master)))
        ]

    for i in range(len(blocks)):
        for copy in copies(i):
            copy.start()
    for i, (c, first) in enumerate(blocks):
        for copy in copies(i):
            copy.wait()
        part = slice(first, first + BASE_ROWS)
        out_ref[c, part] = (master[c, part] - 0.09 * momentum[c, part]).astype(BF16)
    for slot, ref in enumerate(firsts):
        ref[:rows] = out_ref[slot]
        ref[rows:] = out_ref[1 - slot, : ref.shape[0] - rows]


def base_of(pos, momentum, master, square):
    _, capacity, rows, n = momentum.shape
    state = jax.ShapeDtypeStruct((capacity, rows, n), F32)
    base = jax.ShapeDtypeStruct((capacity, rows, n), BF16)
    firsts = [jax.ShapeDtypeStruct((rows + 5 * rows // 6, n), BF16)] * (2 if square else 0)
    base, momentum, master, *firsts = pl.pallas_call(
        base_kernel,
        grid_spec=pltpu.PrefetchScalarGridSpec(
            num_scalar_prefetch=1,
            grid=(1,),
            in_specs=[pl.BlockSpec(memory_space=pl.ANY)] * 2,
            out_specs=[pl.BlockSpec(memory_space=pltpu.VMEM)] * (3 + len(firsts)),
            scratch_shapes=[pltpu.SemaphoreType.DMA((2, capacity * rows // BASE_ROWS))],
        ),
        out_shape=[base, state, state] + firsts,
        compiler_params=params(),
        cost_estimate=cost(),
        name="base",
    )(pos, momentum, master)
    return base, (momentum, master), firsts


def per_device(
    gradients,
    feedback,
    right_init,
    gram_root,
    owners,
    momentum,
    master_weights,
    vector_grads,
    vector_momentum,
    vector_params,
):
    nmat, rows, n = gradients.shape[1:]
    rank = right_init.shape[2]
    unit = rank * nmat // (CORES * lax.axis_size("mp"))
    n_mp = lax.axis_size("mp")
    n_z = lax.axis_size("replica") // CORES
    capacity, replica_rows = momentum.shape[1:3]
    p = lax.axis_index("mp")
    r = lax.axis_index("replica")
    core, z = r % CORES, r // CORES
    upm = CORES * n_mp // nmat
    half = nmat // CORES
    code = core * n_mp + p
    first = r * replica_rows

    places_of = [code // upm, code % upm, core, r, z, p, first % rows // replica_rows, first // rows ^ p]
    pos = jnp.stack(places_of).astype(jnp.int32)
    in_hbm = lambda x: pltpu.with_memory_space_constraint(x, pltpu.HBM)

    square = n_mp == 4 and capacity == 2 and replica_rows % 96 == 0
    base, states, firsts = base_of(pos, in_hbm(momentum), in_hbm(master_weights), square)
    firsts = firsts or [base] * (n_mp - 1)
    early = [exchange(part, "mp", d) for d, part in enumerate(firsts, 1)]

    nvec = vector_grads.shape[1]
    comp, near, far = left_terms(
        pos,
        in_hbm(gradients),
        in_hbm(feedback),
        in_hbm(jnp.swapaxes(right_init, 1, 2)),
        vector_grads,
    )
    piece = add([near, exchange(far, "replica", 1)], BF16)
    along_z = lambda x: [exchange(x, "replica", CORES * d) for d in range(1, n_z)]
    piece = add([piece] + along_z(piece), F32)
    near, far = piece, exchange(piece, "replica", 1)

    send, keep, lt, left, vector_rows = right_terms(pos, near, far, gram_root, comp, upm, [])
    vector_total = vector_rows.reshape(-1)[:nvec]
    recv = exchange(send, "replica", 1)
    own, strip, *chip = chip_sum(pos, keep, recv, lt, replica_rows, [token([keep] + early)])
    plane = [exchange(part, "mp", d) for d, part in enumerate(chip, 1)]
    *final, mine = plane_sum(pos, own, strip, plane, n_z, nmat, rank)
    late = []
    if square:
        late = [exchange(part, "mp", d) for d, part in enumerate(forward(*early, base, mine), 1)]
    final = [final[0]] + [exchange(final[d], "replica", CORES * d) for d in range(1, n_z)]
    final = add(final, BF16)
    new_vector_momentum = 0.9 * vector_momentum + vector_total
    new_vector_params = vector_params - 0.1 * new_vector_momentum

    whole = stack([final] + along_z(final), late + [new_vector_params])
    others = [exchange(whole, "mp", d) for d in range(1, n_mp)]
    slots = collect(square, n_mp, base, early + late)
    common = (pos, owners, comp, left, mine, slots, capacity)
    shape = (half, upm) + whole.shape
    done, near_jobs, after = (), {(0, j): (0, j) for j in range(half)}, [slots]
    if upm == 1:
        *done, after = outputs(*common, [whole[None, None]], {(0, 0): (0, 0)})
        after = [after]
        del near_jobs[0, 0]
    near = stack([whole] + others, after).reshape(shape)
    far = exchange(near, "replica", 1)
    far_jobs = {(1, j): (1, j) for j in range(half)}
    where = {(0, j): (0, j) for j in range(half)} | far_jobs
    *done, _ = outputs(*common, [near], near_jobs, earlier=done)
    new_feedback, new_weights, new_momentum, new_master, _ = outputs(
        *common, [near, far], far_jobs, where, states, done
    )
    return new_feedback, new_momentum, new_master, new_weights, new_vector_momentum, new_vector_params


def solution(mesh):
    return jax.shard_map(
        per_device,
        mesh=mesh,
        in_specs=(
            P("replica", None, "mp", None),
            P("replica", None, "mp", None),
            P(),
            P(),
            P(),
            P("mp", None, "replica", None),
            P("mp", None, "replica", None),
            P("replica", "mp"),
            P("mp"),
            P("mp"),
        ),
        out_specs=(
            P("replica", None, "mp", None),
            P("mp", None, "replica", None),
            P("mp", None, "replica", None),
            P(None, "replica", None),
            P("mp"),
            P("mp"),
        ),
        check_vma=False,
    )
```

```python
import functools

import jax
import jax.numpy as jnp
from jax import lax
from jax.experimental import pallas as pl
from jax.experimental.pallas import tpu as pltpu
from jax.sharding import PartitionSpec as P

CORES = 2
BASE_ROWS = 48
F32 = jnp.float32
BF16 = jnp.bfloat16


def params(mib=12):
    return pltpu.CompilerParams(vmem_limit_bytes=mib * 1024 * 1024)


def cost(flops=1000, bytes_accessed=1000):
    return pl.CostEstimate(flops=flops, bytes_accessed=bytes_accessed, transcendentals=0)


def tree_sum(terms):
    while len(terms) > 1:
        terms = [terms[i] + terms[i + 1] for i in range(0, len(terms), 2)]
    return terms[0]


def exchange(x, axis, distance):
    size = lax.axis_size(axis)
    return lax.ppermute(x, axis, [(i, i ^ distance) for i in range(size)])


def left_kernel(pos, g_ref, f_ref, q_ref, vec_ref, comp_ref, near_ref, far_ref, total, feedback, right, terms, sems):
    nmat, rows, _ = comp_ref.shape
    rank = q_ref.shape[1]
    part = near_ref.shape[0]

    def copies(k):
        return [
            pltpu.make_async_copy(g_ref.at[0, k], comp_ref.at[k], sems.at[k, 0]),
            pltpu.make_async_copy(f_ref.at[0, k], feedback.at[k], sems.at[k, 1]),
            pltpu.make_async_copy(q_ref.at[k], right.at[k], sems.at[k, 2]),
        ]

    @pl.loop(0, nmat)
    def _(k):
        for copy in copies(k):
            copy.start()

    total[...] = jnp.zeros(total.shape, F32)
    width, nvec = total.shape[1], vec_ref.shape[1]
    for i, first in enumerate(range(0, nvec, width)):
        count = min(width, nvec - first)
        total[rows + i : rows + i + 1, :count] = vec_ref[:, first : first + count]

    @pl.loop(0, nmat)
    def _(k):
        for copy in copies(k):
            copy.wait()
        comp = comp_ref[k] + feedback[k]
        comp_ref[k] = comp
        terms[k] = lax.dot_general(
            comp, right[k], (((1,), (1,)), ((), ())), preferred_element_type=F32
        )

    for k in range(nmat):
        total[:rows, k * rank : (k + 1) * rank] = terms[k]
    for ref, core in ((near_ref, pos[2]), (far_ref, 1 - pos[2])):
        ref[...] = total[pl.ds(pl.multiple_of(core * part, 16), part), :]


def left_terms(pos, gradients, feedback, right_t, vec):
    _, nmat, rows, n = gradients.shape
    rank = right_t.shape[1]
    width = nmat * rank
    total = rows + -(-vec.shape[1] // width)
    total += -total % (16 * CORES)
    part = jax.ShapeDtypeStruct((total // CORES, width), F32)
    vmem = pl.BlockSpec(memory_space=pltpu.VMEM)
    any_spec = pl.BlockSpec(memory_space=pl.ANY)
    return pl.pallas_call(
        left_kernel,
        grid_spec=pltpu.PrefetchScalarGridSpec(
            num_scalar_prefetch=1,
            grid=(1,),
            in_specs=[any_spec] * 3 + [vmem],
            out_specs=[vmem] * 3,
            scratch_shapes=[
                pltpu.VMEM((total, width), F32),
                pltpu.VMEM((nmat, rows, n), BF16),
                pltpu.VMEM((nmat, rank, n), BF16),
                pltpu.VMEM((nmat, rows, rank), F32),
                pltpu.SemaphoreType.DMA((nmat, 3)),
            ],
        ),
        out_shape=[jax.ShapeDtypeStruct((nmat, rows, n), BF16), part, part],
        compiler_params=params(20),
        cost_estimate=cost(),
        name="left_terms",
    )(pos, gradients, feedback, right_t, vec)


def add_kernel(*refs):
    out = refs[-1]
    out[...] = tree_sum([ref[...].astype(F32) for ref in refs[:-1]]).astype(out.dtype)


def add(parts, dtype):
    vmem = pl.BlockSpec(memory_space=pltpu.VMEM)
    return pl.pallas_call(
        add_kernel,
        in_specs=[vmem] * len(parts),
        out_specs=vmem,
        out_shape=jax.ShapeDtypeStruct(parts[0].shape, dtype),
        compiler_params=params(),
        cost_estimate=cost(),
        name="add",
    )(*parts)


def send_kernel(half, pos, near_ref, far_ref, gram_ref, comp_ref, send_ref, lt_ref, left_ref, vec_ref, left, gram):
    nmat, rows, _ = comp_ref.shape
    rank = gram_ref.shape[1]
    part = near_ref.shape[0]
    for ref, core in ((near_ref, pos[2]), (far_ref, 1 - pos[2])):
        left[pl.ds(pl.multiple_of(core * part, 16), part), :] = ref[...]
    vec_ref[...] = left[rows:, :]
    gram[...] = jnp.zeros(gram.shape, F32)
    for i in range(nmat):
        gram[i * rank : (i + 1) * rank, i * rank : (i + 1) * rank] = gram_ref[i]
    hat = jnp.dot(
        left[:rows, :], gram[...], precision=lax.Precision.HIGHEST, preferred_element_type=F32
    )
    lt_ref[...] = hat.T.astype(BF16)
    for i in range(nmat):
        left_ref[i] = hat[:, i * rank : (i + 1) * rank].astype(BF16)
    right_rows(half, pos, lt_ref, comp_ref, send_ref)


def right_rows(start, pos, lt_ref, comp_ref, out_ref):
    half, upm, unit, _ = out_ref.shape
    for t in range(half):
        k = (t + start) ^ pos[0]
        rows = pl.ds(pl.multiple_of(k * upm * unit, upm * unit), upm * unit)
        terms = jnp.dot(lt_ref[rows, :], comp_ref[k], preferred_element_type=F32)
        for i in range(upm):
            out_ref[t, i ^ pos[1]] = terms[i * unit : (i + 1) * unit].astype(out_ref.dtype)


def keep_kernel(pos, lt_ref, comp_ref, *refs):
    right_rows(0, pos, lt_ref, comp_ref, refs[-1])


def right_terms(pos, near, far, gram, comp, upm, after):
    nmat, rows, n = comp.shape
    rank = gram.shape[1]
    width = nmat * rank
    half = nmat // CORES
    total = CORES * near.shape[0]
    shape = (half, upm, rank // upm, n)
    vmem = pl.BlockSpec(memory_space=pltpu.VMEM)
    send, lt, left, vec = pl.pallas_call(
        functools.partial(send_kernel, half),
        grid_spec=pltpu.PrefetchScalarGridSpec(
            num_scalar_prefetch=1,
            grid=(1,),
            in_specs=[vmem] * 4,
            out_specs=[vmem] * 4,
            scratch_shapes=[pltpu.VMEM((total, width), F32), pltpu.VMEM((width, width), F32)],
        ),
        out_shape=[
            jax.ShapeDtypeStruct(shape, BF16),
            jax.ShapeDtypeStruct((width, rows), BF16),
            jax.ShapeDtypeStruct((nmat, rows, rank), BF16),
            jax.ShapeDtypeStruct((total - rows, width), F32),
        ],
        compiler_params=params(),
        cost_estimate=cost(),
        name="right_send",
    )(pos, near, far, gram, comp)
    keep = pl.pallas_call(
        keep_kernel,
        grid_spec=pltpu.PrefetchScalarGridSpec(
            num_scalar_prefetch=1,
            grid=(1,),
            in_specs=[vmem, vmem] + [pl.BlockSpec(memory_space=pl.ANY)] * len(after),
            out_specs=vmem,
        ),
        out_shape=jax.ShapeDtypeStruct(shape, F32),
        compiler_params=params(),
        cost_estimate=cost(),
        name="right_keep",
    )(pos, lt, comp, *after)
    return send, keep, lt, left, vec


def chip_kernel(replica_rows, pos, keep_ref, recv_ref, lt_ref, *refs):
    upm = keep_ref.shape[1]
    own_ref, strip_ref, *sends = refs[-(keep_ref.shape[0] * upm + 1) :]
    left = lt_ref[...].astype(F32).T
    strip = left[:replica_rows]
    for i in range(1, left.shape[0] // replica_rows):
        strip = jnp.where(pos[6] == i, left[i * replica_rows : (i + 1) * replica_rows], strip)
    height = strip_ref.shape[0]
    strip = jnp.concatenate(
        [strip[i * height : (i + 1) * height] for i in range(replica_rows // height)], axis=1
    )
    strip_ref[...] = strip
    own_ref[...] = keep_ref[0, 0] + recv_ref[0, 0].astype(F32)
    for d, out in enumerate(sends, 1):
        j, i = d // upm, d % upm
        terms = keep_ref[j, i] + recv_ref[j, i].astype(F32)
        out[...] = jnp.concatenate([terms, strip], axis=0).astype(BF16)


def chip_sum(pos, keep, recv, lt, replica_rows, after):
    half, upm, unit, n = keep.shape
    height = lt.shape[0] * replica_rows // n
    vmem = pl.BlockSpec(memory_space=pltpu.VMEM)
    outs = [jax.ShapeDtypeStruct((unit, n), F32), jax.ShapeDtypeStruct((height, n), F32)]
    outs += [jax.ShapeDtypeStruct((unit + height, n), BF16)] * (half * upm - 1)
    return pl.pallas_call(
        functools.partial(chip_kernel, replica_rows),
        grid_spec=pltpu.PrefetchScalarGridSpec(
            num_scalar_prefetch=1,
            grid=(1,),
            in_specs=[vmem] * 3 + [pl.BlockSpec(memory_space=pl.ANY)] * len(after),
            out_specs=[vmem] * len(outs),
        ),
        out_shape=outs,
        compiler_params=params(),
        cost_estimate=cost(),
        name="chip_sum",
    )(pos, keep, recv, lt, *after)


def plane_kernel(pos, own_ref, strip_ref, *refs):
    n_z = own_ref.shape[1] // refs[-2].shape[1]
    terms, outs, left_ref = refs[: -n_z - 1], refs[-n_z - 1 : -1], refs[-1]
    unit, n = own_ref.shape
    cols = n // n_z
    for d, out in enumerate(outs):
        block = pl.ds(pl.multiple_of((pos[4] ^ d) * cols, cols), cols)
        parts = [own_ref[:, block]] + [term[:, block].astype(F32)[:unit] for term in terms]
        out[...] = tree_sum(parts).astype(out.dtype)
    strip = strip_ref[...]
    for d, term in enumerate(terms, 1):
        strip = jnp.where(pos[7] == d, term[...].astype(F32)[unit:], strip)
    nmat, _, rank = left_ref.shape
    width = nmat * rank
    rows = [strip[:, i * width : (i + 1) * width] for i in range(n // width)]
    rows = jnp.concatenate(rows, axis=0).astype(BF16)
    for i in range(nmat):
        left_ref[i] = rows[:, i * rank : (i + 1) * rank]


def plane_sum(pos, own, strip, terms, n_z, nmat, rank):
    unit, n = own.shape
    count = strip.size // (nmat * rank)
    outs = [jax.ShapeDtypeStruct((unit, n // n_z), BF16 if d else F32) for d in range(n_z)]
    outs.append(jax.ShapeDtypeStruct((nmat, count, rank), BF16))
    vmem = pl.BlockSpec(memory_space=pltpu.VMEM)
    return pl.pallas_call(
        plane_kernel,
        grid_spec=pltpu.PrefetchScalarGridSpec(
            num_scalar_prefetch=1,
            grid=(1,),
            in_specs=[vmem] * (2 + len(terms)),
            out_specs=[vmem] * len(outs),
        ),
        out_shape=outs,
        compiler_params=params(),
        cost_estimate=cost(),
        name="plane_sum",
    )(pos, own, strip, *terms)


def stack_kernel(count, *refs):
    for i in range(count):
        refs[-1][i] = refs[i][...]


def stack(parts, after=()):
    vmem = pl.BlockSpec(memory_space=pltpu.VMEM)
    return pl.pallas_call(
        functools.partial(stack_kernel, len(parts)),
        in_specs=[vmem] * len(parts) + [pl.BlockSpec(memory_space=pl.ANY)] * len(after),
        out_specs=vmem,
        out_shape=jax.ShapeDtypeStruct((len(parts),) + parts[0].shape, parts[0].dtype),
        compiler_params=params(),
        cost_estimate=cost(),
        name="stack",
    )(*parts, *after)


def token_kernel(*refs):
    refs[-1][...] = jnp.zeros(refs[-1].shape, F32)


def token(after):
    return pl.pallas_call(
        token_kernel,
        in_specs=[pl.BlockSpec(memory_space=pl.ANY)] * len(after),
        out_specs=pl.BlockSpec(memory_space=pltpu.VMEM),
        out_shape=jax.ShapeDtypeStruct((8, 128), F32),
        compiler_params=params(),
        cost_estimate=cost(),
        name="token",
    )(*after)


def forward_kernel(later, x_ref, y_ref, base_ref, after_ref, *outs):
    rows = base_ref.shape[1]
    for source, slot, out in ((y_ref, 1, outs[0]), (x_ref, 0, outs[1])):
        out[:rows] = source[:rows]
        out[rows:] = base_ref[slot, rows - later :]


def forward(x, y, base, after):
    _, rows, n = base.shape
    later = 2 * rows - x.shape[0]
    vmem = pl.BlockSpec(memory_space=pltpu.VMEM)
    return pl.pallas_call(
        functools.partial(forward_kernel, later),
        in_specs=[vmem] * 3 + [pl.BlockSpec(memory_space=pl.ANY)],
        out_specs=[vmem] * 2,
        out_shape=[jax.ShapeDtypeStruct((rows + later, n), BF16)] * 2,
        compiler_params=params(),
        cost_estimate=cost(),
        name="forward",
    )(x, y, base, after)


def rank_of(owners, k):
    count = jnp.int32(0)
    for j in range(owners.shape[0]):
        count += jnp.where((owners[j] == owners[k]) & (j < k), 1, 0)
    return count


def collect_kernel(square, base_ref, *refs):
    out = refs[-1]
    capacity, rows, _ = base_ref.shape
    out[:capacity] = base_ref[...]
    if not square:
        for d, ref in enumerate(refs[:-1], 1):
            out[d * capacity : (d + 1) * capacity] = ref[...]
        return
    x, y, more_x, more_y = refs[:-1]
    early = x.shape[0] - rows
    for d, slot, first, second in ((1, 0, x, more_x), (2, 1, y, more_y)):
        out[d * capacity + slot] = first[:rows]
        out[d * capacity + 1 - slot, :early] = first[rows:]
        out[d * capacity + 1 - slot, early:] = second[rows:]
    out[3 * capacity] = more_y[:rows]
    out[3 * capacity + 1] = more_x[:rows]


def collect(square, n_mp, base, parts):
    capacity, rows, n = base.shape
    vmem = pl.BlockSpec(memory_space=pltpu.VMEM)
    return pl.pallas_call(
        functools.partial(collect_kernel, square),
        in_specs=[vmem] * (1 + len(parts)),
        out_specs=vmem,
        out_shape=jax.ShapeDtypeStruct((n_mp * capacity, rows, n), BF16),
        compiler_params=params(),
        cost_estimate=cost(),
        name="collect",
    )(base, *parts)


def outputs_kernel(jobs, where, capacity, pos, owners, comp_ref, left_ref, strip_ref, base_ref, *refs):
    n_right = 1 + max(a for a, _ in (where or jobs).values())
    rights, refs = refs[:n_right], refs[n_right:]
    n_scratch = 6 if where else 3
    scratch = refs[-n_scratch:]
    feedback, weights, out_sem = scratch[:3]
    refs = refs[:-n_scratch]
    token_ref, outs = refs[-1], refs[-5:-1] if where else refs[-3:-1]
    token_ref[...] = jnp.zeros(token_ref.shape, F32)
    _, upm, n_z, _, cols = rights[0].shape
    half = comp_ref.shape[0] // CORES

    def right_of(place, d, block):
        a, entry = place
        parts = [rights[a][entry, i ^ pos[1], d, :, block] for i in range(upm)]
        return parts[0] if upm == 1 else jnp.concatenate(parts, axis=0)

    def columns(d, first=0, size=cols):
        return pl.ds(pl.multiple_of((pos[4] ^ d) * cols + first, 128), size)

    def matrix(other, j):
        return (j + half * other) ^ pos[0]

    step = 256 if cols % 256 == 0 else 128
    pieces = cols // step

    def block_of(b):
        d, first = b // pieces, lax.rem(b, pieces) * step
        return d, pl.ds(pl.multiple_of(first, 128), step), columns(d, first, step)

    if where:
        momentum_ref, master_ref = refs[:2]
        new_momentum, new_master, state_sem = scratch[3:]

        def state_copies(c):
            return [
                pltpu.make_async_copy(new.at[c], outs[2 + i].at[0, c], state_sem.at[i, c])
                for i, new in enumerate((new_momentum, new_master))
            ]

        @pl.loop(0, capacity)
        def _(c):
            mine = jnp.int32(-1)
            for k in range(owners.shape[0]):
                mine = jnp.where((owners[k] == pos[5]) & (rank_of(owners, k) == c), k, mine)
            safe = jnp.maximum(mine, 0)
            strip = strip_ref[safe]

            @pl.loop(0, n_z * pieces)
            def _(b):
                d, block, place = block_of(b)
                right = jnp.zeros((strip.shape[1], step), BF16)
                for job, entry in where.items():
                    right = jnp.where(safe == matrix(*job), right_of(entry, d, block), right)
                approx = jnp.dot(strip, right, preferred_element_type=F32)
                approx = jnp.where(mine >= 0, approx, 0.0)
                momentum = 0.9 * momentum_ref[c, :, place] + approx
                new_momentum[c, :, place] = momentum
                new_master[c, :, place] = master_ref[c, :, place] - 0.1 * momentum

            for copy in state_copies(c):
                copy.start()

    (other, start), (a, entry) = next(iter(jobs.items()))

    def copies(i, d):
        k, place = matrix(other, start + i), columns(d)
        return [
            pltpu.make_async_copy(
                feedback.at[i, :, place], outs[0].at[0, k, :, place], out_sem.at[i, d, 0]
            ),
            pltpu.make_async_copy(
                weights.at[i, :, place], outs[1].at[k, :, place], out_sem.at[i, d, 1]
            ),
        ]

    @pl.loop(0, len(jobs))
    def _(i):
        k = matrix(other, start + i)
        slot = (owners[k] ^ pos[5]) * capacity + rank_of(owners, k)
        left, strip = left_ref[k], strip_ref[k]

        @pl.loop(0, n_z)
        def _(d):
            for first in range(0, cols, step):
                right = right_of((a, entry + i), d, slice(first, first + step))
                place = columns(d, first, step)
                approx = jnp.dot(left, right, preferred_element_type=F32)
                feedback[i, :, place] = (comp_ref[k, :, place].astype(F32) - approx).astype(BF16)
                approx = jnp.dot(strip, right, preferred_element_type=F32)
                base = base_ref[slot, :, place].astype(F32)
                weights[i, :, place] = (base - 0.1 * approx).astype(BF16)
            for copy in copies(i, d):
                copy.start()

    @pl.loop(0, len(jobs))
    def _(i):
        @pl.loop(0, n_z)
        def _(d):
            for copy in copies(i, d):
                copy.wait()

    if where:

        @pl.loop(0, capacity)
        def _(c):
            for copy in state_copies(c):
                copy.wait()


def outputs(pos, owners, comp, left, strip, base, capacity, rights, jobs, where=None, states=(), earlier=()):
    nmat, rows, n = comp.shape
    n_z = rights[0].shape[2]
    replica_rows = base.shape[1]
    any_spec = pl.BlockSpec(memory_space=pl.ANY)
    vmem = pl.BlockSpec(memory_space=pltpu.VMEM)
    scratch = [
        pltpu.VMEM((len(jobs), rows, n), BF16),
        pltpu.VMEM((len(jobs), replica_rows, n), BF16),
        pltpu.SemaphoreType.DMA((len(jobs), n_z, 2)),
    ]
    if states:
        scratch += [pltpu.VMEM((capacity, replica_rows, n), F32)] * 2
        scratch += [pltpu.SemaphoreType.DMA((2, capacity))]
    outs = [
        jax.ShapeDtypeStruct((1, nmat, rows, n), BF16),
        jax.ShapeDtypeStruct((nmat, replica_rows, n), BF16),
    ] + [jax.ShapeDtypeStruct((1,) + x.shape, F32) for x in states]
    first = 6 + len(rights) + len(states)
    return pl.pallas_call(
        functools.partial(outputs_kernel, jobs, where, capacity),
        grid_spec=pltpu.PrefetchScalarGridSpec(
            num_scalar_prefetch=2,
            grid=(1,),
            in_specs=[vmem] * (4 + len(rights) + len(states)) + [any_spec] * len(earlier),
            out_specs=[any_spec] * len(outs) + [vmem],
            scratch_shapes=scratch,
        ),
        out_shape=outs + [jax.ShapeDtypeStruct((8, 128), F32)],
        input_output_aliases={first + i: i for i in range(len(earlier))},
        compiler_params=params(24),
        cost_estimate=cost(),
        name="outputs",
    )(pos, owners, comp, left, strip, base, *rights, *states, *earlier)


def base_kernel(pos, momentum_ref, master_ref, out_ref, momentum, master, *refs):
    firsts, sems = refs[:-1], refs[-1]
    capacity, rows, _ = out_ref.shape
    blocks = [(c, first) for c in range(capacity) for first in range(0, rows, BASE_ROWS)]

    def copies(i):
        c, first = blocks[i]
        part = pl.ds(first, BASE_ROWS)
        return [
            pltpu.make_async_copy(source.at[0, c, part], target.at[c, part], sems.at[j, i])
            for j, (source, target) in enumerate(((momentum_ref, momentum), (master_ref, master)))
        ]

    for i in range(len(blocks)):
        for copy in copies(i):
            copy.start()
    for i, (c, first) in enumerate(blocks):
        for copy in copies(i):
            copy.wait()
        part = slice(first, first + BASE_ROWS)
        out_ref[c, part] = (master[c, part] - 0.09 * momentum[c, part]).astype(BF16)
    for slot, ref in enumerate(firsts):
        ref[:rows] = out_ref[slot]
        ref[rows:] = out_ref[1 - slot, : ref.shape[0] - rows]


def base_of(pos, momentum, master, square):
    _, capacity, rows, n = momentum.shape
    state = jax.ShapeDtypeStruct((capacity, rows, n), F32)
    base = jax.ShapeDtypeStruct((capacity, rows, n), BF16)
    firsts = [jax.ShapeDtypeStruct((rows + 5 * rows // 6, n), BF16)] * (2 if square else 0)
    base, momentum, master, *firsts = pl.pallas_call(
        base_kernel,
        grid_spec=pltpu.PrefetchScalarGridSpec(
            num_scalar_prefetch=1,
            grid=(1,),
            in_specs=[pl.BlockSpec(memory_space=pl.ANY)] * 2,
            out_specs=[pl.BlockSpec(memory_space=pltpu.VMEM)] * (3 + len(firsts)),
            scratch_shapes=[pltpu.SemaphoreType.DMA((2, capacity * rows // BASE_ROWS))],
        ),
        out_shape=[base, state, state] + firsts,
        compiler_params=params(),
        cost_estimate=cost(),
        name="base",
    )(pos, momentum, master)
    return base, (momentum, master), firsts


def per_device(
    gradients,
    feedback,
    right_init,
    gram_root,
    owners,
    momentum,
    master_weights,
    vector_grads,
    vector_momentum,
    vector_params,
):
    nmat, rows, n = gradients.shape[1:]
    rank = right_init.shape[2]
    unit = rank * nmat // (CORES * lax.axis_size("mp"))
    n_mp = lax.axis_size("mp")
    n_z = lax.axis_size("replica") // CORES
    capacity, replica_rows = momentum.shape[1:3]
    p = lax.axis_index("mp")
    r = lax.axis_index("replica")
    core, z = r % CORES, r // CORES
    upm = CORES * n_mp // nmat
    half = nmat // CORES
    code = core * n_mp + p
    first = r * replica_rows

    places_of = [code // upm, code % upm, core, r, z, p, first % rows // replica_rows, first // rows ^ p]
    pos = jnp.stack(places_of).astype(jnp.int32)
    in_hbm = lambda x: pltpu.with_memory_space_constraint(x, pltpu.HBM)

    square = n_mp == 4 and capacity == 2 and replica_rows % 96 == 0
    base, states, firsts = base_of(pos, in_hbm(momentum), in_hbm(master_weights), square)
    firsts = firsts or [base] * (n_mp - 1)
    early = [exchange(part, "mp", d) for d, part in enumerate(firsts, 1)]

    nvec = vector_grads.shape[1]
    comp, near, far = left_terms(
        pos,
        in_hbm(gradients),
        in_hbm(feedback),
        in_hbm(jnp.swapaxes(right_init, 1, 2)),
        vector_grads,
    )
    piece = add([near, exchange(far, "replica", 1)], BF16)
    along_z = lambda x: [exchange(x, "replica", CORES * d) for d in range(1, n_z)]
    piece = add([piece] + along_z(piece), F32)
    near, far = piece, exchange(piece, "replica", 1)

    send, keep, lt, left, vector_rows = right_terms(pos, near, far, gram_root, comp, upm, [])
    vector_total = vector_rows.reshape(-1)[:nvec]
    recv = exchange(send, "replica", 1)
    own, strip, *chip = chip_sum(pos, keep, recv, lt, replica_rows, [token([keep] + early)])
    plane = [exchange(part, "mp", d) for d, part in enumerate(chip, 1)]
    *final, mine = plane_sum(pos, own, strip, plane, n_z, nmat, rank)
    late = []
    if square:
        late = [exchange(part, "mp", d) for d, part in enumerate(forward(*early, base, mine), 1)]
    final = [final[0]] + [exchange(final[d], "replica", CORES * d) for d in range(1, n_z)]
    final = add(final, BF16)
    new_vector_momentum = 0.9 * vector_momentum + vector_total
    new_vector_params = vector_params - 0.1 * new_vector_momentum

    whole = stack([final] + along_z(final), late + [new_vector_params])
    others = [exchange(whole, "mp", d) for d in range(1, n_mp)]
    slots = collect(square, n_mp, base, early + late)
    common = (pos, owners, comp, left, mine, slots, capacity)
    shape = (half, upm) + whole.shape
    done, near_jobs, after = (), {(0, j): (0, j) for j in range(half)}, [slots]
    if upm == 1:
        *done, after = outputs(*common, [whole[None, None]], {(0, 0): (0, 0)})
        after = [after]
        del near_jobs[0, 0]
    near = stack([whole] + others, after).reshape(shape)
    far = exchange(near, "replica", 1)
    far_jobs = {(1, j): (1, j) for j in range(half)}
    where = {(0, j): (0, j) for j in range(half)} | far_jobs
    *done, _ = outputs(*common, [near], near_jobs, earlier=done)
    new_feedback, new_weights, new_momentum, new_master, _ = outputs(
        *common, [near, far], far_jobs, where, states, done
    )
    return new_feedback, new_momentum, new_master, new_weights, new_vector_momentum, new_vector_params


def solution(mesh):
    return jax.shard_map(
        per_device,
        mesh=mesh,
        in_specs=(
            P("replica", None, "mp", None),
            P("replica", None, "mp", None),
            P(),
            P(),
            P(),
            P("mp", None, "replica", None),
            P("mp", None, "replica", None),
            P("replica", "mp"),
            P("mp"),
            P("mp"),
        ),
        out_specs=(
            P("replica", None, "mp", None),
            P("mp", None, "replica", None),
            P("mp", None, "replica", None),
            P(None, "replica", None),
            P("mp"),
            P("mp"),
        ),
        check_vma=False,
    )
```

```python
import functools

import jax
import jax.numpy as jnp
from jax import lax
from jax.experimental import pallas as pl
from jax.experimental.pallas import tpu as pltpu
from jax.sharding import PartitionSpec as P

CORES = 2
BASE_ROWS = 48
F32 = jnp.float32
BF16 = jnp.bfloat16


def params(mib=12):
    return pltpu.CompilerParams(vmem_limit_bytes=mib * 1024 * 1024)


def cost(flops=1000, bytes_accessed=1000):
    return pl.CostEstimate(flops=flops, bytes_accessed=bytes_accessed, transcendentals=0)


def tree_sum(terms):
    while len(terms) > 1:
        terms = [terms[i] + terms[i + 1] for i in range(0, len(terms), 2)]
    return terms[0]


def exchange(x, axis, distance):
    size = lax.axis_size(axis)
    return lax.ppermute(x, axis, [(i, i ^ distance) for i in range(size)])


def left_kernel(pos, g_ref, f_ref, q_ref, vec_ref, comp_ref, near_ref, far_ref, total, feedback, right, terms, sems):
    nmat, rows, _ = comp_ref.shape
    rank = q_ref.shape[1]
    part = near_ref.shape[0]

    def copies(k):
        return [
            pltpu.make_async_copy(g_ref.at[0, k], comp_ref.at[k], sems.at[k, 0]),
            pltpu.make_async_copy(f_ref.at[0, k], feedback.at[k], sems.at[k, 1]),
            pltpu.make_async_copy(q_ref.at[k], right.at[k], sems.at[k, 2]),
        ]

    @pl.loop(0, nmat)
    def _(k):
        for copy in copies(k):
            copy.start()

    total[...] = jnp.zeros(total.shape, F32)
    width, nvec = total.shape[1], vec_ref.shape[1]
    for i, first in enumerate(range(0, nvec, width)):
        count = min(width, nvec - first)
        total[rows + i : rows + i + 1, :count] = vec_ref[:, first : first + count]

    @pl.loop(0, nmat)
    def _(k):
        for copy in copies(k):
            copy.wait()
        comp = comp_ref[k] + feedback[k]
        comp_ref[k] = comp
        terms[k] = lax.dot_general(
            comp, right[k], (((1,), (1,)), ((), ())), preferred_element_type=F32
        )

    for k in range(nmat):
        total[:rows, k * rank : (k + 1) * rank] = terms[k]
    for ref, core in ((near_ref, pos[2]), (far_ref, 1 - pos[2])):
        ref[...] = total[pl.ds(pl.multiple_of(core * part, 16), part), :]


def left_terms(pos, gradients, feedback, right_t, vec):
    _, nmat, rows, n = gradients.shape
    rank = right_t.shape[1]
    width = nmat * rank
    total = rows + -(-vec.shape[1] // width)
    total += -total % (16 * CORES)
    part = jax.ShapeDtypeStruct((total // CORES, width), F32)
    vmem = pl.BlockSpec(memory_space=pltpu.VMEM)
    any_spec = pl.BlockSpec(memory_space=pl.ANY)
    return pl.pallas_call(
        left_kernel,
        grid_spec=pltpu.PrefetchScalarGridSpec(
            num_scalar_prefetch=1,
            grid=(1,),
            in_specs=[any_spec] * 3 + [vmem],
            out_specs=[vmem] * 3,
            scratch_shapes=[
                pltpu.VMEM((total, width), F32),
                pltpu.VMEM((nmat, rows, n), BF16),
                pltpu.VMEM((nmat, rank, n), BF16),
                pltpu.VMEM((nmat, rows, rank), F32),
                pltpu.SemaphoreType.DMA((nmat, 3)),
            ],
        ),
        out_shape=[jax.ShapeDtypeStruct((nmat, rows, n), BF16), part, part],
        compiler_params=params(20),
        cost_estimate=cost(),
        name="left_terms",
    )(pos, gradients, feedback, right_t, vec)


def add_kernel(*refs):
    out = refs[-1]
    out[...] = tree_sum([ref[...].astype(F32) for ref in refs[:-1]]).astype(out.dtype)


def add(parts, dtype):
    vmem = pl.BlockSpec(memory_space=pltpu.VMEM)
    return pl.pallas_call(
        add_kernel,
        in_specs=[vmem] * len(parts),
        out_specs=vmem,
        out_shape=jax.ShapeDtypeStruct(parts[0].shape, dtype),
        compiler_params=params(),
        cost_estimate=cost(),
        name="add",
    )(*parts)


def send_kernel(half, pos, near_ref, far_ref, gram_ref, comp_ref, send_ref, lt_ref, left_ref, vec_ref, left, gram):
    nmat, rows, _ = comp_ref.shape
    rank = gram_ref.shape[1]
    part = near_ref.shape[0]
    for ref, core in ((near_ref, pos[2]), (far_ref, 1 - pos[2])):
        left[pl.ds(pl.multiple_of(core * part, 16), part), :] = ref[...]
    vec_ref[...] = left[rows:, :]
    gram[...] = jnp.zeros(gram.shape, F32)
    for i in range(nmat):
        gram[i * rank : (i + 1) * rank, i * rank : (i + 1) * rank] = gram_ref[i]
    hat = jnp.dot(
        left[:rows, :], gram[...], precision=lax.Precision.HIGHEST, preferred_element_type=F32
    )
    lt_ref[...] = hat.T.astype(BF16)
    for i in range(nmat):
        left_ref[i] = hat[:, i * rank : (i + 1) * rank].astype(BF16)
    right_rows(half, pos, lt_ref, comp_ref, send_ref)


def right_rows(start, pos, lt_ref, comp_ref, out_ref):
    half, upm, unit, _ = out_ref.shape
    for t in range(half):
        k = (t + start) ^ pos[0]
        rows = pl.ds(pl.multiple_of(k * upm * unit, upm * unit), upm * unit)
        terms = jnp.dot(lt_ref[rows, :], comp_ref[k], preferred_element_type=F32)
        for i in range(upm):
            out_ref[t, i ^ pos[1]] = terms[i * unit : (i + 1) * unit].astype(out_ref.dtype)


def keep_kernel(pos, lt_ref, comp_ref, *refs):
    right_rows(0, pos, lt_ref, comp_ref, refs[-1])


def right_terms(pos, near, far, gram, comp, upm, after):
    nmat, rows, n = comp.shape
    rank = gram.shape[1]
    width = nmat * rank
    half = nmat // CORES
    total = CORES * near.shape[0]
    shape = (half, upm, rank // upm, n)
    vmem = pl.BlockSpec(memory_space=pltpu.VMEM)
    send, lt, left, vec = pl.pallas_call(
        functools.partial(send_kernel, half),
        grid_spec=pltpu.PrefetchScalarGridSpec(
            num_scalar_prefetch=1,
            grid=(1,),
            in_specs=[vmem] * 4,
            out_specs=[vmem] * 4,
            scratch_shapes=[pltpu.VMEM((total, width), F32), pltpu.VMEM((width, width), F32)],
        ),
        out_shape=[
            jax.ShapeDtypeStruct(shape, BF16),
            jax.ShapeDtypeStruct((width, rows), BF16),
            jax.ShapeDtypeStruct((nmat, rows, rank), BF16),
            jax.ShapeDtypeStruct((total - rows, width), F32),
        ],
        compiler_params=params(),
        cost_estimate=cost(),
        name="right_send",
    )(pos, near, far, gram, comp)
    keep = pl.pallas_call(
        keep_kernel,
        grid_spec=pltpu.PrefetchScalarGridSpec(
            num_scalar_prefetch=1,
            grid=(1,),
            in_specs=[vmem, vmem] + [pl.BlockSpec(memory_space=pl.ANY)] * len(after),
            out_specs=vmem,
        ),
        out_shape=jax.ShapeDtypeStruct(shape, F32),
        compiler_params=params(),
        cost_estimate=cost(),
        name="right_keep",
    )(pos, lt, comp, *after)
    return send, keep, lt, left, vec


def chip_kernel(replica_rows, pos, keep_ref, recv_ref, lt_ref, *refs):
    upm = keep_ref.shape[1]
    own_ref, strip_ref, *sends = refs[-(keep_ref.shape[0] * upm + 1) :]
    left = lt_ref[...].astype(F32).T
    strip = left[:replica_rows]
    for i in range(1, left.shape[0] // replica_rows):
        strip = jnp.where(pos[6] == i, left[i * replica_rows : (i + 1) * replica_rows], strip)
    height = strip_ref.shape[0]
    strip = jnp.concatenate(
        [strip[i * height : (i + 1) * height] for i in range(replica_rows // height)], axis=1
    )
    strip_ref[...] = strip
    own_ref[...] = keep_ref[0, 0] + recv_ref[0, 0].astype(F32)
    for d, out in enumerate(sends, 1):
        j, i = d // upm, d % upm
        terms = keep_ref[j, i] + recv_ref[j, i].astype(F32)
        out[...] = jnp.concatenate([terms, strip], axis=0).astype(BF16)


def chip_sum(pos, keep, recv, lt, replica_rows, after):
    half, upm, unit, n = keep.shape
    height = lt.shape[0] * replica_rows // n
    vmem = pl.BlockSpec(memory_space=pltpu.VMEM)
    outs = [jax.ShapeDtypeStruct((unit, n), F32), jax.ShapeDtypeStruct((height, n), F32)]
    outs += [jax.ShapeDtypeStruct((unit + height, n), BF16)] * (half * upm - 1)
    return pl.pallas_call(
        functools.partial(chip_kernel, replica_rows),
        grid_spec=pltpu.PrefetchScalarGridSpec(
            num_scalar_prefetch=1,
            grid=(1,),
            in_specs=[vmem] * 3 + [pl.BlockSpec(memory_space=pl.ANY)] * len(after),
            out_specs=[vmem] * len(outs),
        ),
        out_shape=outs,
        compiler_params=params(),
        cost_estimate=cost(),
        name="chip_sum",
    )(pos, keep, recv, lt, *after)


def plane_kernel(pos, own_ref, strip_ref, *refs):
    n_z = own_ref.shape[1] // refs[-2].shape[1]
    terms, outs, left_ref = refs[: -n_z - 1], refs[-n_z - 1 : -1], refs[-1]
    unit, n = own_ref.shape
    cols = n // n_z
    for d, out in enumerate(outs):
        block = pl.ds(pl.multiple_of((pos[4] ^ d) * cols, cols), cols)
        parts = [own_ref[:, block]] + [term[:, block].astype(F32)[:unit] for term in terms]
        out[...] = tree_sum(parts).astype(out.dtype)
    strip = strip_ref[...]
    for d, term in enumerate(terms, 1):
        strip = jnp.where(pos[7] == d, term[...].astype(F32)[unit:], strip)
    nmat, _, rank = left_ref.shape
    width = nmat * rank
    rows = [strip[:, i * width : (i + 1) * width] for i in range(n // width)]
    rows = jnp.concatenate(rows, axis=0).astype(BF16)
    for i in range(nmat):
        left_ref[i] = rows[:, i * rank : (i + 1) * rank]


def plane_sum(pos, own, strip, terms, n_z, nmat, rank):
    unit, n = own.shape
    count = strip.size // (nmat * rank)
    outs = [jax.ShapeDtypeStruct((unit, n // n_z), BF16 if d else F32) for d in range(n_z)]
    outs.append(jax.ShapeDtypeStruct((nmat, count, rank), BF16))
    vmem = pl.BlockSpec(memory_space=pltpu.VMEM)
    return pl.pallas_call(
        plane_kernel,
        grid_spec=pltpu.PrefetchScalarGridSpec(
            num_scalar_prefetch=1,
            grid=(1,),
            in_specs=[vmem] * (2 + len(terms)),
            out_specs=[vmem] * len(outs),
        ),
        out_shape=outs,
        compiler_params=params(),
        cost_estimate=cost(),
        name="plane_sum",
    )(pos, own, strip, *terms)


def stack_kernel(count, *refs):
    for i in range(count):
        refs[-1][i] = refs[i][...]


def stack(parts, after=()):
    vmem = pl.BlockSpec(memory_space=pltpu.VMEM)
    return pl.pallas_call(
        functools.partial(stack_kernel, len(parts)),
        in_specs=[vmem] * len(parts) + [pl.BlockSpec(memory_space=pl.ANY)] * len(after),
        out_specs=vmem,
        out_shape=jax.ShapeDtypeStruct((len(parts),) + parts[0].shape, parts[0].dtype),
        compiler_params=params(),
        cost_estimate=cost(),
        name="stack",
    )(*parts, *after)


def token_kernel(*refs):
    refs[-1][...] = jnp.zeros(refs[-1].shape, F32)


def token(after):
    return pl.pallas_call(
        token_kernel,
        in_specs=[pl.BlockSpec(memory_space=pl.ANY)] * len(after),
        out_specs=pl.BlockSpec(memory_space=pltpu.VMEM),
        out_shape=jax.ShapeDtypeStruct((8, 128), F32),
        compiler_params=params(),
        cost_estimate=cost(),
        name="token",
    )(*after)


def forward_kernel(later, x_ref, y_ref, base_ref, after_ref, *outs):
    rows = base_ref.shape[1]
    for source, slot, out in ((y_ref, 1, outs[0]), (x_ref, 0, outs[1])):
        out[:rows] = source[:rows]
        out[rows:] = base_ref[slot, rows - later :]


def forward(x, y, base, after):
    _, rows, n = base.shape
    later = 2 * rows - x.shape[0]
    vmem = pl.BlockSpec(memory_space=pltpu.VMEM)
    return pl.pallas_call(
        functools.partial(forward_kernel, later),
        in_specs=[vmem] * 3 + [pl.BlockSpec(memory_space=pl.ANY)],
        out_specs=[vmem] * 2,
        out_shape=[jax.ShapeDtypeStruct((rows + later, n), BF16)] * 2,
        compiler_params=params(),
        cost_estimate=cost(),
        name="forward",
    )(x, y, base, after)


def rank_of(owners, k):
    count = jnp.int32(0)
    for j in range(owners.shape[0]):
        count += jnp.where((owners[j] == owners[k]) & (j < k), 1, 0)
    return count


def collect_kernel(square, base_ref, *refs):
    out = refs[-1]
    capacity, rows, _ = base_ref.shape
    out[:capacity] = base_ref[...]
    if not square:
        for d, ref in enumerate(refs[:-1], 1):
            out[d * capacity : (d + 1) * capacity] = ref[...]
        return
    x, y, more_x, more_y = refs[:-1]
    early = x.shape[0] - rows
    for d, slot, first, second in ((1, 0, x, more_x), (2, 1, y, more_y)):
        out[d * capacity + slot] = first[:rows]
        out[d * capacity + 1 - slot, :early] = first[rows:]
        out[d * capacity + 1 - slot, early:] = second[rows:]
    out[3 * capacity] = more_y[:rows]
    out[3 * capacity + 1] = more_x[:rows]


def collect(square, n_mp, base, parts):
    capacity, rows, n = base.shape
    vmem = pl.BlockSpec(memory_space=pltpu.VMEM)
    return pl.pallas_call(
        functools.partial(collect_kernel, square),
        in_specs=[vmem] * (1 + len(parts)),
        out_specs=vmem,
        out_shape=jax.ShapeDtypeStruct((n_mp * capacity, rows, n), BF16),
        compiler_params=params(),
        cost_estimate=cost(),
        name="collect",
    )(base, *parts)


def outputs_kernel(jobs, where, capacity, pos, owners, comp_ref, left_ref, strip_ref, base_ref, *refs):
    n_right = 1 + max(a for a, _ in (where or jobs).values())
    rights, refs = refs[:n_right], refs[n_right:]
    n_scratch = 6 if where else 3
    scratch = refs[-n_scratch:]
    feedback, weights, out_sem = scratch[:3]
    refs = refs[:-n_scratch]
    token_ref, outs = refs[-1], refs[-5:-1] if where else refs[-3:-1]
    token_ref[...] = jnp.zeros(token_ref.shape, F32)
    _, upm, n_z, _, cols = rights[0].shape
    half = comp_ref.shape[0] // CORES

    def right_of(place, d, block):
        a, entry = place
        parts = [rights[a][entry, i ^ pos[1], d, :, block] for i in range(upm)]
        return parts[0] if upm == 1 else jnp.concatenate(parts, axis=0)

    def columns(d, first=0, size=cols):
        return pl.ds(pl.multiple_of((pos[4] ^ d) * cols + first, 128), size)

    def matrix(other, j):
        return (j + half * other) ^ pos[0]

    step = 256 if cols % 256 == 0 else 128
    pieces = [slice(first, first + step) for first in range(0, cols, step)]
    stores = []

    def store(source, target, sem):
        stores.append(pltpu.make_async_copy(source, target, sem))
        stores[-1].start()

    if where:
        momentum_ref, master_ref = refs[:2]
        new_momentum, new_master, state_sem = scratch[3:]
        for c in range(capacity):
            mine = jnp.int32(-1)
            for k in range(owners.shape[0]):
                mine = jnp.where((owners[k] == pos[5]) & (rank_of(owners, k) == c), k, mine)
            safe = jnp.maximum(mine, 0)
            strip = strip_ref[safe]
            for d in range(n_z):
                for block in pieces:
                    right = jnp.zeros((strip.shape[1], step), BF16)
                    for job, place in where.items():
                        right = jnp.where(safe == matrix(*job), right_of(place, d, block), right)
                    approx = jnp.dot(strip, right, preferred_element_type=F32)
                    approx = jnp.where(mine >= 0, approx, 0.0)
                    place = columns(d, block.start, step)
                    momentum = 0.9 * momentum_ref[c, :, place] + approx
                    new_momentum[c, :, place] = momentum
                    new_master[c, :, place] = master_ref[c, :, place] - 0.1 * momentum
                place = columns(d)
                for i, new in enumerate((new_momentum, new_master)):
                    store(
                        new.at[c, :, place], outs[2 + i].at[0, c, :, place], state_sem.at[i, c, d]
                    )

    for i, (job, where_right) in enumerate(jobs.items()):
        k = matrix(*job)
        slot = (owners[k] ^ pos[5]) * capacity + rank_of(owners, k)
        left = jnp.concatenate([left_ref[k], strip_ref[k]], axis=0)
        rows = left_ref.shape[1]
        for d in range(n_z):
            for block in pieces:
                right = right_of(where_right, d, block)
                place = columns(d, block.start, step)
                approx = jnp.dot(left, right, preferred_element_type=F32)
                comp, base = comp_ref[k, :, place].astype(F32), base_ref[slot, :, place].astype(F32)
                feedback[i, :, place] = (comp - approx[:rows]).astype(BF16)
                weights[i, :, place] = (base - 0.1 * approx[rows:]).astype(BF16)
            place = columns(d)
            store(feedback.at[i, :, place], outs[0].at[0, k, :, place], out_sem.at[i, d, 0])
            store(weights.at[i, :, place], outs[1].at[k, :, place], out_sem.at[i, d, 1])

    for copy in stores:
        copy.wait()


def outputs(pos, owners, comp, left, strip, base, capacity, rights, jobs, where=None, states=(), earlier=()):
    nmat, rows, n = comp.shape
    n_z = rights[0].shape[2]
    replica_rows = base.shape[1]
    any_spec = pl.BlockSpec(memory_space=pl.ANY)
    vmem = pl.BlockSpec(memory_space=pltpu.VMEM)
    scratch = [
        pltpu.VMEM((len(jobs), rows, n), BF16),
        pltpu.VMEM((len(jobs), replica_rows, n), BF16),
        pltpu.SemaphoreType.DMA((len(jobs), n_z, 2)),
    ]
    if states:
        scratch += [pltpu.VMEM((capacity, replica_rows, n), F32)] * 2
        scratch += [pltpu.SemaphoreType.DMA((2, capacity, n_z))]
    outs = [
        jax.ShapeDtypeStruct((1, nmat, rows, n), BF16),
        jax.ShapeDtypeStruct((nmat, replica_rows, n), BF16),
    ] + [jax.ShapeDtypeStruct((1,) + x.shape, F32) for x in states]
    first = 6 + len(rights) + len(states)
    return pl.pallas_call(
        functools.partial(outputs_kernel, jobs, where, capacity),
        grid_spec=pltpu.PrefetchScalarGridSpec(
            num_scalar_prefetch=2,
            grid=(1,),
            in_specs=[vmem] * (4 + len(rights) + len(states)) + [any_spec] * len(earlier),
            out_specs=[any_spec] * len(outs) + [vmem],
            scratch_shapes=scratch,
        ),
        out_shape=outs + [jax.ShapeDtypeStruct((8, 128), F32)],
        input_output_aliases={first + i: i for i in range(len(earlier))},
        compiler_params=params(24),
        cost_estimate=cost(),
        name="outputs",
    )(pos, owners, comp, left, strip, base, *rights, *states, *earlier)


def base_kernel(pos, momentum_ref, master_ref, out_ref, momentum, master, *refs):
    firsts, sems = refs[:-1], refs[-1]
    capacity, rows, _ = out_ref.shape
    blocks = [(c, first) for c in range(capacity) for first in range(0, rows, BASE_ROWS)]

    def copies(i):
        c, first = blocks[i]
        part = pl.ds(first, BASE_ROWS)
        return [
            pltpu.make_async_copy(source.at[0, c, part], target.at[c, part], sems.at[j, i])
            for j, (source, target) in enumerate(((momentum_ref, momentum), (master_ref, master)))
        ]

    for i in range(len(blocks)):
        for copy in copies(i):
            copy.start()
    for i, (c, first) in enumerate(blocks):
        for copy in copies(i):
            copy.wait()
        part = slice(first, first + BASE_ROWS)
        out_ref[c, part] = (master[c, part] - 0.09 * momentum[c, part]).astype(BF16)
    for slot, ref in enumerate(firsts):
        ref[:rows] = out_ref[slot]
        ref[rows:] = out_ref[1 - slot, : ref.shape[0] - rows]


def base_of(pos, momentum, master, square):
    _, capacity, rows, n = momentum.shape
    state = jax.ShapeDtypeStruct((capacity, rows, n), F32)
    base = jax.ShapeDtypeStruct((capacity, rows, n), BF16)
    firsts = [jax.ShapeDtypeStruct((rows + 5 * rows // 6, n), BF16)] * (2 if square else 0)
    base, momentum, master, *firsts = pl.pallas_call(
        base_kernel,
        grid_spec=pltpu.PrefetchScalarGridSpec(
            num_scalar_prefetch=1,
            grid=(1,),
            in_specs=[pl.BlockSpec(memory_space=pl.ANY)] * 2,
            out_specs=[pl.BlockSpec(memory_space=pltpu.VMEM)] * (3 + len(firsts)),
            scratch_shapes=[pltpu.SemaphoreType.DMA((2, capacity * rows // BASE_ROWS))],
        ),
        out_shape=[base, state, state] + firsts,
        compiler_params=params(),
        cost_estimate=cost(),
        name="base",
    )(pos, momentum, master)
    return base, (momentum, master), firsts


def per_device(
    gradients,
    feedback,
    right_init,
    gram_root,
    owners,
    momentum,
    master_weights,
    vector_grads,
    vector_momentum,
    vector_params,
):
    nmat, rows, n = gradients.shape[1:]
    rank = right_init.shape[2]
    unit = rank * nmat // (CORES * lax.axis_size("mp"))
    n_mp = lax.axis_size("mp")
    n_z = lax.axis_size("replica") // CORES
    capacity, replica_rows = momentum.shape[1:3]
    p = lax.axis_index("mp")
    r = lax.axis_index("replica")
    core, z = r % CORES, r // CORES
    upm = CORES * n_mp // nmat
    half = nmat // CORES
    code = core * n_mp + p
    first = r * replica_rows

    places_of = [code // upm, code % upm, core, r, z, p, first % rows // replica_rows, first // rows ^ p]
    pos = jnp.stack(places_of).astype(jnp.int32)
    in_hbm = lambda x: pltpu.with_memory_space_constraint(x, pltpu.HBM)

    square = n_mp == 4 and capacity == 2 and replica_rows % 96 == 0
    base, states, firsts = base_of(pos, in_hbm(momentum), in_hbm(master_weights), square)
    firsts = firsts or [base] * (n_mp - 1)
    early = [exchange(part, "mp", d) for d, part in enumerate(firsts, 1)]

    nvec = vector_grads.shape[1]
    comp, near, far = left_terms(
        pos,
        in_hbm(gradients),
        in_hbm(feedback),
        in_hbm(jnp.swapaxes(right_init, 1, 2)),
        vector_grads,
    )
    piece = add([near, exchange(far, "replica", 1)], BF16)
    along_z = lambda x: [exchange(x, "replica", CORES * d) for d in range(1, n_z)]
    piece = add([piece] + along_z(piece), F32)
    near, far = piece, exchange(piece, "replica", 1)

    send, keep, lt, left, vector_rows = right_terms(pos, near, far, gram_root, comp, upm, [])
    vector_total = vector_rows.reshape(-1)[:nvec]
    recv = exchange(send, "replica", 1)
    own, strip, *chip = chip_sum(pos, keep, recv, lt, replica_rows, [token([keep] + early)])
    plane = [exchange(part, "mp", d) for d, part in enumerate(chip, 1)]
    *final, mine = plane_sum(pos, own, strip, plane, n_z, nmat, rank)
    late = []
    if square:
        late = [exchange(part, "mp", d) for d, part in enumerate(forward(*early, base, mine), 1)]
    final = [final[0]] + [exchange(final[d], "replica", CORES * d) for d in range(1, n_z)]
    final = add(final, BF16)
    new_vector_momentum = 0.9 * vector_momentum + vector_total
    new_vector_params = vector_params - 0.1 * new_vector_momentum

    whole = stack([final] + along_z(final), late + [new_vector_params])
    others = [exchange(whole, "mp", d) for d in range(1, n_mp)]
    slots = collect(square, n_mp, base, early + late)
    common = (pos, owners, comp, left, mine, slots, capacity)
    shape = (half, upm) + whole.shape
    done, near_jobs, after = (), {(0, j): (0, j) for j in range(half)}, [slots]
    if upm == 1:
        *done, after = outputs(*common, [whole[None, None]], {(0, 0): (0, 0)})
        after = [after]
        del near_jobs[0, 0]
    near = stack([whole] + others, after).reshape(shape)
    far = exchange(near, "replica", 1)
    far_jobs = {(1, j): (1, j) for j in range(half)}
    where = {(0, j): (0, j) for j in range(half)} | far_jobs
    *done, _ = outputs(*common, [near], near_jobs, earlier=done)
    new_feedback, new_weights, new_momentum, new_master, _ = outputs(
        *common, [near, far], far_jobs, where, states, done
    )
    return new_feedback, new_momentum, new_master, new_weights, new_vector_momentum, new_vector_params


def solution(mesh):
    return jax.shard_map(
        per_device,
        mesh=mesh,
        in_specs=(
            P("replica", None, "mp", None),
            P("replica", None, "mp", None),
            P(),
            P(),
            P(),
            P("mp", None, "replica", None),
            P("mp", None, "replica", None),
            P("replica", "mp"),
            P("mp"),
            P("mp"),
        ),
        out_specs=(
            P("replica", None, "mp", None),
            P("mp", None, "replica", None),
            P("mp", None, "replica", None),
            P(None, "replica", None),
            P("mp"),
            P("mp"),
        ),
        check_vma=False,
    )
```

```python
import functools

import jax
import jax.numpy as jnp
from jax import lax
from jax.experimental import pallas as pl
from jax.experimental.pallas import tpu as pltpu
from jax.sharding import PartitionSpec as P

CORES = 2
BASE_ROWS = 48
F32 = jnp.float32
BF16 = jnp.bfloat16


def params(mib=12):
    return pltpu.CompilerParams(vmem_limit_bytes=mib * 1024 * 1024)


def cost(flops=1000, bytes_accessed=1000):
    return pl.CostEstimate(flops=flops, bytes_accessed=bytes_accessed, transcendentals=0)


def tree_sum(terms):
    while len(terms) > 1:
        terms = [terms[i] + terms[i + 1] for i in range(0, len(terms), 2)]
    return terms[0]


def exchange(x, axis, distance):
    size = lax.axis_size(axis)
    return lax.ppermute(x, axis, [(i, i ^ distance) for i in range(size)])


def left_kernel(pos, g_ref, f_ref, q_ref, vec_ref, comp_ref, near_ref, far_ref, total, feedback, right, terms, sems):
    nmat, rows, _ = comp_ref.shape
    rank = q_ref.shape[1]
    part = near_ref.shape[0]

    def copies(k):
        return [
            pltpu.make_async_copy(g_ref.at[0, k], comp_ref.at[k], sems.at[k, 0]),
            pltpu.make_async_copy(f_ref.at[0, k], feedback.at[k], sems.at[k, 1]),
            pltpu.make_async_copy(q_ref.at[k], right.at[k], sems.at[k, 2]),
        ]

    @pl.loop(0, nmat)
    def _(k):
        for copy in copies(k):
            copy.start()

    total[...] = jnp.zeros(total.shape, F32)
    width, nvec = total.shape[1], vec_ref.shape[1]
    for i, first in enumerate(range(0, nvec, width)):
        count = min(width, nvec - first)
        total[rows + i : rows + i + 1, :count] = vec_ref[:, first : first + count]

    @pl.loop(0, nmat)
    def _(k):
        for copy in copies(k):
            copy.wait()
        comp = comp_ref[k] + feedback[k]
        comp_ref[k] = comp
        terms[k] = lax.dot_general(
            comp, right[k], (((1,), (1,)), ((), ())), preferred_element_type=F32
        )

    for k in range(nmat):
        total[:rows, k * rank : (k + 1) * rank] = terms[k]
    for ref, core in ((near_ref, pos[2]), (far_ref, 1 - pos[2])):
        ref[...] = total[pl.ds(pl.multiple_of(core * part, 16), part), :]


def left_terms(pos, gradients, feedback, right_t, vec):
    _, nmat, rows, n = gradients.shape
    rank = right_t.shape[1]
    width = nmat * rank
    total = rows + -(-vec.shape[1] // width)
    total += -total % (16 * CORES)
    part = jax.ShapeDtypeStruct((total // CORES, width), F32)
    vmem = pl.BlockSpec(memory_space=pltpu.VMEM)
    any_spec = pl.BlockSpec(memory_space=pl.ANY)
    return pl.pallas_call(
        left_kernel,
        grid_spec=pltpu.PrefetchScalarGridSpec(
            num_scalar_prefetch=1,
            grid=(1,),
            in_specs=[any_spec] * 3 + [vmem],
            out_specs=[vmem] * 3,
            scratch_shapes=[
                pltpu.VMEM((total, width), F32),
                pltpu.VMEM((nmat, rows, n), BF16),
                pltpu.VMEM((nmat, rank, n), BF16),
                pltpu.VMEM((nmat, rows, rank), F32),
                pltpu.SemaphoreType.DMA((nmat, 3)),
            ],
        ),
        out_shape=[jax.ShapeDtypeStruct((nmat, rows, n), BF16), part, part],
        compiler_params=params(20),
        cost_estimate=cost(),
        name="left_terms",
    )(pos, gradients, feedback, right_t, vec)


def add_kernel(*refs):
    out = refs[-1]
    out[...] = tree_sum([ref[...].astype(F32) for ref in refs[:-1]]).astype(out.dtype)


def add(parts, dtype):
    vmem = pl.BlockSpec(memory_space=pltpu.VMEM)
    return pl.pallas_call(
        add_kernel,
        in_specs=[vmem] * len(parts),
        out_specs=vmem,
        out_shape=jax.ShapeDtypeStruct(parts[0].shape, dtype),
        compiler_params=params(),
        cost_estimate=cost(),
        name="add",
    )(*parts)


def send_kernel(half, pos, near_ref, far_ref, gram_ref, comp_ref, send_ref, lt_ref, left_ref, vec_ref, left, gram):
    nmat, rows, _ = comp_ref.shape
    rank = gram_ref.shape[1]
    part = near_ref.shape[0]
    for ref, core in ((near_ref, pos[2]), (far_ref, 1 - pos[2])):
        left[pl.ds(pl.multiple_of(core * part, 16), part), :] = ref[...]
    vec_ref[...] = left[rows:, :]
    gram[...] = jnp.zeros(gram.shape, F32)
    for i in range(nmat):
        gram[i * rank : (i + 1) * rank, i * rank : (i + 1) * rank] = gram_ref[i]
    hat = jnp.dot(
        left[:rows, :], gram[...], precision=lax.Precision.HIGHEST, preferred_element_type=F32
    )
    lt_ref[...] = hat.T.astype(BF16)
    for i in range(nmat):
        left_ref[i] = hat[:, i * rank : (i + 1) * rank].astype(BF16)
    right_rows(half, pos, lt_ref, comp_ref, send_ref)


def right_rows(start, pos, lt_ref, comp_ref, out_ref):
    half, upm, unit, _ = out_ref.shape
    for t in range(half):
        k = (t + start) ^ pos[0]
        rows = pl.ds(pl.multiple_of(k * upm * unit, upm * unit), upm * unit)
        terms = jnp.dot(lt_ref[rows, :], comp_ref[k], preferred_element_type=F32)
        for i in range(upm):
            out_ref[t, i ^ pos[1]] = terms[i * unit : (i + 1) * unit].astype(out_ref.dtype)


def keep_kernel(pos, lt_ref, comp_ref, *refs):
    right_rows(0, pos, lt_ref, comp_ref, refs[-1])


def right_terms(pos, near, far, gram, comp, upm, after):
    nmat, rows, n = comp.shape
    rank = gram.shape[1]
    width = nmat * rank
    half = nmat // CORES
    total = CORES * near.shape[0]
    shape = (half, upm, rank // upm, n)
    vmem = pl.BlockSpec(memory_space=pltpu.VMEM)
    send, lt, left, vec = pl.pallas_call(
        functools.partial(send_kernel, half),
        grid_spec=pltpu.PrefetchScalarGridSpec(
            num_scalar_prefetch=1,
            grid=(1,),
            in_specs=[vmem] * 4,
            out_specs=[vmem] * 4,
            scratch_shapes=[pltpu.VMEM((total, width), F32), pltpu.VMEM((width, width), F32)],
        ),
        out_shape=[
            jax.ShapeDtypeStruct(shape, BF16),
            jax.ShapeDtypeStruct((width, rows), BF16),
            jax.ShapeDtypeStruct((nmat, rows, rank), BF16),
            jax.ShapeDtypeStruct((total - rows, width), F32),
        ],
        compiler_params=params(),
        cost_estimate=cost(),
        name="right_send",
    )(pos, near, far, gram, comp)
    keep = pl.pallas_call(
        keep_kernel,
        grid_spec=pltpu.PrefetchScalarGridSpec(
            num_scalar_prefetch=1,
            grid=(1,),
            in_specs=[vmem, vmem] + [pl.BlockSpec(memory_space=pl.ANY)] * len(after),
            out_specs=vmem,
        ),
        out_shape=jax.ShapeDtypeStruct(shape, F32),
        compiler_params=params(),
        cost_estimate=cost(),
        name="right_keep",
    )(pos, lt, comp, *after)
    return send, keep, lt, left, vec


def chip_kernel(replica_rows, pos, keep_ref, recv_ref, lt_ref, *refs):
    upm = keep_ref.shape[1]
    own_ref, strip_ref, *sends = refs[-(keep_ref.shape[0] * upm + 1) :]
    left = lt_ref[...].astype(F32).T
    strip = left[:replica_rows]
    for i in range(1, left.shape[0] // replica_rows):
        strip = jnp.where(pos[6] == i, left[i * replica_rows : (i + 1) * replica_rows], strip)
    height = strip_ref.shape[0]
    strip = jnp.concatenate(
        [strip[i * height : (i + 1) * height] for i in range(replica_rows // height)], axis=1
    )
    strip_ref[...] = strip
    own_ref[...] = keep_ref[0, 0] + recv_ref[0, 0].astype(F32)
    for d, out in enumerate(sends, 1):
        j, i = d // upm, d % upm
        terms = keep_ref[j, i] + recv_ref[j, i].astype(F32)
        out[...] = jnp.concatenate([terms, strip], axis=0).astype(BF16)


def chip_sum(pos, keep, recv, lt, replica_rows, after):
    half, upm, unit, n = keep.shape
    height = lt.shape[0] * replica_rows // n
    vmem = pl.BlockSpec(memory_space=pltpu.VMEM)
    outs = [jax.ShapeDtypeStruct((unit, n), F32), jax.ShapeDtypeStruct((height, n), F32)]
    outs += [jax.ShapeDtypeStruct((unit + height, n), BF16)] * (half * upm - 1)
    return pl.pallas_call(
        functools.partial(chip_kernel, replica_rows),
        grid_spec=pltpu.PrefetchScalarGridSpec(
            num_scalar_prefetch=1,
            grid=(1,),
            in_specs=[vmem] * 3 + [pl.BlockSpec(memory_space=pl.ANY)] * len(after),
            out_specs=[vmem] * len(outs),
        ),
        out_shape=outs,
        compiler_params=params(),
        cost_estimate=cost(),
        name="chip_sum",
    )(pos, keep, recv, lt, *after)


def plane_kernel(pos, own_ref, strip_ref, *refs):
    n_z = own_ref.shape[1] // refs[-2].shape[1]
    terms, outs, left_ref = refs[: -n_z - 1], refs[-n_z - 1 : -1], refs[-1]
    unit, n = own_ref.shape
    cols = n // n_z
    for d, out in enumerate(outs):
        block = pl.ds(pl.multiple_of((pos[4] ^ d) * cols, cols), cols)
        parts = [own_ref[:, block]] + [term[:, block].astype(F32)[:unit] for term in terms]
        out[...] = tree_sum(parts).astype(out.dtype)
    strip = strip_ref[...]
    for d, term in enumerate(terms, 1):
        strip = jnp.where(pos[7] == d, term[...].astype(F32)[unit:], strip)
    nmat, _, rank = left_ref.shape
    width = nmat * rank
    rows = [strip[:, i * width : (i + 1) * width] for i in range(n // width)]
    rows = jnp.concatenate(rows, axis=0).astype(BF16)
    for i in range(nmat):
        left_ref[i] = rows[:, i * rank : (i + 1) * rank]


def plane_sum(pos, own, strip, terms, n_z, nmat, rank):
    unit, n = own.shape
    count = strip.size // (nmat * rank)
    outs = [jax.ShapeDtypeStruct((unit, n // n_z), BF16 if d else F32) for d in range(n_z)]
    outs.append(jax.ShapeDtypeStruct((nmat, count, rank), BF16))
    vmem = pl.BlockSpec(memory_space=pltpu.VMEM)
    return pl.pallas_call(
        plane_kernel,
        grid_spec=pltpu.PrefetchScalarGridSpec(
            num_scalar_prefetch=1,
            grid=(1,),
            in_specs=[vmem] * (2 + len(terms)),
            out_specs=[vmem] * len(outs),
        ),
        out_shape=outs,
        compiler_params=params(),
        cost_estimate=cost(),
        name="plane_sum",
    )(pos, own, strip, *terms)


def stack_kernel(count, *refs):
    for i in range(count):
        refs[-1][i] = refs[i][...]


def stack(parts, after=()):
    vmem = pl.BlockSpec(memory_space=pltpu.VMEM)
    return pl.pallas_call(
        functools.partial(stack_kernel, len(parts)),
        in_specs=[vmem] * len(parts) + [pl.BlockSpec(memory_space=pl.ANY)] * len(after),
        out_specs=vmem,
        out_shape=jax.ShapeDtypeStruct((len(parts),) + parts[0].shape, parts[0].dtype),
        compiler_params=params(),
        cost_estimate=cost(),
        name="stack",
    )(*parts, *after)


def token_kernel(*refs):
    refs[-1][...] = jnp.zeros(refs[-1].shape, F32)


def token(after):
    return pl.pallas_call(
        token_kernel,
        in_specs=[pl.BlockSpec(memory_space=pl.ANY)] * len(after),
        out_specs=pl.BlockSpec(memory_space=pltpu.VMEM),
        out_shape=jax.ShapeDtypeStruct((8, 128), F32),
        compiler_params=params(),
        cost_estimate=cost(),
        name="token",
    )(*after)


def forward_kernel(later, x_ref, y_ref, base_ref, after_ref, *outs):
    rows = base_ref.shape[1]
    for source, slot, out in ((y_ref, 1, outs[0]), (x_ref, 0, outs[1])):
        out[:rows] = source[:rows]
        out[rows:] = base_ref[slot, rows - later :]


def forward(x, y, base, after):
    _, rows, n = base.shape
    later = 2 * rows - x.shape[0]
    vmem = pl.BlockSpec(memory_space=pltpu.VMEM)
    return pl.pallas_call(
        functools.partial(forward_kernel, later),
        in_specs=[vmem] * 3 + [pl.BlockSpec(memory_space=pl.ANY)],
        out_specs=[vmem] * 2,
        out_shape=[jax.ShapeDtypeStruct((rows + later, n), BF16)] * 2,
        compiler_params=params(),
        cost_estimate=cost(),
        name="forward",
    )(x, y, base, after)


def rank_of(owners, k):
    count = jnp.int32(0)
    for j in range(owners.shape[0]):
        count += jnp.where((owners[j] == owners[k]) & (j < k), 1, 0)
    return count


def collect_kernel(square, base_ref, *refs):
    out = refs[-1]
    capacity, rows, _ = base_ref.shape
    out[:capacity] = base_ref[...]
    if not square:
        for d, ref in enumerate(refs[:-1], 1):
            out[d * capacity : (d + 1) * capacity] = ref[...]
        return
    x, y, more_x, more_y = refs[:-1]
    early = x.shape[0] - rows
    for d, slot, first, second in ((1, 0, x, more_x), (2, 1, y, more_y)):
        out[d * capacity + slot] = first[:rows]
        out[d * capacity + 1 - slot, :early] = first[rows:]
        out[d * capacity + 1 - slot, early:] = second[rows:]
    out[3 * capacity] = more_y[:rows]
    out[3 * capacity + 1] = more_x[:rows]


def collect(square, n_mp, base, parts):
    capacity, rows, n = base.shape
    vmem = pl.BlockSpec(memory_space=pltpu.VMEM)
    return pl.pallas_call(
        functools.partial(collect_kernel, square),
        in_specs=[vmem] * (1 + len(parts)),
        out_specs=vmem,
        out_shape=jax.ShapeDtypeStruct((n_mp * capacity, rows, n), BF16),
        compiler_params=params(),
        cost_estimate=cost(),
        name="collect",
    )(base, *parts)


def outputs_kernel(jobs, where, capacity, pos, owners, comp_ref, left_ref, strip_ref, base_ref, *refs):
    n_right = 1 + max(a for a, _ in (where or jobs).values())
    rights, refs = refs[:n_right], refs[n_right:]
    n_scratch = 6 if where else 3
    scratch = refs[-n_scratch:]
    feedback, weights, out_sem = scratch[:3]
    refs = refs[:-n_scratch]
    token_ref, outs = refs[-1], refs[-5:-1] if where else refs[-3:-1]
    token_ref[...] = jnp.zeros(token_ref.shape, F32)
    _, upm, n_z, _, cols = rights[0].shape
    half = comp_ref.shape[0] // CORES

    def right_of(place, d, block):
        a, entry = place
        parts = [rights[a][entry, i ^ pos[1], d, :, block] for i in range(upm)]
        return parts[0] if upm == 1 else jnp.concatenate(parts, axis=0)

    def columns(d, first=0, size=cols):
        return pl.ds(pl.multiple_of((pos[4] ^ d) * cols + first, 128), size)

    def matrix(other, j):
        return (j + half * other) ^ pos[0]

    step = 256 if cols % 256 == 0 else 128
    pieces = [slice(first, first + step) for first in range(0, cols, step)]
    stores = []

    def store(source, target, sem):
        stores.append(pltpu.make_async_copy(source, target, sem))
        stores[-1].start()

    if where:
        momentum_ref, master_ref = refs[:2]
        new_momentum, new_master, state_sem = scratch[3:]
        for c in range(capacity):
            mine = jnp.int32(-1)
            for k in range(owners.shape[0]):
                mine = jnp.where((owners[k] == pos[5]) & (rank_of(owners, k) == c), k, mine)
            safe = jnp.maximum(mine, 0)
            strip = strip_ref[safe]
            for d in range(n_z):
                for block in pieces:
                    right = jnp.zeros((strip.shape[1], step), BF16)
                    for job, place in where.items():
                        right = jnp.where(safe == matrix(*job), right_of(place, d, block), right)
                    approx = jnp.dot(strip, right, preferred_element_type=F32)
                    approx = jnp.where(mine >= 0, approx, 0.0)
                    place = columns(d, block.start, step)
                    momentum = 0.9 * momentum_ref[c, :, place] + approx
                    new_momentum[c, :, place] = momentum
                    new_master[c, :, place] = master_ref[c, :, place] - 0.1 * momentum
                place = columns(d)
                for i, new in enumerate((new_momentum, new_master)):
                    store(
                        new.at[c, :, place], outs[2 + i].at[0, c, :, place], state_sem.at[i, c, d]
                    )

    for i, (job, where_right) in enumerate(jobs.items()):
        k = matrix(*job)
        slot = (owners[k] ^ pos[5]) * capacity + rank_of(owners, k)
        left = jnp.concatenate([left_ref[k], strip_ref[k]], axis=0)
        rows = left_ref.shape[1]
        for d in range(n_z):
            for block in pieces:
                right = right_of(where_right, d, block)
                place = columns(d, block.start, step)
                approx = jnp.dot(left, right, preferred_element_type=F32)
                comp, base = comp_ref[k, :, place].astype(F32), base_ref[slot, :, place].astype(F32)
                feedback[i, :, place] = (comp - approx[:rows]).astype(BF16)
                weights[i, :, place] = (base - 0.1 * approx[rows:]).astype(BF16)
            place = columns(d)
            store(feedback.at[i, :, place], outs[0].at[0, k, :, place], out_sem.at[i, d, 0])
            store(weights.at[i, :, place], outs[1].at[k, :, place], out_sem.at[i, d, 1])

    for copy in stores:
        copy.wait()


def outputs(pos, owners, comp, left, strip, base, capacity, rights, jobs, where=None, states=(), earlier=()):
    nmat, rows, n = comp.shape
    n_z = rights[0].shape[2]
    replica_rows = base.shape[1]
    any_spec = pl.BlockSpec(memory_space=pl.ANY)
    vmem = pl.BlockSpec(memory_space=pltpu.VMEM)
    scratch = [
        pltpu.VMEM((len(jobs), rows, n), BF16),
        pltpu.VMEM((len(jobs), replica_rows, n), BF16),
        pltpu.SemaphoreType.DMA((len(jobs), n_z, 2)),
    ]
    if states:
        scratch += [pltpu.VMEM((capacity, replica_rows, n), F32)] * 2
        scratch += [pltpu.SemaphoreType.DMA((2, capacity, n_z))]
    outs = [
        jax.ShapeDtypeStruct((1, nmat, rows, n), BF16),
        jax.ShapeDtypeStruct((nmat, replica_rows, n), BF16),
    ] + [jax.ShapeDtypeStruct((1,) + x.shape, F32) for x in states]
    first = 6 + len(rights) + len(states)
    return pl.pallas_call(
        functools.partial(outputs_kernel, jobs, where, capacity),
        grid_spec=pltpu.PrefetchScalarGridSpec(
            num_scalar_prefetch=2,
            grid=(1,),
            in_specs=[vmem] * (4 + len(rights) + len(states)) + [any_spec] * len(earlier),
            out_specs=[any_spec] * len(outs) + [vmem],
            scratch_shapes=scratch,
        ),
        out_shape=outs + [jax.ShapeDtypeStruct((8, 128), F32)],
        input_output_aliases={first + i: i for i in range(len(earlier))},
        compiler_params=params(24),
        cost_estimate=cost(),
        name="outputs",
    )(pos, owners, comp, left, strip, base, *rights, *states, *earlier)


def base_kernel(pos, momentum_ref, master_ref, out_ref, momentum, master, *refs):
    firsts, sems = refs[:-1], refs[-1]
    capacity, rows, _ = out_ref.shape
    blocks = [(c, first) for c in range(capacity) for first in range(0, rows, BASE_ROWS)]

    def copies(i):
        c, first = blocks[i]
        part = pl.ds(first, BASE_ROWS)
        return [
            pltpu.make_async_copy(source.at[0, c, part], target.at[c, part], sems.at[j, i])
            for j, (source, target) in enumerate(((momentum_ref, momentum), (master_ref, master)))
        ]

    for i in range(len(blocks)):
        for copy in copies(i):
            copy.start()
    for i, (c, first) in enumerate(blocks):
        for copy in copies(i):
            copy.wait()
        part = slice(first, first + BASE_ROWS)
        out_ref[c, part] = (master[c, part] - 0.09 * momentum[c, part]).astype(BF16)
    for slot, ref in enumerate(firsts):
        ref[:rows] = out_ref[slot]
        ref[rows:] = out_ref[1 - slot, : ref.shape[0] - rows]


def base_of(pos, momentum, master, square):
    _, capacity, rows, n = momentum.shape
    state = jax.ShapeDtypeStruct((capacity, rows, n), F32)
    base = jax.ShapeDtypeStruct((capacity, rows, n), BF16)
    firsts = [jax.ShapeDtypeStruct((rows + 5 * rows // 6, n), BF16)] * (2 if square else 0)
    base, momentum, master, *firsts = pl.pallas_call(
        base_kernel,
        grid_spec=pltpu.PrefetchScalarGridSpec(
            num_scalar_prefetch=1,
            grid=(1,),
            in_specs=[pl.BlockSpec(memory_space=pl.ANY)] * 2,
            out_specs=[pl.BlockSpec(memory_space=pltpu.VMEM)] * (3 + len(firsts)),
            scratch_shapes=[pltpu.SemaphoreType.DMA((2, capacity * rows // BASE_ROWS))],
        ),
        out_shape=[base, state, state] + firsts,
        compiler_params=params(),
        cost_estimate=cost(),
        name="base",
    )(pos, momentum, master)
    return base, (momentum, master), firsts


def per_device(
    gradients,
    feedback,
    right_init,
    gram_root,
    owners,
    momentum,
    master_weights,
    vector_grads,
    vector_momentum,
    vector_params,
):
    nmat, rows, n = gradients.shape[1:]
    rank = right_init.shape[2]
    unit = rank * nmat // (CORES * lax.axis_size("mp"))
    n_mp = lax.axis_size("mp")
    n_z = lax.axis_size("replica") // CORES
    capacity, replica_rows = momentum.shape[1:3]
    p = lax.axis_index("mp")
    r = lax.axis_index("replica")
    core, z = r % CORES, r // CORES
    upm = CORES * n_mp // nmat
    half = nmat // CORES
    code = core * n_mp + p
    first = r * replica_rows

    places_of = [code // upm, code % upm, core, r, z, p, first % rows // replica_rows, first // rows ^ p]
    pos = jnp.stack(places_of).astype(jnp.int32)
    in_hbm = lambda x: pltpu.with_memory_space_constraint(x, pltpu.HBM)

    square = n_mp == 4 and capacity == 2 and replica_rows % 96 == 0
    base, states, firsts = base_of(pos, in_hbm(momentum), in_hbm(master_weights), square)
    firsts = firsts or [base] * (n_mp - 1)
    early = [exchange(part, "mp", d) for d, part in enumerate(firsts, 1)]

    nvec = vector_grads.shape[1]
    comp, near, far = left_terms(
        pos,
        in_hbm(gradients),
        in_hbm(feedback),
        in_hbm(jnp.swapaxes(right_init, 1, 2)),
        vector_grads,
    )
    piece = add([near, exchange(far, "replica", 1)], BF16)
    along_z = lambda x: [exchange(x, "replica", CORES * d) for d in range(1, n_z)]
    piece = add([piece] + along_z(piece), F32)
    near, far = piece, exchange(piece, "replica", 1)

    send, keep, lt, left, vector_rows = right_terms(pos, near, far, gram_root, comp, upm, [])
    vector_total = vector_rows.reshape(-1)[:nvec]
    recv = exchange(send, "replica", 1)
    own, strip, *chip = chip_sum(pos, keep, recv, lt, replica_rows, [token([keep] + early)])
    plane = [exchange(part, "mp", d) for d, part in enumerate(chip, 1)]
    *final, mine = plane_sum(pos, own, strip, plane, n_z, nmat, rank)
    late = []
    if square:
        late = [exchange(part, "mp", d) for d, part in enumerate(forward(*early, base, mine), 1)]
    final = [final[0]] + [exchange(final[d], "replica", CORES * d) for d in range(1, n_z)]
    final = add(final, BF16)
    new_vector_momentum = 0.9 * vector_momentum + vector_total
    new_vector_params = vector_params - 0.1 * new_vector_momentum

    whole = stack([final] + along_z(final), late + [new_vector_params])
    others = [exchange(whole, "mp", d) for d in range(1, n_mp)]
    slots = collect(square, n_mp, base, early + late)
    common = (pos, owners, comp, left, mine, slots, capacity)
    shape = (half, upm) + whole.shape
    done, near_jobs, after = (), {(0, j): (0, j) for j in range(half)}, [slots]
    if upm == 1:
        *done, _ = outputs(*common, [whole[None, None]], {(0, 0): (0, 0)})
        *done, after = outputs(
            *common, [others[-1][None, None]], {(0, half - 1): (0, 0)}, earlier=done
        )
        after = [after]
        del near_jobs[0, 0], near_jobs[0, half - 1]
    near = stack([whole] + others, after).reshape(shape)
    far = exchange(near, "replica", 1)
    far_jobs = {(1, j): (1, j) for j in range(half)}
    where = {(0, j): (0, j) for j in range(half)} | far_jobs
    *done, _ = outputs(*common, [near], near_jobs, earlier=done)
    new_feedback, new_weights, new_momentum, new_master, _ = outputs(
        *common, [near, far], far_jobs, where, states, done
    )
    return new_feedback, new_momentum, new_master, new_weights, new_vector_momentum, new_vector_params


def solution(mesh):
    return jax.shard_map(
        per_device,
        mesh=mesh,
        in_specs=(
            P("replica", None, "mp", None),
            P("replica", None, "mp", None),
            P(),
            P(),
            P(),
            P("mp", None, "replica", None),
            P("mp", None, "replica", None),
            P("replica", "mp"),
            P("mp"),
            P("mp"),
        ),
        out_specs=(
            P("replica", None, "mp", None),
            P("mp", None, "replica", None),
            P("mp", None, "replica", None),
            P(None, "replica", None),
            P("mp"),
            P("mp"),
        ),
        check_vma=False,
    )
```

```python
import functools

import jax
import jax.numpy as jnp
from jax import lax
from jax.experimental import pallas as pl
from jax.experimental.pallas import tpu as pltpu
from jax.sharding import PartitionSpec as P

CORES = 2
BASE_ROWS = 48
F32 = jnp.float32
BF16 = jnp.bfloat16


def params(mib=12):
    return pltpu.CompilerParams(vmem_limit_bytes=mib * 1024 * 1024)


def cost(flops=1000, bytes_accessed=1000):
    return pl.CostEstimate(flops=flops, bytes_accessed=bytes_accessed, transcendentals=0)


def tree_sum(terms):
    while len(terms) > 1:
        terms = [terms[i] + terms[i + 1] for i in range(0, len(terms), 2)]
    return terms[0]


def exchange(x, axis, distance):
    size = lax.axis_size(axis)
    return lax.ppermute(x, axis, [(i, i ^ distance) for i in range(size)])


def left_kernel(pos, g_ref, f_ref, q_ref, vec_ref, comp_ref, near_ref, far_ref, total, feedback, right, terms, sems):
    nmat, rows, _ = comp_ref.shape
    rank = q_ref.shape[1]
    part = near_ref.shape[0]

    def copies(k):
        return [
            pltpu.make_async_copy(g_ref.at[0, k], comp_ref.at[k], sems.at[k, 0]),
            pltpu.make_async_copy(f_ref.at[0, k], feedback.at[k], sems.at[k, 1]),
            pltpu.make_async_copy(q_ref.at[k], right.at[k], sems.at[k, 2]),
        ]

    @pl.loop(0, nmat)
    def _(k):
        for copy in copies(k):
            copy.start()

    total[...] = jnp.zeros(total.shape, F32)
    width, nvec = total.shape[1], vec_ref.shape[1]
    for i, first in enumerate(range(0, nvec, width)):
        count = min(width, nvec - first)
        total[rows + i : rows + i + 1, :count] = vec_ref[:, first : first + count]

    @pl.loop(0, nmat)
    def _(k):
        for copy in copies(k):
            copy.wait()
        comp = comp_ref[k] + feedback[k]
        comp_ref[k] = comp
        terms[k] = lax.dot_general(
            comp, right[k], (((1,), (1,)), ((), ())), preferred_element_type=F32
        )

    for k in range(nmat):
        total[:rows, k * rank : (k + 1) * rank] = terms[k]
    for ref, core in ((near_ref, pos[2]), (far_ref, 1 - pos[2])):
        ref[...] = total[pl.ds(pl.multiple_of(core * part, 16), part), :]


def left_terms(pos, gradients, feedback, right_t, vec):
    _, nmat, rows, n = gradients.shape
    rank = right_t.shape[1]
    width = nmat * rank
    total = rows + -(-vec.shape[1] // width)
    total += -total % (16 * CORES)
    part = jax.ShapeDtypeStruct((total // CORES, width), F32)
    vmem = pl.BlockSpec(memory_space=pltpu.VMEM)
    any_spec = pl.BlockSpec(memory_space=pl.ANY)
    return pl.pallas_call(
        left_kernel,
        grid_spec=pltpu.PrefetchScalarGridSpec(
            num_scalar_prefetch=1,
            grid=(1,),
            in_specs=[any_spec] * 3 + [vmem],
            out_specs=[vmem] * 3,
            scratch_shapes=[
                pltpu.VMEM((total, width), F32),
                pltpu.VMEM((nmat, rows, n), BF16),
                pltpu.VMEM((nmat, rank, n), BF16),
                pltpu.VMEM((nmat, rows, rank), F32),
                pltpu.SemaphoreType.DMA((nmat, 3)),
            ],
        ),
        out_shape=[jax.ShapeDtypeStruct((nmat, rows, n), BF16), part, part],
        compiler_params=params(20),
        cost_estimate=cost(),
        name="left_terms",
    )(pos, gradients, feedback, right_t, vec)


def add_kernel(*refs):
    out = refs[-1]
    out[...] = tree_sum([ref[...].astype(F32) for ref in refs[:-1]]).astype(out.dtype)


def add(parts, dtype):
    vmem = pl.BlockSpec(memory_space=pltpu.VMEM)
    return pl.pallas_call(
        add_kernel,
        in_specs=[vmem] * len(parts),
        out_specs=vmem,
        out_shape=jax.ShapeDtypeStruct(parts[0].shape, dtype),
        compiler_params=params(),
        cost_estimate=cost(),
        name="add",
    )(*parts)


def send_kernel(half, pos, near_ref, far_ref, gram_ref, comp_ref, send_ref, lt_ref, left_ref, vec_ref, left, gram):
    nmat, rows, _ = comp_ref.shape
    rank = gram_ref.shape[1]
    part = near_ref.shape[0]
    for ref, core in ((near_ref, pos[2]), (far_ref, 1 - pos[2])):
        left[pl.ds(pl.multiple_of(core * part, 16), part), :] = ref[...]
    vec_ref[...] = left[rows:, :]
    gram[...] = jnp.zeros(gram.shape, F32)
    for i in range(nmat):
        gram[i * rank : (i + 1) * rank, i * rank : (i + 1) * rank] = gram_ref[i]
    hat = jnp.dot(
        left[:rows, :], gram[...], precision=lax.Precision.HIGHEST, preferred_element_type=F32
    )
    lt_ref[...] = hat.T.astype(BF16)
    for i in range(nmat):
        left_ref[i] = hat[:, i * rank : (i + 1) * rank].astype(BF16)
    right_rows(half, pos, lt_ref, comp_ref, send_ref)


def right_rows(start, pos, lt_ref, comp_ref, out_ref):
    half, upm, unit, _ = out_ref.shape

    @pl.loop(0, half)
    def _(t):
        k = (t + start) ^ pos[0]
        rows = pl.ds(pl.multiple_of(k * upm * unit, upm * unit), upm * unit)
        terms = jnp.dot(lt_ref[rows, :], comp_ref[k], preferred_element_type=F32)
        for i in range(upm):
            out_ref[t, i ^ pos[1]] = terms[i * unit : (i + 1) * unit].astype(out_ref.dtype)


def keep_kernel(pos, lt_ref, comp_ref, *refs):
    right_rows(0, pos, lt_ref, comp_ref, refs[-1])


def right_terms(pos, near, far, gram, comp, upm, after):
    nmat, rows, n = comp.shape
    rank = gram.shape[1]
    width = nmat * rank
    half = nmat // CORES
    total = CORES * near.shape[0]
    shape = (half, upm, rank // upm, n)
    vmem = pl.BlockSpec(memory_space=pltpu.VMEM)
    send, lt, left, vec = pl.pallas_call(
        functools.partial(send_kernel, half),
        grid_spec=pltpu.PrefetchScalarGridSpec(
            num_scalar_prefetch=1,
            grid=(1,),
            in_specs=[vmem] * 4,
            out_specs=[vmem] * 4,
            scratch_shapes=[pltpu.VMEM((total, width), F32), pltpu.VMEM((width, width), F32)],
        ),
        out_shape=[
            jax.ShapeDtypeStruct(shape, BF16),
            jax.ShapeDtypeStruct((width, rows), BF16),
            jax.ShapeDtypeStruct((nmat, rows, rank), BF16),
            jax.ShapeDtypeStruct((total - rows, width), F32),
        ],
        compiler_params=params(),
        cost_estimate=cost(),
        name="right_send",
    )(pos, near, far, gram, comp)
    keep = pl.pallas_call(
        keep_kernel,
        grid_spec=pltpu.PrefetchScalarGridSpec(
            num_scalar_prefetch=1,
            grid=(1,),
            in_specs=[vmem, vmem] + [pl.BlockSpec(memory_space=pl.ANY)] * len(after),
            out_specs=vmem,
        ),
        out_shape=jax.ShapeDtypeStruct(shape, F32),
        compiler_params=params(),
        cost_estimate=cost(),
        name="right_keep",
    )(pos, lt, comp, *after)
    return send, keep, lt, left, vec


def chip_kernel(replica_rows, pos, keep_ref, recv_ref, lt_ref, *refs):
    upm = keep_ref.shape[1]
    own_ref, strip_ref, *sends = refs[-(keep_ref.shape[0] * upm + 1) :]
    left = lt_ref[...].astype(F32).T
    strip = left[:replica_rows]
    for i in range(1, left.shape[0] // replica_rows):
        strip = jnp.where(pos[6] == i, left[i * replica_rows : (i + 1) * replica_rows], strip)
    height = strip_ref.shape[0]
    strip = jnp.concatenate(
        [strip[i * height : (i + 1) * height] for i in range(replica_rows // height)], axis=1
    )
    strip_ref[...] = strip
    own_ref[...] = keep_ref[0, 0] + recv_ref[0, 0].astype(F32)
    for d, out in enumerate(sends, 1):
        j, i = d // upm, d % upm
        terms = keep_ref[j, i] + recv_ref[j, i].astype(F32)
        out[...] = jnp.concatenate([terms, strip], axis=0).astype(BF16)


def chip_sum(pos, keep, recv, lt, replica_rows, after):
    half, upm, unit, n = keep.shape
    height = lt.shape[0] * replica_rows // n
    vmem = pl.BlockSpec(memory_space=pltpu.VMEM)
    outs = [jax.ShapeDtypeStruct((unit, n), F32), jax.ShapeDtypeStruct((height, n), F32)]
    outs += [jax.ShapeDtypeStruct((unit + height, n), BF16)] * (half * upm - 1)
    return pl.pallas_call(
        functools.partial(chip_kernel, replica_rows),
        grid_spec=pltpu.PrefetchScalarGridSpec(
            num_scalar_prefetch=1,
            grid=(1,),
            in_specs=[vmem] * 3 + [pl.BlockSpec(memory_space=pl.ANY)] * len(after),
            out_specs=[vmem] * len(outs),
        ),
        out_shape=outs,
        compiler_params=params(),
        cost_estimate=cost(),
        name="chip_sum",
    )(pos, keep, recv, lt, *after)


def plane_kernel(pos, own_ref, strip_ref, *refs):
    n_z = own_ref.shape[1] // refs[-2].shape[1]
    terms, outs, left_ref = refs[: -n_z - 1], refs[-n_z - 1 : -1], refs[-1]
    unit, n = own_ref.shape
    cols = n // n_z
    for d, out in enumerate(outs):
        block = pl.ds(pl.multiple_of((pos[4] ^ d) * cols, cols), cols)
        parts = [own_ref[:, block]] + [term[:, block].astype(F32)[:unit] for term in terms]
        out[...] = tree_sum(parts).astype(out.dtype)
    strip = strip_ref[...]
    for d, term in enumerate(terms, 1):
        strip = jnp.where(pos[7] == d, term[...].astype(F32)[unit:], strip)
    nmat, _, rank = left_ref.shape
    width = nmat * rank
    rows = [strip[:, i * width : (i + 1) * width] for i in range(n // width)]
    rows = jnp.concatenate(rows, axis=0).astype(BF16)
    for i in range(nmat):
        left_ref[i] = rows[:, i * rank : (i + 1) * rank]


def plane_sum(pos, own, strip, terms, n_z, nmat, rank):
    unit, n = own.shape
    count = strip.size // (nmat * rank)
    outs = [jax.ShapeDtypeStruct((unit, n // n_z), BF16 if d else F32) for d in range(n_z)]
    outs.append(jax.ShapeDtypeStruct((nmat, count, rank), BF16))
    vmem = pl.BlockSpec(memory_space=pltpu.VMEM)
    return pl.pallas_call(
        plane_kernel,
        grid_spec=pltpu.PrefetchScalarGridSpec(
            num_scalar_prefetch=1,
            grid=(1,),
            in_specs=[vmem] * (2 + len(terms)),
            out_specs=[vmem] * len(outs),
        ),
        out_shape=outs,
        compiler_params=params(),
        cost_estimate=cost(),
        name="plane_sum",
    )(pos, own, strip, *terms)


def stack_kernel(count, *refs):
    for i in range(count):
        refs[-1][i] = refs[i][...]


def stack(parts, after=()):
    vmem = pl.BlockSpec(memory_space=pltpu.VMEM)
    return pl.pallas_call(
        functools.partial(stack_kernel, len(parts)),
        in_specs=[vmem] * len(parts) + [pl.BlockSpec(memory_space=pl.ANY)] * len(after),
        out_specs=vmem,
        out_shape=jax.ShapeDtypeStruct((len(parts),) + parts[0].shape, parts[0].dtype),
        compiler_params=params(),
        cost_estimate=cost(),
        name="stack",
    )(*parts, *after)


def token_kernel(*refs):
    refs[-1][...] = jnp.zeros(refs[-1].shape, F32)


def token(after):
    return pl.pallas_call(
        token_kernel,
        in_specs=[pl.BlockSpec(memory_space=pl.ANY)] * len(after),
        out_specs=pl.BlockSpec(memory_space=pltpu.VMEM),
        out_shape=jax.ShapeDtypeStruct((8, 128), F32),
        compiler_params=params(),
        cost_estimate=cost(),
        name="token",
    )(*after)


def forward_kernel(later, x_ref, y_ref, base_ref, after_ref, *outs):
    rows = base_ref.shape[1]
    for source, slot, out in ((y_ref, 1, outs[0]), (x_ref, 0, outs[1])):
        out[:rows] = source[:rows]
        out[rows:] = base_ref[slot, rows - later :]


def forward(x, y, base, after):
    _, rows, n = base.shape
    later = 2 * rows - x.shape[0]
    vmem = pl.BlockSpec(memory_space=pltpu.VMEM)
    return pl.pallas_call(
        functools.partial(forward_kernel, later),
        in_specs=[vmem] * 3 + [pl.BlockSpec(memory_space=pl.ANY)],
        out_specs=[vmem] * 2,
        out_shape=[jax.ShapeDtypeStruct((rows + later, n), BF16)] * 2,
        compiler_params=params(),
        cost_estimate=cost(),
        name="forward",
    )(x, y, base, after)


def rank_of(owners, k):
    count = jnp.int32(0)
    for j in range(owners.shape[0]):
        count += jnp.where((owners[j] == owners[k]) & (j < k), 1, 0)
    return count


def collect_kernel(square, base_ref, *refs):
    out = refs[-1]
    capacity, rows, _ = base_ref.shape
    out[:capacity] = base_ref[...]
    if not square:
        for d, ref in enumerate(refs[:-1], 1):
            out[d * capacity : (d + 1) * capacity] = ref[...]
        return
    x, y, more_x, more_y = refs[:-1]
    early = x.shape[0] - rows
    for d, slot, first, second in ((1, 0, x, more_x), (2, 1, y, more_y)):
        out[d * capacity + slot] = first[:rows]
        out[d * capacity + 1 - slot, :early] = first[rows:]
        out[d * capacity + 1 - slot, early:] = second[rows:]
    out[3 * capacity] = more_y[:rows]
    out[3 * capacity + 1] = more_x[:rows]


def collect(square, n_mp, base, parts):
    capacity, rows, n = base.shape
    vmem = pl.BlockSpec(memory_space=pltpu.VMEM)
    return pl.pallas_call(
        functools.partial(collect_kernel, square),
        in_specs=[vmem] * (1 + len(parts)),
        out_specs=vmem,
        out_shape=jax.ShapeDtypeStruct((n_mp * capacity, rows, n), BF16),
        compiler_params=params(),
        cost_estimate=cost(),
        name="collect",
    )(base, *parts)


def outputs_kernel(jobs, where, capacity, pos, owners, comp_ref, left_ref, strip_ref, base_ref, *refs):
    n_right = 1 + max(a for a, _ in (where or jobs).values())
    rights, refs = refs[:n_right], refs[n_right:]
    n_scratch = 6 if where else 3
    scratch = refs[-n_scratch:]
    feedback, weights, out_sem = scratch[:3]
    refs = refs[:-n_scratch]
    token_ref, outs = refs[-1], refs[-5:-1] if where else refs[-3:-1]
    token_ref[...] = jnp.zeros(token_ref.shape, F32)
    _, upm, n_z, _, cols = rights[0].shape
    half = comp_ref.shape[0] // CORES

    def right_of(place, d, block):
        a, entry = place
        parts = [rights[a][entry, i ^ pos[1], d, :, block] for i in range(upm)]
        return parts[0] if upm == 1 else jnp.concatenate(parts, axis=0)

    def columns(d, first=0, size=cols):
        return pl.ds(pl.multiple_of((pos[4] ^ d) * cols + first, 128), size)

    def matrix(other, j):
        return (j + half * other) ^ pos[0]

    step = 256 if cols % 256 == 0 else 128
    pieces = [slice(first, first + step) for first in range(0, cols, step)]
    stores = []

    def store(source, target, sem):
        stores.append(pltpu.make_async_copy(source, target, sem))
        stores[-1].start()

    if where:
        momentum_ref, master_ref = refs[:2]
        new_momentum, new_master, state_sem = scratch[3:]
        for c in range(capacity):
            mine = jnp.int32(-1)
            for k in range(owners.shape[0]):
                mine = jnp.where((owners[k] == pos[5]) & (rank_of(owners, k) == c), k, mine)
            safe = jnp.maximum(mine, 0)
            strip = strip_ref[safe]
            for d in range(n_z):
                for block in pieces:
                    right = jnp.zeros((strip.shape[1], step), BF16)
                    for job, place in where.items():
                        right = jnp.where(safe == matrix(*job), right_of(place, d, block), right)
                    approx = jnp.dot(strip, right, preferred_element_type=F32)
                    approx = jnp.where(mine >= 0, approx, 0.0)
                    place = columns(d, block.start, step)
                    momentum = 0.9 * momentum_ref[c, :, place] + approx
                    new_momentum[c, :, place] = momentum
                    new_master[c, :, place] = master_ref[c, :, place] - 0.1 * momentum
                place = columns(d)
                for i, new in enumerate((new_momentum, new_master)):
                    store(
                        new.at[c, :, place], outs[2 + i].at[0, c, :, place], state_sem.at[i, c, d]
                    )

    for i, (job, where_right) in enumerate(jobs.items()):
        k = matrix(*job)
        slot = (owners[k] ^ pos[5]) * capacity + rank_of(owners, k)
        left = jnp.concatenate([left_ref[k], strip_ref[k]], axis=0)
        rows = left_ref.shape[1]
        for d in range(n_z):
            for block in pieces:
                right = right_of(where_right, d, block)
                place = columns(d, block.start, step)
                approx = jnp.dot(left, right, preferred_element_type=F32)
                comp, base = comp_ref[k, :, place].astype(F32), base_ref[slot, :, place].astype(F32)
                feedback[i, :, place] = (comp - approx[:rows]).astype(BF16)
                weights[i, :, place] = (base - 0.1 * approx[rows:]).astype(BF16)
            place = columns(d)
            store(feedback.at[i, :, place], outs[0].at[0, k, :, place], out_sem.at[i, d, 0])
            store(weights.at[i, :, place], outs[1].at[k, :, place], out_sem.at[i, d, 1])

    for copy in stores:
        copy.wait()


def outputs(pos, owners, comp, left, strip, base, capacity, rights, jobs, where=None, states=(), earlier=()):
    nmat, rows, n = comp.shape
    n_z = rights[0].shape[2]
    replica_rows = base.shape[1]
    any_spec = pl.BlockSpec(memory_space=pl.ANY)
    vmem = pl.BlockSpec(memory_space=pltpu.VMEM)
    scratch = [
        pltpu.VMEM((len(jobs), rows, n), BF16),
        pltpu.VMEM((len(jobs), replica_rows, n), BF16),
        pltpu.SemaphoreType.DMA((len(jobs), n_z, 2)),
    ]
    if states:
        scratch += [pltpu.VMEM((capacity, replica_rows, n), F32)] * 2
        scratch += [pltpu.SemaphoreType.DMA((2, capacity, n_z))]
    outs = [
        jax.ShapeDtypeStruct((1, nmat, rows, n), BF16),
        jax.ShapeDtypeStruct((nmat, replica_rows, n), BF16),
    ] + [jax.ShapeDtypeStruct((1,) + x.shape, F32) for x in states]
    first = 6 + len(rights) + len(states)
    return pl.pallas_call(
        functools.partial(outputs_kernel, jobs, where, capacity),
        grid_spec=pltpu.PrefetchScalarGridSpec(
            num_scalar_prefetch=2,
            grid=(1,),
            in_specs=[vmem] * (4 + len(rights) + len(states)) + [any_spec] * len(earlier),
            out_specs=[any_spec] * len(outs) + [vmem],
            scratch_shapes=scratch,
        ),
        out_shape=outs + [jax.ShapeDtypeStruct((8, 128), F32)],
        input_output_aliases={first + i: i for i in range(len(earlier))},
        compiler_params=params(24),
        cost_estimate=cost(),
        name="outputs",
    )(pos, owners, comp, left, strip, base, *rights, *states, *earlier)


def base_kernel(pos, momentum_ref, master_ref, out_ref, momentum, master, *refs):
    firsts, sems = refs[:-1], refs[-1]
    capacity, rows, _ = out_ref.shape
    blocks = [(c, first) for c in range(capacity) for first in range(0, rows, BASE_ROWS)]

    def copies(i):
        c, first = blocks[i]
        part = pl.ds(first, BASE_ROWS)
        return [
            pltpu.make_async_copy(source.at[0, c, part], target.at[c, part], sems.at[j, i])
            for j, (source, target) in enumerate(((momentum_ref, momentum), (master_ref, master)))
        ]

    for i in range(len(blocks)):
        for copy in copies(i):
            copy.start()
    for i, (c, first) in enumerate(blocks):
        for copy in copies(i):
            copy.wait()
        part = slice(first, first + BASE_ROWS)
        out_ref[c, part] = (master[c, part] - 0.09 * momentum[c, part]).astype(BF16)
    for slot, ref in enumerate(firsts):
        ref[:rows] = out_ref[slot]
        ref[rows:] = out_ref[1 - slot, : ref.shape[0] - rows]


def base_of(pos, momentum, master, square):
    _, capacity, rows, n = momentum.shape
    state = jax.ShapeDtypeStruct((capacity, rows, n), F32)
    base = jax.ShapeDtypeStruct((capacity, rows, n), BF16)
    firsts = [jax.ShapeDtypeStruct((rows + 5 * rows // 6, n), BF16)] * (2 if square else 0)
    base, momentum, master, *firsts = pl.pallas_call(
        base_kernel,
        grid_spec=pltpu.PrefetchScalarGridSpec(
            num_scalar_prefetch=1,
            grid=(1,),
            in_specs=[pl.BlockSpec(memory_space=pl.ANY)] * 2,
            out_specs=[pl.BlockSpec(memory_space=pltpu.VMEM)] * (3 + len(firsts)),
            scratch_shapes=[pltpu.SemaphoreType.DMA((2, capacity * rows // BASE_ROWS))],
        ),
        out_shape=[base, state, state] + firsts,
        compiler_params=params(),
        cost_estimate=cost(),
        name="base",
    )(pos, momentum, master)
    return base, (momentum, master), firsts


def per_device(
    gradients,
    feedback,
    right_init,
    gram_root,
    owners,
    momentum,
    master_weights,
    vector_grads,
    vector_momentum,
    vector_params,
):
    nmat, rows, n = gradients.shape[1:]
    rank = right_init.shape[2]
    unit = rank * nmat // (CORES * lax.axis_size("mp"))
    n_mp = lax.axis_size("mp")
    n_z = lax.axis_size("replica") // CORES
    capacity, replica_rows = momentum.shape[1:3]
    p = lax.axis_index("mp")
    r = lax.axis_index("replica")
    core, z = r % CORES, r // CORES
    upm = CORES * n_mp // nmat
    half = nmat // CORES
    code = core * n_mp + p
    first = r * replica_rows

    places_of = [code // upm, code % upm, core, r, z, p, first % rows // replica_rows, first // rows ^ p]
    pos = jnp.stack(places_of).astype(jnp.int32)
    in_hbm = lambda x: pltpu.with_memory_space_constraint(x, pltpu.HBM)

    square = n_mp == 4 and capacity == 2 and replica_rows % 96 == 0
    base, states, firsts = base_of(pos, in_hbm(momentum), in_hbm(master_weights), square)
    firsts = firsts or [base] * (n_mp - 1)
    early = [exchange(part, "mp", d) for d, part in enumerate(firsts, 1)]

    nvec = vector_grads.shape[1]
    comp, near, far = left_terms(
        pos,
        in_hbm(gradients),
        in_hbm(feedback),
        in_hbm(jnp.swapaxes(right_init, 1, 2)),
        vector_grads,
    )
    piece = add([near, exchange(far, "replica", 1)], BF16)
    along_z = lambda x: [exchange(x, "replica", CORES * d) for d in range(1, n_z)]
    piece = add([piece] + along_z(piece), F32)
    near, far = piece, exchange(piece, "replica", 1)

    send, keep, lt, left, vector_rows = right_terms(pos, near, far, gram_root, comp, upm, [])
    vector_total = vector_rows.reshape(-1)[:nvec]
    recv = exchange(send, "replica", 1)
    own, strip, *chip = chip_sum(pos, keep, recv, lt, replica_rows, [token([keep] + early)])
    plane = [exchange(part, "mp", d) for d, part in enumerate(chip, 1)]
    *final, mine = plane_sum(pos, own, strip, plane, n_z, nmat, rank)
    late = []
    if square:
        late = [exchange(part, "mp", d) for d, part in enumerate(forward(*early, base, mine), 1)]
    final = [final[0]] + [exchange(final[d], "replica", CORES * d) for d in range(1, n_z)]
    final = add(final, BF16)
    new_vector_momentum = 0.9 * vector_momentum + vector_total
    new_vector_params = vector_params - 0.1 * new_vector_momentum

    whole = stack([final] + along_z(final), late + [new_vector_params])
    others = [exchange(whole, "mp", d) for d in range(1, n_mp)]
    slots = collect(square, n_mp, base, early + late)
    common = (pos, owners, comp, left, mine, slots, capacity)
    shape = (half, upm) + whole.shape
    done, near_jobs, after = (), {(0, j): (0, j) for j in range(half)}, [slots]
    if upm == 1:
        *done, _ = outputs(*common, [whole[None, None]], {(0, 0): (0, 0)})
        *done, after = outputs(
            *common, [others[-1][None, None]], {(0, half - 1): (0, 0)}, earlier=done
        )
        after = [after]
        del near_jobs[0, 0], near_jobs[0, half - 1]
    near = stack([whole] + others, after).reshape(shape)
    far = exchange(near, "replica", 1)
    far_jobs = {(1, j): (1, j) for j in range(half)}
    where = {(0, j): (0, j) for j in range(half)} | far_jobs
    *done, _ = outputs(*common, [near], near_jobs, earlier=done)
    new_feedback, new_weights, new_momentum, new_master, _ = outputs(
        *common, [near, far], far_jobs, where, states, done
    )
    return new_feedback, new_momentum, new_master, new_weights, new_vector_momentum, new_vector_params


def solution(mesh):
    return jax.shard_map(
        per_device,
        mesh=mesh,
        in_specs=(
            P("replica", None, "mp", None),
            P("replica", None, "mp", None),
            P(),
            P(),
            P(),
            P("mp", None, "replica", None),
            P("mp", None, "replica", None),
            P("replica", "mp"),
            P("mp"),
            P("mp"),
        ),
        out_specs=(
            P("replica", None, "mp", None),
            P("mp", None, "replica", None),
            P("mp", None, "replica", None),
            P(None, "replica", None),
            P("mp"),
            P("mp"),
        ),
        check_vma=False,
    )
```
